32 devices in a mesh: batch: 8 (over y, x, core), height: 4 (over z).
Axes of the slice: x: 2, y: 2, z: 4, core: 2. Of those that a mesh axis runs over, the one named last changes fastest.
Arguments:
- image_glob: bfloat16 [96, 32, 32, 192], P('batch', 'height'), may hold values from -10.5 to 10.5
- image_loc: bfloat16 [144, 16, 16, 192], P('batch', 'height'), may hold values from -10.5 to 10.5
- cot_glob: bfloat16 [96, 16, 16, 512], P('batch', 'height'), may hold values from -10.5 to 10.5
- cot_loc: bfloat16 [144, 8, 8, 512], P('batch', 'height'), may hold values from -10.5 to 10.5
- weights: float32 [1753088], P(('batch', 'height')), may hold values from -0.6639528 to 0.6639528
- first_moment: float32 [1753088], P(('batch', 'height')), may hold values from -24.632685 to 24.632685
- second_moment: float32 [1753088], P(('batch', 'height')), may hold values from 0.0408 to 68.93568
- vectors: float32 [8368], replicated, may hold values from -1.5 to 1.5
- vec_first: float32 [8368], replicated, may hold values from -29.41216 to 29.41216
- vec_second: float32 [8368], replicated, may hold values from 0.24 to 67.584
Outputs:
- out_glob: bfloat16 [96, 16, 16, 512], P('batch', 'height')
- out_loc: bfloat16 [144, 8, 8, 512], P('batch', 'height')
- grad_glob: float32 [96, 32, 32, 192], P('batch', 'height')
- grad_loc: float32 [144, 16, 16, 192], P('batch', 'height')
- new_weights: float32 [1753088], P(('batch', 'height'))
- new_first: float32 [1753088], P(('batch', 'height'))
- new_second: float32 [1753088], P(('batch', 'height'))
- new_vectors: float32 [8368], replicated
- new_vec_first: float32 [8368], replicated
- new_vec_second: float32 [8368], replicated
- norms: float32 [2, 11], replicated
The draws below stay inside these ranges and needn't reach their ends.
All inputs are finite; a program needn't handle non-finite values.
Results may differ from the reference program's by a relative error of at most 0.019.
Values may be sent and summed in bfloat16 or wider, within the bound.
No kernel may reach another device: no remote copies, remote signals or barrier semaphores. Data moves between devices by JAX's collectives and lax.ppermute only.
A program may use at most 256 MiB of HBM per device.

```python
import math
import jax
import jax.numpy as jnp
from jax import lax

CIN = 192
C = 512
GW = 64
GROUPS = 8
SE_A = 48
SE_B = 128
GSIDE = 32
LSIDE = 16
STEP = 10
GLOB = 96
LOC = 144
N_BATCH = 8


beta_one = 0.9


beta_two = 0.999


def rising(amount, low_end, high_end):
    place = jnp.arange(amount, dtype=jnp.float32) / max(amount - 1, 1)
    return low_end * (high_end / low_end) ** place


def spread_field(values, low_end, high_end):
    crop_scale = rising(values.shape[0], low_end, high_end)
    row_scale = rising(values.shape[1], low_end, high_end)
    return values * crop_scale[:, None, None, None] * row_scale[None, :, None, None]


def grad_sizes():
    npos_in = GLOB * GSIDE * GSIDE + LOC * LSIDE * LSIDE
    return (0.3 * math.sqrt(npos_in), 0.5 * math.sqrt(npos_in // 4), 0.5 * math.sqrt(GLOB + LOC))


def matrix_table():
    size_in, size_out, size_img = grad_sizes()
    return [(CIN, C, CIN, size_in), (9 * GW, C, 9 * GW, size_out), (C, SE_A, C, size_img), (SE_A, C, SE_A, size_img), (C, C, C, size_out), (CIN, C, CIN, size_out), (C, C, C, size_out), (9 * GW, C, 9 * GW, size_out), (C, SE_B, C, size_img), (SE_B, C, SE_B, size_img), (C, C, C, size_out)]


def vector_table():
    size_in, size_out, size_img = grad_sizes()
    norm_out = 1.4 * size_out
    se_size = 2.0 * size_img
    return [(C, 1, size_in), (C, 0, size_in), (C, 1, norm_out), (C, 0, norm_out), (SE_A, 2, se_size), (C, 2, se_size), (C, 1, norm_out), (C, 0, norm_out), (C, 1, norm_out), (C, 0, norm_out), (C, 1, norm_out), (C, 0, norm_out), (C, 1, norm_out), (C, 0, norm_out), (SE_B, 2, se_size), (C, 2, se_size), (C, 1, norm_out), (C, 0, norm_out)]


def signed_sizes(key, dims_all):
    key_one, key_two = jax.random.split(key)
    sign_val = jnp.where(jax.random.bernoulli(key_one, 0.5, dims_all), 1.0, -1.0)
    size_val = jnp.exp(jax.random.uniform(key_two, dims_all, jnp.float32, math.log(0.5), math.log(2.0)))
    return sign_val * size_val


def draw_image_glob(key, part):
    key = jax.random.fold_in(key, 1)
    dims_all = (GLOB, GSIDE, GSIDE, CIN)
    return spread_field(jax.random.truncated_normal(key, -3.0, 3.0, dims_all, jnp.float32), 0.6, 1.8).astype(jnp.bfloat16)


def draw_image_loc(key, part):
    key = jax.random.fold_in(key, 2)
    dims_all = (LOC, LSIDE, LSIDE, CIN)
    return spread_field(jax.random.truncated_normal(key, -3.0, 3.0, dims_all, jnp.float32), 0.6, 1.8).astype(jnp.bfloat16)


def draw_cot_glob(key, part):
    key = jax.random.fold_in(key, 3)
    dims_all = (GLOB, GSIDE // 2, GSIDE // 2, C)
    return spread_field(jax.random.truncated_normal(key, -3.0, 3.0, dims_all, jnp.float32), 0.6, 1.8).astype(jnp.bfloat16)


def draw_cot_loc(key, part):
    key = jax.random.fold_in(key, 4)
    dims_all = (LOC, LSIDE // 2, LSIDE // 2, C)
    return spread_field(jax.random.truncated_normal(key, -3.0, 3.0, dims_all, jnp.float32), 0.6, 1.8).astype(jnp.bfloat16)


def draw_weights(key, part):
    key = jax.random.fold_in(key, 5)
    pieces = []
    for position, table_row in enumerate(matrix_table()):
        n_rows, n_cols, fan_in, grad_size = table_row
        sub_key = jax.random.fold_in(key, position)
        values = jax.random.truncated_normal(sub_key, -2.5, 2.5, (n_rows, n_cols), jnp.float32)
        row_scale = rising(n_rows, 0.6, 1.8)
        pieces.append((values * row_scale[:, None] / math.sqrt(fan_in)).reshape(-1))
    return jnp.concatenate(pieces)


def draw_first_moment(key, part):
    key = jax.random.fold_in(key, 6)
    pieces = []
    for position, table_row in enumerate(matrix_table()):
        n_rows, n_cols, fan_in, grad_size = table_row
        values = signed_sizes(jax.random.fold_in(key, position), (n_rows, n_cols))
        pieces.append((values * grad_size * (1.0 - beta_one) / beta_one).reshape(-1))
    return jnp.concatenate(pieces)


def draw_second_moment(key, part):
    key = jax.random.fold_in(key, 7)
    pieces = []
    for position, table_row in enumerate(matrix_table()):
        n_rows, n_cols, fan_in, grad_size = table_row
        place = jnp.arange(n_rows, dtype=jnp.float32) / max(n_rows - 1, 1)
        decline = 1.0 + 3.0 * (1.0 - place)
        size_val = jnp.exp(jax.random.uniform(jax.random.fold_in(key, position), (n_rows, n_cols), jnp.float32, math.log(0.7), math.log(1.4)))
        values = size_val * decline[:, None] * grad_size * grad_size * (1.0 - beta_two) / beta_two
        pieces.append(values.reshape(-1))
    return jnp.concatenate(pieces)


def draw_vectors(key, part):
    key = jax.random.fold_in(key, 8)
    pieces = []
    for position, table_row in enumerate(vector_table()):
        length, kind_val, grad_size = table_row
        sub_key = jax.random.fold_in(key, position)
        if kind_val == 1:
            pieces.append(jax.random.uniform(sub_key, (length,), jnp.float32, 0.5, 1.5))
        elif kind_val == 0:
            pieces.append(0.3 * jax.random.truncated_normal(sub_key, -3.0, 3.0, (length,), jnp.float32))
        else:
            pieces.append(0.5 * jax.random.truncated_normal(sub_key, -3.0, 3.0, (length,), jnp.float32))
    return jnp.concatenate(pieces)


def draw_vec_first(key, part):
    key = jax.random.fold_in(key, 9)
    pieces = []
    for position, table_row in enumerate(vector_table()):
        length, kind_val, grad_size = table_row
        values = signed_sizes(jax.random.fold_in(key, position), (length,))
        pieces.append(values * grad_size * (1.0 - beta_one) / beta_one)
    return jnp.concatenate(pieces)


def draw_vec_second(key, part):
    key = jax.random.fold_in(key, 10)
    pieces = []
    for position, table_row in enumerate(vector_table()):
        length, kind_val, grad_size = table_row
        size_val = 2.0 * jnp.exp(jax.random.uniform(jax.random.fold_in(key, position), (length,), jnp.float32, math.log(0.5), math.log(2.0)))
        pieces.append(size_val * grad_size * grad_size * (1.0 - beta_two) / beta_two)
    return jnp.concatenate(pieces)


def setup_inputs(seed: int = 0) -> dict:
    key_of = jax.random.split(jax.random.key(seed), 11)
    image_glob = draw_image_glob(jax.random.fold_in(key_of[10], 71), 0)
    image_loc = draw_image_loc(jax.random.fold_in(key_of[10], 71), 0)
    cot_glob = draw_cot_glob(jax.random.fold_in(key_of[10], 71), 0)
    cot_loc = draw_cot_loc(jax.random.fold_in(key_of[10], 71), 0)
    weights = draw_weights(jax.random.fold_in(key_of[10], 71), 0)
    first_moment = draw_first_moment(jax.random.fold_in(key_of[10], 71), 0)
    second_moment = draw_second_moment(jax.random.fold_in(key_of[10], 71), 0)
    vectors = draw_vectors(jax.random.fold_in(key_of[10], 71), 0)
    vec_first = draw_vec_first(jax.random.fold_in(key_of[10], 71), 0)
    vec_second = draw_vec_second(jax.random.fold_in(key_of[10], 71), 0)
    return {"image_glob": image_glob, "image_loc": image_loc, "cot_glob": cot_glob, "cot_loc": cot_loc, "weights": weights, "first_moment": first_moment, "second_moment": second_moment, "vectors": vectors, "vec_first": vec_first, "vec_second": vec_second}


norm_eps = 1e-05
beta_one = 0.9
beta_two = 0.999
adam_eps = 1e-06
weight_decay = 0.01
learn_rate = 0.4
highest = lax.Precision.HIGHEST

@jax.custom_vjp
def low(v):
    return lax.optimization_barrier(v.astype(jnp.bfloat16)).astype(jnp.float32)

@jax.custom_vjp
def low_back(v):
    return v

def low_keep(v):
    return (low(v), None)

def low_pass(kept, grad):
    return (grad,)

def back_keep(v):
    return (v, None)

def back_low(kept, grad):
    return (low(grad),)
low.defvjp(low_keep, low_pass)
low_back.defvjp(back_keep, back_low)

def matrix_shapes():
    return [(CIN, C), (9 * GW, C), (C, SE_A), (SE_A, C), (C, C), (CIN, C), (C, C), (9 * GW, C), (C, SE_B), (SE_B, C), (C, C)]

def vector_sizes():
    return [C, C, C, C, SE_A, C, C, C, C, C, C, C, C, C, SE_B, C, C, C]

def cut_pieces(flat_vec, lengths):
    pieces = []
    offset = 0
    for length in lengths:
        pieces.append(flat_vec[offset:offset + length])
        offset += length
    return pieces

def point_conv(tensor, weight):
    return jnp.einsum('nhwc,cd->nhwd', tensor, weight, precision=highest)

def pad_both(tensor):
    return jnp.pad(tensor, ((0, 0), (1, 1), (1, 1), (0, 0)))

def group_conv(padded, weight, stride, out_rows, out_cols):
    total_sum = 0.0
    for tap_idx in range(9):
        row_off = tap_idx // 3
        col_off = tap_idx % 3
        window = padded[:, row_off:row_off + stride * (out_rows - 1) + 1:stride, col_off:col_off + stride * (out_cols - 1) + 1:stride, :]
        window = window.reshape(window.shape[:3] + (GROUPS, GW))
        kernel = weight[tap_idx * GW:(tap_idx + 1) * GW].reshape(GW, GROUPS, GW)
        total_sum = total_sum + jnp.einsum('nhwgi,igo->nhwgo', window, kernel, precision=highest)
    return total_sum.reshape(total_sum.shape[:3] + (GROUPS * GW,))

def batch_norm(conv_pair, gain_vec, shift_vec):
    grouped = [tensor.reshape((N_BATCH, tensor.shape[0] // N_BATCH) + tensor.shape[1:]) for tensor in conv_pair]
    amount = sum((group_one.shape[1] * group_one.shape[2] * group_one.shape[3] for group_one in grouped))
    mean_val = sum((lax.optimization_barrier(jnp.sum(group_one, axis=(1, 2, 3))) for group_one in grouped)) / amount
    centered = [group_one - mean_val[:, None, None, None, :] for group_one in grouped]
    var_val = sum((lax.optimization_barrier(jnp.sum(cent_one * cent_one, axis=(1, 2, 3))) for cent_one in centered)) / amount
    scale_val = lax.rsqrt(var_val + norm_eps)[:, None, None, None, :]
    return tuple(((cent_one * scale_val * gain_vec + shift_vec).reshape(tensor.shape) for cent_one, tensor in zip(centered, conv_pair)))

def squeeze_excite(act_pair, w_down, b_down, w_up, b_up):
    result = []
    for tensor in act_pair:
        pooled = lax.optimization_barrier(jnp.mean(tensor, axis=(1, 2)))
        hidden = jax.nn.silu(jnp.dot(pooled, w_down, precision=highest) + b_down)
        gate_val = jax.nn.sigmoid(jnp.dot(hidden, w_up, precision=highest) + b_up)
        result.append(tensor * gate_val[:, None, None, :])
    return tuple(result)

def forward(flat_w, flat_v, glob_in, loc_in):
    shapes = matrix_shapes()
    lengths = [dims_pair[0] * dims_pair[1] for dims_pair in shapes]
    matrices = [flat_piece.reshape(dims_pair) for flat_piece, dims_pair in zip(cut_pieces(low(flat_w), lengths), shapes)]
    vector_list = cut_pieces(flat_v, vector_sizes())
    inputs = (glob_in, loc_in)
    conv_a = tuple((low_back(point_conv(image_one, matrices[0])) for image_one in inputs))
    act_a = tuple((low(jax.nn.silu(norm_one)) for norm_one in batch_norm(conv_a, vector_list[0], vector_list[1])))
    conv_b = tuple((low_back(group_conv(pad_both(act_one), matrices[1], 2, act_one.shape[1] // 2, act_one.shape[2] // 2)) for act_one in act_a))
    act_b = tuple((jax.nn.silu(norm_one) for norm_one in batch_norm(conv_b, vector_list[2], vector_list[3])))
    gated_b = tuple((low(gated_one) for gated_one in squeeze_excite(act_b, matrices[2], vector_list[4], matrices[3], vector_list[5])))
    conv_c = tuple((low_back(point_conv(gated_one, matrices[4])) for gated_one in gated_b))
    conv_s = tuple((low_back(point_conv(image_one[:, ::2, ::2], matrices[5])) for image_one in inputs))
    norm_c = batch_norm(conv_c, vector_list[6], vector_list[7])
    norm_s = batch_norm(conv_s, vector_list[8], vector_list[9])
    middle = tuple((jax.nn.silu(c_one + s_one) for c_one, s_one in zip(norm_c, norm_s)))
    conv_d = tuple((low_back(point_conv(low(mid_one), matrices[6])) for mid_one in middle))
    act_d = tuple((low(jax.nn.silu(norm_one)) for norm_one in batch_norm(conv_d, vector_list[10], vector_list[11])))
    conv_e = tuple((low_back(group_conv(pad_both(act_one), matrices[7], 1, act_one.shape[1], act_one.shape[2])) for act_one in act_d))
    act_e = tuple((jax.nn.silu(norm_one) for norm_one in batch_norm(conv_e, vector_list[12], vector_list[13])))
    gated_e = tuple((low(gated_one) for gated_one in squeeze_excite(act_e, matrices[8], vector_list[14], matrices[9], vector_list[15])))
    conv_f = tuple((low_back(point_conv(gated_one, matrices[10])) for gated_one in gated_e))
    norm_f = batch_norm(conv_f, vector_list[16], vector_list[17])
    return tuple((jax.nn.silu(mid_one + f_one) for mid_one, f_one in zip(middle, norm_f)))

def lamb_terms(param, grad_val, first_old, second_old, decay):
    first_new = beta_one * first_old + (1.0 - beta_one) * grad_val
    second_new = beta_two * second_old + (1.0 - beta_two) * grad_val * grad_val
    update = first_new / (1.0 - beta_one ** STEP) / (jnp.sqrt(second_new / (1.0 - beta_two ** STEP)) + adam_eps) + decay * param
    return (first_new, second_new, update)

def reference(image_glob, image_loc, cot_glob, cot_loc, weights, first_moment, second_moment, vectors, vec_first, vec_second):
    glob_in = image_glob.astype(jnp.float32)
    loc_in = image_loc.astype(jnp.float32)
    outputs, pullback = jax.vjp(forward, weights, vectors, glob_in, loc_in)
    grad_w, grad_v, grad_glob, grad_loc = pullback((cot_glob.astype(jnp.float32), cot_loc.astype(jnp.float32)))
    new_first, new_second, update = lamb_terms(weights, grad_w, first_moment, second_moment, weight_decay)
    lengths = [dims_pair[0] * dims_pair[1] for dims_pair in matrix_shapes()]
    new_pieces = []
    norm_rows = []
    for w_piece, u_piece in zip(cut_pieces(weights, lengths), cut_pieces(update, lengths)):
        w_norm = jnp.sqrt(jnp.sum(w_piece * w_piece))
        u_norm = jnp.sqrt(jnp.sum(u_piece * u_piece))
        new_pieces.append(w_piece - learn_rate * (w_norm / u_norm) * u_piece)
        norm_rows.append(jnp.stack([w_norm, u_norm]))
    new_weights = jnp.concatenate(new_pieces)
    norms = jnp.stack(norm_rows, axis=1)
    vec_one_new, vec_two_new, vec_update = lamb_terms(vectors, grad_v, vec_first, vec_second, 0.0)
    vec_pieces = []
    for p_piece, u_piece in zip(cut_pieces(vectors, vector_sizes()), cut_pieces(vec_update, vector_sizes())):
        ratio_val = jnp.sqrt(jnp.sum(p_piece * p_piece)) / jnp.sqrt(jnp.sum(u_piece * u_piece))
        vec_pieces.append(p_piece - learn_rate * ratio_val * u_piece)
    new_vectors = jnp.concatenate(vec_pieces)
    return (outputs[0].astype(jnp.bfloat16), outputs[1].astype(jnp.bfloat16), grad_glob, grad_loc, new_weights, new_first, new_second, new_vectors, vec_one_new, vec_two_new, norms)
```

```python
import functools

import jax
import jax.numpy as jnp
import numpy as np
from jax import lax
from jax.experimental import pallas as pl
from jax.experimental.pallas import tpu as pltpu
from jax.sharding import PartitionSpec as P

CIN = 192
C = 512
GW = 64
GROUPS = 8
SE_A = 48
SE_B = 128
STEP = 10
HID = 128
HALF = 256

norm_eps = 1e-05
beta_one = 0.9
beta_two = 0.999
adam_eps = 1e-06
weight_decay = 0.01
learn_rate = 0.4
highest = lax.Precision.HIGHEST
bf16 = jnp.bfloat16
f32 = jnp.float32
both_axes = ("batch", "height")

G1A, B1A, G1B, B1B, F1, G1C, B1C, G1S, B1S, G2A, B2A, G2B, B2B, F2, G2C, B2C = range(16)


def matrix_shapes():
    return [
        (CIN, C),
        (9 * GW, C),
        (C, SE_A),
        (SE_A, C),
        (C, C),
        (CIN, C),
        (C, C),
        (9 * GW, C),
        (C, SE_B),
        (SE_B, C),
        (C, C),
    ]


def vector_sizes():
    return [C, C, C, C, SE_A, C, C, C, C, C, C, C, C, C, SE_B, C, C, C]


def cut_pieces(flat_vec, lengths):
    pieces = []
    offset = 0
    for length in lengths:
        pieces.append(flat_vec[offset : offset + length])
        offset += length
    return pieces


class Sizes:
    def __init__(self, image_glob, image_loc, n_height):
        self.ng, self.hg, self.wg = image_glob.shape[:3]
        self.nl, self.hl, self.wl = image_loc.shape[:3]
        self.rg, self.cg = self.hg // 2, self.wg // 2
        self.rl, self.cl = self.hl // 2, self.wl // 2
        self.bg, self.bl = self.ng * self.cg, self.nl * self.cl
        self.mg, self.ml = self.rg * self.bg, self.rl * self.bl
        self.m = self.mg + self.ml
        self.edge = self.bg + self.bl
        self.n_height = n_height
        self.crops = -(-(self.ng + self.nl) // 16) * 16
        self.area_g = self.rg * self.cg * n_height
        self.area_l = self.rl * self.cl * n_height
        self.amount = n_height * self.m
        self.one_l = (self.rg + 1) * self.bg
        self.one = self.one_l + (self.rl + 1) * self.bl
        self.two_l = (self.rg + 2) * self.bg
        self.two = self.two_l + (self.rl + 2) * self.bl


def sigmoid(v):
    return 0.5 * jnp.tanh(0.5 * v) + 0.5


def silu(v):
    return v * sigmoid(v)


def silu_slope(v):
    s = sigmoid(v)
    return s * (1.0 + v * (1.0 - s))


def padded_bytes(shape, dtype):
    size = np.dtype(dtype).itemsize
    dims = list(shape)
    dims[-1] = -(-dims[-1] // 128) * 128
    if len(dims) > 1:
        rows = 32 // size
        dims[-2] = -(-dims[-2] // rows) * rows
    return int(np.prod(dims)) * size


def call(kernel, outs, scratch, *ins, flops=0, smem=0, name=None):
    total = sum(padded_bytes(a.shape, a.dtype) for a in list(ins[smem:]) + list(outs))
    total += sum(padded_bytes(s.shape, s.dtype) for s in scratch)
    touched = sum(a.size * a.dtype.itemsize for a in list(ins) + list(outs))
    return pl.pallas_call(
        kernel,
        out_shape=tuple(outs),
        in_specs=[pl.BlockSpec(memory_space=pltpu.SMEM)] * smem
        + [pl.BlockSpec(memory_space=pltpu.VMEM)] * (len(ins) - smem),
        out_specs=tuple(pl.BlockSpec(memory_space=pltpu.VMEM) for _ in outs),
        scratch_shapes=list(scratch),
        compiler_params=pltpu.CompilerParams(
            vmem_limit_bytes=min(int(total * 1.1) + 6 * 2**20, 56 * 2**20)
        ),
        cost_estimate=pl.CostEstimate(flops=int(flops), bytes_accessed=touched, transcendentals=0),
        name=name,
    )(*ins)


def out(shape, dtype=f32):
    return jax.ShapeDtypeStruct(shape, dtype)


def fold(x):
    return jnp.sum(x.reshape(x.shape[0] // 8, 8, x.shape[1]), axis=0)


def rows_at(start, size, unit=16):
    return pl.ds(pl.multiple_of(start, unit), size)


def put_rows(ref, parts):
    ref[...] = jnp.zeros_like(ref)
    for k, part in enumerate(parts):
        ref[k : k + 1, :] = jnp.sum(part, axis=0, keepdims=True)


def gather_sum(refs):
    total = refs[0][...]
    for ref in refs[1:]:
        total = total + ref[...]
    return total


def norm_terms(total, row, amount, gain, shift):
    mean = total[row : row + 1] / amount
    inverse = lax.rsqrt(total[row + 1 : row + 2] / amount - mean * mean + norm_eps)
    scale = gain * inverse
    return mean, inverse, scale, shift - mean * scale


def put_norm(ref, row, terms):
    for k, term in enumerate(terms):
        ref[row + k : row + k + 1, :] = term


def dot(a, b):
    return jnp.dot(a, b, preferred_element_type=f32)


def dot_t(a, b):
    return lax.dot_general(a, b, (((1,), (1,)), ((), ())), preferred_element_type=f32)


def t_dot(a, b):
    return lax.dot_general(a, b, (((0,), (0,)), ((), ())), preferred_element_type=f32)


def prepare_kernel(sz, ig_ref, il_ref, x_ref, halo_ref, s_ref, t_ref):
    m = sz.m

    def split(x, n_rows):
        s_ref[0:n_rows, :] = x[:, :128]
        t_ref[0:n_rows, 0:64] = x[:, 128:]
        parts = []
        for pc in range(2):
            v = s_ref[pl.ds(pc, n_rows // 2, stride=2), :]
            w = t_ref[pl.ds(pc, n_rows // 2, stride=2), :]
            parts.append(jnp.concatenate([v, w[:, :64]], axis=1))
        return parts

    @pl.loop(0, sz.ng)
    def _(n):
        n_rows = sz.hg * sz.wg
        parts = split(ig_ref[n].astype(f32).reshape(n_rows, CIN), n_rows)
        for pc in range(2):
            v = parts[pc].reshape(sz.hg, sz.cg, CIN).astype(bf16)
            for r in range(sz.hg):
                phase = 2 * (r % 2) + pc
                x_ref[rows_at(phase * m + (r // 2) * sz.bg + n * sz.cg, sz.cg), :] = v[r]

    @pl.loop(0, sz.nl // 2)
    def _(pair):
        n_rows = 2 * sz.hl * sz.wl
        both = jnp.concatenate(
            [
                il_ref[2 * pair + k].astype(f32).reshape(sz.hl * sz.wl, CIN)
                for k in range(2)
            ],
            axis=0,
        )
        parts = split(both, n_rows)
        for pc in range(2):
            v = parts[pc].reshape(2 * sz.hl, sz.cl, CIN)
            for r in range(sz.hl):
                phase = 2 * (r % 2) + pc
                joined = jnp.concatenate([v[r], v[sz.hl + r]], axis=0).astype(bf16)
                x_ref[
                    rows_at(phase * m + sz.mg + (r // 2) * sz.bl + pair * 2 * sz.cl, 2 * sz.cl), :
                ] = joined

    for pc in range(2):
        base = (2 + pc) * m
        halo_ref[pc * sz.edge : pc * sz.edge + sz.bg, :] = x_ref[
            base + sz.mg - sz.bg : base + sz.mg, :
        ]
        halo_ref[pc * sz.edge + sz.bg : (pc + 1) * sz.edge, :] = x_ref[
            base + m - sz.bl : base + m, :
        ]


def input_stats_kernel(sz, x_ref, w_ref, s_ref, zs_ref, st_ref):
    n_rows = sz.m // 3
    zero = jnp.zeros((8, C), f32)

    def step(i, carry):
        total, square = carry
        z = dot(x_ref[rows_at(i * n_rows, n_rows), :], w_ref[...])
        return total + fold(z), square + fold(z * z)

    sum_a, sq_a = lax.fori_loop(0, 12, step, (zero, zero))

    def step_s(i, carry):
        total, square = carry
        z = dot(x_ref[rows_at(i * n_rows, n_rows), :], s_ref[...])
        zs_ref[rows_at(i * n_rows, n_rows), :] = z
        return total + fold(z), square + fold(z * z)

    sum_s, sq_s = lax.fori_loop(0, 3, step_s, (zero, zero))
    put_rows(st_ref, [sum_a, sq_a, sum_s, sq_s])


def block_diagonal_kernel(k_ref, bd_ref):
    rows = lax.broadcasted_iota(jnp.int32, (HALF, HALF), 0) // GW
    cols = lax.broadcasted_iota(jnp.int32, (HALF, HALF), 1) // GW
    same = rows == cols
    for tap in range(9):
        for half in range(2):
            k = k_ref[tap * GW : (tap + 1) * GW, half * HALF : (half + 1) * HALF].astype(f32)
            bd_ref[2 * tap + half] = jnp.where(same, jnp.concatenate([k] * 4, axis=0), 0.0).astype(
                bf16
            )


def block_dense(acc):
    rows = lax.broadcasted_iota(jnp.int32, (HALF, HALF), 0) // GW
    cols = lax.broadcasted_iota(jnp.int32, (HALF, HALF), 1) // GW
    kept = jnp.where(rows == cols, acc, 0.0)
    return jnp.sum(kept.reshape(4, GW, HALF), axis=0)


def shifted(v, by, width):
    n_rows = v.shape[0]
    col = lax.broadcasted_iota(jnp.int32, v.shape, 0) % width
    if by < 0:
        return jnp.where(col == 0, 0.0, pltpu.roll(v, 1, 0))
    return jnp.where(col == width - 1, 0.0, pltpu.roll(v, n_rows - 1, 0))


def segments(sz):
    g_rows = 4 * sz.cg
    l_rows = 6 * sz.cl
    return g_rows, l_rows


def conv_product(windows, bd_ref, half, n_rows, transposed):
    acc = None
    cols = pl.ds(pl.multiple_of(half * HALF, HALF), HALF)
    for tap, ref, start in windows:
        x = ref[start : start + n_rows, cols]
        w = bd_ref[2 * tap + half]
        term = dot_t(x, w) if transposed else dot(x, w)
        acc = term if acc is None else acc + term
    return acc


def windows_one(sz, refs, part):
    a00, a01, a01s, a10, a11, a11s = refs
    plain = 0 if part == "g" else sz.mg
    above = 0 if part == "g" else sz.one_l
    here = above + (sz.bg if part == "g" else sz.bl)
    result = []
    for tap in range(9):
        a, b = tap // 3, tap % 3
        if a == 1:
            result.append((tap, (a01s, a00, a01)[b], plain))
        else:
            result.append((tap, (a11s, a10, a11)[b], above if a == 0 else here))
    return result


def windows_two(sz, refs, part, flipped=False):
    base = 0 if part == "g" else sz.two_l
    block = sz.bg if part == "g" else sz.bl
    result = []
    for tap in range(9):
        a, b = tap // 3, tap % 3
        if flipped:
            a, b = 2 - a, 2 - b
        result.append((tap, refs[b], base + a * block))
    return result


def shift_windows(windows, by):
    return [(tap, ref, start + by) for tap, ref, start in windows]


def conv_forward(sz, windows_of, bd_ref, z_ref, st_ref, sums):
    sums[...] = jnp.zeros_like(sums)

    @pl.loop(0, 2)
    def _(half):
        cols = pl.ds(pl.multiple_of(half * HALF, HALF), HALF)
        for part, first, n_all, n_rows in (
            ("g", 0, sz.mg, sz.mg // 2),
            ("l", sz.mg, sz.ml, sz.ml),
        ):
            for k in range(n_all // n_rows):
                z = conv_product(
                    shift_windows(windows_of(part), k * n_rows), bd_ref, half, n_rows, False
                )
                z_ref[first + k * n_rows : first + (k + 1) * n_rows, cols] = z
                sums[0:8, cols] += fold(z)
                sums[8:16, cols] += fold(z * z)

    put_rows(st_ref, [sums[0:8, :], sums[8:16, :]])


def first_conv_kernel(
    sz,
    flag_ref,
    x_ref,
    halo_ref,
    w_ref,
    bd_ref,
    t0,
    t1,
    t2,
    t3,
    vt_ref,
    z_ref,
    st_ref,
    nrm_ref,
    a00,
    a01,
    a01s,
    a10,
    a11,
    a11s,
    zs,
    sums,
):
    total = gather_sum((t0, t1, t2, t3))
    terms = norm_terms(
        total, 0, 4 * sz.amount, vt_ref[G1A : G1A + 1, :], vt_ref[B1A : B1A + 1, :]
    )
    nrm_ref[...] = jnp.zeros_like(nrm_ref)
    put_norm(nrm_ref, 0, terms)
    put_norm(
        nrm_ref,
        4,
        norm_terms(total, 2, sz.amount, vt_ref[G1S : G1S + 1, :], vt_ref[B1S : B1S + 1, :]),
    )
    scale, shift = terms[2], terms[3]
    g_rows, l_rows = segments(sz)
    third = sz.m // 3

    def activate(src, dst, dst_s, n_rows, width, factor=None):
        v = zs[src, :] * scale + shift
        a = silu(v)
        if factor is not None:
            a = a * factor
        dst[0][dst[1], :] = a.astype(bf16)
        if dst_s is not None:
            dst_s[dst[1], :] = shifted(a, -1, width).astype(bf16)

    plan = [(a00, None, False), (a01, a01s, False), (a10, None, True), (a11, a11s, True)]
    for phase, (dst, dst_s, bordered) in enumerate(plan):

        @pl.loop(0, 3)
        def _(i):
            zs[rows_at(i * third, third), :] = dot(
                x_ref[rows_at(phase * sz.m + i * third, third), :], w_ref[...]
            )

        g_first = sz.bg if bordered else 0
        l_first = sz.one_l + sz.bl if bordered else sz.mg

        @pl.loop(0, sz.mg // g_rows)
        def _(i):
            activate(
                rows_at(i * g_rows, g_rows),
                (dst, rows_at(g_first + i * g_rows, g_rows)),
                dst_s,
                g_rows,
                sz.cg,
            )

        @pl.loop(0, sz.ml // l_rows)
        def _(i):
            activate(
                rows_at(sz.mg + i * l_rows, l_rows),
                (dst, rows_at(l_first + i * l_rows, l_rows)),
                dst_s,
                l_rows,
                sz.cl,
            )

    flag = flag_ref[0]
    for pc, (dst, dst_s) in enumerate(((a10, None), (a11, a11s))):
        zs[0 : sz.edge, :] = dot(halo_ref[pc * sz.edge : (pc + 1) * sz.edge, :], w_ref[...])

        @pl.loop(0, sz.bg // g_rows)
        def _(i):
            rows = rows_at(i * g_rows, g_rows)
            activate(rows, (dst, rows), dst_s, g_rows, sz.cg, flag)

        @pl.loop(0, sz.bl // l_rows)
        def _(i):
            activate(
                rows_at(sz.bg + i * l_rows, l_rows),
                (dst, rows_at(sz.one_l + i * l_rows, l_rows)),
                dst_s,
                l_rows,
                sz.cl,
                flag,
            )

    refs = (a00, a01, a01s, a10, a11, a11s)
    conv_forward(sz, lambda part: windows_one(sz, refs, part), bd_ref, z_ref, st_ref, sums)


def each_crop(sz, one):
    @pl.loop(0, sz.ng)
    def _(n):
        one([rows_at(i * sz.bg + n * sz.cg, sz.cg) for i in range(sz.rg)], (n,))

    @pl.loop(0, sz.nl // 2)
    def _(pair):
        first = sz.ng + 2 * pair
        one(
            [rows_at(sz.mg + i * sz.bl + pair * 2 * sz.cl, 2 * sz.cl) for i in range(sz.rl)],
            (first, first + 1),
        )


def add_pool(ref, crops, value):
    if len(crops) == 1:
        ref[pl.ds(crops[0], 1), :] = jnp.sum(value, axis=0, keepdims=True)
    else:
        n = value.shape[0] // 2
        ref[pl.ds(crops[0], 1), :] = jnp.sum(value[:n], axis=0, keepdims=True)
        ref[pl.ds(crops[1], 1), :] = jnp.sum(value[n:], axis=0, keepdims=True)


def crop_rows(ref, crops, n_rows):
    if len(crops) == 1:
        return ref[pl.ds(crops[0], 1), :]
    n = n_rows // 2
    return jnp.concatenate(
        [jnp.broadcast_to(ref[pl.ds(crop, 1), :], (n, ref.shape[1])) for crop in crops], axis=0
    )


def pool_kernel(sz, gain_row, shift_row, z_ref, t0, t1, t2, t3, vt_ref, c_ref, pool_ref, nrm_ref, ps):
    terms = norm_terms(
        gather_sum((t0, t1, t2, t3)),
        0,
        sz.amount,
        vt_ref[gain_row : gain_row + 1, :],
        vt_ref[shift_row : shift_row + 1, :],
    )
    nrm_ref[...] = jnp.zeros_like(nrm_ref)
    put_norm(nrm_ref, 0, terms)
    scale, shift = terms[2], terms[3]
    ps[...] = jnp.zeros_like(ps)

    def one(pieces, crops):
        acc = None
        for rows in pieces:
            c = silu(z_ref[rows, :] * scale + shift)
            c_ref[rows, :] = c
            acc = c if acc is None else acc + c
        add_pool(ps, crops, acc)

    each_crop(sz, one)
    pool_ref[...] = ps[...].astype(bf16)


def inverse_area(sz):
    crop = lax.broadcasted_iota(jnp.int32, (sz.crops, 1), 0)
    return jnp.where(crop < sz.ng, 1.0 / sz.area_g, 1.0 / sz.area_l).astype(f32)


def dot_high(a, b):
    return jnp.dot(a, b, precision=highest, preferred_element_type=f32)


def gather_short(refs):
    total = refs[0][...].astype(f32)
    for ref in refs[1:]:
        total = total + ref[...].astype(f32)
    return total


def gated_product_kernel(
    sz,
    shift_row,
    c_ref,
    p0,
    p1,
    p2,
    p3,
    d_ref,
    e_ref,
    u_ref,
    w_ref,
    vt_ref,
    q_ref,
    z_ref,
    st_ref,
    gate_ref,
    pooled_ref,
    pre_ref,
):
    pooled = gather_short((p0, p1, p2, p3)) * inverse_area(sz)
    pooled_ref[...] = pooled
    pre = dot_high(pooled, d_ref[...].astype(f32)) + e_ref[...]
    pre_ref[...] = pre
    gate = dot_high(silu(pre), u_ref[...].astype(f32)) + vt_ref[shift_row : shift_row + 1, :]
    gate_ref[...] = sigmoid(gate)

    def one(pieces, crops):
        g = crop_rows(gate_ref, crops, 2 * sz.cl)
        for rows in pieces:
            q_ref[rows, :] = (c_ref[rows, :] * g).astype(bf16)

    each_crop(sz, one)
    n_rows = sz.m // 3
    zero = jnp.zeros((8, C), f32)

    def step(i, carry):
        total, square = carry
        rows = rows_at(i * n_rows, n_rows)
        z = dot(q_ref[rows, :], w_ref[...])
        z_ref[rows, :] = z
        return total + fold(z), square + fold(z * z)

    put_rows(st_ref, lax.fori_loop(0, 3, step, (zero, zero)))


ROWS = 32


def middle_kernel(
    sz, zc_ref, zs_ref, t0, t1, t2, t3, nrm_a_ref, w_ref, vt_ref, pre_ref, mb_ref, z_ref, st_ref, nrm_ref
):
    terms = norm_terms(
        gather_sum((t0, t1, t2, t3)),
        0,
        sz.amount,
        vt_ref[G1C : G1C + 1, :],
        vt_ref[B1C : B1C + 1, :],
    )
    nrm_ref[...] = jnp.zeros_like(nrm_ref)
    put_norm(nrm_ref, 0, terms)
    scale = terms[2]
    scale_s = nrm_a_ref[6:7, :]
    shift = terms[3] + nrm_a_ref[7:8, :]

    @pl.loop(0, sz.m // ROWS)
    def _(i):
        rows = rows_at(i * ROWS, ROWS)
        pre = zc_ref[rows, :] * scale + zs_ref[rows, :] * scale_s + shift
        pre_ref[rows, :] = pre
        mb_ref[rows, :] = silu(pre).astype(bf16)

    n_rows = sz.m // 3
    zero = jnp.zeros((8, C), f32)

    def step(i, carry):
        total, square = carry
        rows = rows_at(i * n_rows, n_rows)
        z = dot(mb_ref[rows, :], w_ref[...])
        z_ref[rows, :] = z
        return total + fold(z), square + fold(z * z)

    put_rows(st_ref, lax.fori_loop(0, 3, step, (zero, zero)))


def put_variants(refs, rows, value, width):
    refs[0][rows, :] = shifted(value, -1, width).astype(bf16)
    refs[1][rows, :] = value.astype(bf16)
    refs[2][rows, :] = shifted(value, 1, width).astype(bf16)


def second_conv_kernel(
    sz,
    flag_ref,
    z_in_ref,
    top_ref,
    bottom_ref,
    w_ref,
    bd_ref,
    t0,
    t1,
    t2,
    t3,
    vt_ref,
    z_ref,
    st_ref,
    nrm_ref,
    a0,
    a1,
    a2,
    zs,
    sums,
):
    terms = norm_terms(
        gather_sum((t0, t1, t2, t3)),
        0,
        sz.amount,
        vt_ref[G2A : G2A + 1, :],
        vt_ref[B2A : B2A + 1, :],
    )
    nrm_ref[...] = jnp.zeros_like(nrm_ref)
    put_norm(nrm_ref, 0, terms)
    scale, shift = terms[2], terms[3]
    g_rows, l_rows = segments(sz)
    refs = (a0, a1, a2)

    @pl.loop(0, sz.mg // g_rows)
    def _(i):
        a = silu(z_in_ref[rows_at(i * g_rows, g_rows), :] * scale + shift)
        put_variants(refs, rows_at(sz.bg + i * g_rows, g_rows), a, sz.cg)

    @pl.loop(0, sz.ml // l_rows)
    def _(i):
        a = silu(z_in_ref[rows_at(sz.mg + i * l_rows, l_rows), :] * scale + shift)
        put_variants(refs, rows_at(sz.two_l + sz.bl + i * l_rows, l_rows), a, sz.cl)

    for k, src in enumerate((top_ref, bottom_ref)):
        flag = flag_ref[k]
        zs[...] = dot(src[...], w_ref[...])
        g_first = 0 if k == 0 else (sz.rg + 1) * sz.bg
        l_first = sz.two_l + (0 if k == 0 else (sz.rl + 1) * sz.bl)

        @pl.loop(0, sz.bg // g_rows)
        def _(i):
            a = silu(zs[rows_at(i * g_rows, g_rows), :] * scale + shift) * flag
            put_variants(refs, rows_at(g_first + i * g_rows, g_rows), a, sz.cg)

        @pl.loop(0, sz.bl // l_rows)
        def _(i):
            a = silu(zs[rows_at(sz.bg + i * l_rows, l_rows), :] * scale + shift) * flag
            put_variants(refs, rows_at(l_first + i * l_rows, l_rows), a, sz.cl)

    conv_forward(sz, lambda part: windows_two(sz, refs, part), bd_ref, z_ref, st_ref, sums)


def output_kernel(
    sz, pre_ref, z_ref, t0, t1, t2, t3, vt_ref, cg_ref, cl_ref, og_ref, ol_ref, dn_ref, st_ref, nrm_ref, sums
):
    terms = norm_terms(
        gather_sum((t0, t1, t2, t3)),
        0,
        sz.amount,
        vt_ref[G2C : G2C + 1, :],
        vt_ref[B2C : B2C + 1, :],
    )
    nrm_ref[...] = jnp.zeros_like(nrm_ref)
    put_norm(nrm_ref, 0, terms)
    mean, inverse, scale, shift = terms
    sums[...] = jnp.zeros_like(sums)

    def piece(rows, cot):
        z = z_ref[rows, :]
        pre = silu(pre_ref[rows, :]) + z * scale + shift
        s = sigmoid(pre)
        dn = cot * (s * (1.0 + pre * (1.0 - s)))
        dn_ref[rows, :] = dn
        sums[0:8, :] += fold(dn)
        sums[8:16, :] += fold(dn * ((z - mean) * inverse))
        return pre * s

    @pl.loop(0, sz.ng)
    def _(n):
        for i in range(sz.rg):
            rows = rows_at(i * sz.bg + n * sz.cg, sz.cg)
            og_ref[n, i] = piece(rows, cg_ref[n, i].astype(f32)).astype(bf16)

    @pl.loop(0, sz.nl // 2)
    def _(pair):
        for i in range(sz.rl):
            rows = rows_at(sz.mg + i * sz.bl + pair * 2 * sz.cl, 2 * sz.cl)
            cot = jnp.concatenate(
                [cl_ref[2 * pair + k, i].astype(f32) for k in range(2)], axis=0
            )
            value = piece(rows, cot)
            for k in range(2):
                ol_ref[2 * pair + k, i] = value[k * sz.cl : (k + 1) * sz.cl].astype(bf16)

    put_rows(st_ref, [sums[0:8, :], sums[8:16, :]])


def back_terms(total, row_one, row_two, amount, nrm_ref, nrm_row):
    mean = nrm_ref[nrm_row : nrm_row + 1, :]
    inverse = nrm_ref[nrm_row + 1 : nrm_row + 2, :]
    scale = nrm_ref[nrm_row + 2 : nrm_row + 3, :]
    one = total[row_one : row_one + 1] / amount
    two = total[row_two : row_two + 1] / amount
    return scale, one, mean, inverse * two


def norm_back(dn, z, terms):
    scale, one, mean, slope = terms
    return scale * (dn - one - (z - mean) * slope)


def gate_grad_kernel(
    sz, n_branch, *refs
):
    dn_ref = refs[0]
    z_refs = refs[1 : 1 + n_branch]
    k = 1 + n_branch
    t0, t1, t2, t3 = refs[k : k + 4]
    nrm_refs = refs[k + 4 : k + 4 + n_branch]
    k = k + 4 + n_branch
    w_ref, c_ref = refs[k : k + 2]
    outs = refs[k + 2 :]
    dz_refs = outs[:n_branch]
    dq_ref, dg_ref, ps = outs[n_branch:]
    total = gather_sum((t0, t1, t2, t3))
    terms = [
        back_terms(total, 0, 1 + b, sz.amount, nrm_refs[b], 0 if b == 0 else 4)
        for b in range(n_branch)
    ]

    @pl.loop(0, sz.m // ROWS)
    def _(i):
        rows = rows_at(i * ROWS, ROWS)
        dn = dn_ref[rows, :]
        for b in range(n_branch):
            dz_refs[b][rows, :] = norm_back(dn, z_refs[b][rows, :], terms[b]).astype(bf16)

    n_rows = sz.m // 3

    @pl.loop(0, 3)
    def _(i):
        rows = rows_at(i * n_rows, n_rows)
        dq_ref[rows, :] = dot_t(dz_refs[0][rows, :], w_ref[...])

    ps[...] = jnp.zeros_like(ps)

    def one(pieces, crops):
        acc = None
        for rows in pieces:
            term = dq_ref[rows, :] * c_ref[rows, :]
            acc = term if acc is None else acc + term
        add_pool(ps, crops, acc)

    each_crop(sz, one)
    dg_ref[...] = ps[...].astype(bf16)


def excite_back_kernel(
    sz,
    dq_ref,
    z_ref,
    nrm_ref,
    g0,
    g1,
    g2,
    g3,
    gate_ref,
    pre_ref,
    d_ref,
    u_ref,
    dn_ref,
    st_ref,
    dv_ref,
    du_ref,
    pool,
    sums,
):
    gate = gate_ref[...]
    dv = gather_short((g0, g1, g2, g3)) * gate * (1.0 - gate)
    dv_ref[...] = dv
    du = lax.dot_general(
        dv,
        u_ref[...].astype(f32),
        (((1,), (1,)), ((), ())),
        precision=highest,
        preferred_element_type=f32,
    ) * silu_slope(pre_ref[...])
    du_ref[...] = du
    pool[...] = (
        lax.dot_general(
            du,
            d_ref[...].astype(f32),
            (((1,), (1,)), ((), ())),
            precision=highest,
            preferred_element_type=f32,
        )
        * inverse_area(sz)
    )
    mean = nrm_ref[0:1, :]
    inverse = nrm_ref[1:2, :]
    scale = nrm_ref[2:3, :]
    shift = nrm_ref[3:4, :]
    sums[...] = jnp.zeros_like(sums)

    def one(pieces, crops):
        g = crop_rows(gate_ref, crops, 2 * sz.cl)
        p = crop_rows(pool, crops, 2 * sz.cl)
        for rows in pieces:
            z = z_ref[rows, :]
            dn = (dq_ref[rows, :] * g + p) * silu_slope(z * scale + shift)
            dn_ref[rows, :] = dn
            sums[0:8, :] += fold(dn)
            sums[8:16, :] += fold(dn * ((z - mean) * inverse))

    each_crop(sz, one)
    put_rows(st_ref, [sums[0:8, :], sums[8:16, :]])


def excite_weights_kernel(flag_ref, dv_ref, du_ref, pooled_ref, pre_ref, dd_ref, de_ref, du_out, df_ref):
    flag = flag_ref[0]
    dv = dv_ref[...] * flag
    du = du_ref[...] * flag

    def cross(a, b):
        return lax.dot_general(
            a, b, (((0,), (0,)), ((), ())), precision=highest, preferred_element_type=f32
        )

    dd_ref[...] = cross(pooled_ref[...], du)
    du_out[...] = cross(silu(pre_ref[...]), dv)
    de_ref[...] = jnp.broadcast_to(jnp.sum(du, axis=0, keepdims=True), de_ref.shape)
    df_ref[...] = jnp.broadcast_to(jnp.sum(dv, axis=0, keepdims=True), df_ref.shape)


def weight_kernel(x_ref, dz_ref, w_ref):
    n = 128 if x_ref.shape[1] % 128 == 0 else x_ref.shape[1]
    for k in range(x_ref.shape[1] // n):
        w_ref[k * n : (k + 1) * n, :] = t_dot(x_ref[:, k * n : (k + 1) * n], dz_ref[...])


def norm_back_kernel(sz, dn_ref, z_ref, t0, t1, t2, t3, nrm_ref, dz_ref):
    terms = back_terms(gather_sum((t0, t1, t2, t3)), 0, 1, sz.amount, nrm_ref, 0)

    @pl.loop(0, sz.m // ROWS)
    def _(i):
        rows = rows_at(i * ROWS, ROWS)
        dz_ref[rows, :] = norm_back(dn_ref[rows, :], z_ref[rows, :], terms).astype(bf16)


def conv_weights(sz, windows_of, dz_ref, dk_ref):
    @pl.loop(0, 2)
    def _(half):
        cols = pl.ds(pl.multiple_of(half * HALF, HALF), HALF)
        win_g = windows_of("g")
        win_l = windows_of("l")
        for tap in range(9):
            _, ref_g, start_g = win_g[tap]
            _, ref_l, start_l = win_l[tap]
            acc = t_dot(ref_g[start_g : start_g + sz.mg, cols], dz_ref[0 : sz.mg, cols])
            acc = acc + t_dot(ref_l[start_l : start_l + sz.ml, cols], dz_ref[sz.mg : sz.m, cols])
            dk_ref[tap * GW : (tap + 1) * GW, cols] = block_dense(acc)


def second_conv_weights_kernel(sz, a0, a1, a2, dz_ref, dk_ref):
    conv_weights(sz, lambda part: windows_two(sz, (a0, a1, a2), part), dz_ref, dk_ref)


def first_conv_weights_kernel(sz, a00, a01, a01s, a10, a11, a11s, dz_ref, dk_ref):
    refs = (a00, a01, a01s, a10, a11, a11s)
    conv_weights(sz, lambda part: windows_one(sz, refs, part), dz_ref, dk_ref)


def second_conv_back_kernel(
    sz, dz_ref, top_ref, bottom_ref, bd_ref, z_ref, nrm_ref, dn_ref, st_ref, v0, v1, v2, sums
):
    refs = (v0, v1, v2)
    g_rows, l_rows = segments(sz)

    @pl.loop(0, sz.mg // g_rows)
    def _(i):
        v = dz_ref[rows_at(i * g_rows, g_rows), :].astype(f32)
        put_variants(refs, rows_at(sz.bg + i * g_rows, g_rows), v, sz.cg)

    @pl.loop(0, sz.ml // l_rows)
    def _(i):
        v = dz_ref[rows_at(sz.mg + i * l_rows, l_rows), :].astype(f32)
        put_variants(refs, rows_at(sz.two_l + sz.bl + i * l_rows, l_rows), v, sz.cl)

    for k, src in enumerate((top_ref, bottom_ref)):
        g_first = 0 if k == 0 else (sz.rg + 1) * sz.bg
        l_first = sz.two_l + (0 if k == 0 else (sz.rl + 1) * sz.bl)

        @pl.loop(0, sz.bg // g_rows)
        def _(i):
            v = src[rows_at(i * g_rows, g_rows), :].astype(f32)
            put_variants(refs, rows_at(g_first + i * g_rows, g_rows), v, sz.cg)

        @pl.loop(0, sz.bl // l_rows)
        def _(i):
            v = src[rows_at(sz.bg + i * l_rows, l_rows), :].astype(f32)
            put_variants(refs, rows_at(l_first + i * l_rows, l_rows), v, sz.cl)

    @pl.loop(0, 2)
    def _(half):
        cols = pl.ds(pl.multiple_of(half * HALF, HALF), HALF)
        for part, first, n_all, n_rows in (
            ("g", 0, sz.mg, sz.mg // 2),
            ("l", sz.mg, sz.ml, sz.ml),
        ):
            for k in range(n_all // n_rows):
                dn_ref[first + k * n_rows : first + (k + 1) * n_rows, cols] = conv_product(
                    shift_windows(windows_two(sz, refs, part, True), k * n_rows),
                    bd_ref,
                    half,
                    n_rows,
                    True,
                )

    slope_pass(sz.m, dn_ref, z_ref, nrm_ref, st_ref, sums)


def slope_pass(n_all, dn_ref, z_ref, nrm_ref, st_ref, sums):
    mean = nrm_ref[0:1, :]
    inverse = nrm_ref[1:2, :]
    scale = nrm_ref[2:3, :]
    shift = nrm_ref[3:4, :]
    sums[...] = jnp.zeros_like(sums)

    @pl.loop(0, n_all // ROWS)
    def _(i):
        rows = rows_at(i * ROWS, ROWS)
        z = z_ref[rows, :]
        dn = dn_ref[rows, :] * silu_slope(z * scale + shift)
        dn_ref[rows, :] = dn
        sums[0:8, :] += fold(dn)
        sums[8:16, :] += fold(dn * ((z - mean) * inverse))

    put_rows(st_ref, [sums[0:8, :], sums[8:16, :]])


def middle_back_kernel(
    sz,
    dn_d_ref,
    zd_ref,
    t0,
    t1,
    t2,
    t3,
    nrm_d_ref,
    w_ref,
    dpre_ref,
    pre_ref,
    zc_ref,
    zs_ref,
    nrm_c_ref,
    nrm_a_ref,
    dz_ref,
    dn_ref,
    st_ref,
    sums,
):
    terms = back_terms(gather_sum((t0, t1, t2, t3)), 0, 1, sz.amount, nrm_d_ref, 0)

    @pl.loop(0, sz.m // ROWS)
    def _(i):
        rows = rows_at(i * ROWS, ROWS)
        dz_ref[rows, :] = norm_back(dn_d_ref[rows, :], zd_ref[rows, :], terms).astype(bf16)

    n_rows = sz.m // 3

    @pl.loop(0, 3)
    def _(i):
        rows = rows_at(i * n_rows, n_rows)
        dn_ref[rows, :] = dot_t(dz_ref[rows, :], w_ref[...])

    mean_c = nrm_c_ref[0:1, :]
    inverse_c = nrm_c_ref[1:2, :]
    mean_s = nrm_a_ref[4:5, :]
    inverse_s = nrm_a_ref[5:6, :]
    sums[...] = jnp.zeros_like(sums)

    @pl.loop(0, sz.m // ROWS)
    def _(i):
        rows = rows_at(i * ROWS, ROWS)
        dn = (dn_ref[rows, :] + dpre_ref[rows, :]) * silu_slope(pre_ref[rows, :])
        dn_ref[rows, :] = dn
        sums[0:8, :] += fold(dn)
        sums[8:16, :] += fold(dn * ((zc_ref[rows, :] - mean_c) * inverse_c))
        sums[16:24, :] += fold(dn * ((zs_ref[rows, :] - mean_s) * inverse_s))

    put_rows(st_ref, [sums[0:8, :], sums[8:16, :], sums[16:24, :]])


def first_conv_back_kernel(
    sz, dz_ref, below_ref, bd_ref, x_ref, w_ref, nrm_ref, dn_ref, st_ref, v0, v1, zs, da, sums
):
    g_rows, l_rows = segments(sz)

    def put(rows, v, width):
        v0[rows, :] = v.astype(bf16)
        v1[rows, :] = shifted(v, 1, width).astype(bf16)

    @pl.loop(0, sz.mg // g_rows)
    def _(i):
        put(rows_at(i * g_rows, g_rows), dz_ref[rows_at(i * g_rows, g_rows), :].astype(f32), sz.cg)

    @pl.loop(0, sz.ml // l_rows)
    def _(i):
        put(
            rows_at(sz.one_l + i * l_rows, l_rows),
            dz_ref[rows_at(sz.mg + i * l_rows, l_rows), :].astype(f32),
            sz.cl,
        )

    @pl.loop(0, sz.bg // g_rows)
    def _(i):
        put(
            rows_at(sz.mg + i * g_rows, g_rows),
            below_ref[rows_at(i * g_rows, g_rows), :].astype(f32),
            sz.cg,
        )

    @pl.loop(0, sz.bl // l_rows)
    def _(i):
        put(
            rows_at(sz.one_l + sz.ml + i * l_rows, l_rows),
            below_ref[rows_at(sz.bg + i * l_rows, l_rows), :].astype(f32),
            sz.cl,
        )

    mean = nrm_ref[0:1, :]
    inverse = nrm_ref[1:2, :]
    scale = nrm_ref[2:3, :]
    shift = nrm_ref[3:4, :]
    sums[...] = jnp.zeros_like(sums)
    third = sz.m // 3
    for phase in range(4):
        pr, pc = phase // 2, phase % 2
        taps = []
        for a, down in (((1, 0),), ((2, 0), (0, 1)))[pr]:
            for b, right in (((1, 0),), ((2, 0), (0, 1)))[pc]:
                taps.append((3 * a + b, down, right))

        @pl.loop(0, 2)
        def _(half):
            cols = pl.ds(pl.multiple_of(half * HALF, HALF), HALF)
            for first, base, block, n_all, n_rows in (
                (0, 0, sz.bg, sz.mg, sz.mg // 2),
                (sz.mg, sz.one_l, sz.bl, sz.ml, sz.ml),
            ):
                for k in range(n_all // n_rows):
                    windows = [
                        (tap, (v0, v1)[right], base + down * block + k * n_rows)
                        for tap, down, right in taps
                    ]
                    da[first + k * n_rows : first + (k + 1) * n_rows, cols] = conv_product(
                        windows, bd_ref, half, n_rows, True
                    )

        @pl.loop(0, 3)
        def _(i):
            zs[rows_at(i * third, third), :] = dot(
                x_ref[rows_at(phase * sz.m + i * third, third), :], w_ref[...]
            )

        @pl.loop(0, sz.m // ROWS)
        def _(i):
            rows = rows_at(i * ROWS, ROWS)
            z = zs[rows, :]
            dn = da[rows, :] * silu_slope(z * scale + shift)
            dn_ref[rows_at(phase * sz.m + i * ROWS, ROWS), :] = dn.astype(bf16)
            sums[0:8, :] += fold(dn)
            sums[8:16, :] += fold(dn * ((z - mean) * inverse))

    put_rows(st_ref, [sums[0:8, :], sums[8:16, :]])


def image_back_kernel(
    sz,
    dn_ref,
    x_ref,
    w_ref,
    t0,
    t1,
    t2,
    t3,
    nrm_ref,
    dzs_ref,
    ws_ref,
    dz_ref,
    gg_ref,
    gl_ref,
    zs,
    dx,
    s_ref,
    t_ref,
):
    terms = back_terms(gather_sum((t0, t1, t2, t3)), 0, 1, 4 * sz.amount, nrm_ref, 0)
    third = sz.m // 3
    for phase in range(4):

        @pl.loop(0, 3)
        def _(i):
            zs[rows_at(i * third, third), :] = dot(
                x_ref[rows_at(phase * sz.m + i * third, third), :], w_ref[...]
            )

        @pl.loop(0, sz.m // ROWS)
        def _(i):
            rows = rows_at(i * ROWS, ROWS)
            rows_all = rows_at(phase * sz.m + i * ROWS, ROWS)
            dz_ref[rows_all, :] = norm_back(
                dn_ref[rows_all, :].astype(f32), zs[rows, :], terms
            ).astype(bf16)

        @pl.loop(0, 3)
        def _(i):
            rows_all = rows_at(phase * sz.m + i * third, third)
            value = dot_t(dz_ref[rows_all, :], w_ref[...])
            if phase == 0:
                value = value + dot_t(dzs_ref[rows_at(i * third, third), :], ws_ref[...])
            dx[rows_all, :] = value

    def place(first, v):
        n = v.shape[0]
        s_ref[pl.ds(first, n, stride=2), :] = v[:, :128]
        t_ref[pl.ds(first, n, stride=2), :] = jnp.concatenate([v[:, 128:], v[:, 128:]], axis=1)

    @pl.loop(0, sz.ng)
    def _(n):
        for r in range(sz.hg):
            for pc in range(2):
                phase = 2 * (r % 2) + pc
                place(
                    r * sz.wg + pc,
                    dx[rows_at(phase * sz.m + (r // 2) * sz.bg + n * sz.cg, sz.cg), :],
                )
        n_rows = sz.hg * sz.wg
        gg_ref[n, :, :, 0:128] = s_ref[0:n_rows, :].reshape(sz.hg, sz.wg, 128)
        gg_ref[n, :, :, 128:CIN] = t_ref[0:n_rows, :][:, :64].reshape(sz.hg, sz.wg, 64)

    @pl.loop(0, sz.nl)
    def _(n):
        for r in range(sz.hl):
            for pc in range(2):
                phase = 2 * (r % 2) + pc
                place(
                    r * sz.wl + pc,
                    dx[
                        rows_at(phase * sz.m + sz.mg + (r // 2) * sz.bl + n * sz.cl, sz.cl, 8), :
                    ],
                )
        n_rows = sz.hl * sz.wl
        gl_ref[n, :, :, 0:128] = s_ref[0:n_rows, :].reshape(sz.hl, sz.wl, 128)
        gl_ref[n, :, :, 128:CIN] = t_ref[0:n_rows, :][:, :64].reshape(sz.hl, sz.wl, 64)


def over_height(x):
    n = lax.axis_size("height")
    return [x] + [lax.ppermute(x, "height", [(i, (i + k) % n) for i in range(n)]) for k in range(1, n)]


def step_down(x):
    n = lax.axis_size("height")
    return lax.ppermute(x, "height", [(i, i + 1) for i in range(n - 1)])


def step_up(x):
    n = lax.axis_size("height")
    return lax.ppermute(x, "height", [(i + 1, i) for i in range(n - 1)])


def edge_rows(sz, x, last):
    if last:
        return jnp.concatenate([x[sz.mg - sz.bg : sz.mg], x[sz.m - sz.bl : sz.m]], axis=0)
    return jnp.concatenate([x[0 : sz.bg], x[sz.mg : sz.mg + sz.bl]], axis=0)


def lamb_terms(param, grad_val, first_old, second_old, decay):
    first_new = beta_one * first_old + (1.0 - beta_one) * grad_val
    second_new = beta_two * second_old + (1.0 - beta_two) * grad_val * grad_val
    update = (
        first_new
        / (1.0 - beta_one**STEP)
        / (jnp.sqrt(second_new / (1.0 - beta_two**STEP)) + adam_eps)
        + decay * param
    )
    return (first_new, second_new, update)


def body(
    image_glob,
    image_loc,
    cot_glob,
    cot_loc,
    weights,
    first_moment,
    second_moment,
    vectors,
    vec_first,
    vec_second,
):
    n_height = lax.axis_size("height")
    place = lax.axis_index("height")
    sz = Sizes(image_glob, image_loc, n_height)
    m = sz.m
    part = functools.partial
    has_above = (place > 0).astype(f32)
    has_below = (place < n_height - 1).astype(f32)
    borders = jnp.stack([has_above, has_below])
    owner = (place == 0).astype(f32).reshape(1)

    gathered = lax.all_gather(weights.astype(bf16), both_axes, axis=0, tiled=True)
    shapes = matrix_shapes()
    mat_lengths = [dims_pair[0] * dims_pair[1] for dims_pair in shapes]
    matrices = [
        flat_piece.reshape(dims_pair)
        for flat_piece, dims_pair in zip(cut_pieces(gathered, mat_lengths), shapes)
    ]
    w1, k1, d1, u1, p1, s1, w2, k2, d2, u2, p2 = matrices
    d1 = jnp.pad(d1, ((0, 0), (0, HID - SE_A)))
    u1 = jnp.pad(u1, ((0, HID - SE_A), (0, 0)))
    vec_list = cut_pieces(vectors, vector_sizes())
    vt = jnp.stack(vec_list[:4] + vec_list[5:14] + vec_list[15:])
    e1 = jnp.pad(vec_list[4], (0, HID - SE_A)).reshape(1, HID)
    e2 = vec_list[14].reshape(1, HID)

    st8 = out((8, C))
    mat = out((m, C))
    mat_low = out((m, C), bf16)
    pool_low = out((sz.crops, C), bf16)
    pool_scr = pltpu.VMEM((sz.crops, C), f32)
    sum_scr = pltpu.VMEM((24, C), f32)
    point_flops = 2 * m * C * C
    conv_flops = 2 * m * C * HALF * 9

    x, x_edge = call(
        part(prepare_kernel, sz),
        [out((4 * m, CIN), bf16), out((2 * sz.edge, CIN), bf16)],
        [pltpu.VMEM((sz.hg * sz.wg, 128), f32)] * 2,
        image_glob,
        image_loc,
    )
    x_above = step_down(x_edge)
    (bd1,) = call(block_diagonal_kernel, [out((18, HALF, HALF), bf16)], [], k1)
    (bd2,) = call(block_diagonal_kernel, [out((18, HALF, HALF), bf16)], [], k2)
    zs, st_a = call(part(input_stats_kernel, sz), [mat, st8], [], x, w1, s1, flops=point_flops * 2)
    st_a = over_height(st_a)

    one_shape = out((sz.one, C), bf16)
    zb, st_b, nrm_a, *act_a = call(
        part(first_conv_kernel, sz),
        [mat, st8, st8, mat_low, mat_low, mat_low, one_shape, one_shape, one_shape],
        [pltpu.VMEM((m, C), f32), sum_scr],
        borders,
        x,
        x_above,
        w1,
        bd1,
        *st_a,
        vt,
        smem=1,
        flops=conv_flops,
    )
    st_b = over_height(st_b)
    cb, pool_b, nrm_b = call(
        part(pool_kernel, sz, G1B, B1B), [mat, pool_low, st8], [pool_scr], zb, *st_b, vt
    )
    pool_b = over_height(pool_b)
    hid = out((sz.crops, HID))
    crop_mat = out((sz.crops, C))
    qb, zc, st_c, gate_b, pooled_b, hidden_b = call(
        part(gated_product_kernel, sz, F1),
        [mat_low, mat, st8, crop_mat, crop_mat, hid],
        [],
        cb,
        *pool_b,
        d1,
        e1,
        u1,
        p1,
        vt,
        flops=point_flops,
    )
    st_c = over_height(st_c)
    pre_mid, mid_low, zd, st_d, nrm_c = call(
        part(middle_kernel, sz),
        [mat, mat_low, mat, st8, st8],
        [],
        zc,
        zs,
        *st_c,
        nrm_a,
        w2,
        vt,
        flops=point_flops,
    )
    mid_above = step_down(edge_rows(sz, mid_low, True))
    mid_below = step_up(edge_rows(sz, mid_low, False))
    st_d = over_height(st_d)
    two_shape = out((sz.two, C), bf16)
    edge_scr = pltpu.VMEM((sz.edge, C), f32)
    ze, st_e, nrm_d, *act_d = call(
        part(second_conv_kernel, sz),
        [mat, st8, st8, two_shape, two_shape, two_shape],
        [edge_scr, sum_scr],
        borders,
        zd,
        mid_above,
        mid_below,
        w2,
        bd2,
        *st_d,
        vt,
        smem=1,
        flops=conv_flops,
    )
    st_e = over_height(st_e)
    ce, pool_e, nrm_e = call(
        part(pool_kernel, sz, G2B, B2B), [mat, pool_low, st8], [pool_scr], ze, *st_e, vt
    )
    pool_e = over_height(pool_e)
    qe, zf, st_f, gate_e, pooled_e, hidden_e = call(
        part(gated_product_kernel, sz, F2),
        [mat_low, mat, st8, crop_mat, crop_mat, hid],
        [],
        ce,
        *pool_e,
        d2,
        e2,
        u2,
        p2,
        vt,
        flops=point_flops,
    )
    st_f = over_height(st_f)
    out_glob, out_loc, dpre, bst_f, nrm_f = call(
        part(output_kernel, sz),
        [out(cot_glob.shape, bf16), out(cot_loc.shape, bf16), mat, st8, st8],
        [sum_scr],
        pre_mid,
        zf,
        *st_f,
        vt,
        cot_glob,
        cot_loc,
    )
    bst_f_all = over_height(bst_f)

    dzf, dqe, dg_e = call(
        part(gate_grad_kernel, sz, 1),
        [mat_low, mat, pool_low],
        [pool_scr],
        dpre,
        zf,
        *bst_f_all,
        nrm_f,
        p2,
        ce,
        flops=point_flops,
    )
    dg_e = over_height(dg_e)
    (mat_f,) = call(weight_kernel, [out((C, C))], [], qe, dzf, flops=point_flops)
    dn_e, bst_e, dv_e, du_e = call(
        part(excite_back_kernel, sz),
        [mat, st8, crop_mat, hid],
        [pool_scr, sum_scr],
        dqe,
        ze,
        nrm_e,
        *dg_e,
        gate_e,
        hidden_e,
        d2,
        u2,
    )
    bst_e_all = over_height(bst_e)
    se_outs = [out((C, HID)), out((8, HID)), out((HID, C)), st8]
    dd2, de2, du2, df2 = call(
        excite_weights_kernel, se_outs, [], owner, dv_e, du_e, pooled_e, hidden_e, smem=1
    )
    (dze,) = call(part(norm_back_kernel, sz), [mat_low], [], dn_e, ze, *bst_e_all, nrm_e)
    dze_above = step_down(edge_rows(sz, dze, True))
    dze_below = step_up(edge_rows(sz, dze, False))
    (mat_e,) = call(
        part(second_conv_weights_kernel, sz),
        [out((9 * GW, C))],
        [],
        *act_d,
        dze,
        flops=conv_flops,
    )
    two_scr = pltpu.VMEM((sz.two, C), bf16)
    dn_d, bst_d = call(
        part(second_conv_back_kernel, sz),
        [mat, st8],
        [two_scr, two_scr, two_scr, sum_scr],
        dze,
        dze_above,
        dze_below,
        bd2,
        zd,
        nrm_d,
        flops=conv_flops,
    )
    bst_d_all = over_height(bst_d)
    dzd, dn_mid, bst_cs = call(
        part(middle_back_kernel, sz),
        [mat_low, mat, st8],
        [sum_scr],
        dn_d,
        zd,
        *bst_d_all,
        nrm_d,
        w2,
        dpre,
        pre_mid,
        zc,
        zs,
        nrm_c,
        nrm_a,
        flops=point_flops,
    )
    bst_cs_all = over_height(bst_cs)
    (mat_d,) = call(weight_kernel, [out((C, C))], [], mid_low, dzd, flops=point_flops)
    dzc, dzs, dqb, dg_b = call(
        part(gate_grad_kernel, sz, 2),
        [mat_low, mat_low, mat, pool_low],
        [pool_scr],
        dn_mid,
        zc,
        zs,
        *bst_cs_all,
        nrm_c,
        nrm_a,
        p1,
        cb,
        flops=point_flops,
    )
    dg_b = over_height(dg_b)
    (mat_c,) = call(weight_kernel, [out((C, C))], [], qb, dzc, flops=point_flops)
    (mat_s,) = call(weight_kernel, [out((CIN, C))], [], x[:m], dzs, flops=point_flops)
    dn_b, bst_b, dv_b, du_b = call(
        part(excite_back_kernel, sz),
        [mat, st8, crop_mat, hid],
        [pool_scr, sum_scr],
        dqb,
        zb,
        nrm_b,
        *dg_b,
        gate_b,
        hidden_b,
        d1,
        u1,
    )
    bst_b_all = over_height(bst_b)
    dd1, de1, du1, df1 = call(
        excite_weights_kernel, se_outs, [], owner, dv_b, du_b, pooled_b, hidden_b, smem=1
    )
    (dzb,) = call(part(norm_back_kernel, sz), [mat_low], [], dn_b, zb, *bst_b_all, nrm_b)
    dzb_below = step_up(edge_rows(sz, dzb, False))
    (mat_b,) = call(
        part(first_conv_weights_kernel, sz),
        [out((9 * GW, C))],
        [],
        *act_a,
        dzb,
        flops=conv_flops,
    )
    one_scr = pltpu.VMEM((sz.one, C), bf16)
    dn_a, bst_a = call(
        part(first_conv_back_kernel, sz),
        [out((4 * m, C), bf16), st8],
        [one_scr, one_scr, pltpu.VMEM((m, C), f32), pltpu.VMEM((m, C), f32), sum_scr],
        dzb,
        dzb_below,
        bd1,
        x,
        w1,
        nrm_a,
        flops=conv_flops,
    )
    bst_a_all = over_height(bst_a)
    dza, grad_glob, grad_loc = call(
        part(image_back_kernel, sz),
        [out((4 * m, C), bf16), out(image_glob.shape), out(image_loc.shape)],
        [
            pltpu.VMEM((m, C), f32),
            pltpu.VMEM((4 * m, CIN), f32),
            pltpu.VMEM((sz.hg * sz.wg, 128), f32),
            pltpu.VMEM((sz.hg * sz.wg, 128), f32),
        ],
        dn_a,
        x,
        w1,
        *bst_a_all,
        nrm_a,
        dzs,
        s1,
        flops=point_flops * 2,
    )
    (mat_a,) = call(weight_kernel, [out((CIN, C))], [], x, dza, flops=point_flops)

    flat_grad = jnp.concatenate(
        [
            piece.reshape(-1)
            for piece in (
                mat_a,
                mat_b,
                dd1[:, :SE_A],
                du1[:SE_A],
                mat_c,
                mat_s,
                mat_d,
                mat_e,
                dd2,
                du2,
                mat_f,
            )
        ]
    )
    vec_grad = jnp.concatenate(
        [
            bst_a[1],
            bst_a[0],
            bst_b[1],
            bst_b[0],
            de1[0, :SE_A],
            df1[0],
            bst_cs[1],
            bst_cs[0],
            bst_cs[2],
            bst_cs[0],
            bst_d[1],
            bst_d[0],
            bst_e[1],
            bst_e[0],
            de2[0],
            df2[0],
            bst_f[1],
            bst_f[0],
        ]
    )
    grad_shard = lax.psum_scatter(flat_grad, both_axes, scatter_dimension=0, tiled=True)
    shard_len = weights.shape[0]
    device_index = lax.axis_index("batch") * n_height + lax.axis_index("height")
    position = device_index * shard_len + lax.iota(jnp.int32, shard_len)
    bounds = np.cumsum([0] + mat_lengths)
    lower_edge = jnp.asarray(bounds[:-1], jnp.int32)
    upper_edge = jnp.asarray(bounds[1:], jnp.int32)
    member = (
        (position[:, None] >= lower_edge[None, :]) & (position[:, None] < upper_edge[None, :])
    ).astype(f32)
    new_first, new_second, update = lamb_terms(
        weights, grad_shard, first_moment, second_moment, weight_decay
    )
    part_sums = jnp.dot(jnp.stack([weights * weights, update * update]), member, precision=highest)
    vec_total, totals = lax.psum((vec_grad, part_sums), both_axes)
    norm_pair = jnp.sqrt(totals)
    trust_ratio = learn_rate * (norm_pair[0] / norm_pair[1])
    new_weights = weights - jnp.dot(member, trust_ratio, precision=highest) * update
    vec_one_new, vec_two_new, vec_update = lamb_terms(vectors, vec_total, vec_first, vec_second, 0.0)
    vec_pieces = []
    for param_piece, update_piece in zip(
        cut_pieces(vectors, vector_sizes()), cut_pieces(vec_update, vector_sizes())
    ):
        ratio_val = jnp.sqrt(jnp.sum(param_piece * param_piece)) / jnp.sqrt(
            jnp.sum(update_piece * update_piece)
        )
        vec_pieces.append(param_piece - learn_rate * ratio_val * update_piece)
    new_vectors = jnp.concatenate(vec_pieces)
    return (
        out_glob,
        out_loc,
        grad_glob,
        grad_loc,
        new_weights,
        new_first,
        new_second,
        new_vectors,
        vec_one_new,
        vec_two_new,
        norm_pair,
    )


def solution(mesh):
    maps = P("batch", "height", None, None)
    entries = P(("batch", "height"))
    return jax.shard_map(
        body,
        mesh=mesh,
        in_specs=(maps, maps, maps, maps, entries, entries, entries, P(), P(), P()),
        out_specs=(maps, maps, maps, maps, entries, entries, entries, P(), P(), P(), P()),
        check_vma=False,
    )
```

```python
import functools

import jax
import jax.numpy as jnp
import numpy as np
from jax import lax
from jax.experimental import pallas as pl
from jax.experimental.pallas import tpu as pltpu
from jax.sharding import PartitionSpec as P

CIN = 192
C = 512
GW = 64
GROUPS = 8
SE_A = 48
SE_B = 128
STEP = 10
HID = 128
HALF = 256

norm_eps = 1e-05
beta_one = 0.9
beta_two = 0.999
adam_eps = 1e-06
weight_decay = 0.01
learn_rate = 0.4
highest = lax.Precision.HIGHEST
bf16 = jnp.bfloat16
f32 = jnp.float32
both_axes = ("batch", "height")

G1A, B1A, G1B, B1B, F1, G1C, B1C, G1S, B1S, G2A, B2A, G2B, B2B, F2, G2C, B2C = range(16)


def matrix_shapes():
    return [
        (CIN, C),
        (9 * GW, C),
        (C, SE_A),
        (SE_A, C),
        (C, C),
        (CIN, C),
        (C, C),
        (9 * GW, C),
        (C, SE_B),
        (SE_B, C),
        (C, C),
    ]


def vector_sizes():
    return [C, C, C, C, SE_A, C, C, C, C, C, C, C, C, C, SE_B, C, C, C]


def cut_pieces(flat_vec, lengths):
    pieces = []
    offset = 0
    for length in lengths:
        pieces.append(flat_vec[offset : offset + length])
        offset += length
    return pieces


class Sizes:
    def __init__(self, image_glob, image_loc, n_height):
        self.ng, self.hg, self.wg = image_glob.shape[:3]
        self.nl, self.hl, self.wl = image_loc.shape[:3]
        self.rg, self.cg = self.hg // 2, self.wg // 2
        self.rl, self.cl = self.hl // 2, self.wl // 2
        self.bg, self.bl = self.ng * self.cg, self.nl * self.cl
        self.mg, self.ml = self.rg * self.bg, self.rl * self.bl
        self.m = self.mg + self.ml
        self.edge = self.bg + self.bl
        self.n_height = n_height
        self.crops = -(-(self.ng + self.nl) // 16) * 16
        self.area_g = self.rg * self.cg * n_height
        self.area_l = self.rl * self.cl * n_height
        self.amount = n_height * self.m
        self.one_l = (self.rg + 1) * self.bg
        self.one = self.one_l + (self.rl + 1) * self.bl
        self.two_l = (self.rg + 2) * self.bg
        self.two = self.two_l + (self.rl + 2) * self.bl


def sigmoid(v):
    return 0.5 * jnp.tanh(0.5 * v) + 0.5


def silu(v):
    return v * sigmoid(v)


def silu_slope(v):
    s = sigmoid(v)
    return s * (1.0 + v * (1.0 - s))


def padded_bytes(shape, dtype):
    size = np.dtype(dtype).itemsize
    dims = list(shape)
    dims[-1] = -(-dims[-1] // 128) * 128
    if len(dims) > 1:
        rows = 32 // size
        dims[-2] = -(-dims[-2] // rows) * rows
    return int(np.prod(dims)) * size


def call(kernel, outs, scratch, *ins, flops=0, smem=0, name=None, after=(), room=0):
    held = sum(padded_bytes(s.shape, s.dtype) for s in scratch)
    touched = sum(a.size * a.dtype.itemsize for a in list(ins) + list(outs))
    n_in, n_after = len(ins), len(after)

    def run(*refs):
        kernel(*refs[:n_in], *refs[n_in + n_after :])

    return pl.pallas_call(
        run,
        out_shape=tuple(outs),
        in_specs=[pl.BlockSpec(memory_space=pltpu.SMEM)] * smem
        + [pl.BlockSpec(memory_space=pltpu.VMEM)] * (n_in - smem)
        + [pl.BlockSpec(memory_space=pl.ANY)] * n_after,
        out_specs=tuple(pl.BlockSpec(memory_space=pltpu.VMEM) for _ in outs),
        scratch_shapes=list(scratch),
        compiler_params=pltpu.CompilerParams(vmem_limit_bytes=held + 4 * 2**20 + room),
        cost_estimate=pl.CostEstimate(flops=int(flops), bytes_accessed=touched, transcendentals=0),
        name=name,
    )(*ins, *after)


def out(shape, dtype=f32):
    return jax.ShapeDtypeStruct(shape, dtype)


def fold(x):
    return jnp.sum(x.reshape(x.shape[0] // 8, 8, x.shape[1]), axis=0)


def rows_at(start, size, unit=16):
    return pl.ds(pl.multiple_of(start, unit), size)


def put_rows(ref, parts):
    ref[...] = jnp.zeros_like(ref)
    for k, part in enumerate(parts):
        ref[k : k + 1, :] = jnp.sum(part, axis=0, keepdims=True)


def gather_sum(refs):
    total = refs[0][...]
    for ref in refs[1:]:
        total = total + ref[...]
    return total


def norm_terms(total, row, amount, gain, shift):
    mean = total[row : row + 1] / amount
    inverse = lax.rsqrt(total[row + 1 : row + 2] / amount - mean * mean + norm_eps)
    scale = gain * inverse
    return mean, inverse, scale, shift - mean * scale


def put_norm(ref, row, terms):
    for k, term in enumerate(terms):
        ref[row + k : row + k + 1, :] = term


def dot(a, b):
    return jnp.dot(a, b, preferred_element_type=f32)


def dot_t(a, b):
    return lax.dot_general(a, b, (((1,), (1,)), ((), ())), preferred_element_type=f32)


def t_dot(a, b):
    return lax.dot_general(a, b, (((0,), (0,)), ((), ())), preferred_element_type=f32)


def prepare_kernel(sz, ig_ref, il_ref, x_ref, halo_ref, s_ref, t_ref):
    m = sz.m

    def split(x, n_rows):
        s_ref[0:n_rows, :] = x[:, :128]
        t_ref[0:n_rows, 0:64] = x[:, 128:]
        parts = []
        for pc in range(2):
            v = s_ref[pl.ds(pc, n_rows // 2, stride=2), :]
            w = t_ref[pl.ds(pc, n_rows // 2, stride=2), :]
            parts.append(jnp.concatenate([v, w[:, :64]], axis=1))
        return parts

    @pl.loop(0, sz.ng)
    def _(n):
        n_rows = sz.hg * sz.wg
        parts = split(ig_ref[n].astype(f32).reshape(n_rows, CIN), n_rows)
        for pc in range(2):
            v = parts[pc].reshape(sz.hg, sz.cg, CIN).astype(bf16)
            for r in range(sz.hg):
                phase = 2 * (r % 2) + pc
                x_ref[rows_at(phase * m + (r // 2) * sz.bg + n * sz.cg, sz.cg), :] = v[r]

    @pl.loop(0, sz.nl // 2)
    def _(pair):
        n_rows = 2 * sz.hl * sz.wl
        both = jnp.concatenate(
            [
                il_ref[2 * pair + k].astype(f32).reshape(sz.hl * sz.wl, CIN)
                for k in range(2)
            ],
            axis=0,
        )
        parts = split(both, n_rows)
        for pc in range(2):
            v = parts[pc].reshape(2 * sz.hl, sz.cl, CIN)
            for r in range(sz.hl):
                phase = 2 * (r % 2) + pc
                joined = jnp.concatenate([v[r], v[sz.hl + r]], axis=0).astype(bf16)
                x_ref[
                    rows_at(phase * m + sz.mg + (r // 2) * sz.bl + pair * 2 * sz.cl, 2 * sz.cl), :
                ] = joined

    for pc in range(2):
        base = (2 + pc) * m
        halo_ref[pc * sz.edge : pc * sz.edge + sz.bg, :] = x_ref[
            base + sz.mg - sz.bg : base + sz.mg, :
        ]
        halo_ref[pc * sz.edge + sz.bg : (pc + 1) * sz.edge, :] = x_ref[
            base + m - sz.bl : base + m, :
        ]


def input_stats_kernel(sz, x_ref, w_ref, s_ref, st_ref):
    n_rows = sz.m // 3
    zero = jnp.zeros((8, C), f32)

    def stats(ref):
        def step(i, carry):
            total, square = carry
            z = dot(x_ref[rows_at(i * n_rows, n_rows), :], ref[...])
            return total + fold(z), square + fold(z * z)

        return step

    sum_a, sq_a = lax.fori_loop(0, 12, stats(w_ref), (zero, zero))
    sum_s, sq_s = lax.fori_loop(0, 3, stats(s_ref), (zero, zero))
    put_rows(st_ref, [sum_a, sq_a, sum_s, sq_s])


def block_diagonal(k_ref, bd_ref):
    rows = lax.broadcasted_iota(jnp.int32, (HALF, HALF), 0) // GW
    cols = lax.broadcasted_iota(jnp.int32, (HALF, HALF), 1) // GW
    same = rows == cols
    for tap in range(9):
        for half in range(2):
            k = k_ref[tap * GW : (tap + 1) * GW, half * HALF : (half + 1) * HALF].astype(f32)
            bd_ref[2 * tap + half] = jnp.where(same, jnp.concatenate([k] * 4, axis=0), 0.0).astype(
                bf16
            )


def strided_product(sz, x_ref, s_ref, zs):
    n_rows = sz.m // 3

    @pl.loop(0, 3)
    def _(i):
        zs[rows_at(i * n_rows, n_rows), :] = dot(x_ref[rows_at(i * n_rows, n_rows), :], s_ref[...])


def block_dense(acc):
    rows = lax.broadcasted_iota(jnp.int32, (HALF, HALF), 0) // GW
    cols = lax.broadcasted_iota(jnp.int32, (HALF, HALF), 1) // GW
    kept = jnp.where(rows == cols, acc, 0.0)
    return jnp.sum(kept.reshape(4, GW, HALF), axis=0)


def shifted(v, by, width):
    n_rows = v.shape[0]
    col = lax.broadcasted_iota(jnp.int32, v.shape, 0) % width
    if by < 0:
        return jnp.where(col == 0, 0.0, pltpu.roll(v, 1, 0))
    return jnp.where(col == width - 1, 0.0, pltpu.roll(v, n_rows - 1, 0))


def segments(sz):
    g_rows = 4 * sz.cg
    l_rows = 6 * sz.cl
    return g_rows, l_rows


def conv_product(windows, bd_ref, half, n_rows, transposed):
    acc = None
    cols = pl.ds(pl.multiple_of(half * HALF, HALF), HALF)
    for tap, ref, start in windows:
        x = ref[start : start + n_rows, cols]
        w = bd_ref[2 * tap + half]
        term = dot_t(x, w) if transposed else dot(x, w)
        acc = term if acc is None else acc + term
    return acc


def windows_one(sz, refs, part):
    a00, a01, a01s, a10, a11, a11s = refs
    plain = 0 if part == "g" else sz.mg
    above = 0 if part == "g" else sz.one_l
    here = above + (sz.bg if part == "g" else sz.bl)
    result = []
    for tap in range(9):
        a, b = tap // 3, tap % 3
        if a == 1:
            result.append((tap, (a01s, a00, a01)[b], plain))
        else:
            result.append((tap, (a11s, a10, a11)[b], above if a == 0 else here))
    return result


def windows_two(sz, refs, part, flipped=False):
    base = 0 if part == "g" else sz.two_l
    block = sz.bg if part == "g" else sz.bl
    result = []
    for tap in range(9):
        a, b = tap // 3, tap % 3
        if flipped:
            a, b = 2 - a, 2 - b
        result.append((tap, refs[b], base + a * block))
    return result


def shift_windows(windows, by):
    return [(tap, ref, start + by) for tap, ref, start in windows]


def conv_forward(sz, windows_of, bd_ref, z_ref, st_ref, sums):
    sums[...] = jnp.zeros_like(sums)

    @pl.loop(0, 2)
    def _(half):
        cols = pl.ds(pl.multiple_of(half * HALF, HALF), HALF)
        for part, first, n_all, n_rows in (
            ("g", 0, sz.mg, sz.mg // 2),
            ("l", sz.mg, sz.ml, sz.ml),
        ):
            for k in range(n_all // n_rows):
                z = conv_product(
                    shift_windows(windows_of(part), k * n_rows), bd_ref, half, n_rows, False
                )
                z_ref[first + k * n_rows : first + (k + 1) * n_rows, cols] = z
                sums[0:8, cols] += fold(z)
                sums[8:16, cols] += fold(z * z)

    put_rows(st_ref, [sums[0:8, :], sums[8:16, :]])


def first_conv_kernel(
    sz,
    flag_ref,
    x_ref,
    halo_ref,
    w_ref,
    k_ref,
    t0,
    t1,
    t2,
    t3,
    vt_ref,
    z_ref,
    st_ref,
    nrm_ref,
    a00,
    a01,
    a10,
    a11,
    a01s,
    a11s,
    bd_ref,
    zs,
    sums,
):
    block_diagonal(k_ref, bd_ref)
    total = gather_sum((t0, t1, t2, t3))
    terms = norm_terms(
        total, 0, 4 * sz.amount, vt_ref[G1A : G1A + 1, :], vt_ref[B1A : B1A + 1, :]
    )
    nrm_ref[...] = jnp.zeros_like(nrm_ref)
    put_norm(nrm_ref, 0, terms)
    put_norm(
        nrm_ref,
        4,
        norm_terms(total, 2, sz.amount, vt_ref[G1S : G1S + 1, :], vt_ref[B1S : B1S + 1, :]),
    )
    scale, shift = terms[2], terms[3]
    g_rows, l_rows = segments(sz)
    third = sz.m // 3

    def activate(src, dst, dst_s, n_rows, width, factor=None):
        v = zs[src, :] * scale + shift
        a = silu(v)
        if factor is not None:
            a = a * factor
        dst[0][dst[1], :] = a.astype(bf16)
        if dst_s is not None:
            dst_s[dst[1], :] = shifted(a, -1, width).astype(bf16)

    plan = [(a00, None, False), (a01, a01s, False), (a10, None, True), (a11, a11s, True)]
    for phase, (dst, dst_s, bordered) in enumerate(plan):

        @pl.loop(0, 3)
        def _(i):
            zs[rows_at(i * third, third), :] = dot(
                x_ref[rows_at(phase * sz.m + i * third, third), :], w_ref[...]
            )

        g_first = sz.bg if bordered else 0
        l_first = sz.one_l + sz.bl if bordered else sz.mg

        @pl.loop(0, sz.mg // g_rows)
        def _(i):
            activate(
                rows_at(i * g_rows, g_rows),
                (dst, rows_at(g_first + i * g_rows, g_rows)),
                dst_s,
                g_rows,
                sz.cg,
            )

        @pl.loop(0, sz.ml // l_rows)
        def _(i):
            activate(
                rows_at(sz.mg + i * l_rows, l_rows),
                (dst, rows_at(l_first + i * l_rows, l_rows)),
                dst_s,
                l_rows,
                sz.cl,
            )

    flag = flag_ref[0]
    for pc, (dst, dst_s) in enumerate(((a10, None), (a11, a11s))):
        zs[0 : sz.edge, :] = dot(halo_ref[pc * sz.edge : (pc + 1) * sz.edge, :], w_ref[...])

        @pl.loop(0, sz.bg // g_rows)
        def _(i):
            rows = rows_at(i * g_rows, g_rows)
            activate(rows, (dst, rows), dst_s, g_rows, sz.cg, flag)

        @pl.loop(0, sz.bl // l_rows)
        def _(i):
            activate(
                rows_at(sz.bg + i * l_rows, l_rows),
                (dst, rows_at(sz.one_l + i * l_rows, l_rows)),
                dst_s,
                l_rows,
                sz.cl,
                flag,
            )

    refs = (a00, a01, a01s, a10, a11, a11s)
    conv_forward(sz, lambda part: windows_one(sz, refs, part), bd_ref, z_ref, st_ref, sums)


def each_crop(sz, one):
    @pl.loop(0, sz.ng)
    def _(n):
        one([rows_at(i * sz.bg + n * sz.cg, sz.cg) for i in range(sz.rg)], (n,))

    @pl.loop(0, sz.nl // 2)
    def _(pair):
        first = sz.ng + 2 * pair
        one(
            [rows_at(sz.mg + i * sz.bl + pair * 2 * sz.cl, 2 * sz.cl) for i in range(sz.rl)],
            (first, first + 1),
        )


def add_pool(ref, crops, value):
    if len(crops) == 1:
        ref[pl.ds(crops[0], 1), :] = jnp.sum(value, axis=0, keepdims=True)
    else:
        n = value.shape[0] // 2
        ref[pl.ds(crops[0], 1), :] = jnp.sum(value[:n], axis=0, keepdims=True)
        ref[pl.ds(crops[1], 1), :] = jnp.sum(value[n:], axis=0, keepdims=True)


def crop_rows(ref, crops, n_rows):
    if len(crops) == 1:
        return ref[pl.ds(crops[0], 1), :]
    n = n_rows // 2
    return jnp.concatenate(
        [jnp.broadcast_to(ref[pl.ds(crop, 1), :], (n, ref.shape[1])) for crop in crops], axis=0
    )


def pool_kernel(sz, gain_row, shift_row, z_ref, t0, t1, t2, t3, vt_ref, pool_ref, nrm_ref, ps):
    terms = norm_terms(
        gather_sum((t0, t1, t2, t3)),
        0,
        sz.amount,
        vt_ref[gain_row : gain_row + 1, :],
        vt_ref[shift_row : shift_row + 1, :],
    )
    nrm_ref[...] = jnp.zeros_like(nrm_ref)
    put_norm(nrm_ref, 0, terms)
    scale, shift = terms[2], terms[3]
    ps[...] = jnp.zeros_like(ps)

    def one(pieces, crops):
        acc = None
        for rows in pieces:
            c = silu(z_ref[rows, :] * scale + shift)
            acc = c if acc is None else acc + c
        add_pool(ps, crops, acc)

    each_crop(sz, one)
    pool_ref[...] = ps[...].astype(bf16)


def inverse_area(sz):
    crop = lax.broadcasted_iota(jnp.int32, (sz.crops, 1), 0)
    return jnp.where(crop < sz.ng, 1.0 / sz.area_g, 1.0 / sz.area_l).astype(f32)


def dot_high(a, b):
    return jnp.dot(a, b, precision=highest, preferred_element_type=f32)


def gather_short(refs):
    total = refs[0][...].astype(f32)
    for ref in refs[1:]:
        total = total + ref[...].astype(f32)
    return total


def gated_product_kernel(
    sz,
    shift_row,
    z_in_ref,
    nrm_ref,
    p0,
    p1,
    p2,
    p3,
    d_ref,
    e_ref,
    u_ref,
    w_ref,
    vt_ref,
    q_ref,
    z_ref,
    st_ref,
    gate_ref,
    pooled_ref,
    pre_ref,
):
    pooled = gather_short((p0, p1, p2, p3)) * inverse_area(sz)
    pooled_ref[...] = pooled
    pre = dot_high(pooled, d_ref[...].astype(f32)) + e_ref[...]
    pre_ref[...] = pre
    gate = dot_high(silu(pre), u_ref[...].astype(f32)) + vt_ref[shift_row : shift_row + 1, :]
    gate_ref[...] = sigmoid(gate)
    scale = nrm_ref[2:3, :]
    shift = nrm_ref[3:4, :]

    def one(pieces, crops):
        g = crop_rows(gate_ref, crops, 2 * sz.cl)
        for rows in pieces:
            c = silu(z_in_ref[rows, :] * scale + shift)
            q_ref[rows, :] = (c * g).astype(bf16)

    each_crop(sz, one)
    n_rows = sz.m // 3
    zero = jnp.zeros((8, C), f32)

    def step(i, carry):
        total, square = carry
        rows = rows_at(i * n_rows, n_rows)
        z = dot(q_ref[rows, :], w_ref[...])
        z_ref[rows, :] = z
        return total + fold(z), square + fold(z * z)

    put_rows(st_ref, lax.fori_loop(0, 3, step, (zero, zero)))


ROWS = 32


def put_edges(sz, src, top_ref, bottom_ref):
    for ref, g, l in (
        (top_ref, 0, sz.mg),
        (bottom_ref, sz.mg - sz.bg, sz.m - sz.bl),
    ):
        if ref is not None:
            ref[0 : sz.bg, :] = src[g : g + sz.bg, :]
            ref[sz.bg : sz.edge, :] = src[l : l + sz.bl, :]


def middle_kernel(
    sz,
    zc_ref,
    x_ref,
    s_ref,
    t0,
    t1,
    t2,
    t3,
    nrm_a_ref,
    vt_ref,
    pre_ref,
    mb_ref,
    nrm_ref,
    top_ref,
    bottom_ref,
    zs,
):
    strided_product(sz, x_ref, s_ref, zs)
    terms = norm_terms(
        gather_sum((t0, t1, t2, t3)),
        0,
        sz.amount,
        vt_ref[G1C : G1C + 1, :],
        vt_ref[B1C : B1C + 1, :],
    )
    nrm_ref[...] = jnp.zeros_like(nrm_ref)
    put_norm(nrm_ref, 0, terms)
    scale = terms[2]
    scale_s = nrm_a_ref[6:7, :]
    shift = terms[3] + nrm_a_ref[7:8, :]

    @pl.loop(0, sz.m // ROWS)
    def _(i):
        rows = rows_at(i * ROWS, ROWS)
        pre = zc_ref[rows, :] * scale + zs[rows, :] * scale_s + shift
        pre_ref[rows, :] = pre
        mb_ref[rows, :] = silu(pre).astype(bf16)

    put_edges(sz, mb_ref, top_ref, bottom_ref)


def product_kernel(sz, x_ref, w_ref, z_ref, st_ref):
    n_rows = sz.m // 3
    zero = jnp.zeros((8, C), f32)

    def step(i, carry):
        total, square = carry
        rows = rows_at(i * n_rows, n_rows)
        z = dot(x_ref[rows, :], w_ref[...])
        z_ref[rows, :] = z
        return total + fold(z), square + fold(z * z)

    put_rows(st_ref, lax.fori_loop(0, 3, step, (zero, zero)))


def put_variants(refs, rows, value, width):
    refs[0][rows, :] = shifted(value, -1, width).astype(bf16)
    refs[1][rows, :] = value.astype(bf16)
    refs[2][rows, :] = shifted(value, 1, width).astype(bf16)


def second_conv_kernel(
    sz,
    flag_ref,
    z_in_ref,
    top_ref,
    bottom_ref,
    w_ref,
    k_ref,
    t0,
    t1,
    t2,
    t3,
    vt_ref,
    z_ref,
    st_ref,
    nrm_ref,
    a1,
    a0,
    a2,
    bd_ref,
    zs,
    sums,
):
    block_diagonal(k_ref, bd_ref)
    terms = norm_terms(
        gather_sum((t0, t1, t2, t3)),
        0,
        sz.amount,
        vt_ref[G2A : G2A + 1, :],
        vt_ref[B2A : B2A + 1, :],
    )
    nrm_ref[...] = jnp.zeros_like(nrm_ref)
    put_norm(nrm_ref, 0, terms)
    scale, shift = terms[2], terms[3]
    g_rows, l_rows = segments(sz)
    refs = (a0, a1, a2)

    @pl.loop(0, sz.mg // g_rows)
    def _(i):
        a = silu(z_in_ref[rows_at(i * g_rows, g_rows), :] * scale + shift)
        put_variants(refs, rows_at(sz.bg + i * g_rows, g_rows), a, sz.cg)

    @pl.loop(0, sz.ml // l_rows)
    def _(i):
        a = silu(z_in_ref[rows_at(sz.mg + i * l_rows, l_rows), :] * scale + shift)
        put_variants(refs, rows_at(sz.two_l + sz.bl + i * l_rows, l_rows), a, sz.cl)

    for k, src in enumerate((top_ref, bottom_ref)):
        flag = flag_ref[k]
        zs[...] = dot(src[...], w_ref[...])
        g_first = 0 if k == 0 else (sz.rg + 1) * sz.bg
        l_first = sz.two_l + (0 if k == 0 else (sz.rl + 1) * sz.bl)

        @pl.loop(0, sz.bg // g_rows)
        def _(i):
            a = silu(zs[rows_at(i * g_rows, g_rows), :] * scale + shift) * flag
            put_variants(refs, rows_at(g_first + i * g_rows, g_rows), a, sz.cg)

        @pl.loop(0, sz.bl // l_rows)
        def _(i):
            a = silu(zs[rows_at(sz.bg + i * l_rows, l_rows), :] * scale + shift) * flag
            put_variants(refs, rows_at(l_first + i * l_rows, l_rows), a, sz.cl)

    conv_forward(sz, lambda part: windows_two(sz, refs, part), bd_ref, z_ref, st_ref, sums)


def output_kernel(
    sz, pre_ref, z_ref, t0, t1, t2, t3, vt_ref, cg_ref, cl_ref, og_ref, ol_ref, dn_ref, st_ref, nrm_ref, sums
):
    terms = norm_terms(
        gather_sum((t0, t1, t2, t3)),
        0,
        sz.amount,
        vt_ref[G2C : G2C + 1, :],
        vt_ref[B2C : B2C + 1, :],
    )
    nrm_ref[...] = jnp.zeros_like(nrm_ref)
    put_norm(nrm_ref, 0, terms)
    mean, inverse, scale, shift = terms
    sums[...] = jnp.zeros_like(sums)

    def piece(rows, cot):
        z = z_ref[rows, :]
        pre = silu(pre_ref[rows, :]) + z * scale + shift
        s = sigmoid(pre)
        dn = cot * (s * (1.0 + pre * (1.0 - s)))
        dn_ref[rows, :] = dn
        sums[0:8, :] += fold(dn)
        sums[8:16, :] += fold(dn * ((z - mean) * inverse))
        return pre * s

    @pl.loop(0, sz.ng)
    def _(n):
        for i in range(sz.rg):
            rows = rows_at(i * sz.bg + n * sz.cg, sz.cg)
            og_ref[n, i] = piece(rows, cg_ref[n, i].astype(f32)).astype(bf16)

    @pl.loop(0, sz.nl // 2)
    def _(pair):
        for i in range(sz.rl):
            rows = rows_at(sz.mg + i * sz.bl + pair * 2 * sz.cl, 2 * sz.cl)
            cot = jnp.concatenate(
                [cl_ref[2 * pair + k, i].astype(f32) for k in range(2)], axis=0
            )
            value = piece(rows, cot)
            for k in range(2):
                ol_ref[2 * pair + k, i] = value[k * sz.cl : (k + 1) * sz.cl].astype(bf16)

    put_rows(st_ref, [sums[0:8, :], sums[8:16, :]])


def back_terms(total, row_one, row_two, amount, nrm_ref, nrm_row):
    mean = nrm_ref[nrm_row : nrm_row + 1, :]
    inverse = nrm_ref[nrm_row + 1 : nrm_row + 2, :]
    scale = nrm_ref[nrm_row + 2 : nrm_row + 3, :]
    one = total[row_one : row_one + 1] / amount
    two = total[row_two : row_two + 1] / amount
    return scale, one, mean, inverse * two


def norm_back(dn, z, terms):
    scale, one, mean, slope = terms
    return scale * (dn - one - (z - mean) * slope)


def gate_grad_kernel(
    sz,
    strided,
    dn_ref,
    z_ref,
    t0,
    t1,
    t2,
    t3,
    nrm_ref,
    w_ref,
    z_in_ref,
    nrm_in_ref,
    *refs,
):
    if strided:
        x_ref, s_ref, nrm_a_ref, dz_ref, dzs_ref, dq_ref, dg_ref, ps, zs = refs
        strided_product(sz, x_ref, s_ref, zs)
    else:
        dz_ref, dq_ref, dg_ref, ps = refs
    total = gather_sum((t0, t1, t2, t3))
    terms = back_terms(total, 0, 1, sz.amount, nrm_ref, 0)

    @pl.loop(0, sz.m // ROWS)
    def _(i):
        rows = rows_at(i * ROWS, ROWS)
        dz_ref[rows, :] = norm_back(dn_ref[rows, :], z_ref[rows, :], terms).astype(bf16)

    if strided:
        terms_s = back_terms(total, 0, 2, sz.amount, nrm_a_ref, 4)

        @pl.loop(0, sz.m // ROWS)
        def _(i):
            rows = rows_at(i * ROWS, ROWS)
            dzs_ref[rows, :] = norm_back(dn_ref[rows, :], zs[rows, :], terms_s).astype(bf16)

    n_rows = sz.m // 3

    @pl.loop(0, 3)
    def _(i):
        rows = rows_at(i * n_rows, n_rows)
        dq_ref[rows, :] = dot_t(dz_ref[rows, :], w_ref[...])

    ps[...] = jnp.zeros_like(ps)
    scale = nrm_in_ref[2:3, :]
    shift = nrm_in_ref[3:4, :]

    def one(pieces, crops):
        acc = None
        for rows in pieces:
            term = dq_ref[rows, :] * silu(z_in_ref[rows, :] * scale + shift)
            acc = term if acc is None else acc + term
        add_pool(ps, crops, acc)

    each_crop(sz, one)
    dg_ref[...] = ps[...].astype(bf16)


def excite_back_kernel(
    sz,
    dq_ref,
    z_ref,
    nrm_ref,
    g0,
    g1,
    g2,
    g3,
    gate_ref,
    pre_ref,
    d_ref,
    u_ref,
    dn_ref,
    st_ref,
    dv_ref,
    du_ref,
    pool,
    sums,
):
    gate = gate_ref[...]
    dv = gather_short((g0, g1, g2, g3)) * gate * (1.0 - gate)
    dv_ref[...] = dv
    du = lax.dot_general(
        dv,
        u_ref[...].astype(f32),
        (((1,), (1,)), ((), ())),
        precision=highest,
        preferred_element_type=f32,
    ) * silu_slope(pre_ref[...])
    du_ref[...] = du
    pool[...] = (
        lax.dot_general(
            du,
            d_ref[...].astype(f32),
            (((1,), (1,)), ((), ())),
            precision=highest,
            preferred_element_type=f32,
        )
        * inverse_area(sz)
    )
    mean = nrm_ref[0:1, :]
    inverse = nrm_ref[1:2, :]
    scale = nrm_ref[2:3, :]
    shift = nrm_ref[3:4, :]
    sums[...] = jnp.zeros_like(sums)

    def one(pieces, crops):
        g = crop_rows(gate_ref, crops, 2 * sz.cl)
        p = crop_rows(pool, crops, 2 * sz.cl)
        for rows in pieces:
            z = z_ref[rows, :]
            dn = (dq_ref[rows, :] * g + p) * silu_slope(z * scale + shift)
            dn_ref[rows, :] = dn
            sums[0:8, :] += fold(dn)
            sums[8:16, :] += fold(dn * ((z - mean) * inverse))

    each_crop(sz, one)
    put_rows(st_ref, [sums[0:8, :], sums[8:16, :]])


def put_flat(value_ref, width, flat_ref, slots):
    if width == 128:
        for j in range(C // 128):
            flat_ref[:, j * 128 : (j + 1) * 128] = value_ref[pl.ds(j, width, stride=C // 128), :]
        return
    n_lines = width // int(np.gcd(C, width))
    n_groups = width // n_lines
    per = C // n_groups
    lane = lax.broadcasted_iota(jnp.int32, (n_groups, C), 1)
    lines = [jnp.zeros((n_groups, C), f32) for _ in range(n_lines)]
    for u in range(per):
        row = value_ref[pl.ds(u, n_groups, stride=per), :]
        row = jnp.concatenate([row] + [jnp.zeros_like(row)] * (C // 128 - 1), axis=1)
        line, at = divmod(u * width, C)
        moved = pltpu.roll(row, at, 1) if at else row
        lines[line] = jnp.where(lane >= at, lines[line] + moved, lines[line])
        if at + width > C:
            lines[line + 1] = jnp.where(
                lane < at + width - C, lines[line + 1] + moved, lines[line + 1]
            )
    for j in range(C // 128):
        for k, line in enumerate(lines):
            slots[pl.ds(k, n_groups, stride=n_lines), :] = line[:, j * 128 : (j + 1) * 128]
        flat_ref[:, j * 128 : (j + 1) * 128] = slots[0:width, :]


def excite_weights_kernel(
    width, flag_ref, dv_ref, du_ref, pooled_ref, pre_ref, dd_ref, de_ref, du_out, df_ref, wide, slots
):
    flag = flag_ref[2]
    dv = dv_ref[...] * flag
    du = du_ref[...] * flag

    def cross(a, b):
        return lax.dot_general(
            a, b, (((0,), (0,)), ((), ())), precision=highest, preferred_element_type=f32
        )

    wide[...] = cross(pooled_ref[...], du)
    put_flat(wide, width, dd_ref, slots)
    du_out[...] = cross(silu(pre_ref[...]), dv)
    de_ref[...] = jnp.broadcast_to(jnp.sum(du, axis=0, keepdims=True), de_ref.shape)
    df_ref[...] = jnp.broadcast_to(jnp.sum(dv, axis=0, keepdims=True), df_ref.shape)


def weight_kernel(x_ref, dz_ref, w_ref):
    n_rows = dz_ref.shape[0]
    n = 128 if x_ref.shape[1] % 128 == 0 else x_ref.shape[1]
    for k in range(x_ref.shape[1] // n):
        w_ref[k * n : (k + 1) * n, :] = t_dot(x_ref[0:n_rows, k * n : (k + 1) * n], dz_ref[...])


def norm_back_kernel(sz, dn_ref, z_ref, t0, t1, t2, t3, nrm_ref, dz_ref, top_ref, bottom_ref=None):
    terms = back_terms(gather_sum((t0, t1, t2, t3)), 0, 1, sz.amount, nrm_ref, 0)

    @pl.loop(0, sz.m // ROWS)
    def _(i):
        rows = rows_at(i * ROWS, ROWS)
        dz_ref[rows, :] = norm_back(dn_ref[rows, :], z_ref[rows, :], terms).astype(bf16)

    put_edges(sz, dz_ref, top_ref, bottom_ref)


def conv_weights(sz, windows_of, dz_ref, dk_ref):
    @pl.loop(0, 2)
    def _(half):
        cols = pl.ds(pl.multiple_of(half * HALF, HALF), HALF)
        win_g = windows_of("g")
        win_l = windows_of("l")
        for tap in range(9):
            _, ref_g, start_g = win_g[tap]
            _, ref_l, start_l = win_l[tap]
            acc = t_dot(ref_g[start_g : start_g + sz.mg, cols], dz_ref[0 : sz.mg, cols])
            acc = acc + t_dot(ref_l[start_l : start_l + sz.ml, cols], dz_ref[sz.mg : sz.m, cols])
            dk_ref[tap * GW : (tap + 1) * GW, cols] = block_dense(acc)


def shift_all(src, dst, by, spans):
    for first, n_all, n_rows, width in spans:

        @pl.loop(0, n_all // n_rows)
        def _(i):
            rows = rows_at(first + i * n_rows, n_rows)
            dst[rows, :] = shifted(src[rows, :].astype(f32), by, width).astype(bf16)


def second_conv_weights_kernel(sz, a1, dz_ref, dk_ref, a0, a2):
    g_rows, l_rows = segments(sz)
    spans = ((0, sz.two_l, g_rows, sz.cg), (sz.two_l, sz.two - sz.two_l, l_rows, sz.cl))
    shift_all(a1, a0, -1, spans)
    shift_all(a1, a2, 1, spans)
    conv_weights(sz, lambda part: windows_two(sz, (a0, a1, a2), part), dz_ref, dk_ref)


def first_conv_weights_kernel(sz, a00, a01, a10, a11, dz_ref, dk_ref, a01s, a11s):
    g_rows, l_rows = segments(sz)
    shift_all(a01, a01s, -1, ((0, sz.mg, g_rows, sz.cg), (sz.mg, sz.ml, l_rows, sz.cl)))
    shift_all(
        a11,
        a11s,
        -1,
        ((0, sz.one_l, g_rows, sz.cg), (sz.one_l, sz.one - sz.one_l, l_rows, sz.cl)),
    )
    refs = (a00, a01, a01s, a10, a11, a11s)
    conv_weights(sz, lambda part: windows_one(sz, refs, part), dz_ref, dk_ref)


def second_conv_back_kernel(
    sz, dz_ref, top_ref, bottom_ref, k_ref, z_ref, nrm_ref, dn_ref, st_ref, v0, v1, v2, bd_ref, sums
):
    block_diagonal(k_ref, bd_ref)
    refs = (v0, v1, v2)
    g_rows, l_rows = segments(sz)

    @pl.loop(0, sz.mg // g_rows)
    def _(i):
        v = dz_ref[rows_at(i * g_rows, g_rows), :].astype(f32)
        put_variants(refs, rows_at(sz.bg + i * g_rows, g_rows), v, sz.cg)

    @pl.loop(0, sz.ml // l_rows)
    def _(i):
        v = dz_ref[rows_at(sz.mg + i * l_rows, l_rows), :].astype(f32)
        put_variants(refs, rows_at(sz.two_l + sz.bl + i * l_rows, l_rows), v, sz.cl)

    for k, src in enumerate((top_ref, bottom_ref)):
        g_first = 0 if k == 0 else (sz.rg + 1) * sz.bg
        l_first = sz.two_l + (0 if k == 0 else (sz.rl + 1) * sz.bl)

        @pl.loop(0, sz.bg // g_rows)
        def _(i):
            v = src[rows_at(i * g_rows, g_rows), :].astype(f32)
            put_variants(refs, rows_at(g_first + i * g_rows, g_rows), v, sz.cg)

        @pl.loop(0, sz.bl // l_rows)
        def _(i):
            v = src[rows_at(sz.bg + i * l_rows, l_rows), :].astype(f32)
            put_variants(refs, rows_at(l_first + i * l_rows, l_rows), v, sz.cl)

    @pl.loop(0, 2)
    def _(half):
        cols = pl.ds(pl.multiple_of(half * HALF, HALF), HALF)
        for part, first, n_all, n_rows in (
            ("g", 0, sz.mg, sz.mg // 2),
            ("l", sz.mg, sz.ml, sz.ml),
        ):
            for k in range(n_all // n_rows):
                dn_ref[first + k * n_rows : first + (k + 1) * n_rows, cols] = conv_product(
                    shift_windows(windows_two(sz, refs, part, True), k * n_rows),
                    bd_ref,
                    half,
                    n_rows,
                    True,
                )

    slope_pass(sz.m, dn_ref, z_ref, nrm_ref, st_ref, sums)


def slope_pass(n_all, dn_ref, z_ref, nrm_ref, st_ref, sums):
    mean = nrm_ref[0:1, :]
    inverse = nrm_ref[1:2, :]
    scale = nrm_ref[2:3, :]
    shift = nrm_ref[3:4, :]
    sums[...] = jnp.zeros_like(sums)

    @pl.loop(0, n_all // ROWS)
    def _(i):
        rows = rows_at(i * ROWS, ROWS)
        z = z_ref[rows, :]
        dn = dn_ref[rows, :] * silu_slope(z * scale + shift)
        dn_ref[rows, :] = dn
        sums[0:8, :] += fold(dn)
        sums[8:16, :] += fold(dn * ((z - mean) * inverse))

    put_rows(st_ref, [sums[0:8, :], sums[8:16, :]])


def middle_back_kernel(
    sz,
    dn_d_ref,
    zd_ref,
    t0,
    t1,
    t2,
    t3,
    nrm_d_ref,
    w_ref,
    dpre_ref,
    pre_ref,
    zc_ref,
    x_ref,
    s_ref,
    nrm_c_ref,
    nrm_a_ref,
    dz_ref,
    dn_ref,
    st_ref,
    zs,
    sums,
):
    strided_product(sz, x_ref, s_ref, zs)
    terms = back_terms(gather_sum((t0, t1, t2, t3)), 0, 1, sz.amount, nrm_d_ref, 0)

    @pl.loop(0, sz.m // ROWS)
    def _(i):
        rows = rows_at(i * ROWS, ROWS)
        dz_ref[rows, :] = norm_back(dn_d_ref[rows, :], zd_ref[rows, :], terms).astype(bf16)

    n_rows = sz.m // 3

    @pl.loop(0, 3)
    def _(i):
        rows = rows_at(i * n_rows, n_rows)
        dn_ref[rows, :] = dot_t(dz_ref[rows, :], w_ref[...])

    mean_c = nrm_c_ref[0:1, :]
    inverse_c = nrm_c_ref[1:2, :]
    mean_s = nrm_a_ref[4:5, :]
    inverse_s = nrm_a_ref[5:6, :]
    sums[...] = jnp.zeros_like(sums)

    @pl.loop(0, sz.m // ROWS)
    def _(i):
        rows = rows_at(i * ROWS, ROWS)
        dn = (dn_ref[rows, :] + dpre_ref[rows, :]) * silu_slope(pre_ref[rows, :])
        dn_ref[rows, :] = dn
        sums[0:8, :] += fold(dn)
        sums[8:16, :] += fold(dn * ((zc_ref[rows, :] - mean_c) * inverse_c))
        sums[16:24, :] += fold(dn * ((zs[rows, :] - mean_s) * inverse_s))

    put_rows(st_ref, [sums[0:8, :], sums[8:16, :], sums[16:24, :]])


def first_conv_back_kernel(
    sz, dz_ref, below_ref, k_ref, x_ref, w_ref, nrm_ref, dn_ref, st_ref, v0, v1, zs, da, bd_ref, sums
):
    block_diagonal(k_ref, bd_ref)
    g_rows, l_rows = segments(sz)

    def put(rows, v, width):
        v0[rows, :] = v.astype(bf16)
        v1[rows, :] = shifted(v, 1, width).astype(bf16)

    @pl.loop(0, sz.mg // g_rows)
    def _(i):
        put(rows_at(i * g_rows, g_rows), dz_ref[rows_at(i * g_rows, g_rows), :].astype(f32), sz.cg)

    @pl.loop(0, sz.ml // l_rows)
    def _(i):
        put(
            rows_at(sz.one_l + i * l_rows, l_rows),
            dz_ref[rows_at(sz.mg + i * l_rows, l_rows), :].astype(f32),
            sz.cl,
        )

    @pl.loop(0, sz.bg // g_rows)
    def _(i):
        put(
            rows_at(sz.mg + i * g_rows, g_rows),
            below_ref[rows_at(i * g_rows, g_rows), :].astype(f32),
            sz.cg,
        )

    @pl.loop(0, sz.bl // l_rows)
    def _(i):
        put(
            rows_at(sz.one_l + sz.ml + i * l_rows, l_rows),
            below_ref[rows_at(sz.bg + i * l_rows, l_rows), :].astype(f32),
            sz.cl,
        )

    mean = nrm_ref[0:1, :]
    inverse = nrm_ref[1:2, :]
    scale = nrm_ref[2:3, :]
    shift = nrm_ref[3:4, :]
    sums[...] = jnp.zeros_like(sums)
    third = sz.m // 3
    for phase in range(4):
        pr, pc = phase // 2, phase % 2
        taps = []
        for a, down in (((1, 0),), ((2, 0), (0, 1)))[pr]:
            for b, right in (((1, 0),), ((2, 0), (0, 1)))[pc]:
                taps.append((3 * a + b, down, right))

        @pl.loop(0, 2)
        def _(half):
            cols = pl.ds(pl.multiple_of(half * HALF, HALF), HALF)
            for first, base, block, n_all, n_rows in (
                (0, 0, sz.bg, sz.mg, sz.mg // 2),
                (sz.mg, sz.one_l, sz.bl, sz.ml, sz.ml),
            ):
                for k in range(n_all // n_rows):
                    windows = [
                        (tap, (v0, v1)[right], base + down * block + k * n_rows)
                        for tap, down, right in taps
                    ]
                    da[first + k * n_rows : first + (k + 1) * n_rows, cols] = conv_product(
                        windows, bd_ref, half, n_rows, True
                    )

        @pl.loop(0, 3)
        def _(i):
            zs[rows_at(i * third, third), :] = dot(
                x_ref[rows_at(phase * sz.m + i * third, third), :], w_ref[...]
            )

        @pl.loop(0, sz.m // ROWS)
        def _(i):
            rows = rows_at(i * ROWS, ROWS)
            z = zs[rows, :]
            dn = da[rows, :] * silu_slope(z * scale + shift)
            dn_ref[rows_at(phase * sz.m + i * ROWS, ROWS), :] = dn.astype(bf16)
            sums[0:8, :] += fold(dn)
            sums[8:16, :] += fold(dn * ((z - mean) * inverse))

    put_rows(st_ref, [sums[0:8, :], sums[8:16, :]])


def image_norm_back_kernel(sz, dn_ref, x_ref, w_ref, t0, t1, t2, t3, nrm_ref, dz_ref, zs):
    terms = back_terms(gather_sum((t0, t1, t2, t3)), 0, 1, 4 * sz.amount, nrm_ref, 0)
    third = sz.m // 3
    for phase in range(4):

        @pl.loop(0, 3)
        def _(i):
            zs[rows_at(i * third, third), :] = dot(
                x_ref[rows_at(phase * sz.m + i * third, third), :], w_ref[...]
            )

        @pl.loop(0, sz.m // ROWS)
        def _(i):
            rows = rows_at(i * ROWS, ROWS)
            rows_all = rows_at(phase * sz.m + i * ROWS, ROWS)
            dz_ref[rows_all, :] = norm_back(
                dn_ref[rows_all, :].astype(f32), zs[rows, :], terms
            ).astype(bf16)


def image_back_kernel(
    sz,
    dz_ref,
    w_ref,
    dzs_ref,
    ws_ref,
    gg_ref,
    gl_ref,
    dx,
    s_ref,
    t_ref,
):
    third = sz.m // 3
    for phase in range(4):

        @pl.loop(0, 3)
        def _(i):
            rows_all = rows_at(phase * sz.m + i * third, third)
            value = dot_t(dz_ref[rows_all, :], w_ref[...])
            if phase == 0:
                value = value + dot_t(dzs_ref[rows_at(i * third, third), :], ws_ref[...])
            dx[rows_all, :] = value

    def place(first, v):
        n = v.shape[0]
        s_ref[pl.ds(first, n, stride=2), :] = v[:, :128]
        t_ref[pl.ds(first, n, stride=2), :] = jnp.concatenate([v[:, 128:], v[:, 128:]], axis=1)

    @pl.loop(0, sz.ng)
    def _(n):
        for r in range(sz.hg):
            for pc in range(2):
                phase = 2 * (r % 2) + pc
                place(
                    r * sz.wg + pc,
                    dx[rows_at(phase * sz.m + (r // 2) * sz.bg + n * sz.cg, sz.cg), :],
                )
        n_rows = sz.hg * sz.wg
        gg_ref[n, :, :, 0:128] = s_ref[0:n_rows, :].reshape(sz.hg, sz.wg, 128)
        gg_ref[n, :, :, 128:CIN] = t_ref[0:n_rows, :][:, :64].reshape(sz.hg, sz.wg, 64)

    @pl.loop(0, sz.nl)
    def _(n):
        for r in range(sz.hl):
            for pc in range(2):
                phase = 2 * (r % 2) + pc
                place(
                    r * sz.wl + pc,
                    dx[
                        rows_at(phase * sz.m + sz.mg + (r // 2) * sz.bl + n * sz.cl, sz.cl, 8), :
                    ],
                )
        n_rows = sz.hl * sz.wl
        gl_ref[n, :, :, 0:128] = s_ref[0:n_rows, :].reshape(sz.hl, sz.wl, 128)
        gl_ref[n, :, :, 128:CIN] = t_ref[0:n_rows, :][:, :64].reshape(sz.hl, sz.wl, 64)


def over_height(x):
    n = lax.axis_size("height")
    return [x] + [lax.ppermute(x, "height", [(i, i ^ k) for i in range(n)]) for k in range(1, n)]


def step_down(x):
    n = lax.axis_size("height")
    return lax.ppermute(x, "height", [(i, i + 1) for i in range(n - 1)])


def step_up(x):
    n = lax.axis_size("height")
    return lax.ppermute(x, "height", [(i + 1, i) for i in range(n - 1)])


MATRIX_ROWS = [a * b // C for a, b in matrix_shapes()]
ROW_BOUNDS = [int(v) for v in np.cumsum([0] + MATRIX_ROWS)]
UNIT = 112


def across(x, mask, senders=None):
    n = lax.axis_size("batch")
    return lax.ppermute(
        x, "batch", [(i, i ^ mask) for i in range(n) if senders is None or i in senders]
    )


def assemble_kernel(n_rows, idx_ref, *refs):
    ins, outs, shards, whole = refs[:8], refs[8:-2], refs[-2], refs[-1]
    for q in range(8):
        for k in range(4):
            shards[idx_ref[4 * q + k], 0:n_rows, :] = ins[q][k].astype(f32)
    for s in range(32):
        whole[s * n_rows : (s + 1) * n_rows, :] = shards[s, 0:n_rows, :]
    for ref, start in zip(outs, ROW_BOUNDS):
        ref[...] = whole[start : start + ref.shape[0], :].astype(bf16)


def gather_weights(weights, n_rows, after):
    mine = weights.astype(bf16).reshape(n_rows, C)
    quarter = jnp.stack(over_height(mine))
    planes = [quarter] + [across(quarter, mask) for mask in (2, 4, 6)]
    planes += [across(plane, 1) for plane in planes]
    batch, height = lax.axis_index("batch"), lax.axis_index("height")
    idx = jnp.stack(
        [
            (batch ^ mask) * 4 + (height ^ k)
            for mask in (0, 2, 4, 6, 1, 3, 5, 7)
            for k in range(4)
        ]
    ).astype(jnp.int32)
    return call(
        functools.partial(assemble_kernel, n_rows),
        [out((rows, C), bf16) for rows in MATRIX_ROWS],
        [pltpu.VMEM((32, UNIT, C), f32), pltpu.VMEM((32 * n_rows, C), f32)],
        idx,
        *planes,
        smem=1,
        name="assemble",
        after=after,
        room=6 * 2**20,
    )


def pack_kernel(n_rows, first_shard, sources, core_ref, *refs):
    n_src = len(sources)
    ins, (mine_ref, other_ref, buf) = refs[:n_src], refs[n_src:]
    buf[...] = jnp.zeros_like(buf)
    for shard in range(16):
        low = (first_shard + shard) * n_rows
        for (start, stop), ref in zip(sources, ins):
            a, b = max(low, start), min(low + n_rows, stop)
            if a < b:
                buf[shard, a - low : b - low, :] = ref[a - start : b - start, :]
    core = core_ref[2]
    for unit in range(2):
        for h in range(4):
            mine_ref[unit * 4 + h] = buf[(unit * 2 + core) * 4 + h]
            other_ref[unit * 4 + h] = buf[(unit * 2 + 1 - core) * 4 + h].astype(bf16)


def height_parts_kernel(place_ref, mine_ref, got_ref, keep_ref, s1, s2, s3):
    place = place_ref[3]
    for unit in range(2):
        for k, ref in enumerate((keep_ref, s1, s2, s3)):
            at = unit * 4 + (place ^ k)
            ref[unit] = (mine_ref[at] + got_ref[at].astype(f32)).astype(ref.dtype)


def height_sum_kernel(keep_ref, r1, r2, r3, sum_ref, low_ref):
    total = keep_ref[...] + r1[...].astype(f32) + r2[...].astype(f32) + r3[...].astype(f32)
    sum_ref[...] = total
    low_ref[...] = total.astype(bf16)


def plane_parts_kernel(x_ref, sum_ref, got_ref, keep_ref, send_ref):
    x = x_ref[1]
    keep_ref[...] = sum_ref[x] + got_ref[x].astype(f32)
    send_ref[...] = (sum_ref[1 - x] + got_ref[1 - x].astype(f32)).astype(bf16)


class Reduction:
    def __init__(self, root, n_rows, place_ids):
        self.root, self.n_rows, self.ids = root, n_rows, place_ids
        self.tag = "_%d" % root

    def pack(self, sources, arrays):
        eight = (8, UNIT, C)
        mine, other = call(
            functools.partial(pack_kernel, self.n_rows, 16 * self.root, sources),
            [out(eight), out(eight, bf16)],
            [pltpu.VMEM((16, UNIT, C), f32)],
            self.ids,
            *arrays,
            smem=1,
            name="pack" + self.tag,
        )
        self.mine, self.got = mine, across(other, 1)
        return [mine]

    def height(self):
        two = (2, UNIT, C)
        low = out(two, bf16)
        self.keep, *sends = call(
            height_parts_kernel,
            [out(two), low, low, low],
            [],
            self.ids,
            self.mine,
            self.got,
            smem=1,
            name="height_parts" + self.tag,
        )
        self.parts = [
            lax.ppermute(send, "height", [(i, i ^ k) for i in range(4)])
            for k, send in zip((1, 2, 3), sends)
        ]
        return [self.keep]

    def add_height(self):
        two = (2, UNIT, C)
        self.total, low = call(
            height_sum_kernel,
            [out(two), out(two, bf16)],
            [],
            self.keep,
            *self.parts,
            name="height_sum" + self.tag,
        )
        self.got = across(low, 4, [b for b in range(8) if b // 4 != self.root])
        return [self.total]

    def plane(self):
        keep, send = call(
            plane_parts_kernel,
            [out((UNIT, C)), out((UNIT, C), bf16)],
            [],
            self.ids,
            self.total,
            self.got,
            smem=1,
            name="plane_parts" + self.tag,
        )
        self.result = keep, across(send, 2, [b for b in range(8) if b // 4 == self.root])
        return [keep]


def halves_kernel(core_ref, g_ref, mine_ref, other_ref):
    core = core_ref[2]
    n = mine_ref.shape[0]
    mine_ref[...] = g_ref[rows_at(core * n, n), :]
    other_ref[...] = g_ref[rows_at((1 - core) * n, n), :].astype(bf16)


def add_kernel(a_ref, b_ref, low_ref):
    low_ref[...] = (a_ref[...].astype(f32) + b_ref[...].astype(f32)).astype(bf16)


def ordered_sum_kernel(place_ref, r0, r1, r2, r3, low_ref, slots):
    place = place_ref[3]
    for k, ref in enumerate((r0, r1, r2, r3)):
        slots[place ^ k] = ref[...]
    total = slots[0].astype(f32)
    for k in range(1, 4):
        total = total + slots[k].astype(f32)
    low_ref[...] = total.astype(bf16)


def sum_everywhere(grad, place_ids):
    half = (grad.shape[0] // 2, C)
    low = out(half, bf16)
    mine, other = call(
        halves_kernel, [out(half), low], [], place_ids, grad, smem=1, name="halves"
    )
    (total,) = call(add_kernel, [low], [], mine, across(other, 1), name="add_core")
    (total,) = call(add_kernel, [low], [], total, across(total, 2), name="add_x")
    (total,) = call(add_kernel, [low], [], total, across(total, 4), name="add_y")
    (total,) = call(
        ordered_sum_kernel,
        [low],
        [pltpu.VMEM((4,) + half, bf16)],
        place_ids,
        *over_height(total),
        smem=1,
        name="add_height",
    )
    return total, across(total, 1)


def lamb_kernel(
    n_rows,
    place_ref,
    ka_ref,
    ra_ref,
    kb_ref,
    rb_ref,
    h_mine_ref,
    h_other_ref,
    w_ref,
    m_ref,
    v_ref,
    first_ref,
    second_ref,
    update_ref,
    sums_ref,
    g_ref,
):
    y, core, shard = place_ref[0], place_ref[2], place_ref[4]
    low_a = ka_ref[...] + ra_ref[...].astype(f32)
    low_b = kb_ref[...] + rb_ref[...].astype(f32)
    g_ref[...] = jnp.where(y == 1, low_a, low_b)
    n_first = MATRIX_ROWS[0]
    half = n_first // 2
    top = jnp.where(core == 0, h_mine_ref[...], h_other_ref[...]).astype(f32)
    end = jnp.where(core == 0, h_other_ref[...], h_mine_ref[...]).astype(f32)

    @pl.when(shard == 0)
    def _():
        g_ref[0:half, :] = top
        g_ref[half:n_rows, :] = end[0 : n_rows - half]

    @pl.when(shard == 1)
    def _():
        g_ref[0 : n_first - n_rows, :] = end[n_rows - half :]

    w = w_ref[...]
    first, second, update = lamb_terms(w, g_ref[0:n_rows, :], m_ref[...], v_ref[...], weight_decay)
    first_ref[...] = first
    second_ref[...] = second
    update_ref[...] = update
    member = membership(n_rows, shard)
    sums_ref[...] = jnp.zeros_like(sums_ref)
    for k, value in enumerate((w, update)):
        by_row = jnp.sum(value * value, axis=1, keepdims=True)
        sums_ref[k : k + 1, 0:128] = jnp.sum(member * by_row, axis=0, keepdims=True)


def membership(n_rows, shard):
    row = lax.broadcasted_iota(jnp.int32, (n_rows, 128), 0) + shard * n_rows
    lane = lax.broadcasted_iota(jnp.int32, (n_rows, 128), 1)
    result = jnp.zeros((n_rows, 128), f32)
    for k in range(len(MATRIX_ROWS)):
        inside = (row >= ROW_BOUNDS[k]) & (row < ROW_BOUNDS[k + 1]) & (lane == k)
        result = jnp.where(inside, 1.0, result)
    return result


VEC_ROWS = 24
PIECES = [0, 1, 2, 3, 16, 4, 5, 6, 7, 8, 9, 10, 11, 12, 17, 13, 14, 15]


def vector_table(flat):
    parts = cut_pieces(flat, vector_sizes())
    rows = [None] * 18
    for part, row in zip(parts, PIECES):
        rows[row] = jnp.pad(part, (0, C - part.shape[0]))
    return jnp.pad(jnp.stack(rows), ((0, VEC_ROWS - 18), (0, 0)))


def flat_vector(table):
    return jnp.concatenate(
        [table[row, :size] for row, size in zip(PIECES, vector_sizes())]
    )


def vector_grads_kernel(a, b, cs, d, e, f, de1, df1, de2, df2, sums_ref, o_ref):
    o_ref[...] = jnp.zeros_like(o_ref)
    plan = [
        (G1A, a, 1),
        (B1A, a, 0),
        (G1B, b, 1),
        (B1B, b, 0),
        (F1, df1, 0),
        (G1C, cs, 1),
        (B1C, cs, 0),
        (G1S, cs, 2),
        (B1S, cs, 0),
        (G2A, d, 1),
        (B2A, d, 0),
        (G2B, e, 1),
        (B2B, e, 0),
        (F2, df2, 0),
        (G2C, f, 1),
        (B2C, f, 0),
    ]
    for row, ref, k in plan:
        o_ref[row : row + 1, :] = ref[k : k + 1, :]
    o_ref[16:17, 0:HID] = de1[0:1, :]
    o_ref[17:18, 0:HID] = de2[0:1, :]
    o_ref[VEC_ROWS : VEC_ROWS + 8, :] = sums_ref[...]


def finish_kernel(
    n_rows,
    place_ref,
    r0,
    r1,
    r2,
    r3,
    w_ref,
    update_ref,
    vec_ref,
    vf_ref,
    vs_ref,
    new_w_ref,
    new_v_ref,
    new_vf_ref,
    new_vs_ref,
    norm_ref,
    slots,
):
    place, shard = place_ref[3], place_ref[4]
    for k, ref in enumerate((r0, r1, r2, r3)):
        slots[place ^ k] = ref[...]
    total = slots[0] + slots[1] + slots[2] + slots[3]
    norms = jnp.sqrt(total[VEC_ROWS : VEC_ROWS + 8, 0:128])
    norm_ref[...] = norms
    lane = lax.broadcasted_iota(jnp.int32, (1, 128), 1)
    ratio = jnp.where(
        lane < len(MATRIX_ROWS), learn_rate * (norms[0:1] / norms[1:2]), 0.0
    )
    by_row = jnp.sum(membership(n_rows, shard) * ratio, axis=1, keepdims=True)
    new_w_ref[...] = w_ref[...] - by_row * update_ref[...]
    vec = vec_ref[...]
    first, second, update = lamb_terms(vec, total[0:VEC_ROWS], vf_ref[...], vs_ref[...], 0.0)
    new_vf_ref[...] = first
    new_vs_ref[...] = second
    size = jnp.sqrt(jnp.sum(vec * vec, axis=1, keepdims=True))
    change = jnp.sqrt(jnp.sum(update * update, axis=1, keepdims=True))
    new_v_ref[...] = vec - learn_rate * (size / change) * update


def lamb_terms(param, grad_val, first_old, second_old, decay):
    first_new = beta_one * first_old + (1.0 - beta_one) * grad_val
    second_new = beta_two * second_old + (1.0 - beta_two) * grad_val * grad_val
    update = (
        first_new
        / (1.0 - beta_one**STEP)
        / (jnp.sqrt(second_new / (1.0 - beta_two**STEP)) + adam_eps)
        + decay * param
    )
    return (first_new, second_new, update)


def body(
    image_glob,
    image_loc,
    cot_glob,
    cot_loc,
    weights,
    first_moment,
    second_moment,
    vectors,
    vec_first,
    vec_second,
):
    n_height = lax.axis_size("height")
    place = lax.axis_index("height")
    sz = Sizes(image_glob, image_loc, n_height)
    m = sz.m
    part = functools.partial
    has_above = (place > 0).astype(f32)
    has_below = (place < n_height - 1).astype(f32)
    borders = jnp.stack([has_above, has_below, (place == 0).astype(f32)])
    batch = lax.axis_index("batch")
    place_ids = jnp.stack(
        [batch // 4, (batch // 2) % 2, batch % 2, place, batch * n_height + place]
    ).astype(jnp.int32)

    shapes = matrix_shapes()
    mat_lengths = [dims_pair[0] * dims_pair[1] for dims_pair in shapes]
    by_rows = (
        weights.shape[0] % C == 0
        and weights.shape[0] // C <= UNIT
        and lax.axis_size("batch") == 8
        and n_height == 4
    )
    shard_rows = weights.shape[0] // C
    vec_list = cut_pieces(vectors, vector_sizes())
    vt = jnp.stack(vec_list[:4] + vec_list[5:14] + vec_list[15:])
    e1 = jnp.pad(vec_list[4], (0, HID - SE_A)).reshape(1, HID)
    e2 = vec_list[14].reshape(1, HID)

    early = [vt, e1, e2]
    if by_rows:
        w_rows, m_rows, v_rows = (
            v.reshape(shard_rows, C) for v in (weights, first_moment, second_moment)
        )
        tables = [vector_table(v) for v in (vectors, vec_first, vec_second)]
        early = early + [w_rows, m_rows, v_rows, place_ids, borders] + tables

    if by_rows:
        matrices = [
            matrix.reshape(dims_pair)
            for matrix, dims_pair in zip(gather_weights(weights, shard_rows, early), shapes)
        ]
    else:
        gathered = lax.all_gather(weights.astype(bf16), both_axes, axis=0, tiled=True)
        matrices = [
            flat_piece.reshape(dims_pair)
            for flat_piece, dims_pair in zip(cut_pieces(gathered, mat_lengths), shapes)
        ]
    w1, k1, d1, u1, p1, s1, w2, k2, d2, u2, p2 = matrices
    d1 = jnp.pad(d1, ((0, 0), (0, HID - SE_A)))
    u1 = jnp.pad(u1, ((0, HID - SE_A), (0, 0)))
    st8 = out((8, C))
    mat = out((m, C))
    mat_low = out((m, C), bf16)
    pool_low = out((sz.crops, C), bf16)
    pool_scr = pltpu.VMEM((sz.crops, C), f32)
    sum_scr = pltpu.VMEM((24, C), f32)
    point_flops = 2 * m * C * C
    conv_flops = 2 * m * C * HALF * 9

    x, x_edge = call(
        part(prepare_kernel, sz),
        [out((4 * m, CIN), bf16), out((2 * sz.edge, CIN), bf16)],
        [pltpu.VMEM((sz.hg * sz.wg, 128), f32)] * 2,
        image_glob,
        image_loc,
        name="prepare",
        room=6 * 2**20,
    )
    x_above = step_down(x_edge)
    bd_scr = pltpu.VMEM((18, HALF, HALF), bf16)
    low_scr = pltpu.VMEM((m, C), bf16)
    mat_scr = pltpu.VMEM((m, C), f32)
    one_scr = pltpu.VMEM((sz.one, C), bf16)
    two_scr = pltpu.VMEM((sz.two, C), bf16)
    edge_scr = pltpu.VMEM((sz.edge, C), f32)
    edge = out((sz.edge, C), bf16)
    (st_a,) = call(
        part(input_stats_kernel, sz), [st8], [], x, w1, s1, flops=point_flops * 2, name="input_stats"
    )
    st_a = over_height(st_a)
    one_shape = out((sz.one, C), bf16)
    zb, st_b, nrm_a, *act_a = call(
        part(first_conv_kernel, sz),
        [mat, st8, st8, mat_low, mat_low, one_shape, one_shape],
        [low_scr, one_scr, bd_scr, mat_scr, sum_scr],
        borders,
        x,
        x_above,
        w1,
        k1,
        *st_a,
        vt,
        smem=1,
        flops=conv_flops,
        name="first_conv",
        after=[d1, u1, d2, u2],
    )
    st_b = over_height(st_b)
    pool_b, nrm_b = call(
        part(pool_kernel, sz, G1B, B1B), [pool_low, st8], [pool_scr], zb, *st_b, vt, name="pool_b"
    )
    pool_b = over_height(pool_b)
    hid = out((sz.crops, HID))
    crop_mat = out((sz.crops, C))
    qb, zc, st_c, gate_b, pooled_b, hidden_b = call(
        part(gated_product_kernel, sz, F1),
        [mat_low, mat, st8, crop_mat, crop_mat, hid],
        [],
        zb,
        nrm_b,
        *pool_b,
        d1,
        e1,
        u1,
        p1,
        vt,
        flops=point_flops,
        name="gated_b",
    )
    st_c = over_height(st_c)
    pre_mid, mid_low, nrm_c, mid_top, mid_bottom = call(
        part(middle_kernel, sz),
        [mat, mat_low, st8, edge, edge],
        [mat_scr],
        zc,
        x,
        s1,
        *st_c,
        nrm_a,
        vt,
        name="middle",
    )
    mid_above = step_down(mid_bottom)
    mid_below = step_up(mid_top)
    zd, st_d = call(
        part(product_kernel, sz), [mat, st8], [], mid_low, w2, flops=point_flops, name="product_d"
    )
    st_d = over_height(st_d)
    two_shape = out((sz.two, C), bf16)
    ze, st_e, nrm_d, act_d = call(
        part(second_conv_kernel, sz),
        [mat, st8, st8, two_shape],
        [two_scr, two_scr, bd_scr, edge_scr, sum_scr],
        borders,
        zd,
        mid_above,
        mid_below,
        w2,
        k2,
        *st_d,
        vt,
        smem=1,
        flops=conv_flops,
        name="second_conv",
    )
    st_e = over_height(st_e)
    pool_e, nrm_e = call(
        part(pool_kernel, sz, G2B, B2B), [pool_low, st8], [pool_scr], ze, *st_e, vt, name="pool_e"
    )
    pool_e = over_height(pool_e)
    qe, zf, st_f, gate_e, pooled_e, hidden_e = call(
        part(gated_product_kernel, sz, F2),
        [mat_low, mat, st8, crop_mat, crop_mat, hid],
        [],
        ze,
        nrm_e,
        *pool_e,
        d2,
        e2,
        u2,
        p2,
        vt,
        flops=point_flops,
        name="gated_e",
    )
    st_f = over_height(st_f)
    out_glob, out_loc, dpre, bst_f, nrm_f = call(
        part(output_kernel, sz),
        [out(cot_glob.shape, bf16), out(cot_loc.shape, bf16), mat, st8, st8],
        [sum_scr],
        pre_mid,
        zf,
        *st_f,
        vt,
        cot_glob,
        cot_loc,
        name="output",
        room=6 * 2**20,
    )
    bst_f_all = over_height(bst_f)

    dzf, dqe, dg_e = call(
        part(gate_grad_kernel, sz, False),
        [mat_low, mat, pool_low],
        [pool_scr],
        dpre,
        zf,
        *bst_f_all,
        nrm_f,
        p2,
        ze,
        nrm_e,
        flops=point_flops,
        name="gate_grad_e",
    )
    dg_e = over_height(dg_e)
    (mat_f,) = call(
        weight_kernel, [out((C, C))], [], qe, dzf, flops=point_flops, name="weight_f"
    )
    dn_e, bst_e, dv_e, du_e = call(
        part(excite_back_kernel, sz),
        [mat, st8, crop_mat, hid],
        [pool_scr, sum_scr],
        dqe,
        ze,
        nrm_e,
        *dg_e,
        gate_e,
        hidden_e,
        d2,
        u2,
        name="excite_back_e",
        after=[mat_f],
    )
    bst_e_all = over_height(bst_e)
    se_outs = lambda width: [out((width, C)), out((8, HID)), out((HID, C)), st8]
    se_scr = [pltpu.VMEM((C, HID), f32), pltpu.VMEM((HID, 128), f32)]
    dd2, de2, du2, df2 = call(
        part(excite_weights_kernel, SE_B),
        se_outs(SE_B),
        se_scr,
        borders,
        dv_e,
        du_e,
        pooled_e,
        hidden_e,
        smem=1,
        name="excite_weights_e",
    )
    dze, dze_top, dze_bottom = call(
        part(norm_back_kernel, sz),
        [mat_low, edge, edge],
        [],
        dn_e,
        ze,
        *bst_e_all,
        nrm_e,
        name="norm_back_e",
        after=[dd2],
    )
    dze_above = step_down(dze_bottom)
    dze_below = step_up(dze_top)
    (mat_e,) = call(
        part(second_conv_weights_kernel, sz),
        [out((9 * GW, C))],
        [two_scr, two_scr],
        act_d,
        dze,
        flops=conv_flops,
        name="second_conv_weights",
    )
    dn_d, bst_d = call(
        part(second_conv_back_kernel, sz),
        [mat, st8],
        [two_scr, two_scr, two_scr, bd_scr, sum_scr],
        dze,
        dze_above,
        dze_below,
        k2,
        zd,
        nrm_d,
        flops=conv_flops,
        name="second_conv_back",
        after=[mat_e],
    )
    bst_d_all = over_height(bst_d)
    dzd, dn_mid, bst_cs = call(
        part(middle_back_kernel, sz),
        [mat_low, mat, st8],
        [mat_scr, sum_scr],
        dn_d,
        zd,
        *bst_d_all,
        nrm_d,
        w2,
        dpre,
        pre_mid,
        zc,
        x,
        s1,
        nrm_c,
        nrm_a,
        flops=point_flops,
        name="middle_back",
    )
    bst_cs_all = over_height(bst_cs)
    (mat_d,) = call(
        weight_kernel, [out((C, C))], [], mid_low, dzd, flops=point_flops, name="weight_d"
    )
    spans = list(zip(ROW_BOUNDS[:-1], ROW_BOUNDS[1:]))
    late = Reduction(1, shard_rows, place_ids) if by_rows else None
    soon = Reduction(0, shard_rows, place_ids) if by_rows else None
    hold = late.pack(spans[6:], [mat_d, mat_e, dd2, du2, mat_f]) if by_rows else [mat_d]
    dzc, dzs, dqb, dg_b = call(
        part(gate_grad_kernel, sz, True),
        [mat_low, mat_low, mat, pool_low],
        [pool_scr, mat_scr],
        dn_mid,
        zc,
        *bst_cs_all,
        nrm_c,
        p1,
        zb,
        nrm_b,
        x,
        s1,
        nrm_a,
        flops=point_flops,
        name="gate_grad_b",
        after=hold,
    )
    dg_b = over_height(dg_b)
    (mat_c,) = call(
        weight_kernel, [out((C, C))], [], qb, dzc, flops=point_flops, name="weight_c"
    )
    (mat_s,) = call(
        weight_kernel, [out((CIN, C))], [], x, dzs, flops=point_flops, name="weight_s"
    )
    hold = late.height() if by_rows else []
    dn_b, bst_b, dv_b, du_b = call(
        part(excite_back_kernel, sz),
        [mat, st8, crop_mat, hid],
        [pool_scr, sum_scr],
        dqb,
        zb,
        nrm_b,
        *dg_b,
        gate_b,
        hidden_b,
        d1,
        u1,
        name="excite_back_b",
        after=[mat_c, mat_s] + hold,
    )
    bst_b_all = over_height(bst_b)
    dd1, de1, du1, df1 = call(
        part(excite_weights_kernel, SE_A),
        se_outs(SE_A),
        se_scr,
        borders,
        dv_b,
        du_b,
        pooled_b,
        hidden_b,
        smem=1,
        name="excite_weights_b",
    )
    dzb, dzb_top = call(
        part(norm_back_kernel, sz),
        [mat_low, edge],
        [],
        dn_b,
        zb,
        *bst_b_all,
        nrm_b,
        name="norm_back_b",
        after=[dd1] + (late.add_height() if by_rows else []),
    )
    dzb_below = step_up(dzb_top)
    (mat_b,) = call(
        part(first_conv_weights_kernel, sz),
        [out((9 * GW, C))],
        [low_scr, one_scr],
        *act_a,
        dzb,
        flops=conv_flops,
        name="first_conv_weights",
    )
    hold = [mat_b]
    if by_rows:
        hold = soon.pack(spans[1:7], [mat_b, dd1, du1, mat_c, mat_s, mat_d])
        hold = hold + late.plane()
    dn_a, bst_a = call(
        part(first_conv_back_kernel, sz),
        [out((4 * m, C), bf16), st8],
        [one_scr, one_scr, mat_scr, mat_scr, bd_scr, sum_scr],
        dzb,
        dzb_below,
        k1,
        x,
        w1,
        nrm_a,
        flops=conv_flops,
        name="first_conv_back",
        after=hold,
    )
    bst_a_all = over_height(bst_a)
    hold = soon.height() + list(late.result) if by_rows else []
    (dza,) = call(
        part(image_norm_back_kernel, sz),
        [out((4 * m, C), bf16)],
        [mat_scr],
        dn_a,
        x,
        w1,
        *bst_a_all,
        nrm_a,
        flops=point_flops * 2,
        name="image_norm_back",
        after=hold,
    )
    (mat_a,) = call(
        weight_kernel, [out((CIN, C))], [], x, dza, flops=point_flops, name="weight_a"
    )
    grad_glob, grad_loc = call(
        part(image_back_kernel, sz),
        [out(image_glob.shape), out(image_loc.shape)],
        [
            pltpu.VMEM((4 * m, CIN), f32),
            pltpu.VMEM((sz.hg * sz.wg, 128), f32),
            pltpu.VMEM((sz.hg * sz.wg, 128), f32),
        ],
        dza,
        w1,
        dzs,
        s1,
        flops=point_flops * 2,
        name="image_back",
        room=8 * 2**20,
    )
    maps_out = (out_glob, out_loc, grad_glob, grad_loc)

    if by_rows:
        soon.add_height()
        soon.plane()
        keep_a, got_a = late.result
        keep_b, got_b = soon.result
        half_mine, half_other = sum_everywhere(mat_a, place_ids)
        shard_out = out((shard_rows, C))
        new_first, new_second, update, sums = call(
            part(lamb_kernel, shard_rows),
            [shard_out, shard_out, shard_out, st8],
            [pltpu.VMEM((UNIT, C), f32)],
            place_ids,
            keep_a,
            got_a,
            keep_b,
            got_b,
            half_mine,
            half_other,
            w_rows,
            m_rows,
            v_rows,
            smem=1,
            name="lamb",
        )
        (small,) = call(
            vector_grads_kernel,
            [out((VEC_ROWS + 8, C))],
            [],
            bst_a,
            bst_b,
            bst_cs,
            bst_d,
            bst_e,
            bst_f,
            de1,
            df1,
            de2,
            df2,
            sums,
            name="vector_grads",
        )
        for mask in (1, 2, 4):
            small = small + across(small, mask)
        table = out((VEC_ROWS, C))
        new_weights, new_v, new_vf, new_vs, norms = call(
            part(finish_kernel, shard_rows),
            [shard_out, table, table, table, out((8, 128))],
            [pltpu.VMEM((4, VEC_ROWS + 8, C), f32)],
            place_ids,
            *over_height(small),
            w_rows,
            update,
            *tables,
            smem=1,
            name="finish",
        )
        return maps_out + (
            new_weights.reshape(-1),
            new_first.reshape(-1),
            new_second.reshape(-1),
            flat_vector(new_v),
            flat_vector(new_vf),
            flat_vector(new_vs),
            norms[:2, : len(MATRIX_ROWS)],
        )

    flat_grad = jnp.concatenate(
        [
            piece.reshape(-1)
            for piece in (
                mat_a,
                mat_b,
                dd1,
                du1[:SE_A],
                mat_c,
                mat_s,
                mat_d,
                mat_e,
                dd2,
                du2,
                mat_f,
            )
        ]
    )
    vec_grad = jnp.concatenate(
        [
            bst_a[1],
            bst_a[0],
            bst_b[1],
            bst_b[0],
            de1[0, :SE_A],
            df1[0],
            bst_cs[1],
            bst_cs[0],
            bst_cs[2],
            bst_cs[0],
            bst_d[1],
            bst_d[0],
            bst_e[1],
            bst_e[0],
            de2[0],
            df2[0],
            bst_f[1],
            bst_f[0],
        ]
    )
    grad_shard = lax.psum_scatter(flat_grad, both_axes, scatter_dimension=0, tiled=True)
    shard_len = weights.shape[0]
    device_index = lax.axis_index("batch") * n_height + lax.axis_index("height")
    position = device_index * shard_len + lax.iota(jnp.int32, shard_len)
    bounds = np.cumsum([0] + mat_lengths)
    lower_edge = jnp.asarray(bounds[:-1], jnp.int32)
    upper_edge = jnp.asarray(bounds[1:], jnp.int32)
    member = (
        (position[:, None] >= lower_edge[None, :]) & (position[:, None] < upper_edge[None, :])
    ).astype(f32)
    new_first, new_second, update = lamb_terms(
        weights, grad_shard, first_moment, second_moment, weight_decay
    )
    part_sums = jnp.dot(jnp.stack([weights * weights, update * update]), member, precision=highest)
    vec_total, totals = lax.psum((vec_grad, part_sums), both_axes)
    norm_pair = jnp.sqrt(totals)
    trust_ratio = learn_rate * (norm_pair[0] / norm_pair[1])
    new_weights = weights - jnp.dot(member, trust_ratio, precision=highest) * update
    vec_one_new, vec_two_new, vec_update = lamb_terms(vectors, vec_total, vec_first, vec_second, 0.0)
    vec_pieces = []
    for param_piece, update_piece in zip(
        cut_pieces(vectors, vector_sizes()), cut_pieces(vec_update, vector_sizes())
    ):
        ratio_val = jnp.sqrt(jnp.sum(param_piece * param_piece)) / jnp.sqrt(
            jnp.sum(update_piece * update_piece)
        )
        vec_pieces.append(param_piece - learn_rate * ratio_val * update_piece)
    new_vectors = jnp.concatenate(vec_pieces)
    return maps_out + (
        new_weights,
        new_first,
        new_second,
        new_vectors,
        vec_one_new,
        vec_two_new,
        norm_pair,
    )


def solution(mesh):
    maps = P("batch", "height", None, None)
    entries = P(("batch", "height"))
    return jax.shard_map(
        body,
        mesh=mesh,
        in_specs=(maps, maps, maps, maps, entries, entries, entries, P(), P(), P()),
        out_specs=(maps, maps, maps, maps, entries, entries, entries, P(), P(), P(), P()),
        check_vma=False,
    )
```

```python
import functools

import jax
import jax.numpy as jnp
import numpy as np
from jax import lax
from jax.experimental import pallas as pl
from jax.experimental.pallas import tpu as pltpu
from jax.sharding import PartitionSpec as P

CIN = 192
C = 512
GW = 64
GROUPS = 8
SE_A = 48
SE_B = 128
STEP = 10
HID = 128
HALF = 256

norm_eps = 1e-05
beta_one = 0.9
beta_two = 0.999
adam_eps = 1e-06
weight_decay = 0.01
learn_rate = 0.4
highest = lax.Precision.HIGHEST
bf16 = jnp.bfloat16
f32 = jnp.float32
both_axes = ("batch", "height")

G1A, B1A, G1B, B1B, E1, F1, G1C, B1C, G1S, B1S, G2A, B2A, G2B, B2B, E2, F2, G2C, B2C = range(18)


def matrix_shapes():
    return [
        (CIN, C),
        (9 * GW, C),
        (C, SE_A),
        (SE_A, C),
        (C, C),
        (CIN, C),
        (C, C),
        (9 * GW, C),
        (C, SE_B),
        (SE_B, C),
        (C, C),
    ]


def vector_sizes():
    return [C, C, C, C, SE_A, C, C, C, C, C, C, C, C, C, SE_B, C, C, C]


def cut_pieces(flat_vec, lengths):
    pieces = []
    offset = 0
    for length in lengths:
        pieces.append(flat_vec[offset : offset + length])
        offset += length
    return pieces


class Sizes:
    def __init__(self, image_glob, image_loc, n_height):
        self.ng, self.hg, self.wg = image_glob.shape[:3]
        self.nl, self.hl, self.wl = image_loc.shape[:3]
        self.rg, self.cg = self.hg // 2, self.wg // 2
        self.rl, self.cl = self.hl // 2, self.wl // 2
        self.bg, self.bl = self.ng * self.cg, self.nl * self.cl
        self.mg, self.ml = self.rg * self.bg, self.rl * self.bl
        self.m = self.mg + self.ml
        self.edge = self.bg + self.bl
        self.n_height = n_height
        self.crops = -(-(self.ng + self.nl) // 16) * 16
        self.area_g = self.rg * self.cg * n_height
        self.area_l = self.rl * self.cl * n_height
        self.amount = n_height * self.m
        self.one_l = (self.rg + 1) * self.bg
        self.one = self.one_l + (self.rl + 1) * self.bl
        self.two_l = (self.rg + 2) * self.bg
        self.two = self.two_l + (self.rl + 2) * self.bl


def sigmoid(v):
    return 0.5 * jnp.tanh(0.5 * v) + 0.5


def silu(v):
    return v * sigmoid(v)


def silu_slope(v):
    s = sigmoid(v)
    return s * (1.0 + v * (1.0 - s))


def padded_bytes(shape, dtype):
    size = np.dtype(dtype).itemsize
    dims = list(shape)
    dims[-1] = -(-dims[-1] // 128) * 128
    if len(dims) > 1:
        rows = 32 // size
        dims[-2] = -(-dims[-2] // rows) * rows
    return int(np.prod(dims)) * size


COST_SCALE = 1.0
MEASURED_US = {
    "first_conv_back": 1.5,
    "parity_back_0": 2.6,
    "parity_back_1": 3.0,
    "parity_back_2": 3.0,
    "parity_back_3": 3.7,
    "first_conv": 13.0,
    "second_conv": 6.3,
    "second_conv_back": 5.9,
    "image_norm_back": 5.8,
    "second_conv_weights": 4.9,
    "first_conv_weights": 4.5,
    "middle_back": 4.4,
    "gate_grad_b": 4.2,
    "gram": 3.6,
    "image_product": 3.6,
    "place_glob": 3.1,
    "output": 2.9,
    "assemble": 2.9,
    "gate_grad_e": 2.7,
    "excite_back_b": 2.6,
    "excite_back_e": 2.6,
    "place_loc": 2.5,
    "gated_b": 2.4,
    "gated_e": 2.4,
    "finish": 1.9,
    "middle": 1.8,
    "prepare": 1.4,
    "excite_weights_b": 1.3,
    "excite_weights_e": 1.2,
    "product_d": 1.1,
    "weight_a": 1.1,
    "pack_0": 1.0,
    "pack_1": 1.0,
    "pool_b": 1.0,
    "pool_e": 1.0,
    "lamb": 1.0,
    "weight_f": 0.9,
    "weight_d": 0.9,
    "weight_c": 0.9,
}


def call(kernel, outs, scratch, *ins, smem=0, name=None, after=(), room=0):
    held = sum(padded_bytes(s.shape, s.dtype) for s in scratch)
    n_in, n_after = len(ins), len(after)

    def run(*refs):
        kernel(*refs[:n_in], *refs[n_in + n_after :])

    return pl.pallas_call(
        run,
        out_shape=tuple(outs),
        in_specs=[pl.BlockSpec(memory_space=pltpu.SMEM)] * smem
        + [pl.BlockSpec(memory_space=pltpu.VMEM)] * (n_in - smem)
        + [pl.BlockSpec(memory_space=pl.ANY)] * n_after,
        out_specs=tuple(pl.BlockSpec(memory_space=pltpu.VMEM) for _ in outs),
        scratch_shapes=list(scratch),
        compiler_params=pltpu.CompilerParams(vmem_limit_bytes=held + 4 * 2**20 + room),
        cost_estimate=pl.CostEstimate(
            flops=int(MEASURED_US.get(name, 0.5) * COST_SCALE * 1.1535e9),
            bytes_accessed=1,
            transcendentals=0,
        ),
        name=name,
    )(*ins, *after)


def out(shape, dtype=f32):
    return jax.ShapeDtypeStruct(shape, dtype)


def above(ids, n_height=0):
    return jnp.where(ids[1] > 0, 1.0, 0.0)


def below(ids, n_height):
    return jnp.where(ids[1] < n_height - 1, 1.0, 0.0)


def first_of_height(ids):
    return jnp.where(ids[1] == 0, 1.0, 0.0)


def y_of(ids):
    return ids[0] // 4


def x_of(ids):
    return lax.rem(ids[0] // 2, 2)


def core_of(ids):
    return lax.rem(ids[0], 2)


def fold(x):
    return jnp.sum(x.reshape(x.shape[0] // 8, 8, x.shape[1]), axis=0)


def rows_at(start, size, unit=16):
    return pl.ds(pl.multiple_of(start, unit), size)


def put_rows(ref, parts):
    ref[...] = jnp.zeros_like(ref)
    for k, part in enumerate(parts):
        ref[k : k + 1, :] = jnp.sum(part, axis=0, keepdims=True)


def gather_sum(refs):
    total = refs[0][...]
    for ref in refs[1:]:
        total = total + ref[...]
    return total


def norm_terms(total, row, amount, gain, shift):
    mean = total[row : row + 1] / amount
    inverse = lax.rsqrt(total[row + 1 : row + 2] / amount - mean * mean + norm_eps)
    scale = gain * inverse
    return mean, inverse, scale, shift - mean * scale


def put_norm(ref, row, terms):
    for k, term in enumerate(terms):
        ref[row + k : row + k + 1, :] = term


def dot(a, b):
    return jnp.dot(a, b, preferred_element_type=f32)


def dot_t(a, b):
    return lax.dot_general(a, b, (((1,), (1,)), ((), ())), preferred_element_type=f32)


def t_dot(a, b):
    return lax.dot_general(a, b, (((0,), (0,)), ((), ())), preferred_element_type=f32)


def prepare_kernel(sz, ig_ref, il_ref, x_ref, halo_ref, s_ref, t_ref):
    m = sz.m

    def split(x, n_rows):
        s_ref[0:n_rows, :] = x[:, :128]
        t_ref[0:n_rows, 0:64] = x[:, 128:]
        parts = []
        for pc in range(2):
            v = s_ref[pl.ds(pc, n_rows // 2, stride=2), :]
            w = t_ref[pl.ds(pc, n_rows // 2, stride=2), :]
            parts.append(jnp.concatenate([v, w[:, :64]], axis=1))
        return parts

    @pl.loop(0, sz.ng)
    def _(n):
        n_rows = sz.hg * sz.wg
        parts = split(ig_ref[n].astype(f32).reshape(n_rows, CIN), n_rows)
        for pc in range(2):
            v = parts[pc].reshape(sz.hg, sz.cg, CIN).astype(bf16)
            for r in range(sz.hg):
                phase = 2 * (r % 2) + pc
                x_ref[rows_at(phase * m + (r // 2) * sz.bg + n * sz.cg, sz.cg), :] = v[r]

    @pl.loop(0, sz.nl // 2)
    def _(pair):
        n_rows = 2 * sz.hl * sz.wl
        both = jnp.concatenate(
            [
                il_ref[2 * pair + k].astype(f32).reshape(sz.hl * sz.wl, CIN)
                for k in range(2)
            ],
            axis=0,
        )
        parts = split(both, n_rows)
        for pc in range(2):
            v = parts[pc].reshape(2 * sz.hl, sz.cl, CIN)
            for r in range(sz.hl):
                phase = 2 * (r % 2) + pc
                joined = jnp.concatenate([v[r], v[sz.hl + r]], axis=0).astype(bf16)
                x_ref[
                    rows_at(phase * m + sz.mg + (r // 2) * sz.bl + pair * 2 * sz.cl, 2 * sz.cl), :
                ] = joined

    for pc in range(2):
        base = (2 + pc) * m
        halo_ref[pc * sz.edge : pc * sz.edge + sz.bg, :] = x_ref[
            base + sz.mg - sz.bg : base + sz.mg, :
        ]
        halo_ref[pc * sz.edge + sz.bg : (pc + 1) * sz.edge, :] = x_ref[
            base + m - sz.bl : base + m, :
        ]


LOW = 128
PACKED = (LOW + 8, 2 * LOW)


def gram_kernel(sz, x_ref, g_ref, full):
    n_rows = sz.m // 3
    ones = jnp.ones((8, n_rows), bf16)
    full[...] = jnp.zeros_like(full)

    @pl.loop(0, 12)
    def _(i):
        x = x_ref[rows_at(i * n_rows, n_rows), :]
        full[0:CIN, :] += t_dot(x, x)
        full[CIN : CIN + 8, :] += dot(ones, x)

    g_ref[...] = jnp.zeros_like(g_ref)
    g_ref[0:LOW, 0:CIN] = full[0:LOW, :]
    g_ref[0 : CIN - LOW, CIN:] = full[LOW:CIN, LOW:CIN]
    g_ref[LOW : LOW + 8, 0:CIN] = full[CIN : CIN + 8, :]


def unpack_gram(packed, full):
    full[0:LOW, :] = packed[0:LOW, 0:CIN]
    full[LOW:CIN, 0:LOW] = jnp.transpose(packed[0:LOW, LOW : 2 * LOW])[0 : CIN - LOW]
    full[LOW:CIN, LOW:CIN] = packed[0 : CIN - LOW, CIN:]
    full[CIN : CIN + 8, :] = packed[LOW : LOW + 8, 0:CIN]


def product_norm_terms(total, w_ref, amount, gain, shift):
    w = w_ref[...].astype(f32)
    mean = dot_high(total[CIN : CIN + 8], w)[0:1] / amount
    square = jnp.sum(w * dot_high(total[0:CIN], w), axis=0, keepdims=True) / amount
    inverse = lax.rsqrt(square - mean * mean + norm_eps)
    scale = gain * inverse
    return mean, inverse, scale, shift - mean * scale


def block_diagonal(k_ref, bd_ref):
    rows = lax.broadcasted_iota(jnp.int32, (HALF, HALF), 0) // GW
    cols = lax.broadcasted_iota(jnp.int32, (HALF, HALF), 1) // GW
    same = rows == cols
    for tap in range(9):
        for half in range(2):
            k = k_ref[tap * GW : (tap + 1) * GW, half * HALF : (half + 1) * HALF].astype(f32)
            bd_ref[2 * tap + half] = jnp.where(same, jnp.concatenate([k] * 4, axis=0), 0.0).astype(
                bf16
            )


def strided_product(sz, x_ref, s_ref, zs):
    n_rows = sz.m // 3

    @pl.loop(0, 3)
    def _(i):
        zs[rows_at(i * n_rows, n_rows), :] = dot(x_ref[rows_at(i * n_rows, n_rows), :], s_ref[...])


def block_dense(acc):
    rows = lax.broadcasted_iota(jnp.int32, (HALF, HALF), 0) // GW
    cols = lax.broadcasted_iota(jnp.int32, (HALF, HALF), 1) // GW
    kept = jnp.where(rows == cols, acc, 0.0)
    return jnp.sum(kept.reshape(4, GW, HALF), axis=0)


def shifted(v, by, width):
    n_rows = v.shape[0]
    col = lax.broadcasted_iota(jnp.int32, v.shape, 0) % width
    if by < 0:
        return jnp.where(col == 0, 0.0, pltpu.roll(v, 1, 0))
    return jnp.where(col == width - 1, 0.0, pltpu.roll(v, n_rows - 1, 0))


def segments(sz):
    g_rows = 4 * sz.cg
    l_rows = 6 * sz.cl
    return g_rows, l_rows


def conv_product(windows, bd_ref, half, n_rows, transposed):
    acc = None
    cols = pl.ds(pl.multiple_of(half * HALF, HALF), HALF)
    for tap, ref, start in windows:
        x = ref[start : start + n_rows, cols]
        w = bd_ref[2 * tap + half]
        term = dot_t(x, w) if transposed else dot(x, w)
        acc = term if acc is None else acc + term
    return acc


def windows_one(sz, refs, part):
    a00, a01, a01s, a10, a11, a11s = refs
    plain = 0 if part == "g" else sz.mg
    above = 0 if part == "g" else sz.one_l
    here = above + (sz.bg if part == "g" else sz.bl)
    result = []
    for tap in range(9):
        a, b = tap // 3, tap % 3
        if a == 1:
            result.append((tap, (a01s, a00, a01)[b], plain))
        else:
            result.append((tap, (a11s, a10, a11)[b], above if a == 0 else here))
    return result


def windows_two(sz, refs, part, flipped=False):
    base = 0 if part == "g" else sz.two_l
    block = sz.bg if part == "g" else sz.bl
    result = []
    for tap in range(9):
        a, b = tap // 3, tap % 3
        if flipped:
            a, b = 2 - a, 2 - b
        result.append((tap, refs[b], base + a * block))
    return result


def shift_windows(windows, by):
    return [(tap, ref, start + by) for tap, ref, start in windows]


def conv_forward(sz, windows_of, bd_ref, z_ref, st_ref, sums, more=()):
    sums[0:16, :] = jnp.zeros((16, C), f32)

    @pl.loop(0, 2)
    def _(half):
        cols = pl.ds(pl.multiple_of(half * HALF, HALF), HALF)
        for part, first, n_all, n_rows in (
            ("g", 0, sz.mg, sz.mg // 2),
            ("l", sz.mg, sz.ml, sz.ml),
        ):
            for k in range(n_all // n_rows):
                z = conv_product(
                    shift_windows(windows_of(part), k * n_rows), bd_ref, half, n_rows, False
                )
                z_ref[first + k * n_rows : first + (k + 1) * n_rows, cols] = z
                sums[0:8, cols] += fold(z)
                sums[8:16, cols] += fold(z * z)

    put_rows(st_ref, [sums[0:8, :], sums[8:16, :]] + list(more))


def first_conv_kernel(
    sz,
    flag_ref,
    x_ref,
    halo_ref,
    w_ref,
    s_ref,
    k_ref,
    t0,
    t1,
    t2,
    t3,
    vt_ref,
    z_ref,
    st_ref,
    nrm_ref,
    a00,
    a01,
    a10,
    a11,
    a01s,
    a11s,
    bd_ref,
    zs,
    sums,
    gram_scr,
):
    block_diagonal(k_ref, bd_ref)
    unpack_gram(gather_sum((t0, t1, t2, t3)), gram_scr)
    terms = product_norm_terms(
        gram_scr, w_ref, 4 * sz.amount, vt_ref[G1A : G1A + 1, :], vt_ref[B1A : B1A + 1, :]
    )
    nrm_ref[...] = jnp.zeros_like(nrm_ref)
    put_norm(nrm_ref, 0, terms)
    scale, shift = terms[2], terms[3]
    g_rows, l_rows = segments(sz)
    third = sz.m // 3

    def activate(src, dst, dst_s, n_rows, width, factor=None):
        v = zs[src, :] * scale + shift
        a = silu(v)
        if factor is not None:
            a = a * factor
        dst[0][dst[1], :] = a.astype(bf16)
        if dst_s is not None:
            dst_s[dst[1], :] = shifted(a, -1, width).astype(bf16)

    plan = [(a00, None, False), (a01, a01s, False), (a10, None, True), (a11, a11s, True)]
    for phase, (dst, dst_s, bordered) in enumerate(plan):

        @pl.loop(0, 3)
        def _(i):
            zs[rows_at(i * third, third), :] = dot(
                x_ref[rows_at(phase * sz.m + i * third, third), :], w_ref[...]
            )

        g_first = sz.bg if bordered else 0
        l_first = sz.one_l + sz.bl if bordered else sz.mg

        @pl.loop(0, sz.mg // g_rows)
        def _(i):
            activate(
                rows_at(i * g_rows, g_rows),
                (dst, rows_at(g_first + i * g_rows, g_rows)),
                dst_s,
                g_rows,
                sz.cg,
            )

        @pl.loop(0, sz.ml // l_rows)
        def _(i):
            activate(
                rows_at(sz.mg + i * l_rows, l_rows),
                (dst, rows_at(l_first + i * l_rows, l_rows)),
                dst_s,
                l_rows,
                sz.cl,
            )

    flag = above(flag_ref)
    for pc, (dst, dst_s) in enumerate(((a10, None), (a11, a11s))):
        zs[0 : sz.edge, :] = dot(halo_ref[pc * sz.edge : (pc + 1) * sz.edge, :], w_ref[...])

        @pl.loop(0, sz.bg // g_rows)
        def _(i):
            rows = rows_at(i * g_rows, g_rows)
            activate(rows, (dst, rows), dst_s, g_rows, sz.cg, flag)

        @pl.loop(0, sz.bl // l_rows)
        def _(i):
            activate(
                rows_at(sz.bg + i * l_rows, l_rows),
                (dst, rows_at(sz.one_l + i * l_rows, l_rows)),
                dst_s,
                l_rows,
                sz.cl,
                flag,
            )

    refs = (a00, a01, a01s, a10, a11, a11s)
    zero = jnp.zeros((8, C), f32)

    def step(i, carry):
        total, square = carry
        z = dot(x_ref[rows_at(i * third, third), :], s_ref[...])
        return total + fold(z), square + fold(z * z)

    more = lax.fori_loop(0, 3, step, (zero, zero))
    conv_forward(
        sz, lambda part: windows_one(sz, refs, part), bd_ref, z_ref, st_ref, sums, more
    )


def each_crop(sz, one):
    @pl.loop(0, sz.ng)
    def _(n):
        one([rows_at(i * sz.bg + n * sz.cg, sz.cg) for i in range(sz.rg)], (n,))

    @pl.loop(0, sz.nl // 2)
    def _(pair):
        first = sz.ng + 2 * pair
        one(
            [rows_at(sz.mg + i * sz.bl + pair * 2 * sz.cl, 2 * sz.cl) for i in range(sz.rl)],
            (first, first + 1),
        )


def add_pool(ref, crops, value):
    if len(crops) == 1:
        ref[pl.ds(crops[0], 1), :] = jnp.sum(value, axis=0, keepdims=True)
    else:
        n = value.shape[0] // 2
        ref[pl.ds(crops[0], 1), :] = jnp.sum(value[:n], axis=0, keepdims=True)
        ref[pl.ds(crops[1], 1), :] = jnp.sum(value[n:], axis=0, keepdims=True)


def crop_rows(ref, crops, n_rows):
    if len(crops) == 1:
        return ref[pl.ds(crops[0], 1), :]
    n = n_rows // 2
    return jnp.concatenate(
        [jnp.broadcast_to(ref[pl.ds(crop, 1), :], (n, ref.shape[1])) for crop in crops], axis=0
    )


def pool_kernel(sz, gain_row, shift_row, strided, z_ref, t0, t1, t2, t3, vt_ref, pool_ref, nrm_ref, ps):
    terms = norm_terms(
        gather_sum((t0, t1, t2, t3)),
        0,
        sz.amount,
        vt_ref[gain_row : gain_row + 1, :],
        vt_ref[shift_row : shift_row + 1, :],
    )
    nrm_ref[...] = jnp.zeros_like(nrm_ref)
    put_norm(nrm_ref, 0, terms)
    if strided:
        put_norm(
            nrm_ref,
            4,
            norm_terms(
                gather_sum((t0, t1, t2, t3)),
                2,
                sz.amount,
                vt_ref[G1S : G1S + 1, :],
                vt_ref[B1S : B1S + 1, :],
            ),
        )
    scale, shift = terms[2], terms[3]
    ps[...] = jnp.zeros_like(ps)

    def one(pieces, crops):
        acc = None
        for rows in pieces:
            c = silu(z_ref[rows, :] * scale + shift)
            acc = c if acc is None else acc + c
        add_pool(ps, crops, acc)

    each_crop(sz, one)
    pool_ref[...] = ps[...].astype(bf16)


def inverse_area(sz):
    crop = lax.broadcasted_iota(jnp.int32, (sz.crops, 1), 0)
    return jnp.where(crop < sz.ng, 1.0 / sz.area_g, 1.0 / sz.area_l).astype(f32)


def dot_high(a, b):
    return jnp.dot(a, b, precision=highest, preferred_element_type=f32)


def gather_short(refs):
    total = refs[0][...].astype(f32)
    for ref in refs[1:]:
        total = total + ref[...].astype(f32)
    return total


def gated_product_kernel(
    sz,
    bias_row,
    shift_row,
    z_in_ref,
    nrm_ref,
    p0,
    p1,
    p2,
    p3,
    d_ref,
    u_ref,
    w_ref,
    vt_ref,
    q_ref,
    z_ref,
    st_ref,
    gate_ref,
    pooled_ref,
    pre_ref,
):
    pooled = gather_short((p0, p1, p2, p3)) * inverse_area(sz)
    pooled_ref[...] = pooled
    pre = dot_high(pooled, d_ref[...].astype(f32)) + vt_ref[bias_row : bias_row + 1, 0:HID]
    pre_ref[...] = pre
    gate = dot_high(silu(pre), u_ref[...].astype(f32)) + vt_ref[shift_row : shift_row + 1, :]
    gate_ref[...] = sigmoid(gate)
    scale = nrm_ref[2:3, :]
    shift = nrm_ref[3:4, :]

    def one(pieces, crops):
        g = crop_rows(gate_ref, crops, 2 * sz.cl)
        for rows in pieces:
            c = silu(z_in_ref[rows, :] * scale + shift)
            q_ref[rows, :] = (c * g).astype(bf16)

    each_crop(sz, one)
    n_rows = sz.m // 3
    zero = jnp.zeros((8, C), f32)

    def step(i, carry):
        total, square = carry
        rows = rows_at(i * n_rows, n_rows)
        z = dot(q_ref[rows, :], w_ref[...])
        z_ref[rows, :] = z
        return total + fold(z), square + fold(z * z)

    put_rows(st_ref, lax.fori_loop(0, 3, step, (zero, zero)))


ROWS = 32


def put_edges(sz, src, top_ref, bottom_ref):
    for ref, g, l in (
        (top_ref, 0, sz.mg),
        (bottom_ref, sz.mg - sz.bg, sz.m - sz.bl),
    ):
        if ref is not None:
            ref[0 : sz.bg, :] = src[g : g + sz.bg, :]
            ref[sz.bg : sz.edge, :] = src[l : l + sz.bl, :]


def middle_kernel(
    sz,
    zc_ref,
    x_ref,
    s_ref,
    t0,
    t1,
    t2,
    t3,
    nrm_a_ref,
    vt_ref,
    pre_ref,
    mb_ref,
    nrm_ref,
    top_ref,
    bottom_ref,
    zs,
):
    strided_product(sz, x_ref, s_ref, zs)
    terms = norm_terms(
        gather_sum((t0, t1, t2, t3)),
        0,
        sz.amount,
        vt_ref[G1C : G1C + 1, :],
        vt_ref[B1C : B1C + 1, :],
    )
    nrm_ref[...] = jnp.zeros_like(nrm_ref)
    put_norm(nrm_ref, 0, terms)
    scale = terms[2]
    scale_s = nrm_a_ref[6:7, :]
    shift = terms[3] + nrm_a_ref[7:8, :]

    @pl.loop(0, sz.m // ROWS)
    def _(i):
        rows = rows_at(i * ROWS, ROWS)
        pre = zc_ref[rows, :] * scale + zs[rows, :] * scale_s + shift
        pre_ref[rows, :] = pre
        mb_ref[rows, :] = silu(pre).astype(bf16)

    put_edges(sz, mb_ref, top_ref, bottom_ref)


def product_kernel(sz, x_ref, w_ref, z_ref, st_ref):
    n_rows = sz.m // 3
    zero = jnp.zeros((8, C), f32)

    def step(i, carry):
        total, square = carry
        rows = rows_at(i * n_rows, n_rows)
        z = dot(x_ref[rows, :], w_ref[...])
        z_ref[rows, :] = z
        return total + fold(z), square + fold(z * z)

    put_rows(st_ref, lax.fori_loop(0, 3, step, (zero, zero)))


def put_variants(refs, rows, value, width):
    refs[0][rows, :] = shifted(value, -1, width).astype(bf16)
    refs[1][rows, :] = value.astype(bf16)
    refs[2][rows, :] = shifted(value, 1, width).astype(bf16)


def second_conv_kernel(
    sz,
    flag_ref,
    z_in_ref,
    top_ref,
    bottom_ref,
    w_ref,
    k_ref,
    t0,
    t1,
    t2,
    t3,
    vt_ref,
    z_ref,
    st_ref,
    nrm_ref,
    a1,
    a0,
    a2,
    bd_ref,
    zs,
    sums,
):
    block_diagonal(k_ref, bd_ref)
    terms = norm_terms(
        gather_sum((t0, t1, t2, t3)),
        0,
        sz.amount,
        vt_ref[G2A : G2A + 1, :],
        vt_ref[B2A : B2A + 1, :],
    )
    nrm_ref[...] = jnp.zeros_like(nrm_ref)
    put_norm(nrm_ref, 0, terms)
    scale, shift = terms[2], terms[3]
    g_rows, l_rows = segments(sz)
    refs = (a0, a1, a2)

    @pl.loop(0, sz.mg // g_rows)
    def _(i):
        a = silu(z_in_ref[rows_at(i * g_rows, g_rows), :] * scale + shift)
        put_variants(refs, rows_at(sz.bg + i * g_rows, g_rows), a, sz.cg)

    @pl.loop(0, sz.ml // l_rows)
    def _(i):
        a = silu(z_in_ref[rows_at(sz.mg + i * l_rows, l_rows), :] * scale + shift)
        put_variants(refs, rows_at(sz.two_l + sz.bl + i * l_rows, l_rows), a, sz.cl)

    for k, src in enumerate((top_ref, bottom_ref)):
        flag = (above, below)[k](flag_ref, sz.n_height)
        zs[...] = dot(src[...], w_ref[...])
        g_first = 0 if k == 0 else (sz.rg + 1) * sz.bg
        l_first = sz.two_l + (0 if k == 0 else (sz.rl + 1) * sz.bl)

        @pl.loop(0, sz.bg // g_rows)
        def _(i):
            a = silu(zs[rows_at(i * g_rows, g_rows), :] * scale + shift) * flag
            put_variants(refs, rows_at(g_first + i * g_rows, g_rows), a, sz.cg)

        @pl.loop(0, sz.bl // l_rows)
        def _(i):
            a = silu(zs[rows_at(sz.bg + i * l_rows, l_rows), :] * scale + shift) * flag
            put_variants(refs, rows_at(l_first + i * l_rows, l_rows), a, sz.cl)

    conv_forward(sz, lambda part: windows_two(sz, refs, part), bd_ref, z_ref, st_ref, sums)


def output_kernel(
    sz, pre_ref, z_ref, t0, t1, t2, t3, vt_ref, cg_ref, cl_ref, og_ref, ol_ref, dn_ref, st_ref, nrm_ref, sums
):
    terms = norm_terms(
        gather_sum((t0, t1, t2, t3)),
        0,
        sz.amount,
        vt_ref[G2C : G2C + 1, :],
        vt_ref[B2C : B2C + 1, :],
    )
    nrm_ref[...] = jnp.zeros_like(nrm_ref)
    put_norm(nrm_ref, 0, terms)
    mean, inverse, scale, shift = terms
    sums[...] = jnp.zeros_like(sums)

    def piece(rows, cot):
        z = z_ref[rows, :]
        pre = silu(pre_ref[rows, :]) + z * scale + shift
        s = sigmoid(pre)
        dn = cot * (s * (1.0 + pre * (1.0 - s)))
        dn_ref[rows, :] = dn
        sums[0:8, :] += fold(dn)
        sums[8:16, :] += fold(dn * ((z - mean) * inverse))
        return pre * s

    @pl.loop(0, sz.ng)
    def _(n):
        for i in range(sz.rg):
            rows = rows_at(i * sz.bg + n * sz.cg, sz.cg)
            og_ref[n, i] = piece(rows, cg_ref[n, i].astype(f32)).astype(bf16)

    @pl.loop(0, sz.nl // 2)
    def _(pair):
        for i in range(sz.rl):
            rows = rows_at(sz.mg + i * sz.bl + pair * 2 * sz.cl, 2 * sz.cl)
            cot = jnp.concatenate(
                [cl_ref[2 * pair + k, i].astype(f32) for k in range(2)], axis=0
            )
            value = piece(rows, cot)
            for k in range(2):
                ol_ref[2 * pair + k, i] = value[k * sz.cl : (k + 1) * sz.cl].astype(bf16)

    put_rows(st_ref, [sums[0:8, :], sums[8:16, :]])


def back_terms(total, row_one, row_two, amount, nrm_ref, nrm_row):
    mean = nrm_ref[nrm_row : nrm_row + 1, :]
    inverse = nrm_ref[nrm_row + 1 : nrm_row + 2, :]
    scale = nrm_ref[nrm_row + 2 : nrm_row + 3, :]
    one = total[row_one : row_one + 1] / amount
    two = total[row_two : row_two + 1] / amount
    return scale, one, mean, inverse * two


def norm_back(dn, z, terms):
    scale, one, mean, slope = terms
    return scale * (dn - one - (z - mean) * slope)


def gate_grad_kernel(
    sz,
    strided,
    dn_ref,
    z_ref,
    t0,
    t1,
    t2,
    t3,
    nrm_ref,
    w_ref,
    z_in_ref,
    nrm_in_ref,
    *refs,
):
    if strided:
        x_ref, s_ref, nrm_a_ref, dz_ref, dzs_ref, dq_ref, dg_ref, ps, zs = refs
        strided_product(sz, x_ref, s_ref, zs)
    else:
        dz_ref, dq_ref, dg_ref, ps = refs
    total = gather_sum((t0, t1, t2, t3))
    terms = back_terms(total, 0, 1, sz.amount, nrm_ref, 0)

    @pl.loop(0, sz.m // ROWS)
    def _(i):
        rows = rows_at(i * ROWS, ROWS)
        dz_ref[rows, :] = norm_back(dn_ref[rows, :], z_ref[rows, :], terms).astype(bf16)

    if strided:
        terms_s = back_terms(total, 0, 2, sz.amount, nrm_a_ref, 4)

        @pl.loop(0, sz.m // ROWS)
        def _(i):
            rows = rows_at(i * ROWS, ROWS)
            dzs_ref[rows, :] = norm_back(dn_ref[rows, :], zs[rows, :], terms_s).astype(bf16)

    n_rows = sz.m // 3

    @pl.loop(0, 3)
    def _(i):
        rows = rows_at(i * n_rows, n_rows)
        dq_ref[rows, :] = dot_t(dz_ref[rows, :], w_ref[...])

    ps[...] = jnp.zeros_like(ps)
    scale = nrm_in_ref[2:3, :]
    shift = nrm_in_ref[3:4, :]

    def one(pieces, crops):
        acc = None
        for rows in pieces:
            term = dq_ref[rows, :] * silu(z_in_ref[rows, :] * scale + shift)
            acc = term if acc is None else acc + term
        add_pool(ps, crops, acc)

    each_crop(sz, one)
    dg_ref[...] = ps[...].astype(bf16)


def excite_back_kernel(
    sz,
    dq_ref,
    z_ref,
    nrm_ref,
    g0,
    g1,
    g2,
    g3,
    gate_ref,
    pre_ref,
    d_ref,
    u_ref,
    dn_ref,
    st_ref,
    dv_ref,
    du_ref,
    pool,
    sums,
):
    gate = gate_ref[...]
    dv = gather_short((g0, g1, g2, g3)) * gate * (1.0 - gate)
    dv_ref[...] = dv
    du = lax.dot_general(
        dv,
        u_ref[...].astype(f32),
        (((1,), (1,)), ((), ())),
        precision=highest,
        preferred_element_type=f32,
    ) * silu_slope(pre_ref[...])
    du_ref[...] = du
    pool[...] = (
        lax.dot_general(
            du,
            d_ref[...].astype(f32),
            (((1,), (1,)), ((), ())),
            precision=highest,
            preferred_element_type=f32,
        )
        * inverse_area(sz)
    )
    mean = nrm_ref[0:1, :]
    inverse = nrm_ref[1:2, :]
    scale = nrm_ref[2:3, :]
    shift = nrm_ref[3:4, :]
    sums[...] = jnp.zeros_like(sums)

    def one(pieces, crops):
        g = crop_rows(gate_ref, crops, 2 * sz.cl)
        p = crop_rows(pool, crops, 2 * sz.cl)
        for rows in pieces:
            z = z_ref[rows, :]
            dn = (dq_ref[rows, :] * g + p) * silu_slope(z * scale + shift)
            dn_ref[rows, :] = dn
            sums[0:8, :] += fold(dn)
            sums[8:16, :] += fold(dn * ((z - mean) * inverse))

    each_crop(sz, one)
    put_rows(st_ref, [sums[0:8, :], sums[8:16, :]])


def put_flat(value_ref, width, flat_ref, slots):
    if width == 128:
        for j in range(C // 128):
            flat_ref[:, j * 128 : (j + 1) * 128] = value_ref[pl.ds(j, width, stride=C // 128), :]
        return
    n_lines = width // int(np.gcd(C, width))
    n_groups = width // n_lines
    per = C // n_groups
    lane = lax.broadcasted_iota(jnp.int32, (n_groups, C), 1)
    lines = [jnp.zeros((n_groups, C), f32) for _ in range(n_lines)]
    for u in range(per):
        row = value_ref[pl.ds(u, n_groups, stride=per), :]
        row = jnp.concatenate([row] + [jnp.zeros_like(row)] * (C // 128 - 1), axis=1)
        line, at = divmod(u * width, C)
        moved = pltpu.roll(row, at, 1) if at else row
        lines[line] = jnp.where(lane >= at, lines[line] + moved, lines[line])
        if at + width > C:
            lines[line + 1] = jnp.where(
                lane < at + width - C, lines[line + 1] + moved, lines[line + 1]
            )
    for j in range(C // 128):
        for k, line in enumerate(lines):
            slots[pl.ds(k, n_groups, stride=n_lines), :] = line[:, j * 128 : (j + 1) * 128]
        flat_ref[:, j * 128 : (j + 1) * 128] = slots[0:width, :]


def excite_weights_kernel(
    width, flag_ref, dv_ref, du_ref, pooled_ref, pre_ref, dd_ref, de_ref, du_out, df_ref, wide, slots
):
    flag = first_of_height(flag_ref)
    dv = dv_ref[...] * flag
    du = du_ref[...] * flag

    def cross(a, b):
        return lax.dot_general(
            a, b, (((0,), (0,)), ((), ())), precision=highest, preferred_element_type=f32
        )

    wide[...] = cross(pooled_ref[...], du)
    put_flat(wide, width, dd_ref, slots)
    du_out[...] = cross(silu(pre_ref[...]), dv)
    de_ref[...] = jnp.broadcast_to(jnp.sum(du, axis=0, keepdims=True), de_ref.shape)
    df_ref[...] = jnp.broadcast_to(jnp.sum(dv, axis=0, keepdims=True), df_ref.shape)


def weight_kernel(x_ref, dz_ref, w_ref):
    n_rows = dz_ref.shape[0]
    n = 128 if x_ref.shape[1] % 128 == 0 else x_ref.shape[1]
    for k in range(x_ref.shape[1] // n):
        w_ref[k * n : (k + 1) * n, :] = t_dot(x_ref[0:n_rows, k * n : (k + 1) * n], dz_ref[...])


def norm_back_kernel(sz, dn_ref, z_ref, t0, t1, t2, t3, nrm_ref, dz_ref, top_ref, bottom_ref=None):
    terms = back_terms(gather_sum((t0, t1, t2, t3)), 0, 1, sz.amount, nrm_ref, 0)

    @pl.loop(0, sz.m // ROWS)
    def _(i):
        rows = rows_at(i * ROWS, ROWS)
        dz_ref[rows, :] = norm_back(dn_ref[rows, :], z_ref[rows, :], terms).astype(bf16)

    put_edges(sz, dz_ref, top_ref, bottom_ref)


def conv_weights(sz, windows_of, dz_ref, dk_ref):
    @pl.loop(0, 2)
    def _(half):
        cols = pl.ds(pl.multiple_of(half * HALF, HALF), HALF)
        win_g = windows_of("g")
        win_l = windows_of("l")
        for tap in range(9):
            _, ref_g, start_g = win_g[tap]
            _, ref_l, start_l = win_l[tap]
            acc = t_dot(ref_g[start_g : start_g + sz.mg, cols], dz_ref[0 : sz.mg, cols])
            acc = acc + t_dot(ref_l[start_l : start_l + sz.ml, cols], dz_ref[sz.mg : sz.m, cols])
            dk_ref[tap * GW : (tap + 1) * GW, cols] = block_dense(acc)


def shift_all(src, dst, by, spans):
    for first, n_all, n_rows, width in spans:

        @pl.loop(0, n_all // n_rows)
        def _(i):
            rows = rows_at(first + i * n_rows, n_rows)
            dst[rows, :] = shifted(src[rows, :].astype(f32), by, width).astype(bf16)


def second_conv_weights_kernel(sz, a1, dz_ref, dk_ref, a0, a2):
    g_rows, l_rows = segments(sz)
    spans = ((0, sz.two_l, g_rows, sz.cg), (sz.two_l, sz.two - sz.two_l, l_rows, sz.cl))
    shift_all(a1, a0, -1, spans)
    shift_all(a1, a2, 1, spans)
    conv_weights(sz, lambda part: windows_two(sz, (a0, a1, a2), part), dz_ref, dk_ref)


def first_conv_weights_kernel(sz, a00, a01, a10, a11, dz_ref, dk_ref, a01s, a11s):
    g_rows, l_rows = segments(sz)
    shift_all(a01, a01s, -1, ((0, sz.mg, g_rows, sz.cg), (sz.mg, sz.ml, l_rows, sz.cl)))
    shift_all(
        a11,
        a11s,
        -1,
        ((0, sz.one_l, g_rows, sz.cg), (sz.one_l, sz.one - sz.one_l, l_rows, sz.cl)),
    )
    refs = (a00, a01, a01s, a10, a11, a11s)
    conv_weights(sz, lambda part: windows_one(sz, refs, part), dz_ref, dk_ref)


def second_conv_back_kernel(
    sz, dz_ref, top_ref, bottom_ref, k_ref, z_ref, nrm_ref, dn_ref, st_ref, v0, v1, v2, bd_ref, sums
):
    block_diagonal(k_ref, bd_ref)
    refs = (v0, v1, v2)
    g_rows, l_rows = segments(sz)

    @pl.loop(0, sz.mg // g_rows)
    def _(i):
        v = dz_ref[rows_at(i * g_rows, g_rows), :].astype(f32)
        put_variants(refs, rows_at(sz.bg + i * g_rows, g_rows), v, sz.cg)

    @pl.loop(0, sz.ml // l_rows)
    def _(i):
        v = dz_ref[rows_at(sz.mg + i * l_rows, l_rows), :].astype(f32)
        put_variants(refs, rows_at(sz.two_l + sz.bl + i * l_rows, l_rows), v, sz.cl)

    for k, src in enumerate((top_ref, bottom_ref)):
        g_first = 0 if k == 0 else (sz.rg + 1) * sz.bg
        l_first = sz.two_l + (0 if k == 0 else (sz.rl + 1) * sz.bl)

        @pl.loop(0, sz.bg // g_rows)
        def _(i):
            v = src[rows_at(i * g_rows, g_rows), :].astype(f32)
            put_variants(refs, rows_at(g_first + i * g_rows, g_rows), v, sz.cg)

        @pl.loop(0, sz.bl // l_rows)
        def _(i):
            v = src[rows_at(sz.bg + i * l_rows, l_rows), :].astype(f32)
            put_variants(refs, rows_at(l_first + i * l_rows, l_rows), v, sz.cl)

    @pl.loop(0, 2)
    def _(half):
        cols = pl.ds(pl.multiple_of(half * HALF, HALF), HALF)
        for part, first, n_all, n_rows in (
            ("g", 0, sz.mg, sz.mg // 2),
            ("l", sz.mg, sz.ml, sz.ml),
        ):
            for k in range(n_all // n_rows):
                dn_ref[first + k * n_rows : first + (k + 1) * n_rows, cols] = conv_product(
                    shift_windows(windows_two(sz, refs, part, True), k * n_rows),
                    bd_ref,
                    half,
                    n_rows,
                    True,
                )

    slope_pass(sz.m, dn_ref, z_ref, nrm_ref, st_ref, sums)


def slope_pass(n_all, dn_ref, z_ref, nrm_ref, st_ref, sums):
    mean = nrm_ref[0:1, :]
    inverse = nrm_ref[1:2, :]
    scale = nrm_ref[2:3, :]
    shift = nrm_ref[3:4, :]
    sums[...] = jnp.zeros_like(sums)

    @pl.loop(0, n_all // ROWS)
    def _(i):
        rows = rows_at(i * ROWS, ROWS)
        z = z_ref[rows, :]
        dn = dn_ref[rows, :] * silu_slope(z * scale + shift)
        dn_ref[rows, :] = dn
        sums[0:8, :] += fold(dn)
        sums[8:16, :] += fold(dn * ((z - mean) * inverse))

    put_rows(st_ref, [sums[0:8, :], sums[8:16, :]])


def middle_back_kernel(
    sz,
    dn_d_ref,
    zd_ref,
    t0,
    t1,
    t2,
    t3,
    nrm_d_ref,
    w_ref,
    dpre_ref,
    pre_ref,
    zc_ref,
    x_ref,
    s_ref,
    nrm_c_ref,
    nrm_a_ref,
    dz_ref,
    dn_ref,
    st_ref,
    zs,
    sums,
):
    strided_product(sz, x_ref, s_ref, zs)
    terms = back_terms(gather_sum((t0, t1, t2, t3)), 0, 1, sz.amount, nrm_d_ref, 0)

    @pl.loop(0, sz.m // ROWS)
    def _(i):
        rows = rows_at(i * ROWS, ROWS)
        dz_ref[rows, :] = norm_back(dn_d_ref[rows, :], zd_ref[rows, :], terms).astype(bf16)

    n_rows = sz.m // 3

    @pl.loop(0, 3)
    def _(i):
        rows = rows_at(i * n_rows, n_rows)
        dn_ref[rows, :] = dot_t(dz_ref[rows, :], w_ref[...])

    mean_c = nrm_c_ref[0:1, :]
    inverse_c = nrm_c_ref[1:2, :]
    mean_s = nrm_a_ref[4:5, :]
    inverse_s = nrm_a_ref[5:6, :]
    sums[...] = jnp.zeros_like(sums)

    @pl.loop(0, sz.m // ROWS)
    def _(i):
        rows = rows_at(i * ROWS, ROWS)
        dn = (dn_ref[rows, :] + dpre_ref[rows, :]) * silu_slope(pre_ref[rows, :])
        dn_ref[rows, :] = dn
        sums[0:8, :] += fold(dn)
        sums[8:16, :] += fold(dn * ((zc_ref[rows, :] - mean_c) * inverse_c))
        sums[16:24, :] += fold(dn * ((zs[rows, :] - mean_s) * inverse_s))

    put_rows(st_ref, [sums[0:8, :], sums[8:16, :], sums[16:24, :]])


def first_conv_back_kernel(sz, dz_ref, below_ref, k_ref, v0, v1, bd_ref):
    block_diagonal(k_ref, bd_ref)
    g_rows, l_rows = segments(sz)

    def put(rows, v, width):
        v0[rows, :] = v.astype(bf16)
        v1[rows, :] = shifted(v, 1, width).astype(bf16)

    for src, g_src, l_src, g_dst, l_dst, g_all, l_all in (
        (dz_ref, 0, sz.mg, 0, sz.one_l, sz.mg, sz.ml),
        (below_ref, 0, sz.bg, sz.mg, sz.one_l + sz.ml, sz.bg, sz.bl),
    ):

        @pl.loop(0, g_all // g_rows)
        def _(i):
            v = src[rows_at(g_src + i * g_rows, g_rows), :].astype(f32)
            put(rows_at(g_dst + i * g_rows, g_rows), v, sz.cg)

        @pl.loop(0, l_all // l_rows)
        def _(i):
            v = src[rows_at(l_src + i * l_rows, l_rows), :].astype(f32)
            put(rows_at(l_dst + i * l_rows, l_rows), v, sz.cl)


def parity_back_kernel(sz, phase, v0, v1, bd_ref, x_ref, w_ref, nrm_ref, *refs):
    if phase:
        st_in, dn_ref, st_ref, zs, da, sums = refs
    else:
        dn_ref, st_ref, zs, da, sums = refs
    mean = nrm_ref[0:1, :]
    inverse = nrm_ref[1:2, :]
    scale = nrm_ref[2:3, :]
    shift = nrm_ref[3:4, :]
    sums[...] = jnp.zeros_like(sums)
    third = sz.m // 3
    pr, pc = phase // 2, phase % 2
    taps = []
    for a, down in (((1, 0),), ((2, 0), (0, 1)))[pr]:
        for b, right in (((1, 0),), ((2, 0), (0, 1)))[pc]:
            taps.append((3 * a + b, down, right))

    @pl.loop(0, 2)
    def _(half):
        cols = pl.ds(pl.multiple_of(half * HALF, HALF), HALF)
        for first, base, block, n_all, n_rows in (
            (0, 0, sz.bg, sz.mg, sz.mg // 2),
            (sz.mg, sz.one_l, sz.bl, sz.ml, sz.ml),
        ):
            for k in range(n_all // n_rows):
                windows = [
                    (tap, (v0, v1)[right], base + down * block + k * n_rows)
                    for tap, down, right in taps
                ]
                da[first + k * n_rows : first + (k + 1) * n_rows, cols] = conv_product(
                    windows, bd_ref, half, n_rows, True
                )

    @pl.loop(0, 3)
    def _(i):
        zs[rows_at(i * third, third), :] = dot(
            x_ref[rows_at(phase * sz.m + i * third, third), :], w_ref[...]
        )

    @pl.loop(0, sz.m // ROWS)
    def _(i):
        rows = rows_at(i * ROWS, ROWS)
        z = zs[rows, :]
        dn = da[rows, :] * silu_slope(z * scale + shift)
        dn_ref[rows, :] = dn.astype(bf16)
        sums[0:8, :] += fold(dn)
        sums[8:16, :] += fold(dn * ((z - mean) * inverse))

    put_rows(st_ref, [sums[0:8, :], sums[8:16, :]])
    if phase:
        st_ref[...] += st_in[...]


def image_norm_back_kernel(sz, dn0, dn1, dn2, dn3, x_ref, w_ref, t0, t1, t2, t3, nrm_ref, dz_ref, zs):
    terms = back_terms(gather_sum((t0, t1, t2, t3)), 0, 1, 4 * sz.amount, nrm_ref, 0)
    third = sz.m // 3
    for phase in range(4):

        @pl.loop(0, 3)
        def _(i):
            zs[rows_at(i * third, third), :] = dot(
                x_ref[rows_at(phase * sz.m + i * third, third), :], w_ref[...]
            )

        @pl.loop(0, sz.m // ROWS)
        def _(i):
            rows = rows_at(i * ROWS, ROWS)
            rows_all = rows_at(phase * sz.m + i * ROWS, ROWS)
            dz_ref[rows_all, :] = norm_back(
                (dn0, dn1, dn2, dn3)[phase][rows, :].astype(f32), zs[rows, :], terms
            ).astype(bf16)


def image_product_kernel(sz, dz_ref, w_ref, dzs_ref, ws_ref, dx_ref):
    third = sz.m // 3
    for phase in range(4):

        @pl.loop(0, 3)
        def _(i):
            rows_all = rows_at(phase * sz.m + i * third, third)
            value = dot_t(dz_ref[rows_all, :], w_ref[...])
            if phase == 0:
                value = value + dot_t(dzs_ref[rows_at(i * third, third), :], ws_ref[...])
            dx_ref[rows_all, :] = value


def place_kernel(n_crops, height, width, first_row, block, m, dx_ref, o_ref, mark_ref, s_ref, t_ref):
    half = width // 2
    mark_ref[...] = jnp.zeros_like(mark_ref)

    @pl.loop(0, n_crops)
    def _(n):
        for r in range(height):
            for pc in range(2):
                at = (2 * (r % 2) + pc) * m + first_row + (r // 2) * block + n * half
                v = dx_ref[rows_at(at, half, 8), :]
                rows = pl.ds(r * width + pc, half, stride=2)
                s_ref[rows, :] = v[:, :128]
                t_ref[rows, :] = jnp.concatenate([v[:, 128:], v[:, 128:]], axis=1)
        o_ref[n, :, :, 0:128] = s_ref[...].reshape(height, width, 128)
        o_ref[n, :, :, 128:CIN] = t_ref[...][:, :64].reshape(height, width, 64)


def over_height(x):
    n = lax.axis_size("height")
    return [x] + [lax.ppermute(x, "height", [(i, i ^ k) for i in range(n)]) for k in range(1, n)]


def step_down(x):
    n = lax.axis_size("height")
    return lax.ppermute(x, "height", [(i, i + 1) for i in range(n - 1)])


def step_up(x):
    n = lax.axis_size("height")
    return lax.ppermute(x, "height", [(i + 1, i) for i in range(n - 1)])


MATRIX_ROWS = [a * b // C for a, b in matrix_shapes()]
ROW_BOUNDS = [int(v) for v in np.cumsum([0] + MATRIX_ROWS)]
UNIT = 112


def across(x, mask, senders=None):
    n = lax.axis_size("batch")
    return lax.ppermute(
        x, "batch", [(i, i ^ mask) for i in range(n) if senders is None or i in senders]
    )


def take_flat(whole, start, width, low_ref, value, slots):
    if width == 128:
        for j in range(C // 128):
            value[pl.ds(j, width, stride=C // 128), :] = whole[
                start : start + width, j * 128 : (j + 1) * 128
            ]
    else:
        n_lines = width // int(np.gcd(C, width))
        n_groups = width // n_lines
        per = C // n_groups
        lane = lax.broadcasted_iota(jnp.int32, (n_groups, C), 1)
        blocks = [[] for _ in range(n_lines)]
        for j in range(C // 128):
            slots[0:width, :] = whole[start : start + width, j * 128 : (j + 1) * 128]
            for k in range(n_lines):
                blocks[k].append(slots[pl.ds(k, n_groups, stride=n_lines), :])
        lines = [jnp.concatenate(block, axis=1) for block in blocks]
        for u in range(per):
            line, at = divmod(u * width, C)
            row = pltpu.roll(lines[line], C - at, 1) if at else lines[line]
            if at + width > C:
                row = jnp.where(lane < C - at, row, pltpu.roll(lines[line + 1], C - at, 1))
            value[pl.ds(u, n_groups, stride=per), :] = jnp.where(lane < width, row, 0.0)[:, 0:128]
    low_ref[...] = value[...].astype(bf16)


def assemble_kernel(n_rows, idx_ref, *refs):
    ins, outs = refs[:8], refs[8:-4]
    shards, whole, value, slots = refs[-4:]
    for q, mask in enumerate((0, 2, 4, 6, 1, 3, 5, 7)):
        for k in range(4):
            at = (idx_ref[0] ^ mask) * 4 + (idx_ref[1] ^ k)
            shards[at, 0:n_rows, :] = ins[q][k].astype(f32)
    for s in range(32):
        whole[s * n_rows : (s + 1) * n_rows, :] = shards[s, 0:n_rows, :]
    for k, (ref, start) in enumerate(zip(outs, ROW_BOUNDS)):
        if k in (2, 8):
            take_flat(whole, start, MATRIX_ROWS[k], ref, value, slots)
        elif k in (3, 9):
            n = MATRIX_ROWS[k]
            value[0:HID, :] = jnp.zeros((HID, 128), f32)
            for j in range(C // 128):
                value[0:n, :] = whole[start : start + n, j * 128 : (j + 1) * 128]
                ref[:, j * 128 : (j + 1) * 128] = value[0:HID, :].astype(bf16)
        else:
            ref[...] = whole[start : start + ref.shape[0], :].astype(bf16)


def gather_weights(lines, n_rows, place_ids, beside):
    (mine,) = call(
        functools.partial(round_rows_kernel, n_rows),
        [out((n_rows, C), bf16)],
        [],
        lines,
        name="round_weights",
        after=[place_ids],
    )
    quarter = jnp.stack(over_height(mine))
    after, extra = beside(quarter)
    planes = [quarter] + [across(quarter, mask) for mask in (2, 4, 6)]
    planes += [across(plane, 1) for plane in planes]
    matrices = call(
        functools.partial(assemble_kernel, n_rows),
        [
            out((C, HID) if k in (2, 8) else (HID if k in (3, 9) else rows, C), bf16)
            for k, rows in enumerate(MATRIX_ROWS)
        ],
        [
            pltpu.VMEM((32, UNIT, C), f32),
            pltpu.VMEM((32 * n_rows, C), f32),
            pltpu.VMEM((C, 128), f32),
            pltpu.VMEM((HID, 128), f32),
        ],
        place_ids,
        *planes,
        smem=1,
        name="assemble",
        after=after,
        room=6 * 2**20,
    )
    return matrices, extra


def pack_kernel(n_rows, first_shard, sources, core_ref, *refs):
    n_src = len(sources)
    ins, (mine_ref, other_ref, buf) = refs[:n_src], refs[n_src:]
    buf[...] = jnp.zeros_like(buf)
    for shard in range(16):
        low = (first_shard + shard) * n_rows
        for (start, stop), ref in zip(sources, ins):
            a, b = max(low, start), min(low + n_rows, stop)
            if a < b:
                buf[shard, a - low : b - low, :] = ref[a - start : b - start, :]
    core = core_of(core_ref)
    for unit in range(2):
        for h in range(4):
            mine_ref[unit * 4 + h] = buf[(unit * 2 + core) * 4 + h]
            other_ref[unit * 4 + h] = buf[(unit * 2 + 1 - core) * 4 + h].astype(bf16)


def height_parts_kernel(place_ref, mine_ref, got_ref, keep_ref, s1, s2, s3):
    place = place_ref[1]
    for unit in range(2):
        for k, ref in enumerate((keep_ref, s1, s2, s3)):
            at = unit * 4 + (place ^ k)
            ref[unit] = (mine_ref[at] + got_ref[at].astype(f32)).astype(ref.dtype)


def height_sum_kernel(keep_ref, r1, r2, r3, sum_ref, low_ref):
    total = keep_ref[...] + r1[...].astype(f32) + r2[...].astype(f32) + r3[...].astype(f32)
    sum_ref[...] = total
    low_ref[...] = total.astype(bf16)


def plane_parts_kernel(x_ref, sum_ref, got_ref, keep_ref, send_ref):
    x = x_of(x_ref)
    keep_ref[...] = sum_ref[x] + got_ref[x].astype(f32)
    send_ref[...] = (sum_ref[1 - x] + got_ref[1 - x].astype(f32)).astype(bf16)


def sum_low_kernel(a_ref, b_ref, sum_ref, *low_refs):
    n = low_refs[0].shape[0]
    for k, ref in enumerate(low_refs):
        total = a_ref[k * n : (k + 1) * n] + b_ref[k * n : (k + 1) * n].astype(f32)
        sum_ref[k * n : (k + 1) * n] = total
        ref[...] = total.astype(bf16)


def unit_parts_kernel(place_ref, sum_ref, g0, g1, g2, g3, keep_ref, send_ref, got_ref):
    for k, ref in enumerate((g0, g1, g2, g3)):
        got_ref[2 * k : 2 * k + 2] = ref[...]
    x = x_of(place_ref)
    for h in range(4):
        mine, other = 4 * x + h, 4 * (1 - x) + h
        keep_ref[h] = sum_ref[mine] + got_ref[mine].astype(f32)
        send_ref[h] = (sum_ref[other] + got_ref[other].astype(f32)).astype(bf16)


def shard_parts_kernel(place_ref, sum_ref, got_ref, keep_ref, s1, s2, s3):
    for k, ref in enumerate((keep_ref, s1, s2, s3)):
        at = place_ref[1] ^ k
        ref[...] = (sum_ref[at] + got_ref[at].astype(f32)).astype(ref.dtype)


class Reduction:
    def __init__(self, root, n_rows, place_ids):
        self.root, self.n_rows, self.ids = root, n_rows, place_ids
        self.tag = "_%d" % root
        self.rooted = [b for b in range(8) if b // 4 == root]
        self.others = [b for b in range(8) if b // 4 != root]

    def over_parts(self, sends):
        return [
            lax.ppermute(send, "height", [(i, i ^ k) for i in range(4)])
            for k, send in zip((1, 2, 3), sends)
        ]

    def pack(self, sources, arrays):
        eight = (8, UNIT, C)
        self.mine, other = call(
            functools.partial(pack_kernel, self.n_rows, 16 * self.root, sources),
            [out(eight), out(eight, bf16)],
            [pltpu.VMEM((16, UNIT, C), f32)],
            self.ids,
            *arrays,
            smem=1,
            name="pack" + self.tag,
        )
        self.got = across(other, 1)
        return [self.mine]


class LateReduction(Reduction):
    def y(self):
        eight = (8, UNIT, C)
        self.total, *lows = call(
            sum_low_kernel,
            [out(eight)] + [out((2, UNIT, C), bf16)] * 4,
            [],
            self.mine,
            self.got,
            name="sum_core" + self.tag,
        )
        self.pieces = [across(low, 4, self.others) for low in lows]
        return [self.total]

    def x(self, after):
        four = (4, UNIT, C)
        self.keep, send = call(
            unit_parts_kernel,
            [out(four), out(four, bf16)],
            [pltpu.VMEM((8, UNIT, C), bf16)],
            self.ids,
            self.total,
            *self.pieces,
            smem=1,
            name="unit_parts" + self.tag,
            after=after,
        )
        self.got = across(send, 2, self.rooted)
        return [self.keep]

    def height(self, after):
        low = out((UNIT, C), bf16)
        keep, *sends = call(
            shard_parts_kernel,
            [out((UNIT, C)), low, low, low],
            [],
            self.ids,
            self.keep,
            self.got,
            smem=1,
            name="shard_parts" + self.tag,
            after=after,
        )
        self.result = [keep] + self.over_parts(sends)
        return [keep]


class SoonReduction(Reduction):
    def height(self, after):
        two = (2, UNIT, C)
        low = out(two, bf16)
        self.keep, *sends = call(
            height_parts_kernel,
            [out(two), low, low, low],
            [],
            self.ids,
            self.mine,
            self.got,
            smem=1,
            name="height_parts" + self.tag,
            after=after,
        )
        self.parts = self.over_parts(sends)
        return [self.keep]

    def y(self, after):
        two = (2, UNIT, C)
        self.total, low = call(
            height_sum_kernel,
            [out(two), out(two, bf16)],
            [],
            self.keep,
            *self.parts,
            name="height_sum" + self.tag,
            after=after,
        )
        self.got = across(low, 4, self.others)
        return [self.total]

    def x(self, after):
        keep, send = call(
            plane_parts_kernel,
            [out((UNIT, C)), out((UNIT, C), bf16)],
            [],
            self.ids,
            self.total,
            self.got,
            smem=1,
            name="plane_parts" + self.tag,
            after=after,
        )
        self.result = [keep, across(send, 2, self.rooted)]
        return [keep]


def pick_kernel(place_ref, r0, r1, r2, r3, o_ref, slots):
    for k, ref in enumerate((r0, r1, r2, r3)):
        slots[k] = ref[...]
    for shard in range(2):
        o_ref[shard] = slots[place_ref[1] ^ shard]


def first_moments_everywhere(first, second, n_rows, place_ids, after):
    pair = call(
        functools.partial(round_rows_kernel, n_rows),
        [out((n_rows, C), bf16)] * 2,
        [],
        first,
        second,
        name="round_moments",
        after=after,
    )
    pair = jnp.stack(pair)
    shape = pair.shape
    got = [
        lax.ppermute(pair, both_axes, [(h, h ^ k) for h in range(2)]) for k in (1, 2, 3)
    ]
    (both,) = call(
        pick_kernel,
        [out((2,) + shape, bf16)],
        [pltpu.VMEM((4,) + shape, bf16)],
        place_ids,
        pair,
        *got,
        smem=1,
        name="pick_moments",
    )
    return both


def spread_moments(both, place_ids, mask):
    got = across(both, mask, list(range(mask)))
    batch = lax.axis_index("batch")
    (both,) = call(
        functools.partial(spread_kernel, mask),
        [out(both.shape, bf16)],
        [],
        place_ids,
        both,
        got,
        smem=1,
        name="spread_moments_%d" % mask,
    )
    return both


def spread_kernel(mask, place_ref, mine_ref, got_ref, o_ref):
    batch = place_ref[0]

    @pl.when(batch < mask)
    def _():
        o_ref[...] = mine_ref[...]

    @pl.when(batch >= mask)
    def _():
        o_ref[...] = got_ref[...]


def halves_kernel(core_ref, g_ref, mine_ref, other_ref):
    core = core_of(core_ref)
    n = mine_ref.shape[0]
    mine_ref[...] = g_ref[rows_at(core * n, n), :]
    other_ref[...] = g_ref[rows_at((1 - core) * n, n), :].astype(bf16)


def ordered_sum_kernel(place_ref, r0, r1, r2, r3, low_ref, slots):
    place = place_ref[1]
    for k, ref in enumerate((r0, r1, r2, r3)):
        slots[place ^ k] = ref[...]
    total = slots[0].astype(f32)
    for k in range(1, 4):
        total = total + slots[k].astype(f32)
    low_ref[...] = total.astype(bf16)


def add_kernel(a_ref, b_ref, c_ref, d_ref, low_ref, small_ref):
    low_ref[...] = (a_ref[...].astype(f32) + b_ref[...].astype(f32)).astype(bf16)
    small_ref[...] = c_ref[...] + d_ref[...]


def sum_everywhere(grad, small, place_ids, work):
    half = (grad.shape[0] // 2, C)
    low = out(half, bf16)
    total, other = call(
        halves_kernel, [out(half), low], [], place_ids, grad, smem=1, name="halves"
    )
    beside = []
    for mask, name in ((1, "add_core"), (2, "add_x"), (4, "add_y")):
        got = across(other if mask == 1 else total, mask)
        got_small = across(small, mask)
        total, small = call(
            add_kernel,
            [low, out(small.shape)],
            [],
            total,
            got,
            small,
            got_small,
            name=name,
            after=beside,
        )
        beside = work.pop(0)([total])
    parts = over_height(total)
    small = over_height(small)
    (total,) = call(
        ordered_sum_kernel,
        [low],
        [pltpu.VMEM((4,) + half, bf16)],
        place_ids,
        *parts,
        smem=1,
        name="add_height",
        after=beside + small[1:],
    )
    return total, across(total, 1), small


def lamb_kernel(
    n_rows,
    place_ref,
    a0,
    a1,
    a2,
    a3,
    b0,
    b1,
    w_ref,
    m_ref,
    v_ref,
    first_ref,
    second_ref,
    update_ref,
    sums_ref,
):
    y, shard = y_of(place_ref), place_ref[0] * 4 + place_ref[1]
    late = a0[...] + a1[...].astype(f32) + a2[...].astype(f32) + a3[...].astype(f32)
    soon = b0[...] + b1[...].astype(f32)
    grad = jnp.where(y == 1, late, soon)[0:n_rows]
    w, m, v = (as_rows(ref, n_rows) for ref in (w_ref, m_ref, v_ref))
    first, second, update = lamb_terms(w, grad, m, v, weight_decay)
    first_ref[...] = first
    second_ref[...] = second
    update_ref[...] = update
    member = membership(n_rows, shard)
    sums_ref[...] = jnp.zeros_like(sums_ref)
    for k, value in enumerate((w, update)):
        by_row = jnp.sum(value * value, axis=1, keepdims=True)
        sums_ref[k : k + 1, 0:128] = jnp.sum(member * by_row, axis=0, keepdims=True)


def membership(n_rows, shard):
    row = lax.broadcasted_iota(jnp.int32, (n_rows, 128), 0) + shard * n_rows
    lane = lax.broadcasted_iota(jnp.int32, (n_rows, 128), 1)
    result = jnp.zeros((n_rows, 128), f32)
    for k in range(len(MATRIX_ROWS)):
        inside = (row >= ROW_BOUNDS[k]) & (row < ROW_BOUNDS[k + 1]) & (lane == k)
        result = jnp.where(inside, 1.0, result)
    return result


VEC_ROWS = 24


LINES = 72
LINE_F1 = 4 * C // 128
LINE_E2 = LINE_F1 + (E2 - F1) * C // 128
LINE_F2 = LINE_E2 + SE_B // 128


def as_lines(flat):
    return jnp.pad(flat, (0, LINES * 128 - flat.shape[0])).reshape(LINES, 128)


def from_lines(lines):
    return lines.reshape(-1)[: sum(vector_sizes())]


def line_pieces():
    return ((LINE_F1, F1, E2 - F1), (LINE_F2, F2, 18 - F2))


def tables_kernel(*refs):
    lines = refs[-1]
    n = len(refs) // 2
    lane = lax.broadcasted_iota(jnp.int32, (LINES, 128), 1)
    for src, dst in zip(refs[:n], refs[n : 2 * n]):
        dst[...] = jnp.zeros_like(dst)
        for j in range(C // 128):
            dst[0:4, j * 128 : (j + 1) * 128] = src[pl.ds(j, 4, stride=C // 128), :]
        head = src[LINE_F1 : LINE_F1 + 1, :]
        dst[E1 : E1 + 1, 0:128] = jnp.where(lane[0:1] < SE_A, head, 0.0)
        here = pltpu.roll(src[...], 128 - SE_A, 1)
        below = pltpu.roll(here, LINES - 1, 0)
        lines[...] = jnp.where(lane < 128 - SE_A, here, below)
        dst[E2 : E2 + 1, 0:128] = lines[LINE_E2 : LINE_E2 + 1, :]
        for line, row, count in line_pieces():
            for j in range(C // 128):
                dst[row : row + count, j * 128 : (j + 1) * 128] = lines[
                    pl.ds(line + j, count, stride=C // 128), :
                ]


def put_lines(table, dst, lines):
    lane = lax.broadcasted_iota(jnp.int32, (LINES, 128), 1)
    line_at = lax.broadcasted_iota(jnp.int32, (LINES, 128), 0)
    lines[...] = jnp.zeros_like(lines)
    lines[LINE_F1 : LINE_F1 + 1, :] = pltpu.roll(table[E1 : E1 + 1, 0:128], 128 - SE_A, 1)
    lines[LINE_E2 + 1 : LINE_E2 + 2, :] = table[E2 : E2 + 1, 0:128]
    for line, row, count in line_pieces():
        for j in range(C // 128):
            lines[pl.ds(line + 1 + j, count, stride=C // 128), :] = table[
                row : row + count, j * 128 : (j + 1) * 128
            ]
    before = pltpu.roll(lines[...], SE_A, 1)
    here = pltpu.roll(before, LINES - 1, 0)
    dst[...] = jnp.where(lane < SE_A, before, here)
    for j in range(C // 128):
        dst[pl.ds(j, 4, stride=C // 128), :] = table[0:4, j * 128 : (j + 1) * 128]


def as_rows(ref, n_rows):
    return jnp.concatenate(
        [ref[pl.ds(j, n_rows, stride=C // 128), :] for j in range(C // 128)], axis=1
    )


def put_as_lines(ref, value):
    for j in range(C // 128):
        ref[pl.ds(j, value.shape[0], stride=C // 128), :] = value[:, j * 128 : (j + 1) * 128]


def round_rows_kernel(n_rows, *refs):
    n = len(refs) // 2
    for src, dst in zip(refs[:n], refs[n:]):
        dst[...] = as_rows(src, n_rows).astype(bf16)


def vector_grads_kernel(a, b, cs, d, e, f, de1, df1, de2, df2, sums_ref, o_ref):
    o_ref[...] = jnp.zeros_like(o_ref)
    plan = [
        (G1A, a, 1),
        (B1A, a, 0),
        (G1B, b, 1),
        (B1B, b, 0),
        (F1, df1, 0),
        (G1C, cs, 1),
        (B1C, cs, 0),
        (G1S, cs, 2),
        (B1S, cs, 0),
        (G2A, d, 1),
        (B2A, d, 0),
        (G2B, e, 1),
        (B2B, e, 0),
        (F2, df2, 0),
        (G2C, f, 1),
        (B2C, f, 0),
    ]
    for row, ref, k in plan:
        o_ref[row : row + 1, :] = ref[k : k + 1, :]
    o_ref[E1 : E1 + 1, 0:HID] = de1[0:1, :]
    o_ref[E2 : E2 + 1, 0:HID] = de2[0:1, :]
    o_ref[VEC_ROWS : VEC_ROWS + 8, :] = sums_ref[...]


def finish_kernel(
    n_rows,
    place_ref,
    r0,
    r1,
    r2,
    r3,
    h_mine_ref,
    h_other_ref,
    moments_ref,
    w1_ref,
    w_ref,
    m_ref,
    v_ref,
    first_in_ref,
    second_in_ref,
    update_in_ref,
    vec_ref,
    vf_ref,
    vs_ref,
    new_w_ref,
    first_ref,
    second_ref,
    new_v_ref,
    new_vf_ref,
    new_vs_ref,
    norm_ref,
    slots,
    grad,
    old,
    kept,
    lines,
):
    core, place = core_of(place_ref), place_ref[1]
    shard = place_ref[0] * 4 + place
    for k, ref in enumerate((r0, r1, r2, r3)):
        slots[place ^ k] = ref[...]
    total = slots[0] + slots[1] + slots[2] + slots[3]
    n_first = MATRIX_ROWS[0]
    half = n_first // 2
    rest = n_first - n_rows
    grad[0:half, :] = jnp.where(core == 0, h_mine_ref[...], h_other_ref[...]).astype(f32)
    grad[half:n_first, :] = jnp.where(core == 0, h_other_ref[...], h_mine_ref[...]).astype(f32)
    for k in range(2):
        old[k, 0:n_rows, :] = moments_ref[0, k].astype(f32)
        old[k, n_rows:n_first, :] = moments_ref[1, k][0:rest].astype(f32)
    _, _, update = lamb_terms(
        w1_ref[...].astype(f32), grad[...], old[0], old[1], weight_decay
    )
    first_square = jnp.sum(update * update)
    lane = lax.broadcasted_iota(jnp.int32, (8, 128), 1)
    line = lax.broadcasted_iota(jnp.int32, (8, 128), 0)
    sums = total[VEC_ROWS : VEC_ROWS + 8, 0:128]
    norms = jnp.sqrt(jnp.where((lane == 0) & (line == 1), first_square, sums))
    norm_ref[...] = norms
    ratio = jnp.where(
        lane[0:1] < len(MATRIX_ROWS), learn_rate * (norms[0:1] / norms[1:2]), 0.0
    )
    by_row = jnp.sum(membership(n_rows, shard) * ratio, axis=1, keepdims=True)
    w, m, v = (as_rows(ref, n_rows) for ref in (w_ref, m_ref, v_ref))
    kept[0] = first_in_ref[...]
    kept[1] = second_in_ref[...]
    kept[2] = w - by_row * update_in_ref[...]
    first_ratio = ratio[0:1, 0:1]
    for owner, start, count in ((0, 0, n_rows), (1, n_rows, rest)):

        @pl.when(shard == owner)
        def _():
            first, second, update = lamb_terms(
                w[0:count], grad[start : start + count, :], m[0:count], v[0:count], weight_decay
            )
            kept[0, 0:count, :] = first
            kept[1, 0:count, :] = second
            kept[2, 0:count, :] = w[0:count] - first_ratio * update

    for k, ref in enumerate((first_ref, second_ref, new_w_ref)):
        put_as_lines(ref, kept[k])
    vec = vec_ref[...]
    first, second, update = lamb_terms(vec, total[0:VEC_ROWS], vf_ref[...], vs_ref[...], 0.0)
    put_lines(first, new_vf_ref, lines)
    put_lines(second, new_vs_ref, lines)
    size = jnp.sqrt(jnp.sum(vec * vec, axis=1, keepdims=True))
    change = jnp.sqrt(jnp.sum(update * update, axis=1, keepdims=True))
    put_lines(vec - learn_rate * (size / change) * update, new_v_ref, lines)


def lamb_terms(param, grad_val, first_old, second_old, decay):
    first_new = beta_one * first_old + (1.0 - beta_one) * grad_val
    second_new = beta_two * second_old + (1.0 - beta_two) * grad_val * grad_val
    update = (
        first_new
        / (1.0 - beta_one**STEP)
        / (jnp.sqrt(second_new / (1.0 - beta_two**STEP)) + adam_eps)
        + decay * param
    )
    return (first_new, second_new, update)


def body(
    image_glob,
    image_loc,
    cot_glob,
    cot_loc,
    weights,
    first_moment,
    second_moment,
    vectors,
    vec_first,
    vec_second,
):
    n_height = lax.axis_size("height")
    place = lax.axis_index("height")
    sz = Sizes(image_glob, image_loc, n_height)
    m = sz.m
    part = functools.partial
    place_ids = jnp.stack([lax.axis_index("batch"), place]).astype(jnp.int32)
    shapes = matrix_shapes()
    mat_lengths = [dims_pair[0] * dims_pair[1] for dims_pair in shapes]
    x, x_edge = call(
        part(prepare_kernel, sz),
        [out((4 * m, CIN), bf16), out((2 * sz.edge, CIN), bf16)],
        [pltpu.VMEM((sz.hg * sz.wg, 128), f32)] * 2,
        image_glob,
        image_loc,
        name="prepare",
        room=6 * 2**20,
    )
    x_above = step_down(x_edge)
    gram_scr = pltpu.VMEM((CIN + 8, CIN), f32)
    (gram,) = call(part(gram_kernel, sz), [out(PACKED)], [gram_scr], x, name="gram", after=[x_above])
    gram = over_height(gram)
    by_rows = (
        weights.shape[0] % C == 0
        and weights.shape[0] // C <= UNIT
        and lax.axis_size("batch") == 8
        and n_height == 4
    )
    shard_rows = weights.shape[0] // C
    table = out((VEC_ROWS, C))
    tables = call(
        tables_kernel,
        [table] * 3,
        [pltpu.VMEM((LINES, 128), f32)],
        *(as_lines(v) for v in (vectors, vec_first, vec_second)),
        name="tables",
    )
    vt = tables[0]
    early = list(tables)
    if by_rows:
        w_lines, m_lines, v_lines = (
            v.reshape(-1, 128) for v in (weights, first_moment, second_moment)
        )
        early = early + [x_above] + gram[1:]

    if by_rows:

        def beside(quarter):
            moments = first_moments_everywhere(
                m_lines, v_lines, shard_rows, place_ids, gram[1:]
            )
            return early + [moments], moments

        matrices, moments = gather_weights(w_lines, shard_rows, place_ids, beside)
    else:
        gathered = lax.all_gather(weights.astype(bf16), both_axes, axis=0, tiled=True)
        matrices = [
            flat_piece.reshape(dims_pair)
            for flat_piece, dims_pair in zip(cut_pieces(gathered, mat_lengths), shapes)
        ]
    w1, k1, d1, u1, p1, s1, w2, k2, d2, u2, p2 = matrices
    if not by_rows:
        d1 = jnp.pad(d1, ((0, 0), (0, HID - SE_A)))
        u1 = jnp.pad(u1, ((0, HID - SE_A), (0, 0)))
    st8 = out((8, C))
    mat = out((m, C))
    mat_low = out((m, C), bf16)
    pool_low = out((sz.crops, C), bf16)
    pool_scr = pltpu.VMEM((sz.crops, C), f32)
    sum_scr = pltpu.VMEM((24, C), f32)

    bd_scr = pltpu.VMEM((18, HALF, HALF), bf16)
    low_scr = pltpu.VMEM((m, C), bf16)
    mat_scr = pltpu.VMEM((m, C), f32)
    one_scr = pltpu.VMEM((sz.one, C), bf16)
    two_scr = pltpu.VMEM((sz.two, C), bf16)
    edge_scr = pltpu.VMEM((sz.edge, C), f32)
    edge = out((sz.edge, C), bf16)
    one_shape = out((sz.one, C), bf16)
    zb, st_b, nrm_a, *act_a = call(
        part(first_conv_kernel, sz),
        [mat, st8, st8, mat_low, mat_low, one_shape, one_shape],
        [low_scr, one_scr, bd_scr, mat_scr, sum_scr, gram_scr],
        place_ids,
        x,
        x_above,
        w1,
        s1,
        k1,
        *gram,
        vt,
        smem=1,
        name="first_conv",
    )
    st_b = over_height(st_b)
    if by_rows:
        moments = spread_moments(moments, place_ids, 1)
    pool_b, nrm_b = call(
        part(pool_kernel, sz, G1B, B1B, True), [pool_low, st8], [pool_scr], zb, *st_b, vt, name="pool_b",
        after=[moments] if by_rows else [],
    )
    pool_b = over_height(pool_b)
    hid = out((sz.crops, HID))
    crop_mat = out((sz.crops, C))
    qb, zc, st_c, gate_b, pooled_b, hidden_b = call(
        part(gated_product_kernel, sz, E1, F1),
        [mat_low, mat, st8, crop_mat, crop_mat, hid],
        [],
        zb,
        nrm_b,
        *pool_b,
        d1,
        u1,
        p1,
        vt,
        name="gated_b",
    )
    st_c = over_height(st_c)
    if by_rows:
        moments = spread_moments(moments, place_ids, 2)
    pre_mid, mid_low, nrm_c, mid_top, mid_bottom = call(
        part(middle_kernel, sz),
        [mat, mat_low, st8, edge, edge],
        [mat_scr],
        zc,
        x,
        s1,
        *st_c,
        nrm_b,
        vt,
        name="middle",
        after=[moments] if by_rows else [],
    )
    mid_above = step_down(mid_bottom)
    mid_below = step_up(mid_top)
    zd, st_d = call(
        part(product_kernel, sz), [mat, st8], [], mid_low, w2, name="product_d"
    )
    st_d = over_height(st_d)
    two_shape = out((sz.two, C), bf16)
    ze, st_e, nrm_d, act_d = call(
        part(second_conv_kernel, sz),
        [mat, st8, st8, two_shape],
        [two_scr, two_scr, bd_scr, edge_scr, sum_scr],
        place_ids,
        zd,
        mid_above,
        mid_below,
        w2,
        k2,
        *st_d,
        vt,
        smem=1,
        name="second_conv",
    )
    st_e = over_height(st_e)
    if by_rows:
        moments = spread_moments(moments, place_ids, 4)
    pool_e, nrm_e = call(
        part(pool_kernel, sz, G2B, B2B, False), [pool_low, st8], [pool_scr], ze, *st_e, vt, name="pool_e",
        after=[moments] if by_rows else [],
    )
    pool_e = over_height(pool_e)
    qe, zf, st_f, gate_e, pooled_e, hidden_e = call(
        part(gated_product_kernel, sz, E2, F2),
        [mat_low, mat, st8, crop_mat, crop_mat, hid],
        [],
        ze,
        nrm_e,
        *pool_e,
        d2,
        u2,
        p2,
        vt,
        name="gated_e",
    )
    st_f = over_height(st_f)
    out_glob, out_loc, dpre, bst_f, nrm_f = call(
        part(output_kernel, sz),
        [out(cot_glob.shape, bf16), out(cot_loc.shape, bf16), mat, st8, st8],
        [sum_scr],
        pre_mid,
        zf,
        *st_f,
        vt,
        cot_glob,
        cot_loc,
        name="output",
        room=6 * 2**20,
    )
    bst_f_all = over_height(bst_f)

    dzf, dqe, dg_e = call(
        part(gate_grad_kernel, sz, False),
        [mat_low, mat, pool_low],
        [pool_scr],
        dpre,
        zf,
        *bst_f_all,
        nrm_f,
        p2,
        ze,
        nrm_e,
        name="gate_grad_e",
    )
    dg_e = over_height(dg_e)
    (mat_f,) = call(
        weight_kernel, [out((C, C))], [], qe, dzf, name="weight_f"
    )
    dn_e, bst_e, dv_e, du_e = call(
        part(excite_back_kernel, sz),
        [mat, st8, crop_mat, hid],
        [pool_scr, sum_scr],
        dqe,
        ze,
        nrm_e,
        *dg_e,
        gate_e,
        hidden_e,
        d2,
        u2,
        name="excite_back_e",
        after=[mat_f],
    )
    bst_e_all = over_height(bst_e)
    se_outs = lambda width: [out((width, C)), out((8, HID)), out((HID, C)), st8]
    se_scr = [pltpu.VMEM((C, HID), f32), pltpu.VMEM((HID, 128), f32)]
    dd2, de2, du2, df2 = call(
        part(excite_weights_kernel, SE_B),
        se_outs(SE_B),
        se_scr,
        place_ids,
        dv_e,
        du_e,
        pooled_e,
        hidden_e,
        smem=1,
        name="excite_weights_e",
    )
    dze, dze_top, dze_bottom = call(
        part(norm_back_kernel, sz),
        [mat_low, edge, edge],
        [],
        dn_e,
        ze,
        *bst_e_all,
        nrm_e,
        name="norm_back_e",
        after=[dd2],
    )
    dze_above = step_down(dze_bottom)
    dze_below = step_up(dze_top)
    (mat_e,) = call(
        part(second_conv_weights_kernel, sz),
        [out((9 * GW, C))],
        [two_scr, two_scr],
        act_d,
        dze,
        name="second_conv_weights",
    )
    dn_d, bst_d = call(
        part(second_conv_back_kernel, sz),
        [mat, st8],
        [two_scr, two_scr, two_scr, bd_scr, sum_scr],
        dze,
        dze_above,
        dze_below,
        k2,
        zd,
        nrm_d,
        name="second_conv_back",
        after=[mat_e],
    )
    bst_d_all = over_height(bst_d)
    dzd, dn_mid, bst_cs = call(
        part(middle_back_kernel, sz),
        [mat_low, mat, st8],
        [mat_scr, sum_scr],
        dn_d,
        zd,
        *bst_d_all,
        nrm_d,
        w2,
        dpre,
        pre_mid,
        zc,
        x,
        s1,
        nrm_c,
        nrm_b,
        name="middle_back",
    )
    bst_cs_all = over_height(bst_cs)
    spans = list(zip(ROW_BOUNDS[:-1], ROW_BOUNDS[1:]))
    late = LateReduction(1, shard_rows, place_ids) if by_rows else None
    soon = SoonReduction(0, shard_rows, place_ids) if by_rows else None
    (mat_d,) = call(
        weight_kernel,
        [out((C, C))],
        [],
        mid_low,
        dzd,
        name="weight_d",
        after=bst_cs_all[1:],
    )
    hold = []
    if by_rows:
        hold = late.pack(spans[6:], [mat_d, mat_e, dd2, du2, mat_f])
    dzc, dzs, dqb, dg_b = call(
        part(gate_grad_kernel, sz, True),
        [mat_low, mat_low, mat, pool_low],
        [pool_scr, mat_scr],
        dn_mid,
        zc,
        *bst_cs_all,
        nrm_c,
        p1,
        zb,
        nrm_b,
        x,
        s1,
        nrm_b,
        name="gate_grad_b",
        after=hold,
    )
    dg_b = over_height(dg_b)
    (mat_c,) = call(
        weight_kernel, [out((C, C))], [], qb, dzc, name="weight_c"
    )
    (mat_s,) = call(
        weight_kernel, [out((CIN, C))], [], x, dzs, name="weight_s"
    )
    hold = late.y() if by_rows else [mat_d]
    dn_b, bst_b, dv_b, du_b = call(
        part(excite_back_kernel, sz),
        [mat, st8, crop_mat, hid],
        [pool_scr, sum_scr],
        dqb,
        zb,
        nrm_b,
        *dg_b,
        gate_b,
        hidden_b,
        d1,
        u1,
        name="excite_back_b",
        after=[mat_c, mat_s] + hold,
    )
    bst_b_all = over_height(bst_b)
    dd1, de1, du1, df1 = call(
        part(excite_weights_kernel, SE_A),
        se_outs(SE_A),
        se_scr,
        place_ids,
        dv_b,
        du_b,
        pooled_b,
        hidden_b,
        smem=1,
        name="excite_weights_b",
    )
    dzb, dzb_top = call(
        part(norm_back_kernel, sz),
        [mat_low, edge],
        [],
        dn_b,
        zb,
        *bst_b_all,
        nrm_b,
        name="norm_back_b",
        after=[dd1] + (late.pieces[:1] if by_rows else []),
    )
    dzb_below = step_up(dzb_top)
    (mat_b,) = call(
        part(first_conv_weights_kernel, sz),
        [out((9 * GW, C))],
        [low_scr, one_scr],
        *act_a,
        dzb,
        name="first_conv_weights",
    )
    hold = [mat_b]
    if by_rows:
        hold = soon.pack(spans[1:7], [mat_b, dd1, du1, mat_c, mat_s, mat_d])
        hold = hold + soon.height([dzb_below])
    v0, v1, bd1 = call(
        part(first_conv_back_kernel, sz),
        [one_shape, one_shape, out((18, HALF, HALF), bf16)],
        [],
        dzb,
        dzb_below,
        k1,
        name="first_conv_back",
        after=hold,
    )
    dn_a, bst_a = [], []
    for phase in range(4):
        dn_phase, *bst_a = call(
            part(parity_back_kernel, sz, phase),
            [mat_low, st8],
            [mat_scr, mat_scr, sum_scr],
            v0,
            v1,
            bd1,
            x,
            w1,
            nrm_a,
            *bst_a,
            name="parity_back_%d" % phase,
            after=late.x(bst_a) if by_rows and phase == 3 else [],
        )
        dn_a.append(dn_phase)
    (bst_a,) = bst_a
    bst_a_all = over_height(bst_a)
    hold = soon.y([bst_a]) + late.height([bst_a]) if by_rows else []
    (dza,) = call(
        part(image_norm_back_kernel, sz),
        [out((4 * m, C), bf16)],
        [mat_scr],
        *dn_a,
        x,
        w1,
        *bst_a_all,
        nrm_a,
        name="image_norm_back",
        after=hold,
    )
    (mat_a,) = call(
        weight_kernel,
        [out((CIN, C))],
        [],
        x,
        dza,
        name="weight_a",

    )
    made = {}

    def image_product(beside):
        (made["dx"],) = call(
            part(image_product_kernel, sz),
            [out((4 * m, CIN))],
            [],
            dza,
            w1,
            dzs,
            s1,
            name="image_product",
            after=beside,
        )
        return [made["dx"]]

    def place_maps(key, shape, first_row, block, beside):
        n_crops, height, width = shape[:3]
        made[key], mark = call(
            part(place_kernel, n_crops, height, width, first_row, block, m),
            [out(shape), out((8, 128))],
            [pltpu.VMEM((height * width, 128), f32)] * 2,
            made["dx"],
            name="place_" + key,
            room=8 * 2**20,
            after=beside,
        )
        return [mark]

    work = [
        image_product,
        lambda beside: place_maps("glob", image_glob.shape, 0, sz.bg, beside),
        lambda beside: place_maps("loc", image_loc.shape, sz.mg, sz.bl, beside),
    ]
    if not by_rows:
        for one_work in work:
            one_work([])
    if by_rows:
        soon.x([mat_a])
        shard_out = out((shard_rows, C))
        new_first, new_second, update, sums = call(
            part(lamb_kernel, shard_rows),
            [shard_out, shard_out, shard_out, st8],
            [],
            place_ids,
            *late.result,
            *soon.result,
            w_lines,
            m_lines,
            v_lines,
            smem=1,
            name="lamb",
        )
        (small,) = call(
            vector_grads_kernel,
            [out((VEC_ROWS + 8, C))],
            [],
            bst_a,
            bst_b,
            bst_cs,
            bst_d,
            bst_e,
            bst_f,
            de1,
            df1,
            de2,
            df2,
            sums,
            name="vector_grads",
        )
        half_mine, half_other, small = sum_everywhere(mat_a, small, place_ids, work)
        new_weights, new_first, new_second, new_v, new_vf, new_vs, norms = call(
            part(finish_kernel, shard_rows),
            [out(w_lines.shape)] * 3 + [out((LINES, 128))] * 3 + [out((8, 128))],
            [
                pltpu.VMEM((4, VEC_ROWS + 8, C), f32),
                pltpu.VMEM((MATRIX_ROWS[0], C), f32),
                pltpu.VMEM((2, MATRIX_ROWS[0], C), f32),
                pltpu.VMEM((3, shard_rows, C), f32),
                pltpu.VMEM((LINES, 128), f32),
            ],
            place_ids,
            *small,
            half_mine,
            half_other,
            moments,
            w1,
            w_lines,
            m_lines,
            v_lines,
            new_first,
            new_second,
            update,
            *tables,
            smem=1,
            name="finish",
            room=2 * 2**20,
        )
        maps_out = (out_glob, out_loc, made["glob"], made["loc"])
        return maps_out + (
            new_weights.reshape(-1),
            new_first.reshape(-1),
            new_second.reshape(-1),
            from_lines(new_v),
            from_lines(new_vf),
            from_lines(new_vs),
            norms[:2, : len(MATRIX_ROWS)],
        )

    maps_out = (out_glob, out_loc, made["glob"], made["loc"])
    flat_grad = jnp.concatenate(
        [
            piece.reshape(-1)
            for piece in (
                mat_a,
                mat_b,
                dd1,
                du1[:SE_A],
                mat_c,
                mat_s,
                mat_d,
                mat_e,
                dd2,
                du2,
                mat_f,
            )
        ]
    )
    vec_grad = jnp.concatenate(
        [
            bst_a[1],
            bst_a[0],
            bst_b[1],
            bst_b[0],
            de1[0, :SE_A],
            df1[0],
            bst_cs[1],
            bst_cs[0],
            bst_cs[2],
            bst_cs[0],
            bst_d[1],
            bst_d[0],
            bst_e[1],
            bst_e[0],
            de2[0],
            df2[0],
            bst_f[1],
            bst_f[0],
        ]
    )
    grad_shard = lax.psum_scatter(flat_grad, both_axes, scatter_dimension=0, tiled=True)
    shard_len = weights.shape[0]
    device_index = lax.axis_index("batch") * n_height + lax.axis_index("height")
    position = device_index * shard_len + lax.iota(jnp.int32, shard_len)
    bounds = np.cumsum([0] + mat_lengths)
    lower_edge = jnp.asarray(bounds[:-1], jnp.int32)
    upper_edge = jnp.asarray(bounds[1:], jnp.int32)
    member = (
        (position[:, None] >= lower_edge[None, :]) & (position[:, None] < upper_edge[None, :])
    ).astype(f32)
    new_first, new_second, update = lamb_terms(
        weights, grad_shard, first_moment, second_moment, weight_decay
    )
    part_sums = jnp.dot(jnp.stack([weights * weights, update * update]), member, precision=highest)
    vec_total, totals = lax.psum((vec_grad, part_sums), both_axes)
    norm_pair = jnp.sqrt(totals)
    trust_ratio = learn_rate * (norm_pair[0] / norm_pair[1])
    new_weights = weights - jnp.dot(member, trust_ratio, precision=highest) * update
    vec_one_new, vec_two_new, vec_update = lamb_terms(vectors, vec_total, vec_first, vec_second, 0.0)
    vec_pieces = []
    for param_piece, update_piece in zip(
        cut_pieces(vectors, vector_sizes()), cut_pieces(vec_update, vector_sizes())
    ):
        ratio_val = jnp.sqrt(jnp.sum(param_piece * param_piece)) / jnp.sqrt(
            jnp.sum(update_piece * update_piece)
        )
        vec_pieces.append(param_piece - learn_rate * ratio_val * update_piece)
    new_vectors = jnp.concatenate(vec_pieces)
    return maps_out + (
        new_weights,
        new_first,
        new_second,
        new_vectors,
        vec_one_new,
        vec_two_new,
        norm_pair,
    )


def solution(mesh):
    maps = P("batch", "height", None, None)
    entries = P(("batch", "height"))
    return jax.shard_map(
        body,
        mesh=mesh,
        in_specs=(maps, maps, maps, maps, entries, entries, entries, P(), P(), P()),
        out_specs=(maps, maps, maps, maps, entries, entries, entries, P(), P(), P(), P()),
        check_vma=False,
    )
```

```python
import functools

import jax
import jax.numpy as jnp
import numpy as np
from jax import lax
from jax.experimental import pallas as pl
from jax.experimental.pallas import tpu as pltpu
from jax.sharding import PartitionSpec as P

CIN = 192
C = 512
GW = 64
GROUPS = 8
SE_A = 48
SE_B = 128
STEP = 10
HID = 128
HALF = 256

norm_eps = 1e-05
beta_one = 0.9
beta_two = 0.999
adam_eps = 1e-06
weight_decay = 0.01
learn_rate = 0.4
highest = lax.Precision.HIGHEST
bf16 = jnp.bfloat16
f32 = jnp.float32
both_axes = ("batch", "height")

G1A, B1A, G1B, B1B, E1, F1, G1C, B1C, G1S, B1S, G2A, B2A, G2B, B2B, E2, F2, G2C, B2C = range(18)


def matrix_shapes():
    return [
        (CIN, C),
        (9 * GW, C),
        (C, SE_A),
        (SE_A, C),
        (C, C),
        (CIN, C),
        (C, C),
        (9 * GW, C),
        (C, SE_B),
        (SE_B, C),
        (C, C),
    ]


def vector_sizes():
    return [C, C, C, C, SE_A, C, C, C, C, C, C, C, C, C, SE_B, C, C, C]


def cut_pieces(flat_vec, lengths):
    pieces = []
    offset = 0
    for length in lengths:
        pieces.append(flat_vec[offset : offset + length])
        offset += length
    return pieces


class Sizes:
    def __init__(self, image_glob, image_loc, n_height):
        self.ng, self.hg, self.wg = image_glob.shape[:3]
        self.nl, self.hl, self.wl = image_loc.shape[:3]
        self.rg, self.cg = self.hg // 2, self.wg // 2
        self.rl, self.cl = self.hl // 2, self.wl // 2
        self.bg, self.bl = self.ng * self.cg, self.nl * self.cl
        self.mg, self.ml = self.rg * self.bg, self.rl * self.bl
        self.m = self.mg + self.ml
        self.edge = self.bg + self.bl
        self.n_height = n_height
        self.crops = -(-(self.ng + self.nl) // 16) * 16
        self.area_g = self.rg * self.cg * n_height
        self.area_l = self.rl * self.cl * n_height
        self.amount = n_height * self.m
        self.one_l = (self.rg + 1) * self.bg
        self.one = self.one_l + (self.rl + 1) * self.bl
        self.two_l = (self.rg + 2) * self.bg
        self.two = self.two_l + (self.rl + 2) * self.bl


def sigmoid(v):
    return 0.5 * jnp.tanh(0.5 * v) + 0.5


def silu(v):
    return v * sigmoid(v)


def silu_slope(v):
    s = sigmoid(v)
    return s * (1.0 + v * (1.0 - s))


def padded_bytes(shape, dtype):
    size = np.dtype(dtype).itemsize
    dims = list(shape)
    dims[-1] = -(-dims[-1] // 128) * 128
    if len(dims) > 1:
        rows = 32 // size
        dims[-2] = -(-dims[-2] // rows) * rows
    return int(np.prod(dims)) * size


COST_SCALE = 1.0
MEASURED_US = {
    "first_conv_back": 1.5,
    "parity_back_0": 2.6,
    "parity_back_1": 3.0,
    "parity_back_2": 3.0,
    "parity_back_3": 3.7,
    "first_conv": 5.0,
    "first_act": 7.5,
    "second_conv": 6.3,
    "second_conv_back": 5.9,
    "image_norm_back": 5.8,
    "second_conv_weights": 4.9,
    "first_conv_weights": 4.5,
    "middle_back": 4.4,
    "gate_grad_b": 4.2,
    "gram": 3.6,
    "image_product": 3.6,
    "place_glob": 3.1,
    "output": 2.9,
    "assemble": 2.9,
    "gate_grad_e": 2.7,
    "excite_back_b": 2.6,
    "excite_back_e": 2.6,
    "place_loc": 2.5,
    "gated_b": 2.4,
    "gated_e": 2.4,
    "finish": 1.9,
    "middle": 1.8,
    "prepare": 1.4,
    "excite_weights_b": 1.3,
    "excite_weights_e": 1.2,
    "product_d": 1.1,
    "weight_a": 1.1,
    "pack_0": 1.0,
    "pack_1": 1.0,
    "pool_b": 1.0,
    "pool_e": 1.0,
    "lamb": 1.0,
    "weight_f": 0.9,
    "weight_d": 0.9,
    "weight_c": 0.9,
}


def call(kernel, outs, scratch, *ins, smem=0, name=None, after=(), room=0):
    held = sum(padded_bytes(s.shape, s.dtype) for s in scratch)
    n_in, n_after = len(ins), len(after)

    def run(*refs):
        kernel(*refs[:n_in], *refs[n_in + n_after :])

    return pl.pallas_call(
        run,
        out_shape=tuple(outs),
        in_specs=[pl.BlockSpec(memory_space=pltpu.SMEM)] * smem
        + [pl.BlockSpec(memory_space=pltpu.VMEM)] * (n_in - smem)
        + [pl.BlockSpec(memory_space=pl.ANY)] * n_after,
        out_specs=tuple(pl.BlockSpec(memory_space=pltpu.VMEM) for _ in outs),
        scratch_shapes=list(scratch),
        compiler_params=pltpu.CompilerParams(vmem_limit_bytes=held + 4 * 2**20 + room),
        cost_estimate=pl.CostEstimate(
            flops=int(MEASURED_US.get(name, 0.5) * COST_SCALE * 1.1535e9),
            bytes_accessed=1,
            transcendentals=0,
        ),
        name=name,
    )(*ins, *after)


def out(shape, dtype=f32):
    return jax.ShapeDtypeStruct(shape, dtype)


def above(ids, n_height=0):
    return jnp.where(ids[1] > 0, 1.0, 0.0)


def below(ids, n_height):
    return jnp.where(ids[1] < n_height - 1, 1.0, 0.0)


def first_of_height(ids):
    return jnp.where(ids[1] == 0, 1.0, 0.0)


def y_of(ids):
    return ids[0] // 4


def x_of(ids):
    return lax.rem(ids[0] // 2, 2)


def core_of(ids):
    return lax.rem(ids[0], 2)


def fold(x):
    return jnp.sum(x.reshape(x.shape[0] // 8, 8, x.shape[1]), axis=0)


def rows_at(start, size, unit=16):
    return pl.ds(pl.multiple_of(start, unit), size)


def put_rows(ref, parts):
    ref[...] = jnp.zeros_like(ref)
    for k, part in enumerate(parts):
        ref[k : k + 1, :] = jnp.sum(part, axis=0, keepdims=True)


def gather_sum(refs):
    total = refs[0][...]
    for ref in refs[1:]:
        total = total + ref[...]
    return total


def norm_terms(total, row, amount, gain, shift):
    mean = total[row : row + 1] / amount
    inverse = lax.rsqrt(total[row + 1 : row + 2] / amount - mean * mean + norm_eps)
    scale = gain * inverse
    return mean, inverse, scale, shift - mean * scale


def put_norm(ref, row, terms):
    for k, term in enumerate(terms):
        ref[row + k : row + k + 1, :] = term


def dot(a, b):
    return jnp.dot(a, b, preferred_element_type=f32)


def dot_t(a, b):
    return lax.dot_general(a, b, (((1,), (1,)), ((), ())), preferred_element_type=f32)


def t_dot(a, b):
    return lax.dot_general(a, b, (((0,), (0,)), ((), ())), preferred_element_type=f32)


def prepare_kernel(sz, ig_ref, il_ref, x_ref, halo_ref, s_ref, t_ref):
    m = sz.m

    def split(x, n_rows):
        s_ref[0:n_rows, :] = x[:, :128]
        t_ref[0:n_rows, 0:64] = x[:, 128:]
        parts = []
        for pc in range(2):
            v = s_ref[pl.ds(pc, n_rows // 2, stride=2), :]
            w = t_ref[pl.ds(pc, n_rows // 2, stride=2), :]
            parts.append(jnp.concatenate([v, w[:, :64]], axis=1))
        return parts

    @pl.loop(0, sz.ng)
    def _(n):
        n_rows = sz.hg * sz.wg
        parts = split(ig_ref[n].astype(f32).reshape(n_rows, CIN), n_rows)
        for pc in range(2):
            v = parts[pc].reshape(sz.hg, sz.cg, CIN).astype(bf16)
            for r in range(sz.hg):
                phase = 2 * (r % 2) + pc
                x_ref[rows_at(phase * m + (r // 2) * sz.bg + n * sz.cg, sz.cg), :] = v[r]

    @pl.loop(0, sz.nl // 2)
    def _(pair):
        n_rows = 2 * sz.hl * sz.wl
        both = jnp.concatenate(
            [
                il_ref[2 * pair + k].astype(f32).reshape(sz.hl * sz.wl, CIN)
                for k in range(2)
            ],
            axis=0,
        )
        parts = split(both, n_rows)
        for pc in range(2):
            v = parts[pc].reshape(2 * sz.hl, sz.cl, CIN)
            for r in range(sz.hl):
                phase = 2 * (r % 2) + pc
                joined = jnp.concatenate([v[r], v[sz.hl + r]], axis=0).astype(bf16)
                x_ref[
                    rows_at(phase * m + sz.mg + (r // 2) * sz.bl + pair * 2 * sz.cl, 2 * sz.cl), :
                ] = joined

    for pc in range(2):
        base = (2 + pc) * m
        halo_ref[pc * sz.edge : pc * sz.edge + sz.bg, :] = x_ref[
            base + sz.mg - sz.bg : base + sz.mg, :
        ]
        halo_ref[pc * sz.edge + sz.bg : (pc + 1) * sz.edge, :] = x_ref[
            base + m - sz.bl : base + m, :
        ]


LOW = 128
PACKED = (LOW + 8, 2 * LOW)


def gram_kernel(sz, x_ref, g_ref, full):
    n_rows = sz.m // 3
    ones = jnp.ones((8, n_rows), bf16)
    full[...] = jnp.zeros_like(full)

    @pl.loop(0, 12)
    def _(i):
        x = x_ref[rows_at(i * n_rows, n_rows), :]
        full[0:CIN, :] += t_dot(x, x)
        full[CIN : CIN + 8, :] += dot(ones, x)

    g_ref[...] = jnp.zeros_like(g_ref)
    g_ref[0:LOW, 0:CIN] = full[0:LOW, :]
    g_ref[0 : CIN - LOW, CIN:] = full[LOW:CIN, LOW:CIN]
    g_ref[LOW : LOW + 8, 0:CIN] = full[CIN : CIN + 8, :]


def unpack_gram(packed, full):
    full[0:LOW, :] = packed[0:LOW, 0:CIN]
    full[LOW:CIN, 0:LOW] = jnp.transpose(packed[0:LOW, LOW : 2 * LOW])[0 : CIN - LOW]
    full[LOW:CIN, LOW:CIN] = packed[0 : CIN - LOW, CIN:]
    full[CIN : CIN + 8, :] = packed[LOW : LOW + 8, 0:CIN]


def product_norm_terms(total, w_ref, amount, gain, shift):
    w = w_ref[...].astype(f32)
    mean = dot_high(total[CIN : CIN + 8], w)[0:1] / amount
    square = jnp.sum(w * dot_high(total[0:CIN], w), axis=0, keepdims=True) / amount
    inverse = lax.rsqrt(square - mean * mean + norm_eps)
    scale = gain * inverse
    return mean, inverse, scale, shift - mean * scale


def block_diagonal(k_ref, bd_ref):
    rows = lax.broadcasted_iota(jnp.int32, (HALF, HALF), 0) // GW
    cols = lax.broadcasted_iota(jnp.int32, (HALF, HALF), 1) // GW
    same = rows == cols
    for tap in range(9):
        for half in range(2):
            k = k_ref[tap * GW : (tap + 1) * GW, half * HALF : (half + 1) * HALF].astype(f32)
            bd_ref[2 * tap + half] = jnp.where(same, jnp.concatenate([k] * 4, axis=0), 0.0).astype(
                bf16
            )


def strided_product(sz, x_ref, s_ref, zs):
    n_rows = sz.m // 3

    @pl.loop(0, 3)
    def _(i):
        zs[rows_at(i * n_rows, n_rows), :] = dot(x_ref[rows_at(i * n_rows, n_rows), :], s_ref[...])


def block_dense(acc):
    rows = lax.broadcasted_iota(jnp.int32, (HALF, HALF), 0) // GW
    cols = lax.broadcasted_iota(jnp.int32, (HALF, HALF), 1) // GW
    kept = jnp.where(rows == cols, acc, 0.0)
    return jnp.sum(kept.reshape(4, GW, HALF), axis=0)


def shifted(v, by, width):
    n_rows = v.shape[0]
    col = lax.broadcasted_iota(jnp.int32, v.shape, 0) % width
    if by < 0:
        return jnp.where(col == 0, 0.0, pltpu.roll(v, 1, 0))
    return jnp.where(col == width - 1, 0.0, pltpu.roll(v, n_rows - 1, 0))


def segments(sz):
    g_rows = 4 * sz.cg
    l_rows = 6 * sz.cl
    return g_rows, l_rows


def conv_product(windows, bd_ref, half, n_rows, transposed):
    acc = None
    cols = pl.ds(pl.multiple_of(half * HALF, HALF), HALF)
    for tap, ref, start in windows:
        x = ref[start : start + n_rows, cols]
        w = bd_ref[2 * tap + half]
        term = dot_t(x, w) if transposed else dot(x, w)
        acc = term if acc is None else acc + term
    return acc


def windows_one(sz, refs, part):
    a00, a01, a01s, a10, a11, a11s = refs
    plain = 0 if part == "g" else sz.mg
    above = 0 if part == "g" else sz.one_l
    here = above + (sz.bg if part == "g" else sz.bl)
    result = []
    for tap in range(9):
        a, b = tap // 3, tap % 3
        if a == 1:
            result.append((tap, (a01s, a00, a01)[b], plain))
        else:
            result.append((tap, (a11s, a10, a11)[b], above if a == 0 else here))
    return result


def windows_two(sz, refs, part, flipped=False):
    base = 0 if part == "g" else sz.two_l
    block = sz.bg if part == "g" else sz.bl
    result = []
    for tap in range(9):
        a, b = tap // 3, tap % 3
        if flipped:
            a, b = 2 - a, 2 - b
        result.append((tap, refs[b], base + a * block))
    return result


def shift_windows(windows, by):
    return [(tap, ref, start + by) for tap, ref, start in windows]


def conv_forward(sz, windows_of, bd_ref, z_ref, st_ref, sums, more=()):
    sums[0:16, :] = jnp.zeros((16, C), f32)

    @pl.loop(0, 2)
    def _(half):
        cols = pl.ds(pl.multiple_of(half * HALF, HALF), HALF)
        for part, first, n_all, n_rows in (
            ("g", 0, sz.mg, sz.mg // 2),
            ("l", sz.mg, sz.ml, sz.ml),
        ):
            for k in range(n_all // n_rows):
                z = conv_product(
                    shift_windows(windows_of(part), k * n_rows), bd_ref, half, n_rows, False
                )
                z_ref[first + k * n_rows : first + (k + 1) * n_rows, cols] = z
                sums[0:8, cols] += fold(z)
                sums[8:16, cols] += fold(z * z)

    put_rows(st_ref, [sums[0:8, :], sums[8:16, :]] + list(more))


def first_act_kernel(
    sz,
    flag_ref,
    x_ref,
    halo_ref,
    w_ref,
    t0,
    t1,
    t2,
    t3,
    vt_ref,
    nrm_ref,
    a00,
    a01,
    a10,
    a11,
    a01s,
    a11s,
    zs,
    gram_scr,
):
    unpack_gram(gather_sum((t0, t1, t2, t3)), gram_scr)
    terms = product_norm_terms(
        gram_scr, w_ref, 4 * sz.amount, vt_ref[G1A : G1A + 1, :], vt_ref[B1A : B1A + 1, :]
    )
    nrm_ref[...] = jnp.zeros_like(nrm_ref)
    put_norm(nrm_ref, 0, terms)
    scale, shift = terms[2], terms[3]
    g_rows, l_rows = segments(sz)
    third = sz.m // 3

    def activate(src, dst, dst_s, n_rows, width, factor=None):
        v = zs[src, :] * scale + shift
        a = silu(v)
        if factor is not None:
            a = a * factor
        dst[0][dst[1], :] = a.astype(bf16)
        if dst_s is not None:
            dst_s[dst[1], :] = shifted(a, -1, width).astype(bf16)

    plan = [(a00, None, False), (a01, a01s, False), (a10, None, True), (a11, a11s, True)]
    for phase, (dst, dst_s, bordered) in enumerate(plan):

        @pl.loop(0, 3)
        def _(i):
            zs[rows_at(i * third, third), :] = dot(
                x_ref[rows_at(phase * sz.m + i * third, third), :], w_ref[...]
            )

        g_first = sz.bg if bordered else 0
        l_first = sz.one_l + sz.bl if bordered else sz.mg

        @pl.loop(0, sz.mg // g_rows)
        def _(i):
            activate(
                rows_at(i * g_rows, g_rows),
                (dst, rows_at(g_first + i * g_rows, g_rows)),
                dst_s,
                g_rows,
                sz.cg,
            )

        @pl.loop(0, sz.ml // l_rows)
        def _(i):
            activate(
                rows_at(sz.mg + i * l_rows, l_rows),
                (dst, rows_at(l_first + i * l_rows, l_rows)),
                dst_s,
                l_rows,
                sz.cl,
            )

    flag = above(flag_ref)
    for pc, (dst, dst_s) in enumerate(((a10, None), (a11, a11s))):
        zs[0 : sz.edge, :] = dot(halo_ref[pc * sz.edge : (pc + 1) * sz.edge, :], w_ref[...])

        @pl.loop(0, sz.bg // g_rows)
        def _(i):
            rows = rows_at(i * g_rows, g_rows)
            activate(rows, (dst, rows), dst_s, g_rows, sz.cg, flag)

        @pl.loop(0, sz.bl // l_rows)
        def _(i):
            activate(
                rows_at(sz.bg + i * l_rows, l_rows),
                (dst, rows_at(sz.one_l + i * l_rows, l_rows)),
                dst_s,
                l_rows,
                sz.cl,
                flag,
            )


def first_conv_kernel(
    sz, x_ref, s_ref, k_ref, a00, a01, a10, a11, a01s, a11s, z_ref, st_ref, bd_ref, sums
):
    block_diagonal(k_ref, bd_ref)
    third = sz.m // 3
    refs = (a00, a01, a01s, a10, a11, a11s)
    zero = jnp.zeros((8, C), f32)

    def step(i, carry):
        total, square = carry
        z = dot(x_ref[rows_at(i * third, third), :], s_ref[...])
        return total + fold(z), square + fold(z * z)

    more = lax.fori_loop(0, 3, step, (zero, zero))
    conv_forward(
        sz, lambda part: windows_one(sz, refs, part), bd_ref, z_ref, st_ref, sums, more
    )


def each_crop(sz, one):
    @pl.loop(0, sz.ng)
    def _(n):
        one([rows_at(i * sz.bg + n * sz.cg, sz.cg) for i in range(sz.rg)], (n,))

    @pl.loop(0, sz.nl // 2)
    def _(pair):
        first = sz.ng + 2 * pair
        one(
            [rows_at(sz.mg + i * sz.bl + pair * 2 * sz.cl, 2 * sz.cl) for i in range(sz.rl)],
            (first, first + 1),
        )


def add_pool(ref, crops, value):
    if len(crops) == 1:
        ref[pl.ds(crops[0], 1), :] = jnp.sum(value, axis=0, keepdims=True)
    else:
        n = value.shape[0] // 2
        ref[pl.ds(crops[0], 1), :] = jnp.sum(value[:n], axis=0, keepdims=True)
        ref[pl.ds(crops[1], 1), :] = jnp.sum(value[n:], axis=0, keepdims=True)


def crop_rows(ref, crops, n_rows):
    if len(crops) == 1:
        return ref[pl.ds(crops[0], 1), :]
    n = n_rows // 2
    return jnp.concatenate(
        [jnp.broadcast_to(ref[pl.ds(crop, 1), :], (n, ref.shape[1])) for crop in crops], axis=0
    )


def pool_kernel(sz, gain_row, shift_row, strided, z_ref, t0, t1, t2, t3, vt_ref, pool_ref, nrm_ref, ps):
    terms = norm_terms(
        gather_sum((t0, t1, t2, t3)),
        0,
        sz.amount,
        vt_ref[gain_row : gain_row + 1, :],
        vt_ref[shift_row : shift_row + 1, :],
    )
    nrm_ref[...] = jnp.zeros_like(nrm_ref)
    put_norm(nrm_ref, 0, terms)
    if strided:
        put_norm(
            nrm_ref,
            4,
            norm_terms(
                gather_sum((t0, t1, t2, t3)),
                2,
                sz.amount,
                vt_ref[G1S : G1S + 1, :],
                vt_ref[B1S : B1S + 1, :],
            ),
        )
    scale, shift = terms[2], terms[3]
    ps[...] = jnp.zeros_like(ps)

    def one(pieces, crops):
        acc = None
        for rows in pieces:
            c = silu(z_ref[rows, :] * scale + shift)
            acc = c if acc is None else acc + c
        add_pool(ps, crops, acc)

    each_crop(sz, one)
    pool_ref[...] = ps[...].astype(bf16)


def inverse_area(sz):
    crop = lax.broadcasted_iota(jnp.int32, (sz.crops, 1), 0)
    return jnp.where(crop < sz.ng, 1.0 / sz.area_g, 1.0 / sz.area_l).astype(f32)


def dot_high(a, b):
    return jnp.dot(a, b, precision=highest, preferred_element_type=f32)


def gather_short(refs):
    total = refs[0][...].astype(f32)
    for ref in refs[1:]:
        total = total + ref[...].astype(f32)
    return total


def gated_product_kernel(
    sz,
    bias_row,
    shift_row,
    z_in_ref,
    nrm_ref,
    p0,
    p1,
    p2,
    p3,
    d_ref,
    u_ref,
    w_ref,
    vt_ref,
    q_ref,
    z_ref,
    st_ref,
    gate_ref,
    pooled_ref,
    pre_ref,
):
    pooled = gather_short((p0, p1, p2, p3)) * inverse_area(sz)
    pooled_ref[...] = pooled
    pre = dot_high(pooled, d_ref[...].astype(f32)) + vt_ref[bias_row : bias_row + 1, 0:HID]
    pre_ref[...] = pre
    gate = dot_high(silu(pre), u_ref[...].astype(f32)) + vt_ref[shift_row : shift_row + 1, :]
    gate_ref[...] = sigmoid(gate)
    scale = nrm_ref[2:3, :]
    shift = nrm_ref[3:4, :]

    def one(pieces, crops):
        g = crop_rows(gate_ref, crops, 2 * sz.cl)
        for rows in pieces:
            c = silu(z_in_ref[rows, :] * scale + shift)
            q_ref[rows, :] = (c * g).astype(bf16)

    each_crop(sz, one)
    n_rows = sz.m // 3
    zero = jnp.zeros((8, C), f32)

    def step(i, carry):
        total, square = carry
        rows = rows_at(i * n_rows, n_rows)
        z = dot(q_ref[rows, :], w_ref[...])
        z_ref[rows, :] = z
        return total + fold(z), square + fold(z * z)

    put_rows(st_ref, lax.fori_loop(0, 3, step, (zero, zero)))


ROWS = 32


def put_edges(sz, src, top_ref, bottom_ref):
    for ref, g, l in (
        (top_ref, 0, sz.mg),
        (bottom_ref, sz.mg - sz.bg, sz.m - sz.bl),
    ):
        if ref is not None:
            ref[0 : sz.bg, :] = src[g : g + sz.bg, :]
            ref[sz.bg : sz.edge, :] = src[l : l + sz.bl, :]


def middle_kernel(
    sz,
    zc_ref,
    x_ref,
    s_ref,
    t0,
    t1,
    t2,
    t3,
    nrm_a_ref,
    vt_ref,
    pre_ref,
    mb_ref,
    nrm_ref,
    top_ref,
    bottom_ref,
    zs,
):
    strided_product(sz, x_ref, s_ref, zs)
    terms = norm_terms(
        gather_sum((t0, t1, t2, t3)),
        0,
        sz.amount,
        vt_ref[G1C : G1C + 1, :],
        vt_ref[B1C : B1C + 1, :],
    )
    nrm_ref[...] = jnp.zeros_like(nrm_ref)
    put_norm(nrm_ref, 0, terms)
    scale = terms[2]
    scale_s = nrm_a_ref[6:7, :]
    shift = terms[3] + nrm_a_ref[7:8, :]

    @pl.loop(0, sz.m // ROWS)
    def _(i):
        rows = rows_at(i * ROWS, ROWS)
        pre = zc_ref[rows, :] * scale + zs[rows, :] * scale_s + shift
        pre_ref[rows, :] = pre
        mb_ref[rows, :] = silu(pre).astype(bf16)

    put_edges(sz, mb_ref, top_ref, bottom_ref)


def product_kernel(sz, x_ref, w_ref, z_ref, st_ref):
    n_rows = sz.m // 3
    zero = jnp.zeros((8, C), f32)

    def step(i, carry):
        total, square = carry
        rows = rows_at(i * n_rows, n_rows)
        z = dot(x_ref[rows, :], w_ref[...])
        z_ref[rows, :] = z
        return total + fold(z), square + fold(z * z)

    put_rows(st_ref, lax.fori_loop(0, 3, step, (zero, zero)))


def put_variants(refs, rows, value, width):
    refs[0][rows, :] = shifted(value, -1, width).astype(bf16)
    refs[1][rows, :] = value.astype(bf16)
    refs[2][rows, :] = shifted(value, 1, width).astype(bf16)


def second_conv_kernel(
    sz,
    flag_ref,
    z_in_ref,
    top_ref,
    bottom_ref,
    w_ref,
    k_ref,
    t0,
    t1,
    t2,
    t3,
    vt_ref,
    z_ref,
    st_ref,
    nrm_ref,
    a1,
    a0,
    a2,
    bd_ref,
    zs,
    sums,
):
    block_diagonal(k_ref, bd_ref)
    terms = norm_terms(
        gather_sum((t0, t1, t2, t3)),
        0,
        sz.amount,
        vt_ref[G2A : G2A + 1, :],
        vt_ref[B2A : B2A + 1, :],
    )
    nrm_ref[...] = jnp.zeros_like(nrm_ref)
    put_norm(nrm_ref, 0, terms)
    scale, shift = terms[2], terms[3]
    g_rows, l_rows = segments(sz)
    refs = (a0, a1, a2)

    @pl.loop(0, sz.mg // g_rows)
    def _(i):
        a = silu(z_in_ref[rows_at(i * g_rows, g_rows), :] * scale + shift)
        put_variants(refs, rows_at(sz.bg + i * g_rows, g_rows), a, sz.cg)

    @pl.loop(0, sz.ml // l_rows)
    def _(i):
        a = silu(z_in_ref[rows_at(sz.mg + i * l_rows, l_rows), :] * scale + shift)
        put_variants(refs, rows_at(sz.two_l + sz.bl + i * l_rows, l_rows), a, sz.cl)

    for k, src in enumerate((top_ref, bottom_ref)):
        flag = (above, below)[k](flag_ref, sz.n_height)
        zs[...] = dot(src[...], w_ref[...])
        g_first = 0 if k == 0 else (sz.rg + 1) * sz.bg
        l_first = sz.two_l + (0 if k == 0 else (sz.rl + 1) * sz.bl)

        @pl.loop(0, sz.bg // g_rows)
        def _(i):
            a = silu(zs[rows_at(i * g_rows, g_rows), :] * scale + shift) * flag
            put_variants(refs, rows_at(g_first + i * g_rows, g_rows), a, sz.cg)

        @pl.loop(0, sz.bl // l_rows)
        def _(i):
            a = silu(zs[rows_at(sz.bg + i * l_rows, l_rows), :] * scale + shift) * flag
            put_variants(refs, rows_at(l_first + i * l_rows, l_rows), a, sz.cl)

    conv_forward(sz, lambda part: windows_two(sz, refs, part), bd_ref, z_ref, st_ref, sums)


def output_kernel(
    sz, pre_ref, z_ref, t0, t1, t2, t3, vt_ref, cg_ref, cl_ref, og_ref, ol_ref, dn_ref, st_ref, nrm_ref, sums
):
    terms = norm_terms(
        gather_sum((t0, t1, t2, t3)),
        0,
        sz.amount,
        vt_ref[G2C : G2C + 1, :],
        vt_ref[B2C : B2C + 1, :],
    )
    nrm_ref[...] = jnp.zeros_like(nrm_ref)
    put_norm(nrm_ref, 0, terms)
    mean, inverse, scale, shift = terms
    sums[...] = jnp.zeros_like(sums)

    def piece(rows, cot):
        z = z_ref[rows, :]
        pre = silu(pre_ref[rows, :]) + z * scale + shift
        s = sigmoid(pre)
        dn = cot * (s * (1.0 + pre * (1.0 - s)))
        dn_ref[rows, :] = dn
        sums[0:8, :] += fold(dn)
        sums[8:16, :] += fold(dn * ((z - mean) * inverse))
        return pre * s

    @pl.loop(0, sz.ng)
    def _(n):
        for i in range(sz.rg):
            rows = rows_at(i * sz.bg + n * sz.cg, sz.cg)
            og_ref[n, i] = piece(rows, cg_ref[n, i].astype(f32)).astype(bf16)

    @pl.loop(0, sz.nl // 2)
    def _(pair):
        for i in range(sz.rl):
            rows = rows_at(sz.mg + i * sz.bl + pair * 2 * sz.cl, 2 * sz.cl)
            cot = jnp.concatenate(
                [cl_ref[2 * pair + k, i].astype(f32) for k in range(2)], axis=0
            )
            value = piece(rows, cot)
            for k in range(2):
                ol_ref[2 * pair + k, i] = value[k * sz.cl : (k + 1) * sz.cl].astype(bf16)

    put_rows(st_ref, [sums[0:8, :], sums[8:16, :]])


def back_terms(total, row_one, row_two, amount, nrm_ref, nrm_row):
    mean = nrm_ref[nrm_row : nrm_row + 1, :]
    inverse = nrm_ref[nrm_row + 1 : nrm_row + 2, :]
    scale = nrm_ref[nrm_row + 2 : nrm_row + 3, :]
    one = total[row_one : row_one + 1] / amount
    two = total[row_two : row_two + 1] / amount
    return scale, one, mean, inverse * two


def norm_back(dn, z, terms):
    scale, one, mean, slope = terms
    return scale * (dn - one - (z - mean) * slope)


def gate_grad_kernel(
    sz,
    strided,
    dn_ref,
    z_ref,
    t0,
    t1,
    t2,
    t3,
    nrm_ref,
    w_ref,
    z_in_ref,
    nrm_in_ref,
    *refs,
):
    if strided:
        x_ref, s_ref, nrm_a_ref, dz_ref, dzs_ref, dq_ref, dg_ref, ps, zs = refs
        strided_product(sz, x_ref, s_ref, zs)
    else:
        dz_ref, dq_ref, dg_ref, ps = refs
    total = gather_sum((t0, t1, t2, t3))
    terms = back_terms(total, 0, 1, sz.amount, nrm_ref, 0)

    @pl.loop(0, sz.m // ROWS)
    def _(i):
        rows = rows_at(i * ROWS, ROWS)
        dz_ref[rows, :] = norm_back(dn_ref[rows, :], z_ref[rows, :], terms).astype(bf16)

    if strided:
        terms_s = back_terms(total, 0, 2, sz.amount, nrm_a_ref, 4)

        @pl.loop(0, sz.m // ROWS)
        def _(i):
            rows = rows_at(i * ROWS, ROWS)
            dzs_ref[rows, :] = norm_back(dn_ref[rows, :], zs[rows, :], terms_s).astype(bf16)

    n_rows = sz.m // 3

    @pl.loop(0, 3)
    def _(i):
        rows = rows_at(i * n_rows, n_rows)
        dq_ref[rows, :] = dot_t(dz_ref[rows, :], w_ref[...])

    ps[...] = jnp.zeros_like(ps)
    scale = nrm_in_ref[2:3, :]
    shift = nrm_in_ref[3:4, :]

    def one(pieces, crops):
        acc = None
        for rows in pieces:
            term = dq_ref[rows, :] * silu(z_in_ref[rows, :] * scale + shift)
            acc = term if acc is None else acc + term
        add_pool(ps, crops, acc)

    each_crop(sz, one)
    dg_ref[...] = ps[...].astype(bf16)


def excite_back_kernel(
    sz,
    dq_ref,
    z_ref,
    nrm_ref,
    g0,
    g1,
    g2,
    g3,
    gate_ref,
    pre_ref,
    d_ref,
    u_ref,
    dn_ref,
    st_ref,
    dv_ref,
    du_ref,
    pool,
    sums,
):
    gate = gate_ref[...]
    dv = gather_short((g0, g1, g2, g3)) * gate * (1.0 - gate)
    dv_ref[...] = dv
    du = lax.dot_general(
        dv,
        u_ref[...].astype(f32),
        (((1,), (1,)), ((), ())),
        precision=highest,
        preferred_element_type=f32,
    ) * silu_slope(pre_ref[...])
    du_ref[...] = du
    pool[...] = (
        lax.dot_general(
            du,
            d_ref[...].astype(f32),
            (((1,), (1,)), ((), ())),
            precision=highest,
            preferred_element_type=f32,
        )
        * inverse_area(sz)
    )
    mean = nrm_ref[0:1, :]
    inverse = nrm_ref[1:2, :]
    scale = nrm_ref[2:3, :]
    shift = nrm_ref[3:4, :]
    sums[...] = jnp.zeros_like(sums)

    def one(pieces, crops):
        g = crop_rows(gate_ref, crops, 2 * sz.cl)
        p = crop_rows(pool, crops, 2 * sz.cl)
        for rows in pieces:
            z = z_ref[rows, :]
            dn = (dq_ref[rows, :] * g + p) * silu_slope(z * scale + shift)
            dn_ref[rows, :] = dn
            sums[0:8, :] += fold(dn)
            sums[8:16, :] += fold(dn * ((z - mean) * inverse))

    each_crop(sz, one)
    put_rows(st_ref, [sums[0:8, :], sums[8:16, :]])


def put_flat(value_ref, width, flat_ref, slots):
    if width == 128:
        for j in range(C // 128):
            flat_ref[:, j * 128 : (j + 1) * 128] = value_ref[pl.ds(j, width, stride=C // 128), :]
        return
    n_lines = width // int(np.gcd(C, width))
    n_groups = width // n_lines
    per = C // n_groups
    lane = lax.broadcasted_iota(jnp.int32, (n_groups, C), 1)
    lines = [jnp.zeros((n_groups, C), f32) for _ in range(n_lines)]
    for u in range(per):
        row = value_ref[pl.ds(u, n_groups, stride=per), :]
        row = jnp.concatenate([row] + [jnp.zeros_like(row)] * (C // 128 - 1), axis=1)
        line, at = divmod(u * width, C)
        moved = pltpu.roll(row, at, 1) if at else row
        lines[line] = jnp.where(lane >= at, lines[line] + moved, lines[line])
        if at + width > C:
            lines[line + 1] = jnp.where(
                lane < at + width - C, lines[line + 1] + moved, lines[line + 1]
            )
    for j in range(C // 128):
        for k, line in enumerate(lines):
            slots[pl.ds(k, n_groups, stride=n_lines), :] = line[:, j * 128 : (j + 1) * 128]
        flat_ref[:, j * 128 : (j + 1) * 128] = slots[0:width, :]


def excite_weights_kernel(
    width, flag_ref, dv_ref, du_ref, pooled_ref, pre_ref, dd_ref, de_ref, du_out, df_ref, wide, slots
):
    flag = first_of_height(flag_ref)
    dv = dv_ref[...] * flag
    du = du_ref[...] * flag

    def cross(a, b):
        return lax.dot_general(
            a, b, (((0,), (0,)), ((), ())), precision=highest, preferred_element_type=f32
        )

    wide[...] = cross(pooled_ref[...], du)
    put_flat(wide, width, dd_ref, slots)
    du_out[...] = cross(silu(pre_ref[...]), dv)
    de_ref[...] = jnp.broadcast_to(jnp.sum(du, axis=0, keepdims=True), de_ref.shape)
    df_ref[...] = jnp.broadcast_to(jnp.sum(dv, axis=0, keepdims=True), df_ref.shape)


def weight_kernel(x_ref, dz_ref, w_ref):
    n_rows = dz_ref.shape[0]
    n = 128 if x_ref.shape[1] % 128 == 0 else x_ref.shape[1]
    for k in range(x_ref.shape[1] // n):
        w_ref[k * n : (k + 1) * n, :] = t_dot(x_ref[0:n_rows, k * n : (k + 1) * n], dz_ref[...])


def norm_back_kernel(sz, dn_ref, z_ref, t0, t1, t2, t3, nrm_ref, dz_ref, top_ref, bottom_ref=None):
    terms = back_terms(gather_sum((t0, t1, t2, t3)), 0, 1, sz.amount, nrm_ref, 0)

    @pl.loop(0, sz.m // ROWS)
    def _(i):
        rows = rows_at(i * ROWS, ROWS)
        dz_ref[rows, :] = norm_back(dn_ref[rows, :], z_ref[rows, :], terms).astype(bf16)

    put_edges(sz, dz_ref, top_ref, bottom_ref)


def conv_weights(sz, windows_of, dz_ref, dk_ref):
    @pl.loop(0, 2)
    def _(half):
        cols = pl.ds(pl.multiple_of(half * HALF, HALF), HALF)
        win_g = windows_of("g")
        win_l = windows_of("l")
        for tap in range(9):
            _, ref_g, start_g = win_g[tap]
            _, ref_l, start_l = win_l[tap]
            acc = t_dot(ref_g[start_g : start_g + sz.mg, cols], dz_ref[0 : sz.mg, cols])
            acc = acc + t_dot(ref_l[start_l : start_l + sz.ml, cols], dz_ref[sz.mg : sz.m, cols])
            dk_ref[tap * GW : (tap + 1) * GW, cols] = block_dense(acc)


def shift_all(src, dst, by, spans):
    for first, n_all, n_rows, width in spans:

        @pl.loop(0, n_all // n_rows)
        def _(i):
            rows = rows_at(first + i * n_rows, n_rows)
            dst[rows, :] = shifted(src[rows, :].astype(f32), by, width).astype(bf16)


def second_conv_weights_kernel(sz, a1, dz_ref, dk_ref, a0, a2):
    g_rows, l_rows = segments(sz)
    spans = ((0, sz.two_l, g_rows, sz.cg), (sz.two_l, sz.two - sz.two_l, l_rows, sz.cl))
    shift_all(a1, a0, -1, spans)
    shift_all(a1, a2, 1, spans)
    conv_weights(sz, lambda part: windows_two(sz, (a0, a1, a2), part), dz_ref, dk_ref)


def first_conv_weights_kernel(sz, a00, a01, a10, a11, dz_ref, dk_ref, a01s, a11s):
    g_rows, l_rows = segments(sz)
    shift_all(a01, a01s, -1, ((0, sz.mg, g_rows, sz.cg), (sz.mg, sz.ml, l_rows, sz.cl)))
    shift_all(
        a11,
        a11s,
        -1,
        ((0, sz.one_l, g_rows, sz.cg), (sz.one_l, sz.one - sz.one_l, l_rows, sz.cl)),
    )
    refs = (a00, a01, a01s, a10, a11, a11s)
    conv_weights(sz, lambda part: windows_one(sz, refs, part), dz_ref, dk_ref)


def second_conv_back_kernel(
    sz, dz_ref, top_ref, bottom_ref, k_ref, z_ref, nrm_ref, dn_ref, st_ref, v0, v1, v2, bd_ref, sums
):
    block_diagonal(k_ref, bd_ref)
    refs = (v0, v1, v2)
    g_rows, l_rows = segments(sz)

    @pl.loop(0, sz.mg // g_rows)
    def _(i):
        v = dz_ref[rows_at(i * g_rows, g_rows), :].astype(f32)
        put_variants(refs, rows_at(sz.bg + i * g_rows, g_rows), v, sz.cg)

    @pl.loop(0, sz.ml // l_rows)
    def _(i):
        v = dz_ref[rows_at(sz.mg + i * l_rows, l_rows), :].astype(f32)
        put_variants(refs, rows_at(sz.two_l + sz.bl + i * l_rows, l_rows), v, sz.cl)

    for k, src in enumerate((top_ref, bottom_ref)):
        g_first = 0 if k == 0 else (sz.rg + 1) * sz.bg
        l_first = sz.two_l + (0 if k == 0 else (sz.rl + 1) * sz.bl)

        @pl.loop(0, sz.bg // g_rows)
        def _(i):
            v = src[rows_at(i * g_rows, g_rows), :].astype(f32)
            put_variants(refs, rows_at(g_first + i * g_rows, g_rows), v, sz.cg)

        @pl.loop(0, sz.bl // l_rows)
        def _(i):
            v = src[rows_at(sz.bg + i * l_rows, l_rows), :].astype(f32)
            put_variants(refs, rows_at(l_first + i * l_rows, l_rows), v, sz.cl)

    @pl.loop(0, 2)
    def _(half):
        cols = pl.ds(pl.multiple_of(half * HALF, HALF), HALF)
        for part, first, n_all, n_rows in (
            ("g", 0, sz.mg, sz.mg // 2),
            ("l", sz.mg, sz.ml, sz.ml),
        ):
            for k in range(n_all // n_rows):
                dn_ref[first + k * n_rows : first + (k + 1) * n_rows, cols] = conv_product(
                    shift_windows(windows_two(sz, refs, part, True), k * n_rows),
                    bd_ref,
                    half,
                    n_rows,
                    True,
                )

    slope_pass(sz.m, dn_ref, z_ref, nrm_ref, st_ref, sums)


def slope_pass(n_all, dn_ref, z_ref, nrm_ref, st_ref, sums):
    mean = nrm_ref[0:1, :]
    inverse = nrm_ref[1:2, :]
    scale = nrm_ref[2:3, :]
    shift = nrm_ref[3:4, :]
    sums[...] = jnp.zeros_like(sums)

    @pl.loop(0, n_all // ROWS)
    def _(i):
        rows = rows_at(i * ROWS, ROWS)
        z = z_ref[rows, :]
        dn = dn_ref[rows, :] * silu_slope(z * scale + shift)
        dn_ref[rows, :] = dn
        sums[0:8, :] += fold(dn)
        sums[8:16, :] += fold(dn * ((z - mean) * inverse))

    put_rows(st_ref, [sums[0:8, :], sums[8:16, :]])


def middle_back_kernel(
    sz,
    dn_d_ref,
    zd_ref,
    t0,
    t1,
    t2,
    t3,
    nrm_d_ref,
    w_ref,
    dpre_ref,
    pre_ref,
    zc_ref,
    x_ref,
    s_ref,
    nrm_c_ref,
    nrm_a_ref,
    dz_ref,
    dn_ref,
    st_ref,
    zs,
    sums,
):
    strided_product(sz, x_ref, s_ref, zs)
    terms = back_terms(gather_sum((t0, t1, t2, t3)), 0, 1, sz.amount, nrm_d_ref, 0)

    @pl.loop(0, sz.m // ROWS)
    def _(i):
        rows = rows_at(i * ROWS, ROWS)
        dz_ref[rows, :] = norm_back(dn_d_ref[rows, :], zd_ref[rows, :], terms).astype(bf16)

    n_rows = sz.m // 3

    @pl.loop(0, 3)
    def _(i):
        rows = rows_at(i * n_rows, n_rows)
        dn_ref[rows, :] = dot_t(dz_ref[rows, :], w_ref[...])

    mean_c = nrm_c_ref[0:1, :]
    inverse_c = nrm_c_ref[1:2, :]
    mean_s = nrm_a_ref[4:5, :]
    inverse_s = nrm_a_ref[5:6, :]
    sums[...] = jnp.zeros_like(sums)

    @pl.loop(0, sz.m // ROWS)
    def _(i):
        rows = rows_at(i * ROWS, ROWS)
        dn = (dn_ref[rows, :] + dpre_ref[rows, :]) * silu_slope(pre_ref[rows, :])
        dn_ref[rows, :] = dn
        sums[0:8, :] += fold(dn)
        sums[8:16, :] += fold(dn * ((zc_ref[rows, :] - mean_c) * inverse_c))
        sums[16:24, :] += fold(dn * ((zs[rows, :] - mean_s) * inverse_s))

    put_rows(st_ref, [sums[0:8, :], sums[8:16, :], sums[16:24, :]])


def first_conv_back_kernel(sz, dz_ref, below_ref, k_ref, v0, v1, bd_ref):
    block_diagonal(k_ref, bd_ref)
    g_rows, l_rows = segments(sz)

    def put(rows, v, width):
        v0[rows, :] = v.astype(bf16)
        v1[rows, :] = shifted(v, 1, width).astype(bf16)

    for src, g_src, l_src, g_dst, l_dst, g_all, l_all in (
        (dz_ref, 0, sz.mg, 0, sz.one_l, sz.mg, sz.ml),
        (below_ref, 0, sz.bg, sz.mg, sz.one_l + sz.ml, sz.bg, sz.bl),
    ):

        @pl.loop(0, g_all // g_rows)
        def _(i):
            v = src[rows_at(g_src + i * g_rows, g_rows), :].astype(f32)
            put(rows_at(g_dst + i * g_rows, g_rows), v, sz.cg)

        @pl.loop(0, l_all // l_rows)
        def _(i):
            v = src[rows_at(l_src + i * l_rows, l_rows), :].astype(f32)
            put(rows_at(l_dst + i * l_rows, l_rows), v, sz.cl)


def parity_back_kernel(sz, phase, v0, v1, bd_ref, x_ref, w_ref, nrm_ref, *refs):
    if phase:
        st_in, dn_ref, st_ref, zs, da, sums = refs
    else:
        dn_ref, st_ref, zs, da, sums = refs
    mean = nrm_ref[0:1, :]
    inverse = nrm_ref[1:2, :]
    scale = nrm_ref[2:3, :]
    shift = nrm_ref[3:4, :]
    sums[...] = jnp.zeros_like(sums)
    third = sz.m // 3
    pr, pc = phase // 2, phase % 2
    taps = []
    for a, down in (((1, 0),), ((2, 0), (0, 1)))[pr]:
        for b, right in (((1, 0),), ((2, 0), (0, 1)))[pc]:
            taps.append((3 * a + b, down, right))

    @pl.loop(0, 2)
    def _(half):
        cols = pl.ds(pl.multiple_of(half * HALF, HALF), HALF)
        for first, base, block, n_all, n_rows in (
            (0, 0, sz.bg, sz.mg, sz.mg // 2),
            (sz.mg, sz.one_l, sz.bl, sz.ml, sz.ml),
        ):
            for k in range(n_all // n_rows):
                windows = [
                    (tap, (v0, v1)[right], base + down * block + k * n_rows)
                    for tap, down, right in taps
                ]
                da[first + k * n_rows : first + (k + 1) * n_rows, cols] = conv_product(
                    windows, bd_ref, half, n_rows, True
                )

    @pl.loop(0, 3)
    def _(i):
        zs[rows_at(i * third, third), :] = dot(
            x_ref[rows_at(phase * sz.m + i * third, third), :], w_ref[...]
        )

    @pl.loop(0, sz.m // ROWS)
    def _(i):
        rows = rows_at(i * ROWS, ROWS)
        z = zs[rows, :]
        dn = da[rows, :] * silu_slope(z * scale + shift)
        dn_ref[rows, :] = dn.astype(bf16)
        sums[0:8, :] += fold(dn)
        sums[8:16, :] += fold(dn * ((z - mean) * inverse))

    put_rows(st_ref, [sums[0:8, :], sums[8:16, :]])
    if phase:
        st_ref[...] += st_in[...]


def image_norm_back_kernel(sz, dn0, dn1, dn2, dn3, x_ref, w_ref, t0, t1, t2, t3, nrm_ref, dz_ref, zs):
    terms = back_terms(gather_sum((t0, t1, t2, t3)), 0, 1, 4 * sz.amount, nrm_ref, 0)
    third = sz.m // 3
    for phase in range(4):

        @pl.loop(0, 3)
        def _(i):
            zs[rows_at(i * third, third), :] = dot(
                x_ref[rows_at(phase * sz.m + i * third, third), :], w_ref[...]
            )

        @pl.loop(0, sz.m // ROWS)
        def _(i):
            rows = rows_at(i * ROWS, ROWS)
            rows_all = rows_at(phase * sz.m + i * ROWS, ROWS)
            dz_ref[rows_all, :] = norm_back(
                (dn0, dn1, dn2, dn3)[phase][rows, :].astype(f32), zs[rows, :], terms
            ).astype(bf16)


def image_product_kernel(sz, dz_ref, w_ref, dzs_ref, ws_ref, dx_ref):
    third = sz.m // 3
    for phase in range(4):

        @pl.loop(0, 3)
        def _(i):
            rows_all = rows_at(phase * sz.m + i * third, third)
            value = dot_t(dz_ref[rows_all, :], w_ref[...])
            if phase == 0:
                value = value + dot_t(dzs_ref[rows_at(i * third, third), :], ws_ref[...])
            dx_ref[rows_all, :] = value


def place_kernel(n_crops, height, width, first_row, block, m, dx_ref, o_ref, mark_ref, s_ref, t_ref):
    half = width // 2
    mark_ref[...] = jnp.zeros_like(mark_ref)

    @pl.loop(0, n_crops)
    def _(n):
        for r in range(height):
            for pc in range(2):
                at = (2 * (r % 2) + pc) * m + first_row + (r // 2) * block + n * half
                v = dx_ref[rows_at(at, half, 8), :]
                rows = pl.ds(r * width + pc, half, stride=2)
                s_ref[rows, :] = v[:, :128]
                t_ref[rows, :] = jnp.concatenate([v[:, 128:], v[:, 128:]], axis=1)
        o_ref[n, :, :, 0:128] = s_ref[...].reshape(height, width, 128)
        o_ref[n, :, :, 128:CIN] = t_ref[...][:, :64].reshape(height, width, 64)


def over_height(x):
    n = lax.axis_size("height")
    return [x] + [lax.ppermute(x, "height", [(i, i ^ k) for i in range(n)]) for k in range(1, n)]


def step_down(x):
    n = lax.axis_size("height")
    return lax.ppermute(x, "height", [(i, i + 1) for i in range(n - 1)])


def step_up(x):
    n = lax.axis_size("height")
    return lax.ppermute(x, "height", [(i + 1, i) for i in range(n - 1)])


MATRIX_ROWS = [a * b // C for a, b in matrix_shapes()]
ROW_BOUNDS = [int(v) for v in np.cumsum([0] + MATRIX_ROWS)]
UNIT = 112


def across(x, mask, senders=None):
    n = lax.axis_size("batch")
    return lax.ppermute(
        x, "batch", [(i, i ^ mask) for i in range(n) if senders is None or i in senders]
    )


def take_flat(whole, start, width, low_ref, value, slots):
    if width == 128:
        for j in range(C // 128):
            value[pl.ds(j, width, stride=C // 128), :] = whole[
                start : start + width, j * 128 : (j + 1) * 128
            ]
    else:
        n_lines = width // int(np.gcd(C, width))
        n_groups = width // n_lines
        per = C // n_groups
        lane = lax.broadcasted_iota(jnp.int32, (n_groups, C), 1)
        blocks = [[] for _ in range(n_lines)]
        for j in range(C // 128):
            slots[0:width, :] = whole[start : start + width, j * 128 : (j + 1) * 128]
            for k in range(n_lines):
                blocks[k].append(slots[pl.ds(k, n_groups, stride=n_lines), :])
        lines = [jnp.concatenate(block, axis=1) for block in blocks]
        for u in range(per):
            line, at = divmod(u * width, C)
            row = pltpu.roll(lines[line], C - at, 1) if at else lines[line]
            if at + width > C:
                row = jnp.where(lane < C - at, row, pltpu.roll(lines[line + 1], C - at, 1))
            value[pl.ds(u, n_groups, stride=per), :] = jnp.where(lane < width, row, 0.0)[:, 0:128]
    low_ref[...] = value[...].astype(bf16)


def assemble_kernel(n_rows, idx_ref, *refs):
    ins, outs = refs[:2], refs[2:-4]
    shards, whole, value, slots = refs[-4:]
    for core, ref in enumerate(ins):
        for q in range(4):
            for k in range(4):
                at = (idx_ref[0] ^ (2 * q + core)) * 4 + (idx_ref[1] ^ k)
                shards[at] = ref[4 * q + k].astype(f32)
    for s in range(32):
        whole[s * n_rows : (s + 1) * n_rows, :] = shards[s, 0:n_rows, :]
    for k, (ref, start) in enumerate(zip(outs, ROW_BOUNDS)):
        if k in (2, 8):
            take_flat(whole, start, MATRIX_ROWS[k], ref, value, slots)
        elif k in (3, 9):
            n = MATRIX_ROWS[k]
            value[0:HID, :] = jnp.zeros((HID, 128), f32)
            for j in range(C // 128):
                value[0:n, :] = whole[start : start + n, j * 128 : (j + 1) * 128]
                ref[:, j * 128 : (j + 1) * 128] = value[0:HID, :].astype(bf16)
        else:
            ref[...] = whole[start : start + ref.shape[0], :].astype(bf16)


def merge_kernel(*refs):
    *ins, merged = refs
    n = ins[0].shape[0]
    for q, ref in enumerate(ins):
        merged[q * n : (q + 1) * n] = ref[...]


def gather_weights(lines, n_rows, place_ids, beside):
    (mine,) = call(
        functools.partial(round_rows_kernel, n_rows),
        [out((UNIT, C), bf16)],
        [],
        lines,
        name="round_weights",
        after=[place_ids],
    )
    quarter = jnp.stack(over_height(mine))
    after, extra = beside(quarter)
    planes = [quarter] + [across(quarter, mask) for mask in (2, 4, 6)]
    (merged,) = call(
        merge_kernel, [out((16, UNIT, C), bf16)], [], *planes, name="merge_planes", after=after
    )
    planes = [merged, across(merged, 1)]
    matrices = call(
        functools.partial(assemble_kernel, n_rows),
        [
            out((C, HID) if k in (2, 8) else (HID if k in (3, 9) else rows, C), bf16)
            for k, rows in enumerate(MATRIX_ROWS)
        ],
        [
            pltpu.VMEM((32, UNIT, C), f32),
            pltpu.VMEM((32 * n_rows, C), f32),
            pltpu.VMEM((C, 128), f32),
            pltpu.VMEM((HID, 128), f32),
        ],
        place_ids,
        *planes,
        smem=1,
        name="assemble",
        room=6 * 2**20,
    )
    return matrices, extra


def pack_kernel(n_rows, first_shard, sources, core_ref, *refs):
    n_src = len(sources)
    ins, (mine_ref, other_ref, buf) = refs[:n_src], refs[n_src:]
    for shard in range(buf.shape[0]):
        low = (first_shard + shard) * n_rows
        for (start, stop), ref in zip(sources, ins):
            a, b = max(low, start), min(low + n_rows, stop)
            if a < b:
                buf[shard, a - low : b - low, :] = ref[a - start : b - start, :]
        buf[shard, n_rows:, :] = jnp.zeros((UNIT - n_rows, C), f32)
    core = core_of(core_ref)
    for unit in range(buf.shape[0] // 8):
        for h in range(4):
            mine_ref[unit * 4 + h] = buf[(unit * 2 + core) * 4 + h]
            other_ref[unit * 4 + h] = buf[(unit * 2 + 1 - core) * 4 + h].astype(bf16)


def pack(n_rows, first_unit, n_units, sources, arrays, place_ids, name, after=()):
    shape = (4 * n_units, UNIT, C)
    mine, other = call(
        functools.partial(pack_kernel, n_rows, 8 * first_unit, sources),
        [out(shape), out(shape, bf16)],
        [pltpu.VMEM((8 * n_units, UNIT, C), f32)],
        place_ids,
        *arrays,
        smem=1,
        name=name,
        after=after,
    )
    return mine, across(other, 1)


def sum_core_kernel(place_ref, a_ref, b_ref, sum_ref, *low_refs):
    sum_ref[...] = a_ref[...] + b_ref[...].astype(f32)
    first = jnp.where(y_of(place_ref) == 0, 4, 0)
    for k, ref in enumerate(low_refs):
        for i in range(2):
            ref[i] = sum_ref[first + 2 * k + i].astype(bf16)


def unit_parts_kernel(place_ref, sum_ref, g0, g1, g2, g3, keep_ref, send_ref, got_ref):
    for k, ref in enumerate((g0, g1, g2, g3)):
        got_ref[2 * k : 2 * k + 2] = ref[...]
    y, x = y_of(place_ref), x_of(place_ref)
    for h in range(4):
        mine, other = 4 * x * y + h, 4 * (1 - x) * y + h
        keep_ref[h] = sum_ref[4 * y + mine] + got_ref[mine].astype(f32)
        send_ref[h] = (sum_ref[4 * y + other] + got_ref[other].astype(f32)).astype(bf16)


def shard_parts_kernel(place_ref, sum_ref, got_ref, keep_ref, s1, s2, s3):
    for k, ref in enumerate((keep_ref, s1, s2, s3)):
        at = place_ref[1] ^ k
        ref[...] = (sum_ref[at] + got_ref[at].astype(f32)).astype(ref.dtype)


def sum_low_kernel(*refs):
    *ins, sum_ref, low_ref = refs
    total = ins[0][...]
    for ref in ins[1:]:
        total = total + ref[...].astype(f32)
    sum_ref[...] = total
    low_ref[...] = total.astype(bf16)


class EarlySum:
    def __init__(self, n_rows, place_ids):
        self.n_rows, self.ids = n_rows, place_ids

    def pack(self, sources, arrays):
        self.mine, self.got = pack(
            self.n_rows, 1, 3, sources, arrays, self.ids, "pack_early"
        )
        return [self.mine]

    def y(self, after):
        shape = (12, UNIT, C)
        self.total, *lows = call(
            sum_core_kernel,
            [out(shape)] + [out((2, UNIT, C), bf16)] * 4,
            [],
            self.ids,
            self.mine,
            self.got,
            smem=1,
            name="sum_core",
            after=after,
        )
        self.pieces = [
            across(low, 4, None if k < 2 else [0, 1, 2, 3]) for k, low in enumerate(lows)
        ]
        return [self.total]

    def x(self, after):
        four = (4, UNIT, C)
        self.keep, send = call(
            unit_parts_kernel,
            [out(four), out(four, bf16)],
            [pltpu.VMEM((8, UNIT, C), bf16)],
            self.ids,
            self.total,
            *self.pieces,
            smem=1,
            name="unit_parts",
            after=after,
        )
        self.got = across(send, 2, [0, 1, 4, 5, 6, 7])
        return [self.keep]

    def height(self, after):
        self.result = spread_height(self.keep, self.got, self.ids, "shard_parts", after)
        return [self.result[0]]


def spread_height(keep, got, place_ids, name, after=()):
    low = out((UNIT, C), bf16)
    mine, *sends = call(
        shard_parts_kernel,
        [out((UNIT, C)), low, low, low],
        [],
        place_ids,
        keep,
        got,
        smem=1,
        name=name,
        after=after,
    )
    return [mine] + [
        lax.ppermute(send, "height", [(i, i ^ k) for i in range(4)])
        for k, send in zip((1, 2, 3), sends)
    ]


def sum_last_unit(n_rows, sources, arrays, place_ids, work):
    mine, got = pack(n_rows, 0, 1, sources, arrays, place_ids, "pack_last")
    beside = work.pop(0)([mine])
    parts = spread_height(mine, got, place_ids, "height_parts", beside)
    beside = []
    while work:
        beside = beside + work.pop(0)([parts[0]])
    shapes = [out((UNIT, C)), out((UNIT, C), bf16)]
    total, low = call(sum_low_kernel, shapes, [], *parts, name="sum_height", after=beside)
    got = across(low, 4, [4, 5, 6, 7])
    total, low = call(sum_low_kernel, shapes, [], total, got, name="sum_y")
    return [total, across(low, 2, [2, 3])]


def lamb_kernel(
    n_rows,
    place_ref,
    a0,
    a1,
    a2,
    a3,
    b0,
    b1,
    w_ref,
    m_ref,
    v_ref,
    first_ref,
    second_ref,
    update_ref,
    sums_ref,
    g_ref,
):
    shard = place_ref[0] * 4 + place_ref[1]
    early = a0[...] + a1[...].astype(f32) + a2[...].astype(f32) + a3[...].astype(f32)
    last = b0[...] + b1[...].astype(f32)
    g_ref[...] = jnp.where(place_ref[0] < 2, last, early)
    w, m, v = (as_rows(ref, n_rows) for ref in (w_ref, m_ref, v_ref))
    first, second, update = lamb_terms(w, g_ref[0:n_rows, :], m, v, weight_decay)
    put_as_lines(first_ref, first)
    put_as_lines(second_ref, second)
    update_ref[...] = update
    member = membership(n_rows, shard)
    sums_ref[...] = jnp.zeros_like(sums_ref)
    for k, value in enumerate((w, update)):
        by_row = jnp.sum(value * value, axis=1, keepdims=True)
        sums_ref[k : k + 1, 0:128] = jnp.sum(member * by_row, axis=0, keepdims=True)


def membership(n_rows, shard):
    row = lax.broadcasted_iota(jnp.int32, (n_rows, 128), 0) + shard * n_rows
    lane = lax.broadcasted_iota(jnp.int32, (n_rows, 128), 1)
    result = jnp.zeros((n_rows, 128), f32)
    for k in range(len(MATRIX_ROWS)):
        inside = (row >= ROW_BOUNDS[k]) & (row < ROW_BOUNDS[k + 1]) & (lane == k)
        result = jnp.where(inside, 1.0, result)
    return result


VEC_ROWS = 24


LINES = 72
LINE_F1 = 4 * C // 128
LINE_E2 = LINE_F1 + (E2 - F1) * C // 128
LINE_F2 = LINE_E2 + SE_B // 128


def as_lines(flat):
    return jnp.pad(flat, (0, LINES * 128 - flat.shape[0])).reshape(LINES, 128)


def from_lines(lines):
    return lines.reshape(-1)[: sum(vector_sizes())]


def line_pieces():
    return ((LINE_F1, F1, E2 - F1), (LINE_F2, F2, 18 - F2))


def tables_kernel(*refs):
    lines = refs[-1]
    n = len(refs) // 2
    lane = lax.broadcasted_iota(jnp.int32, (LINES, 128), 1)
    for src, dst in zip(refs[:n], refs[n : 2 * n]):
        dst[...] = jnp.zeros_like(dst)
        for j in range(C // 128):
            dst[0:4, j * 128 : (j + 1) * 128] = src[pl.ds(j, 4, stride=C // 128), :]
        head = src[LINE_F1 : LINE_F1 + 1, :]
        dst[E1 : E1 + 1, 0:128] = jnp.where(lane[0:1] < SE_A, head, 0.0)
        here = pltpu.roll(src[...], 128 - SE_A, 1)
        below = pltpu.roll(here, LINES - 1, 0)
        lines[...] = jnp.where(lane < 128 - SE_A, here, below)
        dst[E2 : E2 + 1, 0:128] = lines[LINE_E2 : LINE_E2 + 1, :]
        for line, row, count in line_pieces():
            for j in range(C // 128):
                dst[row : row + count, j * 128 : (j + 1) * 128] = lines[
                    pl.ds(line + j, count, stride=C // 128), :
                ]


def put_lines(table, dst, lines):
    lane = lax.broadcasted_iota(jnp.int32, (LINES, 128), 1)
    line_at = lax.broadcasted_iota(jnp.int32, (LINES, 128), 0)
    lines[...] = jnp.zeros_like(lines)
    lines[LINE_F1 : LINE_F1 + 1, :] = pltpu.roll(table[E1 : E1 + 1, 0:128], 128 - SE_A, 1)
    lines[LINE_E2 + 1 : LINE_E2 + 2, :] = table[E2 : E2 + 1, 0:128]
    for line, row, count in line_pieces():
        for j in range(C // 128):
            lines[pl.ds(line + 1 + j, count, stride=C // 128), :] = table[
                row : row + count, j * 128 : (j + 1) * 128
            ]
    before = pltpu.roll(lines[...], SE_A, 1)
    here = pltpu.roll(before, LINES - 1, 0)
    dst[...] = jnp.where(lane < SE_A, before, here)
    for j in range(C // 128):
        dst[pl.ds(j, 4, stride=C // 128), :] = table[0:4, j * 128 : (j + 1) * 128]


def as_rows(ref, n_rows):
    return jnp.concatenate(
        [ref[pl.ds(j, n_rows, stride=C // 128), :] for j in range(C // 128)], axis=1
    )


def put_as_lines(ref, value):
    for j in range(C // 128):
        ref[pl.ds(j, value.shape[0], stride=C // 128), :] = value[:, j * 128 : (j + 1) * 128]


def round_rows_kernel(n_rows, *refs):
    n = len(refs) // 2
    for src, dst in zip(refs[:n], refs[n:]):
        rows = as_rows(src, n_rows)
        fill = jnp.zeros((dst.shape[0] - n_rows, C), f32)
        dst[...] = jnp.concatenate([rows, fill], axis=0).astype(bf16)


def vector_grads_kernel(a, b, cs, d, e, f, de1, df1, de2, df2, sums_ref, o_ref):
    o_ref[...] = jnp.zeros_like(o_ref)
    plan = [
        (G1A, a, 1),
        (B1A, a, 0),
        (G1B, b, 1),
        (B1B, b, 0),
        (F1, df1, 0),
        (G1C, cs, 1),
        (B1C, cs, 0),
        (G1S, cs, 2),
        (B1S, cs, 0),
        (G2A, d, 1),
        (B2A, d, 0),
        (G2B, e, 1),
        (B2B, e, 0),
        (F2, df2, 0),
        (G2C, f, 1),
        (B2C, f, 0),
    ]
    for row, ref, k in plan:
        o_ref[row : row + 1, :] = ref[k : k + 1, :]
    o_ref[E1 : E1 + 1, 0:HID] = de1[0:1, :]
    o_ref[E2 : E2 + 1, 0:HID] = de2[0:1, :]
    o_ref[VEC_ROWS : VEC_ROWS + 8, :] = sums_ref[...]


def finish_kernel(
    n_rows,
    place_ref,
    r0,
    r1,
    r2,
    r3,
    w_ref,
    update_ref,
    vec_ref,
    vf_ref,
    vs_ref,
    new_w_ref,
    new_v_ref,
    new_vf_ref,
    new_vs_ref,
    norm_ref,
    slots,
    lines,
):
    place = place_ref[1]
    shard = place_ref[0] * 4 + place
    for k, ref in enumerate((r0, r1, r2, r3)):
        slots[place ^ k] = ref[...]
    total = slots[0] + slots[1] + slots[2] + slots[3]
    norms = jnp.sqrt(total[VEC_ROWS : VEC_ROWS + 8, 0:128])
    norm_ref[...] = norms
    lane = lax.broadcasted_iota(jnp.int32, (1, 128), 1)
    ratio = jnp.where(
        lane < len(MATRIX_ROWS), learn_rate * (norms[0:1] / norms[1:2]), 0.0
    )
    by_row = jnp.sum(membership(n_rows, shard) * ratio, axis=1, keepdims=True)
    put_as_lines(new_w_ref, as_rows(w_ref, n_rows) - by_row * update_ref[...])
    vec = vec_ref[...]
    first, second, update = lamb_terms(vec, total[0:VEC_ROWS], vf_ref[...], vs_ref[...], 0.0)
    put_lines(first, new_vf_ref, lines)
    put_lines(second, new_vs_ref, lines)
    size = jnp.sqrt(jnp.sum(vec * vec, axis=1, keepdims=True))
    change = jnp.sqrt(jnp.sum(update * update, axis=1, keepdims=True))
    put_lines(vec - learn_rate * (size / change) * update, new_v_ref, lines)


def lamb_terms(param, grad_val, first_old, second_old, decay):
    first_new = beta_one * first_old + (1.0 - beta_one) * grad_val
    second_new = beta_two * second_old + (1.0 - beta_two) * grad_val * grad_val
    update = (
        first_new
        / (1.0 - beta_one**STEP)
        / (jnp.sqrt(second_new / (1.0 - beta_two**STEP)) + adam_eps)
        + decay * param
    )
    return (first_new, second_new, update)


def body(
    image_glob,
    image_loc,
    cot_glob,
    cot_loc,
    weights,
    first_moment,
    second_moment,
    vectors,
    vec_first,
    vec_second,
):
    n_height = lax.axis_size("height")
    place = lax.axis_index("height")
    sz = Sizes(image_glob, image_loc, n_height)
    m = sz.m
    part = functools.partial
    place_ids = jnp.stack([lax.axis_index("batch"), place]).astype(jnp.int32)
    shapes = matrix_shapes()
    mat_lengths = [dims_pair[0] * dims_pair[1] for dims_pair in shapes]
    def prepare(before):
        x, x_edge = call(
            part(prepare_kernel, sz),
            [out((4 * m, CIN), bf16), out((2 * sz.edge, CIN), bf16)],
            [pltpu.VMEM((sz.hg * sz.wg, 128), f32)] * 2,
            image_glob,
            image_loc,
            name="prepare",
            after=before,
            room=6 * 2**20,
        )
        x_above = step_down(x_edge)
        gram_scr = pltpu.VMEM((CIN + 8, CIN), f32)
        (gram,) = call(part(gram_kernel, sz), [out(PACKED)], [gram_scr], x, name="gram", after=[x_above])
        gram = over_height(gram)
        return x, x_above, gram, gram_scr

    by_rows = (
        weights.shape[0] % C == 0
        and weights.shape[0] // C <= UNIT
        and lax.axis_size("batch") == 8
        and n_height == 4
    )
    shard_rows = weights.shape[0] // C
    table = out((VEC_ROWS, C))
    tables = call(
        tables_kernel,
        [table] * 3,
        [pltpu.VMEM((LINES, 128), f32)],
        *(as_lines(v) for v in (vectors, vec_first, vec_second)),
        name="tables",
    )
    vt = tables[0]
    early = list(tables)
    if by_rows:
        w_lines, m_lines, v_lines = (
            v.reshape(-1, 128) for v in (weights, first_moment, second_moment)
        )

    if by_rows:

        def beside(quarter):
            prepared = prepare([quarter])
            return early + [prepared[1]] + prepared[2][1:], prepared

        matrices, prepared = gather_weights(w_lines, shard_rows, place_ids, beside)
    else:
        prepared = prepare([])
        gathered = lax.all_gather(weights.astype(bf16), both_axes, axis=0, tiled=True)
        matrices = [
            flat_piece.reshape(dims_pair)
            for flat_piece, dims_pair in zip(cut_pieces(gathered, mat_lengths), shapes)
        ]
    w1, k1, d1, u1, p1, s1, w2, k2, d2, u2, p2 = matrices
    x, x_above, gram, gram_scr = prepared
    if not by_rows:
        d1 = jnp.pad(d1, ((0, 0), (0, HID - SE_A)))
        u1 = jnp.pad(u1, ((0, HID - SE_A), (0, 0)))
    st8 = out((8, C))
    mat = out((m, C))
    mat_low = out((m, C), bf16)
    pool_low = out((sz.crops, C), bf16)
    pool_scr = pltpu.VMEM((sz.crops, C), f32)
    sum_scr = pltpu.VMEM((24, C), f32)

    bd_scr = pltpu.VMEM((18, HALF, HALF), bf16)
    low_scr = pltpu.VMEM((m, C), bf16)
    mat_scr = pltpu.VMEM((m, C), f32)
    one_scr = pltpu.VMEM((sz.one, C), bf16)
    two_scr = pltpu.VMEM((sz.two, C), bf16)
    edge_scr = pltpu.VMEM((sz.edge, C), f32)
    edge = out((sz.edge, C), bf16)
    one_shape = out((sz.one, C), bf16)
    nrm_a, *act_a = call(
        part(first_act_kernel, sz),
        [st8, mat_low, mat_low, one_shape, one_shape, mat_low, one_shape],
        [mat_scr, gram_scr],
        place_ids,
        x,
        x_above,
        w1,
        *gram,
        vt,
        smem=1,
        name="first_act",
    )
    zb, st_b = call(
        part(first_conv_kernel, sz),
        [mat, st8],
        [bd_scr, sum_scr],
        x,
        s1,
        k1,
        *act_a,
        name="first_conv",
    )
    act_a = act_a[:4]
    st_b = over_height(st_b)
    pool_b, nrm_b = call(
        part(pool_kernel, sz, G1B, B1B, True), [pool_low, st8], [pool_scr], zb, *st_b, vt, name="pool_b",
    )
    pool_b = over_height(pool_b)
    hid = out((sz.crops, HID))
    crop_mat = out((sz.crops, C))
    qb, zc, st_c, gate_b, pooled_b, hidden_b = call(
        part(gated_product_kernel, sz, E1, F1),
        [mat_low, mat, st8, crop_mat, crop_mat, hid],
        [],
        zb,
        nrm_b,
        *pool_b,
        d1,
        u1,
        p1,
        vt,
        name="gated_b",
    )
    st_c = over_height(st_c)
    pre_mid, mid_low, nrm_c, mid_top, mid_bottom = call(
        part(middle_kernel, sz),
        [mat, mat_low, st8, edge, edge],
        [mat_scr],
        zc,
        x,
        s1,
        *st_c,
        nrm_b,
        vt,
        name="middle",
    )
    mid_above = step_down(mid_bottom)
    mid_below = step_up(mid_top)
    zd, st_d = call(
        part(product_kernel, sz), [mat, st8], [], mid_low, w2, name="product_d"
    )
    st_d = over_height(st_d)
    two_shape = out((sz.two, C), bf16)
    ze, st_e, nrm_d, act_d = call(
        part(second_conv_kernel, sz),
        [mat, st8, st8, two_shape],
        [two_scr, two_scr, bd_scr, edge_scr, sum_scr],
        place_ids,
        zd,
        mid_above,
        mid_below,
        w2,
        k2,
        *st_d,
        vt,
        smem=1,
        name="second_conv",
    )
    st_e = over_height(st_e)
    pool_e, nrm_e = call(
        part(pool_kernel, sz, G2B, B2B, False), [pool_low, st8], [pool_scr], ze, *st_e, vt, name="pool_e",
    )
    pool_e = over_height(pool_e)
    qe, zf, st_f, gate_e, pooled_e, hidden_e = call(
        part(gated_product_kernel, sz, E2, F2),
        [mat_low, mat, st8, crop_mat, crop_mat, hid],
        [],
        ze,
        nrm_e,
        *pool_e,
        d2,
        u2,
        p2,
        vt,
        name="gated_e",
    )
    st_f = over_height(st_f)
    out_glob, out_loc, dpre, bst_f, nrm_f = call(
        part(output_kernel, sz),
        [out(cot_glob.shape, bf16), out(cot_loc.shape, bf16), mat, st8, st8],
        [sum_scr],
        pre_mid,
        zf,
        *st_f,
        vt,
        cot_glob,
        cot_loc,
        name="output",
        room=6 * 2**20,
    )
    bst_f_all = over_height(bst_f)

    dzf, dqe, dg_e = call(
        part(gate_grad_kernel, sz, False),
        [mat_low, mat, pool_low],
        [pool_scr],
        dpre,
        zf,
        *bst_f_all,
        nrm_f,
        p2,
        ze,
        nrm_e,
        name="gate_grad_e",
    )
    dg_e = over_height(dg_e)
    (mat_f,) = call(
        weight_kernel, [out((C, C))], [], qe, dzf, name="weight_f"
    )
    dn_e, bst_e, dv_e, du_e = call(
        part(excite_back_kernel, sz),
        [mat, st8, crop_mat, hid],
        [pool_scr, sum_scr],
        dqe,
        ze,
        nrm_e,
        *dg_e,
        gate_e,
        hidden_e,
        d2,
        u2,
        name="excite_back_e",
        after=[mat_f],
    )
    bst_e_all = over_height(bst_e)
    se_outs = lambda width: [out((width, C)), out((8, HID)), out((HID, C)), st8]
    se_scr = [pltpu.VMEM((C, HID), f32), pltpu.VMEM((HID, 128), f32)]
    dd2, de2, du2, df2 = call(
        part(excite_weights_kernel, SE_B),
        se_outs(SE_B),
        se_scr,
        place_ids,
        dv_e,
        du_e,
        pooled_e,
        hidden_e,
        smem=1,
        name="excite_weights_e",
    )
    dze, dze_top, dze_bottom = call(
        part(norm_back_kernel, sz),
        [mat_low, edge, edge],
        [],
        dn_e,
        ze,
        *bst_e_all,
        nrm_e,
        name="norm_back_e",
        after=[dd2],
    )
    dze_above = step_down(dze_bottom)
    dze_below = step_up(dze_top)
    (mat_e,) = call(
        part(second_conv_weights_kernel, sz),
        [out((9 * GW, C))],
        [two_scr, two_scr],
        act_d,
        dze,
        name="second_conv_weights",
    )
    dn_d, bst_d = call(
        part(second_conv_back_kernel, sz),
        [mat, st8],
        [two_scr, two_scr, two_scr, bd_scr, sum_scr],
        dze,
        dze_above,
        dze_below,
        k2,
        zd,
        nrm_d,
        name="second_conv_back",
        after=[mat_e],
    )
    bst_d_all = over_height(bst_d)
    dzd, dn_mid, bst_cs = call(
        part(middle_back_kernel, sz),
        [mat_low, mat, st8],
        [mat_scr, sum_scr],
        dn_d,
        zd,
        *bst_d_all,
        nrm_d,
        w2,
        dpre,
        pre_mid,
        zc,
        x,
        s1,
        nrm_c,
        nrm_b,
        name="middle_back",
    )
    bst_cs_all = over_height(bst_cs)
    spans = list(zip(ROW_BOUNDS[:-1], ROW_BOUNDS[1:]))
    early = EarlySum(shard_rows, place_ids)
    dzc, dzs, dqb, dg_b = call(
        part(gate_grad_kernel, sz, True),
        [mat_low, mat_low, mat, pool_low],
        [pool_scr, mat_scr],
        dn_mid,
        zc,
        *bst_cs_all,
        nrm_c,
        p1,
        zb,
        nrm_b,
        x,
        s1,
        nrm_b,
        name="gate_grad_b",
    )
    dg_b = over_height(dg_b)
    (mat_d,) = call(
        weight_kernel,
        [out((C, C))],
        [],
        mid_low,
        dzd,
        name="weight_d",
        after=[dzc],
    )
    (mat_c,) = call(
        weight_kernel, [out((C, C))], [], qb, dzc, name="weight_c"
    )
    (mat_s,) = call(
        weight_kernel, [out((CIN, C))], [], x, dzs, name="weight_s"
    )
    dn_b, bst_b, dv_b, du_b = call(
        part(excite_back_kernel, sz),
        [mat, st8, crop_mat, hid],
        [pool_scr, sum_scr],
        dqb,
        zb,
        nrm_b,
        *dg_b,
        gate_b,
        hidden_b,
        d1,
        u1,
        name="excite_back_b",
        after=[mat_d, mat_c, mat_s],
    )
    bst_b_all = over_height(bst_b)
    dd1, de1, du1, df1 = call(
        part(excite_weights_kernel, SE_A),
        se_outs(SE_A),
        se_scr,
        place_ids,
        dv_b,
        du_b,
        pooled_b,
        hidden_b,
        smem=1,
        name="excite_weights_b",
    )
    dzb, dzb_top = call(
        part(norm_back_kernel, sz),
        [mat_low, edge],
        [],
        dn_b,
        zb,
        *bst_b_all,
        nrm_b,
        name="norm_back_b",
        after=early.pack(spans[3:], [du1, mat_c, mat_s, mat_d, mat_e, dd2, du2, mat_f])
        if by_rows
        else [dd1],
    )
    dzb_below = step_up(dzb_top)
    (mat_b,) = call(
        part(first_conv_weights_kernel, sz),
        [out((9 * GW, C))],
        [low_scr, one_scr],
        *act_a,
        dzb,
        name="first_conv_weights",
    )
    hold = [mat_b]
    if by_rows:
        hold = hold + early.y([])
    v0, v1, bd1 = call(
        part(first_conv_back_kernel, sz),
        [one_shape, one_shape, out((18, HALF, HALF), bf16)],
        [],
        dzb,
        dzb_below,
        k1,
        name="first_conv_back",
        after=hold,
    )
    dn_a, bst_a = [], []
    hold = [[], [], [], []]
    if by_rows:
        hold[2] = early.pieces[0:1]
        hold[3] = early.pieces[1:2]
    for phase in range(4):
        dn_phase, *bst_a = call(
            part(parity_back_kernel, sz, phase),
            [mat_low, st8],
            [mat_scr, mat_scr, sum_scr],
            v0,
            v1,
            bd1,
            x,
            w1,
            nrm_a,
            *bst_a,
            name="parity_back_%d" % phase,
            after=hold[phase],
        )
        dn_a.append(dn_phase)
    (bst_a,) = bst_a
    bst_a_all = over_height(bst_a)
    hold = []
    if by_rows:
        hold = early.x([bst_a])
    (dza,) = call(
        part(image_norm_back_kernel, sz),
        [out((4 * m, C), bf16)],
        [mat_scr],
        *dn_a,
        x,
        w1,
        *bst_a_all,
        nrm_a,
        name="image_norm_back",
        after=hold,
    )
    (mat_a,) = call(
        weight_kernel,
        [out((CIN, C))],
        [],
        x,
        dza,
        name="weight_a",

    )
    made = {}

    def image_product(beside):
        (made["dx"],) = call(
            part(image_product_kernel, sz),
            [out((4 * m, CIN))],
            [],
            dza,
            w1,
            dzs,
            s1,
            name="image_product",
            after=beside,
        )
        return [made["dx"]]

    def place_maps(key, shape, first_row, block, beside):
        n_crops, height, width = shape[:3]
        made[key], mark = call(
            part(place_kernel, n_crops, height, width, first_row, block, m),
            [out(shape), out((8, 128))],
            [pltpu.VMEM((height * width, 128), f32)] * 2,
            made["dx"],
            name="place_" + key,
            room=8 * 2**20,
            after=beside,
        )
        return [mark]

    work = [
        image_product,
        lambda beside: place_maps("glob", image_glob.shape, 0, sz.bg, beside),
        lambda beside: place_maps("loc", image_loc.shape, sz.mg, sz.bl, beside),
    ]
    if not by_rows:
        for one_work in work:
            one_work([])
    if by_rows:
        early.height([dza])
        last = sum_last_unit(
            shard_rows, spans[:4], [mat_a, mat_b, dd1, du1], place_ids, work
        )
        shard_out = out((shard_rows, C))
        lines_out = out(w_lines.shape)
        new_first, new_second, update, sums = call(
            part(lamb_kernel, shard_rows),
            [lines_out, lines_out, shard_out, st8],
            [pltpu.VMEM((UNIT, C), f32)],
            place_ids,
            *early.result,
            *last,
            w_lines,
            m_lines,
            v_lines,
            smem=1,
            name="lamb",
        )
        (small,) = call(
            vector_grads_kernel,
            [out((VEC_ROWS + 8, C))],
            [],
            bst_a,
            bst_b,
            bst_cs,
            bst_d,
            bst_e,
            bst_f,
            de1,
            df1,
            de2,
            df2,
            sums,
            name="vector_grads",
        )
        for mask in (1, 2, 4):
            small = small + across(small, mask)
        new_weights, new_v, new_vf, new_vs, norms = call(
            part(finish_kernel, shard_rows),
            [lines_out] + [out((LINES, 128))] * 3 + [out((8, 128))],
            [pltpu.VMEM((4, VEC_ROWS + 8, C), f32), pltpu.VMEM((LINES, 128), f32)],
            place_ids,
            *over_height(small),
            w_lines,
            update,
            *tables,
            smem=1,
            name="finish",
            room=2 * 2**20,
        )
        maps_out = (out_glob, out_loc, made["glob"], made["loc"])
        return maps_out + (
            new_weights.reshape(-1),
            new_first.reshape(-1),
            new_second.reshape(-1),
            from_lines(new_v),
            from_lines(new_vf),
            from_lines(new_vs),
            norms[:2, : len(MATRIX_ROWS)],
        )

    maps_out = (out_glob, out_loc, made["glob"], made["loc"])
    flat_grad = jnp.concatenate(
        [
            piece.reshape(-1)
            for piece in (
                mat_a,
                mat_b,
                dd1,
                du1[:SE_A],
                mat_c,
                mat_s,
                mat_d,
                mat_e,
                dd2,
                du2,
                mat_f,
            )
        ]
    )
    vec_grad = jnp.concatenate(
        [
            bst_a[1],
            bst_a[0],
            bst_b[1],
            bst_b[0],
            de1[0, :SE_A],
            df1[0],
            bst_cs[1],
            bst_cs[0],
            bst_cs[2],
            bst_cs[0],
            bst_d[1],
            bst_d[0],
            bst_e[1],
            bst_e[0],
            de2[0],
            df2[0],
            bst_f[1],
            bst_f[0],
        ]
    )
    grad_shard = lax.psum_scatter(flat_grad, both_axes, scatter_dimension=0, tiled=True)
    shard_len = weights.shape[0]
    device_index = lax.axis_index("batch") * n_height + lax.axis_index("height")
    position = device_index * shard_len + lax.iota(jnp.int32, shard_len)
    bounds = np.cumsum([0] + mat_lengths)
    lower_edge = jnp.asarray(bounds[:-1], jnp.int32)
    upper_edge = jnp.asarray(bounds[1:], jnp.int32)
    member = (
        (position[:, None] >= lower_edge[None, :]) & (position[:, None] < upper_edge[None, :])
    ).astype(f32)
    new_first, new_second, update = lamb_terms(
        weights, grad_shard, first_moment, second_moment, weight_decay
    )
    part_sums = jnp.dot(jnp.stack([weights * weights, update * update]), member, precision=highest)
    vec_total, totals = lax.psum((vec_grad, part_sums), both_axes)
    norm_pair = jnp.sqrt(totals)
    trust_ratio = learn_rate * (norm_pair[0] / norm_pair[1])
    new_weights = weights - jnp.dot(member, trust_ratio, precision=highest) * update
    vec_one_new, vec_two_new, vec_update = lamb_terms(vectors, vec_total, vec_first, vec_second, 0.0)
    vec_pieces = []
    for param_piece, update_piece in zip(
        cut_pieces(vectors, vector_sizes()), cut_pieces(vec_update, vector_sizes())
    ):
        ratio_val = jnp.sqrt(jnp.sum(param_piece * param_piece)) / jnp.sqrt(
            jnp.sum(update_piece * update_piece)
        )
        vec_pieces.append(param_piece - learn_rate * ratio_val * update_piece)
    new_vectors = jnp.concatenate(vec_pieces)
    return maps_out + (
        new_weights,
        new_first,
        new_second,
        new_vectors,
        vec_one_new,
        vec_two_new,
        norm_pair,
    )


def solution(mesh):
    maps = P("batch", "height", None, None)
    entries = P(("batch", "height"))
    return jax.shard_map(
        body,
        mesh=mesh,
        in_specs=(maps, maps, maps, maps, entries, entries, entries, P(), P(), P()),
        out_specs=(maps, maps, maps, maps, entries, entries, entries, P(), P(), P(), P()),
        check_vma=False,
    )
```

```python
import functools

import jax
import jax.numpy as jnp
import numpy as np
from jax import lax
from jax.experimental import pallas as pl
from jax.experimental.pallas import tpu as pltpu
from jax.sharding import PartitionSpec as P

CIN = 192
C = 512
GW = 64
GROUPS = 8
SE_A = 48
SE_B = 128
STEP = 10
HID = 128
HALF = 256

norm_eps = 1e-05
beta_one = 0.9
beta_two = 0.999
adam_eps = 1e-06
weight_decay = 0.01
learn_rate = 0.4
highest = lax.Precision.HIGHEST
bf16 = jnp.bfloat16
f32 = jnp.float32
both_axes = ("batch", "height")

G1A, B1A, G1B, B1B, E1, F1, G1C, B1C, G1S, B1S, G2A, B2A, G2B, B2B, E2, F2, G2C, B2C = range(18)


def matrix_shapes():
    return [
        (CIN, C),
        (9 * GW, C),
        (C, SE_A),
        (SE_A, C),
        (C, C),
        (CIN, C),
        (C, C),
        (9 * GW, C),
        (C, SE_B),
        (SE_B, C),
        (C, C),
    ]


def vector_sizes():
    return [C, C, C, C, SE_A, C, C, C, C, C, C, C, C, C, SE_B, C, C, C]


def cut_pieces(flat_vec, lengths):
    pieces = []
    offset = 0
    for length in lengths:
        pieces.append(flat_vec[offset : offset + length])
        offset += length
    return pieces


class Sizes:
    def __init__(self, image_glob, image_loc, n_height):
        self.ng, self.hg, self.wg = image_glob.shape[:3]
        self.nl, self.hl, self.wl = image_loc.shape[:3]
        self.rg, self.cg = self.hg // 2, self.wg // 2
        self.rl, self.cl = self.hl // 2, self.wl // 2
        self.bg, self.bl = self.ng * self.cg, self.nl * self.cl
        self.mg, self.ml = self.rg * self.bg, self.rl * self.bl
        self.m = self.mg + self.ml
        self.edge = self.bg + self.bl
        self.n_height = n_height
        self.crops = -(-(self.ng + self.nl) // 16) * 16
        self.area_g = self.rg * self.cg * n_height
        self.area_l = self.rl * self.cl * n_height
        self.amount = n_height * self.m
        self.one_l = (self.rg + 1) * self.bg
        self.one = self.one_l + (self.rl + 1) * self.bl
        self.two_l = (self.rg + 2) * self.bg
        self.two = self.two_l + (self.rl + 2) * self.bl


def sigmoid(v):
    return 0.5 * jnp.tanh(0.5 * v) + 0.5


def silu(v):
    return v * sigmoid(v)


def silu_slope(v):
    s = sigmoid(v)
    return s * (1.0 + v * (1.0 - s))


def padded_bytes(shape, dtype):
    size = np.dtype(dtype).itemsize
    dims = list(shape)
    dims[-1] = -(-dims[-1] // 128) * 128
    if len(dims) > 1:
        rows = 32 // size
        dims[-2] = -(-dims[-2] // rows) * rows
    return int(np.prod(dims)) * size


COST_SCALE = 1.0
MEASURED_US = {
    "first_conv_back": 1.5,
    "parity_back_0": 2.6,
    "parity_back_1": 3.0,
    "parity_back_2": 3.0,
    "parity_back_3": 3.7,
    "first_conv": 5.0,
    "first_act": 7.5,
    "second_conv": 6.3,
    "second_conv_back": 5.9,
    "image_norm_back": 5.8,
    "second_conv_weights": 4.9,
    "first_conv_weights": 4.5,
    "middle_back": 4.4,
    "gate_grad_b": 4.2,
    "gram": 3.6,
    "image_product": 3.6,
    "place_glob": 3.1,
    "output": 2.9,
    "assemble": 2.9,
    "gate_grad_e": 2.7,
    "excite_back_b": 2.6,
    "excite_back_e": 2.6,
    "place_loc": 2.5,
    "gated_b": 2.4,
    "gated_e": 2.4,
    "finish": 1.9,
    "middle": 1.8,
    "prepare": 1.4,
    "excite_weights_b": 1.3,
    "excite_weights_e": 1.2,
    "product_d": 1.1,
    "weight_a": 1.1,
    "pack_0": 1.0,
    "pack_1": 1.0,
    "pool_b": 1.0,
    "pool_e": 1.0,
    "lamb": 1.0,
    "weight_f": 0.9,
    "weight_d": 0.9,
    "weight_c": 0.9,
}


def call(kernel, outs, scratch, *ins, smem=0, name=None, after=(), room=0):
    held = sum(padded_bytes(s.shape, s.dtype) for s in scratch)
    n_in, n_after = len(ins), len(after)

    def run(*refs):
        kernel(*refs[:n_in], *refs[n_in + n_after :])

    return pl.pallas_call(
        run,
        out_shape=tuple(outs),
        in_specs=[pl.BlockSpec(memory_space=pltpu.SMEM)] * smem
        + [pl.BlockSpec(memory_space=pltpu.VMEM)] * (n_in - smem)
        + [pl.BlockSpec(memory_space=pl.ANY)] * n_after,
        out_specs=tuple(pl.BlockSpec(memory_space=pltpu.VMEM) for _ in outs),
        scratch_shapes=list(scratch),
        compiler_params=pltpu.CompilerParams(vmem_limit_bytes=held + 4 * 2**20 + room),
        cost_estimate=pl.CostEstimate(
            flops=int(MEASURED_US.get(name, 0.5) * COST_SCALE * 1.1535e9),
            bytes_accessed=1,
            transcendentals=0,
        ),
        name=name,
    )(*ins, *after)


def out(shape, dtype=f32):
    return jax.ShapeDtypeStruct(shape, dtype)


def above(ids, n_height=0):
    return jnp.where(ids[1] > 0, 1.0, 0.0)


def below(ids, n_height):
    return jnp.where(ids[1] < n_height - 1, 1.0, 0.0)


def first_of_height(ids):
    return jnp.where(ids[1] == 0, 1.0, 0.0)


def y_of(ids):
    return ids[0] // 4


def x_of(ids):
    return lax.rem(ids[0] // 2, 2)


def core_of(ids):
    return lax.rem(ids[0], 2)


def fold(x):
    return jnp.sum(x.reshape(x.shape[0] // 8, 8, x.shape[1]), axis=0)


def rows_at(start, size, unit=16):
    return pl.ds(pl.multiple_of(start, unit), size)


def put_rows(ref, parts):
    ref[...] = jnp.zeros_like(ref)
    for k, part in enumerate(parts):
        ref[k : k + 1, :] = jnp.sum(part, axis=0, keepdims=True)


def put_back_sums(ref, one, two, mean, inverse):
    one = jnp.sum(one, axis=0, keepdims=True)
    two = jnp.sum(two, axis=0, keepdims=True)
    put_rows(ref, [one, (two - mean * one) * inverse])


def gather_sum(refs):
    total = refs[0][...]
    for ref in refs[1:]:
        total = total + ref[...]
    return total


def norm_terms(total, row, amount, gain, shift):
    mean = total[row : row + 1] / amount
    inverse = lax.rsqrt(total[row + 1 : row + 2] / amount - mean * mean + norm_eps)
    scale = gain * inverse
    return mean, inverse, scale, shift - mean * scale


def put_norm(ref, row, terms):
    for k, term in enumerate(terms):
        ref[row + k : row + k + 1, :] = term


def dot(a, b):
    return jnp.dot(a, b, preferred_element_type=f32)


def dot_t(a, b):
    return lax.dot_general(a, b, (((1,), (1,)), ((), ())), preferred_element_type=f32)


def t_dot(a, b):
    return lax.dot_general(a, b, (((0,), (0,)), ((), ())), preferred_element_type=f32)


def prepare_kernel(sz, ig_ref, il_ref, x_ref, halo_ref, s_ref, t_ref):
    m = sz.m

    def split(x, n_rows):
        s_ref[0:n_rows, :] = x[:, :128]
        t_ref[0:n_rows, 0:64] = x[:, 128:]
        parts = []
        for pc in range(2):
            v = s_ref[pl.ds(pc, n_rows // 2, stride=2), :]
            w = t_ref[pl.ds(pc, n_rows // 2, stride=2), :]
            parts.append(jnp.concatenate([v, w[:, :64]], axis=1))
        return parts

    @pl.loop(0, sz.ng)
    def _(n):
        n_rows = sz.hg * sz.wg
        parts = split(ig_ref[n].astype(f32).reshape(n_rows, CIN), n_rows)
        for pc in range(2):
            v = parts[pc].reshape(sz.hg, sz.cg, CIN).astype(bf16)
            for r in range(sz.hg):
                phase = 2 * (r % 2) + pc
                x_ref[rows_at(phase * m + (r // 2) * sz.bg + n * sz.cg, sz.cg), :] = v[r]

    @pl.loop(0, sz.nl // 2)
    def _(pair):
        n_rows = 2 * sz.hl * sz.wl
        both = jnp.concatenate(
            [
                il_ref[2 * pair + k].astype(f32).reshape(sz.hl * sz.wl, CIN)
                for k in range(2)
            ],
            axis=0,
        )
        parts = split(both, n_rows)
        for pc in range(2):
            v = parts[pc].reshape(2 * sz.hl, sz.cl, CIN)
            for r in range(sz.hl):
                phase = 2 * (r % 2) + pc
                joined = jnp.concatenate([v[r], v[sz.hl + r]], axis=0).astype(bf16)
                x_ref[
                    rows_at(phase * m + sz.mg + (r // 2) * sz.bl + pair * 2 * sz.cl, 2 * sz.cl), :
                ] = joined

    for pc in range(2):
        base = (2 + pc) * m
        halo_ref[pc * sz.edge : pc * sz.edge + sz.bg, :] = x_ref[
            base + sz.mg - sz.bg : base + sz.mg, :
        ]
        halo_ref[pc * sz.edge + sz.bg : (pc + 1) * sz.edge, :] = x_ref[
            base + m - sz.bl : base + m, :
        ]


LOW = 128
PACKED = (LOW + 8, 2 * LOW)


def gram_kernel(sz, x_ref, g_ref, full):
    n_rows = sz.m // PARTS
    ones = jnp.ones((8, n_rows), bf16)
    full[...] = jnp.zeros_like(full)

    @pl.loop(0, 4 * PARTS)
    def _(i):
        x = x_ref[rows_at(i * n_rows, n_rows), :]
        full[0:CIN, :] += t_dot(x, x)
        full[CIN : CIN + 8, :] += dot(ones, x)

    g_ref[...] = jnp.zeros_like(g_ref)
    g_ref[0:LOW, 0:CIN] = full[0:LOW, :]
    g_ref[0 : CIN - LOW, CIN:] = full[LOW:CIN, LOW:CIN]
    g_ref[LOW : LOW + 8, 0:CIN] = full[CIN : CIN + 8, :]


def unpack_gram(packed, full):
    full[0:LOW, :] = packed[0:LOW, 0:CIN]
    full[LOW:CIN, 0:LOW] = jnp.transpose(packed[0:LOW, LOW : 2 * LOW])[0 : CIN - LOW]
    full[LOW:CIN, LOW:CIN] = packed[0 : CIN - LOW, CIN:]
    full[CIN : CIN + 8, :] = packed[LOW : LOW + 8, 0:CIN]


def product_norm_terms(total, w_ref, amount, gain, shift):
    w = w_ref[...].astype(f32)
    mean = dot_high(total[CIN : CIN + 8], w)[0:1] / amount
    square = jnp.sum(w * dot_high(total[0:CIN], w), axis=0, keepdims=True) / amount
    inverse = lax.rsqrt(square - mean * mean + norm_eps)
    scale = gain * inverse
    return mean, inverse, scale, shift - mean * scale


def block_diagonal(k_ref, bd_ref):
    rows = lax.broadcasted_iota(jnp.int32, (HALF, HALF), 0) // GW
    cols = lax.broadcasted_iota(jnp.int32, (HALF, HALF), 1) // GW
    same = rows == cols
    for tap in range(9):
        for half in range(2):
            k = k_ref[tap * GW : (tap + 1) * GW, half * HALF : (half + 1) * HALF].astype(f32)
            bd_ref[2 * tap + half] = jnp.where(same, jnp.concatenate([k] * 4, axis=0), 0.0).astype(
                bf16
            )


def strided_product(sz, x_ref, s_ref, zs):
    n_rows = sz.m // PARTS

    @pl.loop(0, PARTS)
    def _(i):
        zs[rows_at(i * n_rows, n_rows), :] = dot(x_ref[rows_at(i * n_rows, n_rows), :], s_ref[...])


def block_dense(acc):
    rows = lax.broadcasted_iota(jnp.int32, (HALF, HALF), 0) // GW
    cols = lax.broadcasted_iota(jnp.int32, (HALF, HALF), 1) // GW
    kept = jnp.where(rows == cols, acc, 0.0)
    return jnp.sum(kept.reshape(4, GW, HALF), axis=0)


def shifted(v, by, width):
    n_rows = v.shape[0]
    col = lax.broadcasted_iota(jnp.int32, v.shape, 0) % width
    if by < 0:
        return jnp.where(col == 0, 0.0, pltpu.roll(v, 1, 0))
    return jnp.where(col == width - 1, 0.0, pltpu.roll(v, n_rows - 1, 0))


def segments(sz):
    g_rows = sz.bg
    l_rows = sz.bl
    return g_rows, l_rows


def conv_product(windows, bd_ref, half, n_rows, transposed):
    acc = None
    cols = pl.ds(pl.multiple_of(half * HALF, HALF), HALF)
    for tap, ref, start in windows:
        x = ref[start : start + n_rows, cols]
        w = bd_ref[2 * tap + half]
        term = dot_t(x, w) if transposed else dot(x, w)
        acc = term if acc is None else acc + term
    return acc


def windows_one(sz, refs, part):
    a00, a01, a01s, a10, a11, a11s = refs
    plain = 0 if part == "g" else sz.mg
    above = 0 if part == "g" else sz.one_l
    here = above + (sz.bg if part == "g" else sz.bl)
    result = []
    for tap in range(9):
        a, b = tap // 3, tap % 3
        if a == 1:
            result.append((tap, (a01s, a00, a01)[b], plain))
        else:
            result.append((tap, (a11s, a10, a11)[b], above if a == 0 else here))
    return result


def windows_two(sz, refs, part, flipped=False):
    base = 0 if part == "g" else sz.two_l
    block = sz.bg if part == "g" else sz.bl
    result = []
    for tap in range(9):
        a, b = tap // 3, tap % 3
        if flipped:
            a, b = 2 - a, 2 - b
        result.append((tap, refs[b], base + a * block))
    return result


def shift_windows(windows, by):
    return [(tap, ref, start + by) for tap, ref, start in windows]


def conv_forward(sz, windows_of, bd_ref, z_ref, st_ref, sums, more=()):
    sums[0:16, :] = jnp.zeros((16, C), f32)

    @pl.loop(0, 2)
    def _(half):
        cols = pl.ds(pl.multiple_of(half * HALF, HALF), HALF)
        for part, first, n_all, n_rows in (
            ("g", 0, sz.mg, sz.mg // 2),
            ("l", sz.mg, sz.ml, sz.ml),
        ):
            for k in range(n_all // n_rows):
                z = conv_product(
                    shift_windows(windows_of(part), k * n_rows), bd_ref, half, n_rows, False
                )
                z_ref[first + k * n_rows : first + (k + 1) * n_rows, cols] = z
                sums[0:8, cols] += fold(z)
                sums[8:16, cols] += fold(z * z)

    put_rows(st_ref, [sums[0:8, :], sums[8:16, :]] + list(more))


def first_act_kernel(
    sz,
    flag_ref,
    x_ref,
    halo_ref,
    w_ref,
    t0,
    t1,
    t2,
    t3,
    vt_ref,
    nrm_ref,
    a00,
    a01,
    a10,
    a11,
    a01s,
    a11s,
    zs,
    gram_scr,
):
    unpack_gram(gather_sum((t0, t1, t2, t3)), gram_scr)
    terms = product_norm_terms(
        gram_scr, w_ref, 4 * sz.amount, vt_ref[G1A : G1A + 1, :], vt_ref[B1A : B1A + 1, :]
    )
    nrm_ref[...] = jnp.zeros_like(nrm_ref)
    put_norm(nrm_ref, 0, terms)
    scale, shift = terms[2], terms[3]
    g_rows, l_rows = segments(sz)
    third = sz.m // PARTS

    def activate(src, dst, dst_s, n_rows, width, factor=None):
        v = zs[src, :] * scale + shift
        a = silu(v)
        if factor is not None:
            a = a * factor
        dst[0][dst[1], :] = a.astype(bf16)
        if dst_s is not None:
            dst_s[dst[1], :] = shifted(a, -1, width).astype(bf16)

    plan = [(a00, None, False), (a01, a01s, False), (a10, None, True), (a11, a11s, True)]
    for phase, (dst, dst_s, bordered) in enumerate(plan):

        @pl.loop(0, PARTS)
        def _(i):
            zs[rows_at(i * third, third), :] = dot(
                x_ref[rows_at(phase * sz.m + i * third, third), :], w_ref[...]
            )

        g_first = sz.bg if bordered else 0
        l_first = sz.one_l + sz.bl if bordered else sz.mg

        @pl.loop(0, sz.mg // g_rows)
        def _(i):
            activate(
                rows_at(i * g_rows, g_rows),
                (dst, rows_at(g_first + i * g_rows, g_rows)),
                dst_s,
                g_rows,
                sz.cg,
            )

        @pl.loop(0, sz.ml // l_rows)
        def _(i):
            activate(
                rows_at(sz.mg + i * l_rows, l_rows),
                (dst, rows_at(l_first + i * l_rows, l_rows)),
                dst_s,
                l_rows,
                sz.cl,
            )

    flag = above(flag_ref)
    for pc, (dst, dst_s) in enumerate(((a10, None), (a11, a11s))):
        zs[0 : sz.edge, :] = dot(halo_ref[pc * sz.edge : (pc + 1) * sz.edge, :], w_ref[...])

        @pl.loop(0, sz.bg // g_rows)
        def _(i):
            rows = rows_at(i * g_rows, g_rows)
            activate(rows, (dst, rows), dst_s, g_rows, sz.cg, flag)

        @pl.loop(0, sz.bl // l_rows)
        def _(i):
            activate(
                rows_at(sz.bg + i * l_rows, l_rows),
                (dst, rows_at(sz.one_l + i * l_rows, l_rows)),
                dst_s,
                l_rows,
                sz.cl,
                flag,
            )


def first_conv_kernel(
    sz, x_ref, s_ref, k_ref, a00, a01, a10, a11, a01s, a11s, z_ref, st_ref, bd_ref, sums
):
    block_diagonal(k_ref, bd_ref)
    third = sz.m // PARTS
    refs = (a00, a01, a01s, a10, a11, a11s)
    zero = jnp.zeros((8, C), f32)

    def step(i, carry):
        total, square = carry
        z = dot(x_ref[rows_at(i * third, third), :], s_ref[...])
        return total + fold(z), square + fold(z * z)

    more = lax.fori_loop(0, PARTS, step, (zero, zero))
    conv_forward(
        sz, lambda part: windows_one(sz, refs, part), bd_ref, z_ref, st_ref, sums, more
    )


def each_crop(sz, one):
    @pl.loop(0, sz.ng, unroll=2)
    def _(n):
        one([rows_at(i * sz.bg + n * sz.cg, sz.cg) for i in range(sz.rg)], (n,))

    @pl.loop(0, sz.nl // 2, unroll=3)
    def _(pair):
        first = sz.ng + 2 * pair
        one(
            [rows_at(sz.mg + i * sz.bl + pair * 2 * sz.cl, 2 * sz.cl) for i in range(sz.rl)],
            (first, first + 1),
        )


def add_pool(ref, crops, value):
    if len(crops) == 1:
        ref[pl.ds(crops[0], 1), :] = jnp.sum(value, axis=0, keepdims=True)
    else:
        n = value.shape[0] // 2
        ref[pl.ds(crops[0], 1), :] = jnp.sum(value[:n], axis=0, keepdims=True)
        ref[pl.ds(crops[1], 1), :] = jnp.sum(value[n:], axis=0, keepdims=True)


def crop_rows(ref, crops, n_rows):
    if len(crops) == 1:
        return ref[pl.ds(crops[0], 1), :]
    n = n_rows // 2
    return jnp.concatenate(
        [jnp.broadcast_to(ref[pl.ds(crop, 1), :], (n, ref.shape[1])) for crop in crops], axis=0
    )


def pool_kernel(sz, gain_row, shift_row, strided, z_ref, t0, t1, t2, t3, vt_ref, pool_ref, nrm_ref, ps):
    terms = norm_terms(
        gather_sum((t0, t1, t2, t3)),
        0,
        sz.amount,
        vt_ref[gain_row : gain_row + 1, :],
        vt_ref[shift_row : shift_row + 1, :],
    )
    nrm_ref[...] = jnp.zeros_like(nrm_ref)
    put_norm(nrm_ref, 0, terms)
    if strided:
        put_norm(
            nrm_ref,
            4,
            norm_terms(
                gather_sum((t0, t1, t2, t3)),
                2,
                sz.amount,
                vt_ref[G1S : G1S + 1, :],
                vt_ref[B1S : B1S + 1, :],
            ),
        )
    scale, shift = terms[2], terms[3]
    ps[...] = jnp.zeros_like(ps)

    def one(pieces, crops):
        acc = None
        for rows in pieces:
            c = silu(z_ref[rows, :] * scale + shift)
            acc = c if acc is None else acc + c
        add_pool(ps, crops, acc)

    each_crop(sz, one)
    pool_ref[...] = ps[...].astype(bf16)


def inverse_area(sz):
    crop = lax.broadcasted_iota(jnp.int32, (sz.crops, 1), 0)
    return jnp.where(crop < sz.ng, 1.0 / sz.area_g, 1.0 / sz.area_l).astype(f32)


def dot_high(a, b):
    return jnp.dot(a, b, precision=highest, preferred_element_type=f32)


def gather_short(refs):
    total = refs[0][...].astype(f32)
    for ref in refs[1:]:
        total = total + ref[...].astype(f32)
    return total


def gated_product_kernel(
    sz,
    bias_row,
    shift_row,
    z_in_ref,
    nrm_ref,
    p0,
    p1,
    p2,
    p3,
    d_ref,
    u_ref,
    w_ref,
    vt_ref,
    q_ref,
    z_ref,
    st_ref,
    gate_ref,
    pooled_ref,
    pre_ref,
):
    pooled = gather_short((p0, p1, p2, p3)) * inverse_area(sz)
    pooled_ref[...] = pooled
    pre = dot_high(pooled, d_ref[...].astype(f32)) + vt_ref[bias_row : bias_row + 1, 0:HID]
    pre_ref[...] = pre
    gate = dot_high(silu(pre), u_ref[...].astype(f32)) + vt_ref[shift_row : shift_row + 1, :]
    gate_ref[...] = sigmoid(gate)
    scale = nrm_ref[2:3, :]
    shift = nrm_ref[3:4, :]

    def one(pieces, crops):
        g = crop_rows(gate_ref, crops, 2 * sz.cl)
        for rows in pieces:
            c = silu(z_in_ref[rows, :] * scale + shift)
            q_ref[rows, :] = (c * g).astype(bf16)

    each_crop(sz, one)
    n_rows = sz.m // PARTS
    zero = jnp.zeros((8, C), f32)

    def step(i, carry):
        total, square = carry
        rows = rows_at(i * n_rows, n_rows)
        z = dot(q_ref[rows, :], w_ref[...])
        z_ref[rows, :] = z
        return total + fold(z), square + fold(z * z)

    put_rows(st_ref, lax.fori_loop(0, PARTS, step, (zero, zero)))


ROWS = 352
PARTS = 1


def put_edges(sz, src, top_ref, bottom_ref):
    for ref, g, l in (
        (top_ref, 0, sz.mg),
        (bottom_ref, sz.mg - sz.bg, sz.m - sz.bl),
    ):
        if ref is not None:
            ref[0 : sz.bg, :] = src[g : g + sz.bg, :]
            ref[sz.bg : sz.edge, :] = src[l : l + sz.bl, :]


def middle_kernel(
    sz,
    zc_ref,
    x_ref,
    s_ref,
    t0,
    t1,
    t2,
    t3,
    nrm_a_ref,
    vt_ref,
    pre_ref,
    mb_ref,
    nrm_ref,
    top_ref,
    bottom_ref,
    zs,
):
    strided_product(sz, x_ref, s_ref, zs)
    terms = norm_terms(
        gather_sum((t0, t1, t2, t3)),
        0,
        sz.amount,
        vt_ref[G1C : G1C + 1, :],
        vt_ref[B1C : B1C + 1, :],
    )
    nrm_ref[...] = jnp.zeros_like(nrm_ref)
    put_norm(nrm_ref, 0, terms)
    scale = terms[2]
    scale_s = nrm_a_ref[6:7, :]
    shift = terms[3] + nrm_a_ref[7:8, :]

    @pl.loop(0, sz.m // ROWS)
    def _(i):
        rows = rows_at(i * ROWS, ROWS)
        pre = zc_ref[rows, :] * scale + zs[rows, :] * scale_s + shift
        pre_ref[rows, :] = pre
        mb_ref[rows, :] = silu(pre).astype(bf16)

    put_edges(sz, mb_ref, top_ref, bottom_ref)


def product_kernel(sz, x_ref, w_ref, z_ref, st_ref):
    n_rows = sz.m // PARTS
    zero = jnp.zeros((8, C), f32)

    def step(i, carry):
        total, square = carry
        rows = rows_at(i * n_rows, n_rows)
        z = dot(x_ref[rows, :], w_ref[...])
        z_ref[rows, :] = z
        return total + fold(z), square + fold(z * z)

    put_rows(st_ref, lax.fori_loop(0, PARTS, step, (zero, zero)))


def put_variants(refs, rows, value, width):
    refs[0][rows, :] = shifted(value, -1, width).astype(bf16)
    refs[1][rows, :] = value.astype(bf16)
    refs[2][rows, :] = shifted(value, 1, width).astype(bf16)


def second_conv_kernel(
    sz,
    flag_ref,
    z_in_ref,
    top_ref,
    bottom_ref,
    w_ref,
    k_ref,
    t0,
    t1,
    t2,
    t3,
    vt_ref,
    z_ref,
    st_ref,
    nrm_ref,
    a1,
    a0,
    a2,
    bd_ref,
    zs,
    sums,
):
    block_diagonal(k_ref, bd_ref)
    terms = norm_terms(
        gather_sum((t0, t1, t2, t3)),
        0,
        sz.amount,
        vt_ref[G2A : G2A + 1, :],
        vt_ref[B2A : B2A + 1, :],
    )
    nrm_ref[...] = jnp.zeros_like(nrm_ref)
    put_norm(nrm_ref, 0, terms)
    scale, shift = terms[2], terms[3]
    g_rows, l_rows = segments(sz)
    refs = (a0, a1, a2)

    @pl.loop(0, sz.mg // g_rows)
    def _(i):
        a = silu(z_in_ref[rows_at(i * g_rows, g_rows), :] * scale + shift)
        put_variants(refs, rows_at(sz.bg + i * g_rows, g_rows), a, sz.cg)

    @pl.loop(0, sz.ml // l_rows)
    def _(i):
        a = silu(z_in_ref[rows_at(sz.mg + i * l_rows, l_rows), :] * scale + shift)
        put_variants(refs, rows_at(sz.two_l + sz.bl + i * l_rows, l_rows), a, sz.cl)

    for k, src in enumerate((top_ref, bottom_ref)):
        flag = (above, below)[k](flag_ref, sz.n_height)
        zs[...] = dot(src[...], w_ref[...])
        g_first = 0 if k == 0 else (sz.rg + 1) * sz.bg
        l_first = sz.two_l + (0 if k == 0 else (sz.rl + 1) * sz.bl)

        @pl.loop(0, sz.bg // g_rows)
        def _(i):
            a = silu(zs[rows_at(i * g_rows, g_rows), :] * scale + shift) * flag
            put_variants(refs, rows_at(g_first + i * g_rows, g_rows), a, sz.cg)

        @pl.loop(0, sz.bl // l_rows)
        def _(i):
            a = silu(zs[rows_at(sz.bg + i * l_rows, l_rows), :] * scale + shift) * flag
            put_variants(refs, rows_at(l_first + i * l_rows, l_rows), a, sz.cl)

    conv_forward(sz, lambda part: windows_two(sz, refs, part), bd_ref, z_ref, st_ref, sums)


def output_kernel(
    sz, pre_ref, z_ref, t0, t1, t2, t3, vt_ref, cg_ref, cl_ref, og_ref, ol_ref, dn_ref, st_ref, nrm_ref, sums
):
    terms = norm_terms(
        gather_sum((t0, t1, t2, t3)),
        0,
        sz.amount,
        vt_ref[G2C : G2C + 1, :],
        vt_ref[B2C : B2C + 1, :],
    )
    nrm_ref[...] = jnp.zeros_like(nrm_ref)
    put_norm(nrm_ref, 0, terms)
    mean, inverse, scale, shift = terms
    sums[...] = jnp.zeros_like(sums)

    def piece(rows, cot):
        z = z_ref[rows, :]
        pre = silu(pre_ref[rows, :]) + z * scale + shift
        s = sigmoid(pre)
        dn = cot * (s * (1.0 + pre * (1.0 - s)))
        dn_ref[rows, :] = dn
        return pre * s, fold(dn), fold(dn * z)

    @pl.loop(0, sz.ng, unroll=2)
    def _(n):
        one, two = 0.0, 0.0
        for i in range(sz.rg):
            rows = rows_at(i * sz.bg + n * sz.cg, sz.cg)
            value, add_one, add_two = piece(rows, cg_ref[n, i].astype(f32))
            og_ref[n, i] = value.astype(bf16)
            one, two = one + add_one, two + add_two
        sums[0:8, :] += one
        sums[8:16, :] += two

    @pl.loop(0, sz.nl // 2, unroll=3)
    def _(pair):
        one, two = 0.0, 0.0
        for i in range(sz.rl):
            rows = rows_at(sz.mg + i * sz.bl + pair * 2 * sz.cl, 2 * sz.cl)
            cot = jnp.concatenate(
                [cl_ref[2 * pair + k, i].astype(f32) for k in range(2)], axis=0
            )
            value, add_one, add_two = piece(rows, cot)
            for k in range(2):
                ol_ref[2 * pair + k, i] = value[k * sz.cl : (k + 1) * sz.cl].astype(bf16)
            one, two = one + add_one, two + add_two
        sums[0:8, :] += one
        sums[8:16, :] += two

    put_back_sums(st_ref, sums[0:8, :], sums[8:16, :], mean, inverse)


def back_terms(total, row_one, row_two, amount, nrm_ref, nrm_row):
    mean = nrm_ref[nrm_row : nrm_row + 1, :]
    inverse = nrm_ref[nrm_row + 1 : nrm_row + 2, :]
    scale = nrm_ref[nrm_row + 2 : nrm_row + 3, :]
    one = total[row_one : row_one + 1] / amount
    two = total[row_two : row_two + 1] / amount
    return scale, one, mean, inverse * two


def norm_back(dn, z, terms):
    scale, one, mean, slope = terms
    return scale * (dn - one - (z - mean) * slope)


def gate_grad_kernel(
    sz,
    strided,
    dn_ref,
    z_ref,
    t0,
    t1,
    t2,
    t3,
    nrm_ref,
    w_ref,
    z_in_ref,
    nrm_in_ref,
    *refs,
):
    if strided:
        x_ref, s_ref, nrm_a_ref, dz_ref, dzs_ref, dq_ref, dg_ref, ps, zs = refs
        strided_product(sz, x_ref, s_ref, zs)
    else:
        dz_ref, dq_ref, dg_ref, ps = refs
    total = gather_sum((t0, t1, t2, t3))
    terms = back_terms(total, 0, 1, sz.amount, nrm_ref, 0)

    @pl.loop(0, sz.m // ROWS)
    def _(i):
        rows = rows_at(i * ROWS, ROWS)
        dz_ref[rows, :] = norm_back(dn_ref[rows, :], z_ref[rows, :], terms).astype(bf16)

    if strided:
        terms_s = back_terms(total, 0, 2, sz.amount, nrm_a_ref, 4)

        @pl.loop(0, sz.m // ROWS)
        def _(i):
            rows = rows_at(i * ROWS, ROWS)
            dzs_ref[rows, :] = norm_back(dn_ref[rows, :], zs[rows, :], terms_s).astype(bf16)

    n_rows = sz.m // PARTS

    @pl.loop(0, PARTS)
    def _(i):
        rows = rows_at(i * n_rows, n_rows)
        dq_ref[rows, :] = dot_t(dz_ref[rows, :], w_ref[...])

    ps[...] = jnp.zeros_like(ps)
    scale = nrm_in_ref[2:3, :]
    shift = nrm_in_ref[3:4, :]

    def one(pieces, crops):
        acc = None
        for rows in pieces:
            term = dq_ref[rows, :] * silu(z_in_ref[rows, :] * scale + shift)
            acc = term if acc is None else acc + term
        add_pool(ps, crops, acc)

    each_crop(sz, one)
    dg_ref[...] = ps[...].astype(bf16)


def excite_back_kernel(
    sz,
    dq_ref,
    z_ref,
    nrm_ref,
    g0,
    g1,
    g2,
    g3,
    gate_ref,
    pre_ref,
    d_ref,
    u_ref,
    dn_ref,
    st_ref,
    dv_ref,
    du_ref,
    pool,
    sums,
):
    gate = gate_ref[...]
    dv = gather_short((g0, g1, g2, g3)) * gate * (1.0 - gate)
    dv_ref[...] = dv
    du = lax.dot_general(
        dv,
        u_ref[...].astype(f32),
        (((1,), (1,)), ((), ())),
        precision=highest,
        preferred_element_type=f32,
    ) * silu_slope(pre_ref[...])
    du_ref[...] = du
    pool[...] = (
        lax.dot_general(
            du,
            d_ref[...].astype(f32),
            (((1,), (1,)), ((), ())),
            precision=highest,
            preferred_element_type=f32,
        )
        * inverse_area(sz)
    )
    mean = nrm_ref[0:1, :]
    inverse = nrm_ref[1:2, :]
    scale = nrm_ref[2:3, :]
    shift = nrm_ref[3:4, :]
    sums[...] = jnp.zeros_like(sums)

    def one(pieces, crops):
        g = crop_rows(gate_ref, crops, 2 * sz.cl)
        p = crop_rows(pool, crops, 2 * sz.cl)
        total, with_z = 0.0, 0.0
        for rows in pieces:
            z = z_ref[rows, :]
            dn = (dq_ref[rows, :] * g + p) * silu_slope(z * scale + shift)
            dn_ref[rows, :] = dn
            total, with_z = total + fold(dn), with_z + fold(dn * z)
        sums[0:8, :] += total
        sums[8:16, :] += with_z

    each_crop(sz, one)
    put_back_sums(st_ref, sums[0:8, :], sums[8:16, :], mean, inverse)


def put_flat(value_ref, width, flat_ref, slots):
    if width == 128:
        for j in range(C // 128):
            flat_ref[:, j * 128 : (j + 1) * 128] = value_ref[pl.ds(j, width, stride=C // 128), :]
        return
    n_lines = width // int(np.gcd(C, width))
    n_groups = width // n_lines
    per = C // n_groups
    lane = lax.broadcasted_iota(jnp.int32, (n_groups, C), 1)
    lines = [jnp.zeros((n_groups, C), f32) for _ in range(n_lines)]
    for u in range(per):
        row = value_ref[pl.ds(u, n_groups, stride=per), :]
        row = jnp.concatenate([row] + [jnp.zeros_like(row)] * (C // 128 - 1), axis=1)
        line, at = divmod(u * width, C)
        moved = pltpu.roll(row, at, 1) if at else row
        lines[line] = jnp.where(lane >= at, lines[line] + moved, lines[line])
        if at + width > C:
            lines[line + 1] = jnp.where(
                lane < at + width - C, lines[line + 1] + moved, lines[line + 1]
            )
    for j in range(C // 128):
        for k, line in enumerate(lines):
            slots[pl.ds(k, n_groups, stride=n_lines), :] = line[:, j * 128 : (j + 1) * 128]
        flat_ref[:, j * 128 : (j + 1) * 128] = slots[0:width, :]


def excite_weights_kernel(
    width, flag_ref, dv_ref, du_ref, pooled_ref, pre_ref, dd_ref, de_ref, du_out, df_ref, wide, slots
):
    flag = first_of_height(flag_ref)
    dv = dv_ref[...] * flag
    du = du_ref[...] * flag

    def cross(a, b):
        return lax.dot_general(
            a, b, (((0,), (0,)), ((), ())), precision=highest, preferred_element_type=f32
        )

    wide[...] = cross(pooled_ref[...], du)
    put_flat(wide, width, dd_ref, slots)
    du_out[...] = cross(silu(pre_ref[...]), dv)
    de_ref[...] = jnp.broadcast_to(jnp.sum(du, axis=0, keepdims=True), de_ref.shape)
    df_ref[...] = jnp.broadcast_to(jnp.sum(dv, axis=0, keepdims=True), df_ref.shape)


def weight_kernel(x_ref, dz_ref, w_ref):
    n_rows = dz_ref.shape[0]
    n = 128 if x_ref.shape[1] % 128 == 0 else x_ref.shape[1]
    for k in range(x_ref.shape[1] // n):
        w_ref[k * n : (k + 1) * n, :] = t_dot(x_ref[0:n_rows, k * n : (k + 1) * n], dz_ref[...])


def norm_back_kernel(sz, dn_ref, z_ref, t0, t1, t2, t3, nrm_ref, dz_ref, top_ref, bottom_ref=None):
    terms = back_terms(gather_sum((t0, t1, t2, t3)), 0, 1, sz.amount, nrm_ref, 0)

    @pl.loop(0, sz.m // ROWS)
    def _(i):
        rows = rows_at(i * ROWS, ROWS)
        dz_ref[rows, :] = norm_back(dn_ref[rows, :], z_ref[rows, :], terms).astype(bf16)

    put_edges(sz, dz_ref, top_ref, bottom_ref)


def conv_weights(sz, windows_of, dz_ref, dk_ref):
    @pl.loop(0, 2)
    def _(half):
        cols = pl.ds(pl.multiple_of(half * HALF, HALF), HALF)
        win_g = windows_of("g")
        win_l = windows_of("l")
        for tap in range(9):
            _, ref_g, start_g = win_g[tap]
            _, ref_l, start_l = win_l[tap]
            acc = t_dot(ref_g[start_g : start_g + sz.mg, cols], dz_ref[0 : sz.mg, cols])
            acc = acc + t_dot(ref_l[start_l : start_l + sz.ml, cols], dz_ref[sz.mg : sz.m, cols])
            dk_ref[tap * GW : (tap + 1) * GW, cols] = block_dense(acc)


def shift_all(src, dst, by, spans):
    for first, n_all, n_rows, width in spans:

        @pl.loop(0, n_all // n_rows)
        def _(i):
            rows = rows_at(first + i * n_rows, n_rows)
            dst[rows, :] = shifted(src[rows, :].astype(f32), by, width).astype(bf16)


def second_conv_weights_kernel(sz, a1, dz_ref, dk_ref, a0, a2):
    g_rows, l_rows = segments(sz)
    spans = ((0, sz.two_l, g_rows, sz.cg), (sz.two_l, sz.two - sz.two_l, l_rows, sz.cl))
    shift_all(a1, a0, -1, spans)
    shift_all(a1, a2, 1, spans)
    conv_weights(sz, lambda part: windows_two(sz, (a0, a1, a2), part), dz_ref, dk_ref)


def first_conv_weights_kernel(sz, a00, a01, a10, a11, dz_ref, dk_ref, a01s, a11s):
    g_rows, l_rows = segments(sz)
    shift_all(a01, a01s, -1, ((0, sz.mg, g_rows, sz.cg), (sz.mg, sz.ml, l_rows, sz.cl)))
    shift_all(
        a11,
        a11s,
        -1,
        ((0, sz.one_l, g_rows, sz.cg), (sz.one_l, sz.one - sz.one_l, l_rows, sz.cl)),
    )
    refs = (a00, a01, a01s, a10, a11, a11s)
    conv_weights(sz, lambda part: windows_one(sz, refs, part), dz_ref, dk_ref)


def second_conv_back_kernel(
    sz, dz_ref, top_ref, bottom_ref, k_ref, z_ref, nrm_ref, dn_ref, st_ref, v0, v1, v2, bd_ref, sums
):
    block_diagonal(k_ref, bd_ref)
    refs = (v0, v1, v2)
    g_rows, l_rows = segments(sz)

    @pl.loop(0, sz.mg // g_rows)
    def _(i):
        v = dz_ref[rows_at(i * g_rows, g_rows), :].astype(f32)
        put_variants(refs, rows_at(sz.bg + i * g_rows, g_rows), v, sz.cg)

    @pl.loop(0, sz.ml // l_rows)
    def _(i):
        v = dz_ref[rows_at(sz.mg + i * l_rows, l_rows), :].astype(f32)
        put_variants(refs, rows_at(sz.two_l + sz.bl + i * l_rows, l_rows), v, sz.cl)

    for k, src in enumerate((top_ref, bottom_ref)):
        g_first = 0 if k == 0 else (sz.rg + 1) * sz.bg
        l_first = sz.two_l + (0 if k == 0 else (sz.rl + 1) * sz.bl)

        @pl.loop(0, sz.bg // g_rows)
        def _(i):
            v = src[rows_at(i * g_rows, g_rows), :].astype(f32)
            put_variants(refs, rows_at(g_first + i * g_rows, g_rows), v, sz.cg)

        @pl.loop(0, sz.bl // l_rows)
        def _(i):
            v = src[rows_at(sz.bg + i * l_rows, l_rows), :].astype(f32)
            put_variants(refs, rows_at(l_first + i * l_rows, l_rows), v, sz.cl)

    @pl.loop(0, 2)
    def _(half):
        cols = pl.ds(pl.multiple_of(half * HALF, HALF), HALF)
        for part, first, n_all, n_rows in (
            ("g", 0, sz.mg, sz.mg // 2),
            ("l", sz.mg, sz.ml, sz.ml),
        ):
            for k in range(n_all // n_rows):
                dn_ref[first + k * n_rows : first + (k + 1) * n_rows, cols] = conv_product(
                    shift_windows(windows_two(sz, refs, part, True), k * n_rows),
                    bd_ref,
                    half,
                    n_rows,
                    True,
                )

    slope_pass(sz.m, dn_ref, z_ref, nrm_ref, st_ref, sums)


def slope_pass(n_all, dn_ref, z_ref, nrm_ref, st_ref, sums):
    mean = nrm_ref[0:1, :]
    inverse = nrm_ref[1:2, :]
    scale = nrm_ref[2:3, :]
    shift = nrm_ref[3:4, :]
    sums[...] = jnp.zeros_like(sums)

    @pl.loop(0, n_all // ROWS)
    def _(i):
        rows = rows_at(i * ROWS, ROWS)
        z = z_ref[rows, :]
        dn = dn_ref[rows, :] * silu_slope(z * scale + shift)
        dn_ref[rows, :] = dn
        sums[0:8, :] += fold(dn)
        sums[8:16, :] += fold(dn * ((z - mean) * inverse))

    put_rows(st_ref, [sums[0:8, :], sums[8:16, :]])


def middle_back_kernel(
    sz,
    dn_d_ref,
    zd_ref,
    t0,
    t1,
    t2,
    t3,
    nrm_d_ref,
    w_ref,
    dpre_ref,
    pre_ref,
    zc_ref,
    x_ref,
    s_ref,
    nrm_c_ref,
    nrm_a_ref,
    dz_ref,
    dn_ref,
    st_ref,
    zs,
    sums,
):
    strided_product(sz, x_ref, s_ref, zs)
    terms = back_terms(gather_sum((t0, t1, t2, t3)), 0, 1, sz.amount, nrm_d_ref, 0)

    @pl.loop(0, sz.m // ROWS)
    def _(i):
        rows = rows_at(i * ROWS, ROWS)
        dz_ref[rows, :] = norm_back(dn_d_ref[rows, :], zd_ref[rows, :], terms).astype(bf16)

    n_rows = sz.m // PARTS

    @pl.loop(0, PARTS)
    def _(i):
        rows = rows_at(i * n_rows, n_rows)
        dn_ref[rows, :] = dot_t(dz_ref[rows, :], w_ref[...])

    mean_c = nrm_c_ref[0:1, :]
    inverse_c = nrm_c_ref[1:2, :]
    mean_s = nrm_a_ref[4:5, :]
    inverse_s = nrm_a_ref[5:6, :]
    sums[...] = jnp.zeros_like(sums)

    @pl.loop(0, sz.m // ROWS)
    def _(i):
        rows = rows_at(i * ROWS, ROWS)
        dn = (dn_ref[rows, :] + dpre_ref[rows, :]) * silu_slope(pre_ref[rows, :])
        dn_ref[rows, :] = dn
        sums[0:8, :] += fold(dn)
        sums[8:16, :] += fold(dn * ((zc_ref[rows, :] - mean_c) * inverse_c))
        sums[16:24, :] += fold(dn * ((zs[rows, :] - mean_s) * inverse_s))

    put_rows(st_ref, [sums[0:8, :], sums[8:16, :], sums[16:24, :]])


def first_conv_back_kernel(sz, dz_ref, below_ref, k_ref, v0, v1, bd_ref):
    block_diagonal(k_ref, bd_ref)
    g_rows, l_rows = segments(sz)

    def put(rows, v, width):
        v0[rows, :] = v.astype(bf16)
        v1[rows, :] = shifted(v, 1, width).astype(bf16)

    for src, g_src, l_src, g_dst, l_dst, g_all, l_all in (
        (dz_ref, 0, sz.mg, 0, sz.one_l, sz.mg, sz.ml),
        (below_ref, 0, sz.bg, sz.mg, sz.one_l + sz.ml, sz.bg, sz.bl),
    ):

        @pl.loop(0, g_all // g_rows)
        def _(i):
            v = src[rows_at(g_src + i * g_rows, g_rows), :].astype(f32)
            put(rows_at(g_dst + i * g_rows, g_rows), v, sz.cg)

        @pl.loop(0, l_all // l_rows)
        def _(i):
            v = src[rows_at(l_src + i * l_rows, l_rows), :].astype(f32)
            put(rows_at(l_dst + i * l_rows, l_rows), v, sz.cl)


def parity_back_kernel(sz, phase, v0, v1, bd_ref, x_ref, w_ref, nrm_ref, *refs):
    if phase:
        st_in, dn_ref, st_ref, zs, da, sums = refs
    else:
        dn_ref, st_ref, zs, da, sums = refs
    mean = nrm_ref[0:1, :]
    inverse = nrm_ref[1:2, :]
    scale = nrm_ref[2:3, :]
    shift = nrm_ref[3:4, :]
    sums[...] = jnp.zeros_like(sums)
    third = sz.m // PARTS
    pr, pc = phase // 2, phase % 2
    taps = []
    for a, down in (((1, 0),), ((2, 0), (0, 1)))[pr]:
        for b, right in (((1, 0),), ((2, 0), (0, 1)))[pc]:
            taps.append((3 * a + b, down, right))

    @pl.loop(0, 2)
    def _(half):
        cols = pl.ds(pl.multiple_of(half * HALF, HALF), HALF)
        for first, base, block, n_all, n_rows in (
            (0, 0, sz.bg, sz.mg, sz.mg // 2),
            (sz.mg, sz.one_l, sz.bl, sz.ml, sz.ml),
        ):
            for k in range(n_all // n_rows):
                windows = [
                    (tap, (v0, v1)[right], base + down * block + k * n_rows)
                    for tap, down, right in taps
                ]
                da[first + k * n_rows : first + (k + 1) * n_rows, cols] = conv_product(
                    windows, bd_ref, half, n_rows, True
                )

    @pl.loop(0, PARTS)
    def _(i):
        zs[rows_at(i * third, third), :] = dot(
            x_ref[rows_at(phase * sz.m + i * third, third), :], w_ref[...]
        )

    @pl.loop(0, sz.m // ROWS)
    def _(i):
        rows = rows_at(i * ROWS, ROWS)
        z = zs[rows, :]
        dn = da[rows, :] * silu_slope(z * scale + shift)
        dn_ref[rows, :] = dn.astype(bf16)
        sums[0:8, :] += fold(dn)
        sums[8:16, :] += fold(dn * ((z - mean) * inverse))

    put_rows(st_ref, [sums[0:8, :], sums[8:16, :]])
    if phase:
        st_ref[...] += st_in[...]


def image_norm_back_kernel(sz, dn0, dn1, dn2, dn3, x_ref, w_ref, t0, t1, t2, t3, nrm_ref, dz_ref, zs):
    terms = back_terms(gather_sum((t0, t1, t2, t3)), 0, 1, 4 * sz.amount, nrm_ref, 0)
    zs[...] = dot(x_ref[...], w_ref[...])
    for phase in range(4):

        @pl.loop(0, sz.m // ROWS)
        def _(i):
            rows = rows_at(i * ROWS, ROWS)
            rows_all = rows_at(phase * sz.m + i * ROWS, ROWS)
            dz_ref[rows_all, :] = norm_back(
                (dn0, dn1, dn2, dn3)[phase][rows, :].astype(f32), zs[rows_all, :], terms
            ).astype(bf16)


def image_product_kernel(sz, dz_ref, w_ref, dzs_ref, ws_ref, dx_ref):
    dx_ref[...] = dot_t(dz_ref[...], w_ref[...])
    dx_ref[0 : sz.m, :] += dot_t(dzs_ref[...], ws_ref[...])


def place_kernel(n_crops, height, width, first_row, block, m, dx_ref, o_ref, mark_ref, s_ref, t_ref):
    half = width // 2
    mark_ref[...] = jnp.zeros_like(mark_ref)
    count = s_ref.shape[0]

    @pl.loop(0, n_crops // count)
    def _(step):
        for c in range(count):
            n = step * count + c
            for r in range(height):
                for pc in range(2):
                    at = (2 * (r % 2) + pc) * m + first_row + (r // 2) * block + n * half
                    v = dx_ref[rows_at(at, half, 8), :]
                    rows = pl.ds(r * width + pc, half, stride=2)
                    s_ref[c, rows, :] = v[:, :128]
                    t_ref[c, rows, :] = jnp.concatenate([v[:, 128:], v[:, 128:]], axis=1)
        for c in range(count):
            n = step * count + c
            o_ref[n, :, :, 0:128] = s_ref[c].reshape(height, width, 128)
            o_ref[n, :, :, 128:CIN] = t_ref[c][:, :64].reshape(height, width, 64)


def over_height(x):
    n = lax.axis_size("height")
    return [x] + [lax.ppermute(x, "height", [(i, i ^ k) for i in range(n)]) for k in range(1, n)]


def step_down(x):
    n = lax.axis_size("height")
    return lax.ppermute(x, "height", [(i, i + 1) for i in range(n - 1)])


def step_up(x):
    n = lax.axis_size("height")
    return lax.ppermute(x, "height", [(i + 1, i) for i in range(n - 1)])


MATRIX_ROWS = [a * b // C for a, b in matrix_shapes()]
ROW_BOUNDS = [int(v) for v in np.cumsum([0] + MATRIX_ROWS)]
UNIT = 112


def across(x, mask, senders=None):
    n = lax.axis_size("batch")
    return lax.ppermute(
        x, "batch", [(i, i ^ mask) for i in range(n) if senders is None or i in senders]
    )


def take_flat(whole, start, width, low_ref, value, slots):
    if width == 128:
        for j in range(C // 128):
            value[pl.ds(j, width, stride=C // 128), :] = whole[
                start : start + width, j * 128 : (j + 1) * 128
            ]
    else:
        n_lines = width // int(np.gcd(C, width))
        n_groups = width // n_lines
        per = C // n_groups
        lane = lax.broadcasted_iota(jnp.int32, (n_groups, C), 1)
        blocks = [[] for _ in range(n_lines)]
        for j in range(C // 128):
            slots[0:width, :] = whole[start : start + width, j * 128 : (j + 1) * 128]
            for k in range(n_lines):
                blocks[k].append(slots[pl.ds(k, n_groups, stride=n_lines), :])
        lines = [jnp.concatenate(block, axis=1) for block in blocks]
        for u in range(per):
            line, at = divmod(u * width, C)
            row = pltpu.roll(lines[line], C - at, 1) if at else lines[line]
            if at + width > C:
                row = jnp.where(lane < C - at, row, pltpu.roll(lines[line + 1], C - at, 1))
            value[pl.ds(u, n_groups, stride=per), :] = jnp.where(lane < width, row, 0.0)[:, 0:128]
    low_ref[...] = value[...].astype(bf16)


def assemble_kernel(n_rows, idx_ref, *refs):
    ins, outs = refs[:2], refs[2:-4]
    shards, whole, value, slots = refs[-4:]
    for core, ref in enumerate(ins):
        for q in range(4):
            for k in range(4):
                at = (idx_ref[0] ^ (2 * q + core)) * 4 + (idx_ref[1] ^ k)
                shards[at] = ref[4 * q + k].astype(f32)
    for s in range(32):
        whole[s * n_rows : (s + 1) * n_rows, :] = shards[s, 0:n_rows, :]
    for k, (ref, start) in enumerate(zip(outs, ROW_BOUNDS)):
        if k in (2, 8):
            take_flat(whole, start, MATRIX_ROWS[k], ref, value, slots)
        elif k in (3, 9):
            n = MATRIX_ROWS[k]
            value[0:HID, :] = jnp.zeros((HID, 128), f32)
            for j in range(C // 128):
                value[0:n, :] = whole[start : start + n, j * 128 : (j + 1) * 128]
                ref[:, j * 128 : (j + 1) * 128] = value[0:HID, :].astype(bf16)
        else:
            ref[...] = whole[start : start + ref.shape[0], :].astype(bf16)


def merge_kernel(*refs):
    *ins, merged = refs
    n = ins[0].shape[0]
    for q, ref in enumerate(ins):
        merged[q * n : (q + 1) * n] = ref[...]


def gather_weights(lines, n_rows, place_ids, beside):
    (mine,) = call(
        functools.partial(round_rows_kernel, n_rows),
        [out((UNIT, C), bf16)],
        [],
        lines,
        name="round_weights",
        after=[place_ids],
    )
    quarter = jnp.stack(over_height(mine))
    after, extra = beside(quarter)
    planes = [quarter] + [across(quarter, mask) for mask in (2, 4, 6)]
    (merged,) = call(
        merge_kernel, [out((16, UNIT, C), bf16)], [], *planes, name="merge_planes", after=after
    )
    planes = [merged, across(merged, 1)]
    matrices = call(
        functools.partial(assemble_kernel, n_rows),
        [
            out((C, HID) if k in (2, 8) else (HID if k in (3, 9) else rows, C), bf16)
            for k, rows in enumerate(MATRIX_ROWS)
        ],
        [
            pltpu.VMEM((32, UNIT, C), f32),
            pltpu.VMEM((32 * n_rows, C), f32),
            pltpu.VMEM((C, 128), f32),
            pltpu.VMEM((HID, 128), f32),
        ],
        place_ids,
        *planes,
        smem=1,
        name="assemble",
        room=6 * 2**20,
    )
    return matrices, extra


def pack_kernel(n_rows, first_shard, sources, core_ref, *refs):
    n_src = len(sources)
    ins, (mine_ref, other_ref, buf) = refs[:n_src], refs[n_src:]
    for shard in range(buf.shape[0]):
        low = (first_shard + shard) * n_rows
        for (start, stop), ref in zip(sources, ins):
            a, b = max(low, start), min(low + n_rows, stop)
            if a < b:
                buf[shard, a - low : b - low, :] = ref[a - start : b - start, :]
        buf[shard, n_rows:, :] = jnp.zeros((UNIT - n_rows, C), f32)
    core = core_of(core_ref)
    for unit in range(buf.shape[0] // 8):
        for h in range(4):
            mine_ref[unit * 4 + h] = buf[(unit * 2 + core) * 4 + h]
            other_ref[unit * 4 + h] = buf[(unit * 2 + 1 - core) * 4 + h].astype(bf16)


def pack(n_rows, first_unit, n_units, sources, arrays, place_ids, name, after=()):
    shape = (4 * n_units, UNIT, C)
    mine, other = call(
        functools.partial(pack_kernel, n_rows, 8 * first_unit, sources),
        [out(shape), out(shape, bf16)],
        [pltpu.VMEM((8 * n_units, UNIT, C), f32)],
        place_ids,
        *arrays,
        smem=1,
        name=name,
        after=after,
    )
    return mine, across(other, 1)


def sum_core_kernel(place_ref, a_ref, b_ref, sum_ref, *low_refs):
    sum_ref[...] = a_ref[...] + b_ref[...].astype(f32)
    first = jnp.where(y_of(place_ref) == 0, 4, 0)
    for k, ref in enumerate(low_refs):
        for i in range(2):
            ref[i] = sum_ref[first + 2 * k + i].astype(bf16)


def unit_parts_kernel(place_ref, sum_ref, g0, g1, g2, g3, keep_ref, send_ref, got_ref):
    for k, ref in enumerate((g0, g1, g2, g3)):
        got_ref[2 * k : 2 * k + 2] = ref[...]
    y, x = y_of(place_ref), x_of(place_ref)
    for h in range(4):
        mine, other = 4 * x * y + h, 4 * (1 - x) * y + h
        keep_ref[h] = sum_ref[4 * y + mine] + got_ref[mine].astype(f32)
        send_ref[h] = (sum_ref[4 * y + other] + got_ref[other].astype(f32)).astype(bf16)


def shard_parts_kernel(place_ref, sum_ref, got_ref, keep_ref, s1, s2, s3):
    for k, ref in enumerate((keep_ref, s1, s2, s3)):
        at = place_ref[1] ^ k
        ref[...] = (sum_ref[at] + got_ref[at].astype(f32)).astype(ref.dtype)


def sum_low_kernel(*refs):
    *ins, sum_ref, low_ref = refs
    total = ins[0][...]
    for ref in ins[1:]:
        total = total + ref[...].astype(f32)
    sum_ref[...] = total
    low_ref[...] = total.astype(bf16)


class EarlySum:
    def __init__(self, n_rows, place_ids):
        self.n_rows, self.ids = n_rows, place_ids

    def pack(self, sources, arrays):
        self.mine, self.got = pack(
            self.n_rows, 1, 3, sources, arrays, self.ids, "pack_early"
        )
        return [self.mine]

    def y(self, after):
        shape = (12, UNIT, C)
        self.total, *lows = call(
            sum_core_kernel,
            [out(shape)] + [out((2, UNIT, C), bf16)] * 4,
            [],
            self.ids,
            self.mine,
            self.got,
            smem=1,
            name="sum_core",
            after=after,
        )
        self.pieces = [
            across(low, 4, None if k < 2 else [0, 1, 2, 3]) for k, low in enumerate(lows)
        ]
        return [self.total]

    def x(self, after):
        four = (4, UNIT, C)
        self.keep, send = call(
            unit_parts_kernel,
            [out(four), out(four, bf16)],
            [pltpu.VMEM((8, UNIT, C), bf16)],
            self.ids,
            self.total,
            *self.pieces,
            smem=1,
            name="unit_parts",
            after=after,
        )
        self.got = across(send, 2, [0, 1, 4, 5, 6, 7])
        return [self.keep]

    def height(self, after):
        self.result = spread_height(
            self.keep, self.got, self.ids, "shard_parts", after, range(2, 8)
        )
        return [self.result[0]]


def spread_height(keep, got, place_ids, name, after, lines):
    low = out((UNIT, C), bf16)
    mine, *sends = call(
        shard_parts_kernel,
        [out((UNIT, C)), low, low, low],
        [],
        place_ids,
        keep,
        got,
        smem=1,
        name=name,
        after=after,
    )
    return [mine] + [
        lax.ppermute(
            send, both_axes, [(4 * b + h, 4 * b + (h ^ k)) for b in lines for h in range(4)]
        )
        for k, send in zip((1, 2, 3), sends)
    ]


def sum_last_unit(n_rows, sources, arrays, place_ids, work):
    mine, got = pack(n_rows, 0, 1, sources, arrays, place_ids, "pack_last")
    beside = work.pop(0)([mine])
    parts = spread_height(mine, got, place_ids, "height_parts", beside, range(8))
    beside = []
    while work:
        beside = beside + work.pop(0)([parts[0]])
    total, low = call(
        sum_low_kernel,
        [out((UNIT, C)), out((UNIT, C), bf16)],
        [],
        *parts,
        name="sum_height",
        after=beside,
    )
    return [total] + [across(low, mask, [mask, mask + 1]) for mask in (2, 4, 6)]


def lamb_kernel(
    n_rows,
    place_ref,
    a0,
    a1,
    a2,
    a3,
    b0,
    b1,
    b2,
    b3,
    w_ref,
    m_ref,
    v_ref,
    first_ref,
    second_ref,
    update_ref,
    sums_ref,
    g_ref,
):
    shard = place_ref[0] * 4 + place_ref[1]
    early = a0[...] + a1[...].astype(f32) + a2[...].astype(f32) + a3[...].astype(f32)
    last = b0[...] + b1[...].astype(f32) + b2[...].astype(f32) + b3[...].astype(f32)
    g_ref[...] = jnp.where(place_ref[0] < 2, last, early)
    w, m, v = (as_rows(ref, n_rows) for ref in (w_ref, m_ref, v_ref))
    first, second, update = lamb_terms(w, g_ref[0:n_rows, :], m, v, weight_decay)
    put_as_lines(first_ref, first)
    put_as_lines(second_ref, second)
    update_ref[...] = update
    member = membership(n_rows, shard)
    sums_ref[...] = jnp.zeros_like(sums_ref)
    for k, value in enumerate((w, update)):
        by_row = jnp.sum(value * value, axis=1, keepdims=True)
        sums_ref[k : k + 1, 0:128] = jnp.sum(member * by_row, axis=0, keepdims=True)


def membership(n_rows, shard):
    row = lax.broadcasted_iota(jnp.int32, (n_rows, 128), 0) + shard * n_rows
    lane = lax.broadcasted_iota(jnp.int32, (n_rows, 128), 1)
    result = jnp.zeros((n_rows, 128), f32)
    for k in range(len(MATRIX_ROWS)):
        inside = (row >= ROW_BOUNDS[k]) & (row < ROW_BOUNDS[k + 1]) & (lane == k)
        result = jnp.where(inside, 1.0, result)
    return result


VEC_ROWS = 24


LINES = 72
LINE_F1 = 4 * C // 128
LINE_E2 = LINE_F1 + (E2 - F1) * C // 128
LINE_F2 = LINE_E2 + SE_B // 128


def as_lines(flat):
    return jnp.pad(flat, (0, LINES * 128 - flat.shape[0])).reshape(LINES, 128)


def from_lines(lines):
    return lines.reshape(-1)[: sum(vector_sizes())]


def line_pieces():
    return ((LINE_F1, F1, E2 - F1), (LINE_F2, F2, 18 - F2))


def tables_kernel(*refs):
    lines = refs[-1]
    n = len(refs) // 2
    lane = lax.broadcasted_iota(jnp.int32, (LINES, 128), 1)
    for src, dst in zip(refs[:n], refs[n : 2 * n]):
        dst[...] = jnp.zeros_like(dst)
        for j in range(C // 128):
            dst[0:4, j * 128 : (j + 1) * 128] = src[pl.ds(j, 4, stride=C // 128), :]
        head = src[LINE_F1 : LINE_F1 + 1, :]
        dst[E1 : E1 + 1, 0:128] = jnp.where(lane[0:1] < SE_A, head, 0.0)
        here = pltpu.roll(src[...], 128 - SE_A, 1)
        below = pltpu.roll(here, LINES - 1, 0)
        lines[...] = jnp.where(lane < 128 - SE_A, here, below)
        dst[E2 : E2 + 1, 0:128] = lines[LINE_E2 : LINE_E2 + 1, :]
        for line, row, count in line_pieces():
            for j in range(C // 128):
                dst[row : row + count, j * 128 : (j + 1) * 128] = lines[
                    pl.ds(line + j, count, stride=C // 128), :
                ]


def put_lines(table, dst, lines):
    lane = lax.broadcasted_iota(jnp.int32, (LINES, 128), 1)
    line_at = lax.broadcasted_iota(jnp.int32, (LINES, 128), 0)
    lines[...] = jnp.zeros_like(lines)
    lines[LINE_F1 : LINE_F1 + 1, :] = pltpu.roll(table[E1 : E1 + 1, 0:128], 128 - SE_A, 1)
    lines[LINE_E2 + 1 : LINE_E2 + 2, :] = table[E2 : E2 + 1, 0:128]
    for line, row, count in line_pieces():
        for j in range(C // 128):
            lines[pl.ds(line + 1 + j, count, stride=C // 128), :] = table[
                row : row + count, j * 128 : (j + 1) * 128
            ]
    before = pltpu.roll(lines[...], SE_A, 1)
    here = pltpu.roll(before, LINES - 1, 0)
    dst[...] = jnp.where(lane < SE_A, before, here)
    for j in range(C // 128):
        dst[pl.ds(j, 4, stride=C // 128), :] = table[0:4, j * 128 : (j + 1) * 128]


def as_rows(ref, n_rows):
    return jnp.concatenate(
        [ref[pl.ds(j, n_rows, stride=C // 128), :] for j in range(C // 128)], axis=1
    )


def put_as_lines(ref, value):
    for j in range(C // 128):
        ref[pl.ds(j, value.shape[0], stride=C // 128), :] = value[:, j * 128 : (j + 1) * 128]


def round_rows_kernel(n_rows, *refs):
    n = len(refs) // 2
    for src, dst in zip(refs[:n], refs[n:]):
        rows = as_rows(src, n_rows)
        fill = jnp.zeros((dst.shape[0] - n_rows, C), f32)
        dst[...] = jnp.concatenate([rows, fill], axis=0).astype(bf16)


def vector_grads_kernel(a, b, cs, d, e, f, de1, df1, de2, df2, sums_ref, o_ref):
    o_ref[...] = jnp.zeros_like(o_ref)
    plan = [
        (G1A, a, 1),
        (B1A, a, 0),
        (G1B, b, 1),
        (B1B, b, 0),
        (F1, df1, 0),
        (G1C, cs, 1),
        (B1C, cs, 0),
        (G1S, cs, 2),
        (B1S, cs, 0),
        (G2A, d, 1),
        (B2A, d, 0),
        (G2B, e, 1),
        (B2B, e, 0),
        (F2, df2, 0),
        (G2C, f, 1),
        (B2C, f, 0),
    ]
    for row, ref, k in plan:
        o_ref[row : row + 1, :] = ref[k : k + 1, :]
    o_ref[E1 : E1 + 1, 0:HID] = de1[0:1, :]
    o_ref[E2 : E2 + 1, 0:HID] = de2[0:1, :]
    o_ref[VEC_ROWS : VEC_ROWS + 8, :] = sums_ref[...]


def finish_kernel(
    n_rows,
    place_ref,
    r0,
    r1,
    r2,
    r3,
    w_ref,
    update_ref,
    vec_ref,
    vf_ref,
    vs_ref,
    new_w_ref,
    new_v_ref,
    new_vf_ref,
    new_vs_ref,
    norm_ref,
    slots,
    lines,
):
    place = place_ref[1]
    shard = place_ref[0] * 4 + place
    for k, ref in enumerate((r0, r1, r2, r3)):
        slots[place ^ k] = ref[...]
    total = slots[0] + slots[1] + slots[2] + slots[3]
    norms = jnp.sqrt(total[VEC_ROWS : VEC_ROWS + 8, 0:128])
    norm_ref[...] = norms
    lane = lax.broadcasted_iota(jnp.int32, (1, 128), 1)
    ratio = jnp.where(
        lane < len(MATRIX_ROWS), learn_rate * (norms[0:1] / norms[1:2]), 0.0
    )
    by_row = jnp.sum(membership(n_rows, shard) * ratio, axis=1, keepdims=True)
    put_as_lines(new_w_ref, as_rows(w_ref, n_rows) - by_row * update_ref[...])
    vec = vec_ref[...]
    first, second, update = lamb_terms(vec, total[0:VEC_ROWS], vf_ref[...], vs_ref[...], 0.0)
    put_lines(first, new_vf_ref, lines)
    put_lines(second, new_vs_ref, lines)
    size = jnp.sqrt(jnp.sum(vec * vec, axis=1, keepdims=True))
    change = jnp.sqrt(jnp.sum(update * update, axis=1, keepdims=True))
    put_lines(vec - learn_rate * (size / change) * update, new_v_ref, lines)


def lamb_terms(param, grad_val, first_old, second_old, decay):
    first_new = beta_one * first_old + (1.0 - beta_one) * grad_val
    second_new = beta_two * second_old + (1.0 - beta_two) * grad_val * grad_val
    update = (
        first_new
        / (1.0 - beta_one**STEP)
        / (jnp.sqrt(second_new / (1.0 - beta_two**STEP)) + adam_eps)
        + decay * param
    )
    return (first_new, second_new, update)


def body(
    image_glob,
    image_loc,
    cot_glob,
    cot_loc,
    weights,
    first_moment,
    second_moment,
    vectors,
    vec_first,
    vec_second,
):
    n_height = lax.axis_size("height")
    place = lax.axis_index("height")
    sz = Sizes(image_glob, image_loc, n_height)
    m = sz.m
    part = functools.partial
    place_ids = jnp.stack([lax.axis_index("batch"), place]).astype(jnp.int32)
    shapes = matrix_shapes()
    mat_lengths = [dims_pair[0] * dims_pair[1] for dims_pair in shapes]
    def prepare(before):
        x, x_edge = call(
            part(prepare_kernel, sz),
            [out((4 * m, CIN), bf16), out((2 * sz.edge, CIN), bf16)],
            [pltpu.VMEM((sz.hg * sz.wg, 128), f32)] * 2,
            image_glob,
            image_loc,
            name="prepare",
            after=before,
            room=6 * 2**20,
        )
        x_above = step_down(x_edge)
        gram_scr = pltpu.VMEM((CIN + 8, CIN), f32)
        (gram,) = call(part(gram_kernel, sz), [out(PACKED)], [gram_scr], x, name="gram", after=[x_above])
        gram = over_height(gram)
        return x, x_above, gram, gram_scr

    by_rows = (
        weights.shape[0] % C == 0
        and weights.shape[0] // C <= UNIT
        and lax.axis_size("batch") == 8
        and n_height == 4
    )
    shard_rows = weights.shape[0] // C
    table = out((VEC_ROWS, C))
    tables = call(
        tables_kernel,
        [table] * 3,
        [pltpu.VMEM((LINES, 128), f32)],
        *(as_lines(v) for v in (vectors, vec_first, vec_second)),
        name="tables",
    )
    vt = tables[0]
    early = list(tables)
    if by_rows:
        w_lines, m_lines, v_lines = (
            v.reshape(-1, 128) for v in (weights, first_moment, second_moment)
        )

    if by_rows:

        def beside(quarter):
            prepared = prepare([quarter])
            return early + [prepared[1]] + prepared[2][1:], prepared

        matrices, prepared = gather_weights(w_lines, shard_rows, place_ids, beside)
    else:
        prepared = prepare([])
        gathered = lax.all_gather(weights.astype(bf16), both_axes, axis=0, tiled=True)
        matrices = [
            flat_piece.reshape(dims_pair)
            for flat_piece, dims_pair in zip(cut_pieces(gathered, mat_lengths), shapes)
        ]
    w1, k1, d1, u1, p1, s1, w2, k2, d2, u2, p2 = matrices
    x, x_above, gram, gram_scr = prepared
    if not by_rows:
        d1 = jnp.pad(d1, ((0, 0), (0, HID - SE_A)))
        u1 = jnp.pad(u1, ((0, HID - SE_A), (0, 0)))
    st8 = out((8, C))
    mat = out((m, C))
    mat_low = out((m, C), bf16)
    pool_low = out((sz.crops, C), bf16)
    pool_scr = pltpu.VMEM((sz.crops, C), f32)
    sum_scr = pltpu.VMEM((24, C), f32)

    bd_scr = pltpu.VMEM((18, HALF, HALF), bf16)
    low_scr = pltpu.VMEM((m, C), bf16)
    mat_scr = pltpu.VMEM((m, C), f32)
    one_scr = pltpu.VMEM((sz.one, C), bf16)
    two_scr = pltpu.VMEM((sz.two, C), bf16)
    edge_scr = pltpu.VMEM((sz.edge, C), f32)
    edge = out((sz.edge, C), bf16)
    one_shape = out((sz.one, C), bf16)
    nrm_a, *act_a = call(
        part(first_act_kernel, sz),
        [st8, mat_low, mat_low, one_shape, one_shape, mat_low, one_shape],
        [mat_scr, gram_scr],
        place_ids,
        x,
        x_above,
        w1,
        *gram,
        vt,
        smem=1,
        name="first_act",
    )
    zb, st_b = call(
        part(first_conv_kernel, sz),
        [mat, st8],
        [bd_scr, sum_scr],
        x,
        s1,
        k1,
        *act_a,
        name="first_conv",
    )
    act_a = act_a[:4]
    st_b = over_height(st_b)
    pool_b, nrm_b = call(
        part(pool_kernel, sz, G1B, B1B, True), [pool_low, st8], [pool_scr], zb, *st_b, vt, name="pool_b",
    )
    pool_b = over_height(pool_b)
    hid = out((sz.crops, HID))
    crop_mat = out((sz.crops, C))
    qb, zc, st_c, gate_b, pooled_b, hidden_b = call(
        part(gated_product_kernel, sz, E1, F1),
        [mat_low, mat, st8, crop_mat, crop_mat, hid],
        [],
        zb,
        nrm_b,
        *pool_b,
        d1,
        u1,
        p1,
        vt,
        name="gated_b",
    )
    st_c = over_height(st_c)
    pre_mid, mid_low, nrm_c, mid_top, mid_bottom = call(
        part(middle_kernel, sz),
        [mat, mat_low, st8, edge, edge],
        [mat_scr],
        zc,
        x,
        s1,
        *st_c,
        nrm_b,
        vt,
        name="middle",
    )
    mid_above = step_down(mid_bottom)
    mid_below = step_up(mid_top)
    zd, st_d = call(
        part(product_kernel, sz), [mat, st8], [], mid_low, w2, name="product_d"
    )
    st_d = over_height(st_d)
    two_shape = out((sz.two, C), bf16)
    ze, st_e, nrm_d, act_d = call(
        part(second_conv_kernel, sz),
        [mat, st8, st8, two_shape],
        [two_scr, two_scr, bd_scr, edge_scr, sum_scr],
        place_ids,
        zd,
        mid_above,
        mid_below,
        w2,
        k2,
        *st_d,
        vt,
        smem=1,
        name="second_conv",
    )
    st_e = over_height(st_e)
    pool_e, nrm_e = call(
        part(pool_kernel, sz, G2B, B2B, False), [pool_low, st8], [pool_scr], ze, *st_e, vt, name="pool_e",
    )
    pool_e = over_height(pool_e)
    qe, zf, st_f, gate_e, pooled_e, hidden_e = call(
        part(gated_product_kernel, sz, E2, F2),
        [mat_low, mat, st8, crop_mat, crop_mat, hid],
        [],
        ze,
        nrm_e,
        *pool_e,
        d2,
        u2,
        p2,
        vt,
        name="gated_e",
    )
    st_f = over_height(st_f)
    out_glob, out_loc, dpre, bst_f, nrm_f = call(
        part(output_kernel, sz),
        [out(cot_glob.shape, bf16), out(cot_loc.shape, bf16), mat, st8, st8],
        [sum_scr],
        pre_mid,
        zf,
        *st_f,
        vt,
        cot_glob,
        cot_loc,
        name="output",
        room=6 * 2**20,
    )
    bst_f_all = over_height(bst_f)

    dzf, dqe, dg_e = call(
        part(gate_grad_kernel, sz, False),
        [mat_low, mat, pool_low],
        [pool_scr],
        dpre,
        zf,
        *bst_f_all,
        nrm_f,
        p2,
        ze,
        nrm_e,
        name="gate_grad_e",
    )
    dg_e = over_height(dg_e)
    (mat_f,) = call(
        weight_kernel, [out((C, C))], [], qe, dzf, name="weight_f"
    )
    dn_e, bst_e, dv_e, du_e = call(
        part(excite_back_kernel, sz),
        [mat, st8, crop_mat, hid],
        [pool_scr, sum_scr],
        dqe,
        ze,
        nrm_e,
        *dg_e,
        gate_e,
        hidden_e,
        d2,
        u2,
        name="excite_back_e",
        after=[mat_f],
    )
    bst_e_all = over_height(bst_e)
    se_outs = lambda width: [out((width, C)), out((8, HID)), out((HID, C)), st8]
    se_scr = [pltpu.VMEM((C, HID), f32), pltpu.VMEM((HID, 128), f32)]
    dd2, de2, du2, df2 = call(
        part(excite_weights_kernel, SE_B),
        se_outs(SE_B),
        se_scr,
        place_ids,
        dv_e,
        du_e,
        pooled_e,
        hidden_e,
        smem=1,
        name="excite_weights_e",
    )
    dze, dze_top, dze_bottom = call(
        part(norm_back_kernel, sz),
        [mat_low, edge, edge],
        [],
        dn_e,
        ze,
        *bst_e_all,
        nrm_e,
        name="norm_back_e",
        after=[dd2],
    )
    dze_above = step_down(dze_bottom)
    dze_below = step_up(dze_top)
    (mat_e,) = call(
        part(second_conv_weights_kernel, sz),
        [out((9 * GW, C))],
        [two_scr, two_scr],
        act_d,
        dze,
        name="second_conv_weights",
    )
    dn_d, bst_d = call(
        part(second_conv_back_kernel, sz),
        [mat, st8],
        [two_scr, two_scr, two_scr, bd_scr, sum_scr],
        dze,
        dze_above,
        dze_below,
        k2,
        zd,
        nrm_d,
        name="second_conv_back",
        after=[mat_e],
    )
    bst_d_all = over_height(bst_d)
    dzd, dn_mid, bst_cs = call(
        part(middle_back_kernel, sz),
        [mat_low, mat, st8],
        [mat_scr, sum_scr],
        dn_d,
        zd,
        *bst_d_all,
        nrm_d,
        w2,
        dpre,
        pre_mid,
        zc,
        x,
        s1,
        nrm_c,
        nrm_b,
        name="middle_back",
    )
    bst_cs_all = over_height(bst_cs)
    spans = list(zip(ROW_BOUNDS[:-1], ROW_BOUNDS[1:]))
    early = EarlySum(shard_rows, place_ids)
    dzc, dzs, dqb, dg_b = call(
        part(gate_grad_kernel, sz, True),
        [mat_low, mat_low, mat, pool_low],
        [pool_scr, mat_scr],
        dn_mid,
        zc,
        *bst_cs_all,
        nrm_c,
        p1,
        zb,
        nrm_b,
        x,
        s1,
        nrm_b,
        name="gate_grad_b",
    )
    dg_b = over_height(dg_b)
    (mat_d,) = call(
        weight_kernel,
        [out((C, C))],
        [],
        mid_low,
        dzd,
        name="weight_d",
        after=[dzc],
    )
    (mat_c,) = call(
        weight_kernel, [out((C, C))], [], qb, dzc, name="weight_c"
    )
    (mat_s,) = call(
        weight_kernel, [out((CIN, C))], [], x, dzs, name="weight_s"
    )
    dn_b, bst_b, dv_b, du_b = call(
        part(excite_back_kernel, sz),
        [mat, st8, crop_mat, hid],
        [pool_scr, sum_scr],
        dqb,
        zb,
        nrm_b,
        *dg_b,
        gate_b,
        hidden_b,
        d1,
        u1,
        name="excite_back_b",
        after=[mat_d, mat_c, mat_s],
    )
    bst_b_all = over_height(bst_b)
    dd1, de1, du1, df1 = call(
        part(excite_weights_kernel, SE_A),
        se_outs(SE_A),
        se_scr,
        place_ids,
        dv_b,
        du_b,
        pooled_b,
        hidden_b,
        smem=1,
        name="excite_weights_b",
    )
    dzb, dzb_top = call(
        part(norm_back_kernel, sz),
        [mat_low, edge],
        [],
        dn_b,
        zb,
        *bst_b_all,
        nrm_b,
        name="norm_back_b",
        after=early.pack(spans[3:], [du1, mat_c, mat_s, mat_d, mat_e, dd2, du2, mat_f])
        if by_rows
        else [dd1],
    )
    dzb_below = step_up(dzb_top)
    (mat_b,) = call(
        part(first_conv_weights_kernel, sz),
        [out((9 * GW, C))],
        [low_scr, one_scr],
        *act_a,
        dzb,
        name="first_conv_weights",
    )
    hold = [mat_b]
    if by_rows:
        hold = hold + early.y([])
    v0, v1, bd1 = call(
        part(first_conv_back_kernel, sz),
        [one_shape, one_shape, out((18, HALF, HALF), bf16)],
        [],
        dzb,
        dzb_below,
        k1,
        name="first_conv_back",
        after=hold,
    )
    dn_a, bst_a = [], []
    hold = [[], [], [], []]
    if by_rows:
        hold[2] = early.pieces[0:1]
        hold[3] = early.pieces[1:2]
    for phase in range(4):
        dn_phase, *bst_a = call(
            part(parity_back_kernel, sz, phase),
            [mat_low, st8],
            [mat_scr, mat_scr, sum_scr],
            v0,
            v1,
            bd1,
            x,
            w1,
            nrm_a,
            *bst_a,
            name="parity_back_%d" % phase,
            after=hold[phase],
        )
        dn_a.append(dn_phase)
    (bst_a,) = bst_a
    bst_a_all = over_height(bst_a)
    hold = []
    if by_rows:
        hold = early.x([bst_a])
    (dza,) = call(
        part(image_norm_back_kernel, sz),
        [out((4 * m, C), bf16)],
        [pltpu.VMEM((4 * m, C), f32)],
        *dn_a,
        x,
        w1,
        *bst_a_all,
        nrm_a,
        name="image_norm_back",
        after=hold,
    )
    (mat_a,) = call(
        weight_kernel,
        [out((CIN, C))],
        [],
        x,
        dza,
        name="weight_a",

    )
    made = {}

    def image_product(beside):
        (made["dx"],) = call(
            part(image_product_kernel, sz),
            [out((4 * m, CIN))],
            [],
            dza,
            w1,
            dzs,
            s1,
            name="image_product",
            after=beside,
        )
        return [made["dx"]]

    def place_maps(key, shape, first_row, block, beside):
        n_crops, height, width = shape[:3]
        made[key], mark = call(
            part(place_kernel, n_crops, height, width, first_row, block, m),
            [out(shape), out((8, 128))],
            [pltpu.VMEM((6, height * width, 128), f32)] * 2,
            made["dx"],
            name="place_" + key,
            room=8 * 2**20,
            after=beside,
        )
        return [mark]

    work = [
        image_product,
        lambda beside: place_maps("glob", image_glob.shape, 0, sz.bg, beside),
        lambda beside: place_maps("loc", image_loc.shape, sz.mg, sz.bl, beside),
    ]
    if not by_rows:
        for one_work in work:
            one_work([])
    if by_rows:
        early.height([dza])
        last = sum_last_unit(
            shard_rows, spans[:4], [mat_a, mat_b, dd1, du1], place_ids, work
        )
        shard_out = out((shard_rows, C))
        lines_out = out(w_lines.shape)
        new_first, new_second, update, sums = call(
            part(lamb_kernel, shard_rows),
            [lines_out, lines_out, shard_out, st8],
            [pltpu.VMEM((UNIT, C), f32)],
            place_ids,
            *early.result,
            *last,
            w_lines,
            m_lines,
            v_lines,
            smem=1,
            name="lamb",
        )
        (small,) = call(
            vector_grads_kernel,
            [out((VEC_ROWS + 8, C))],
            [],
            bst_a,
            bst_b,
            bst_cs,
            bst_d,
            bst_e,
            bst_f,
            de1,
            df1,
            de2,
            df2,
            sums,
            name="vector_grads",
        )
        small = small + across(small, 1)
        other_x, other_y, other_both = (across(small, mask) for mask in (2, 4, 6))
        small = (small + other_x) + (other_y + other_both)
        new_weights, new_v, new_vf, new_vs, norms = call(
            part(finish_kernel, shard_rows),
            [lines_out] + [out((LINES, 128))] * 3 + [out((8, 128))],
            [pltpu.VMEM((4, VEC_ROWS + 8, C), f32), pltpu.VMEM((LINES, 128), f32)],
            place_ids,
            *over_height(small),
            w_lines,
            update,
            *tables,
            smem=1,
            name="finish",
            room=2 * 2**20,
        )
        maps_out = (out_glob, out_loc, made["glob"], made["loc"])
        return maps_out + (
            new_weights.reshape(-1),
            new_first.reshape(-1),
            new_second.reshape(-1),
            from_lines(new_v),
            from_lines(new_vf),
            from_lines(new_vs),
            norms[:2, : len(MATRIX_ROWS)],
        )

    maps_out = (out_glob, out_loc, made["glob"], made["loc"])
    flat_grad = jnp.concatenate(
        [
            piece.reshape(-1)
            for piece in (
                mat_a,
                mat_b,
                dd1,
                du1[:SE_A],
                mat_c,
                mat_s,
                mat_d,
                mat_e,
                dd2,
                du2,
                mat_f,
            )
        ]
    )
    vec_grad = jnp.concatenate(
        [
            bst_a[1],
            bst_a[0],
            bst_b[1],
            bst_b[0],
            de1[0, :SE_A],
            df1[0],
            bst_cs[1],
            bst_cs[0],
            bst_cs[2],
            bst_cs[0],
            bst_d[1],
            bst_d[0],
            bst_e[1],
            bst_e[0],
            de2[0],
            df2[0],
            bst_f[1],
            bst_f[0],
        ]
    )
    grad_shard = lax.psum_scatter(flat_grad, both_axes, scatter_dimension=0, tiled=True)
    shard_len = weights.shape[0]
    device_index = lax.axis_index("batch") * n_height + lax.axis_index("height")
    position = device_index * shard_len + lax.iota(jnp.int32, shard_len)
    bounds = np.cumsum([0] + mat_lengths)
    lower_edge = jnp.asarray(bounds[:-1], jnp.int32)
    upper_edge = jnp.asarray(bounds[1:], jnp.int32)
    member = (
        (position[:, None] >= lower_edge[None, :]) & (position[:, None] < upper_edge[None, :])
    ).astype(f32)
    new_first, new_second, update = lamb_terms(
        weights, grad_shard, first_moment, second_moment, weight_decay
    )
    part_sums = jnp.dot(jnp.stack([weights * weights, update * update]), member, precision=highest)
    vec_total, totals = lax.psum((vec_grad, part_sums), both_axes)
    norm_pair = jnp.sqrt(totals)
    trust_ratio = learn_rate * (norm_pair[0] / norm_pair[1])
    new_weights = weights - jnp.dot(member, trust_ratio, precision=highest) * update
    vec_one_new, vec_two_new, vec_update = lamb_terms(vectors, vec_total, vec_first, vec_second, 0.0)
    vec_pieces = []
    for param_piece, update_piece in zip(
        cut_pieces(vectors, vector_sizes()), cut_pieces(vec_update, vector_sizes())
    ):
        ratio_val = jnp.sqrt(jnp.sum(param_piece * param_piece)) / jnp.sqrt(
            jnp.sum(update_piece * update_piece)
        )
        vec_pieces.append(param_piece - learn_rate * ratio_val * update_piece)
    new_vectors = jnp.concatenate(vec_pieces)
    return maps_out + (
        new_weights,
        new_first,
        new_second,
        new_vectors,
        vec_one_new,
        vec_two_new,
        norm_pair,
    )


def solution(mesh):
    maps = P("batch", "height", None, None)
    entries = P(("batch", "height"))
    return jax.shard_map(
        body,
        mesh=mesh,
        in_specs=(maps, maps, maps, maps, entries, entries, entries, P(), P(), P()),
        out_specs=(maps, maps, maps, maps, entries, entries, entries, P(), P(), P(), P()),
        check_vma=False,
    )
```

```python
import functools

import jax
import jax.numpy as jnp
import numpy as np
from jax import lax
from jax.experimental import pallas as pl
from jax.experimental.pallas import tpu as pltpu
from jax.sharding import PartitionSpec as P

CIN = 192
C = 512
GW = 64
GROUPS = 8
SE_A = 48
SE_B = 128
STEP = 10
HID = 128
HALF = 256

norm_eps = 1e-05
beta_one = 0.9
beta_two = 0.999
adam_eps = 1e-06
weight_decay = 0.01
learn_rate = 0.4
highest = lax.Precision.HIGHEST
bf16 = jnp.bfloat16
f32 = jnp.float32
both_axes = ("batch", "height")

G1A, B1A, G1B, B1B, E1, F1, G1C, B1C, G1S, B1S, G2A, B2A, G2B, B2B, E2, F2, G2C, B2C = range(18)


def matrix_shapes():
    return [
        (CIN, C),
        (9 * GW, C),
        (C, SE_A),
        (SE_A, C),
        (C, C),
        (CIN, C),
        (C, C),
        (9 * GW, C),
        (C, SE_B),
        (SE_B, C),
        (C, C),
    ]


def vector_sizes():
    return [C, C, C, C, SE_A, C, C, C, C, C, C, C, C, C, SE_B, C, C, C]


def cut_pieces(flat_vec, lengths):
    pieces = []
    offset = 0
    for length in lengths:
        pieces.append(flat_vec[offset : offset + length])
        offset += length
    return pieces


class Sizes:
    def __init__(self, image_glob, image_loc, n_height):
        self.ng, self.hg, self.wg = image_glob.shape[:3]
        self.nl, self.hl, self.wl = image_loc.shape[:3]
        self.rg, self.cg = self.hg // 2, self.wg // 2
        self.rl, self.cl = self.hl // 2, self.wl // 2
        self.bg, self.bl = self.ng * self.cg, self.nl * self.cl
        self.mg, self.ml = self.rg * self.bg, self.rl * self.bl
        self.m = self.mg + self.ml
        self.edge = self.bg + self.bl
        self.n_height = n_height
        self.crops = -(-(self.ng + self.nl) // 16) * 16
        self.area_g = self.rg * self.cg * n_height
        self.area_l = self.rl * self.cl * n_height
        self.amount = n_height * self.m
        self.one_l = (self.rg + 1) * self.bg
        self.one = self.one_l + (self.rl + 1) * self.bl
        self.two_l = (self.rg + 2) * self.bg
        self.two = self.two_l + (self.rl + 2) * self.bl


def sigmoid(v):
    return 0.5 * jnp.tanh(0.5 * v) + 0.5


def silu(v):
    return v * sigmoid(v)


def silu_slope(v):
    s = sigmoid(v)
    return s * (1.0 + v * (1.0 - s))


def padded_bytes(shape, dtype):
    size = np.dtype(dtype).itemsize
    dims = list(shape)
    dims[-1] = -(-dims[-1] // 128) * 128
    if len(dims) > 1:
        rows = 32 // size
        dims[-2] = -(-dims[-2] // rows) * rows
    return int(np.prod(dims)) * size


COST_SCALE = 1.0
MEASURED_US = {
    "first_conv_back": 1.5,
    "parity_back_0": 2.6,
    "parity_back_1": 3.0,
    "parity_back_2": 3.0,
    "parity_back_3": 3.7,
    "first_conv": 5.0,
    "first_act": 7.5,
    "second_conv": 6.3,
    "second_conv_back": 5.9,
    "image_norm_back": 5.8,
    "second_conv_weights": 4.9,
    "first_conv_weights": 4.5,
    "middle_back": 4.4,
    "gate_grad_b": 4.2,
    "gram": 3.6,
    "image_product": 3.6,
    "place_glob": 3.1,
    "output": 2.9,
    "assemble": 2.9,
    "gate_grad_e": 2.7,
    "excite_back_b": 2.6,
    "excite_back_e": 2.6,
    "place_loc": 2.5,
    "gated_b": 2.4,
    "gated_e": 2.4,
    "finish": 1.9,
    "middle": 1.8,
    "prepare": 1.4,
    "excite_weights_b": 1.3,
    "excite_weights_e": 1.2,
    "product_d": 1.1,
    "weight_a": 1.1,
    "pack_0": 1.0,
    "pack_1": 1.0,
    "pool_b": 1.0,
    "pool_e": 1.0,
    "lamb": 1.0,
    "weight_f": 0.9,
    "weight_d": 0.9,
    "weight_c": 0.9,
}


def call(kernel, outs, scratch, *ins, smem=0, name=None, after=(), room=0):
    held = sum(padded_bytes(s.shape, s.dtype) for s in scratch)
    n_in, n_after = len(ins), len(after)

    def run(*refs):
        kernel(*refs[:n_in], *refs[n_in + n_after :])

    return pl.pallas_call(
        run,
        out_shape=tuple(outs),
        in_specs=[pl.BlockSpec(memory_space=pltpu.SMEM)] * smem
        + [pl.BlockSpec(memory_space=pltpu.VMEM)] * (n_in - smem)
        + [pl.BlockSpec(memory_space=pl.ANY)] * n_after,
        out_specs=tuple(pl.BlockSpec(memory_space=pltpu.VMEM) for _ in outs),
        scratch_shapes=list(scratch),
        compiler_params=pltpu.CompilerParams(vmem_limit_bytes=held + 4 * 2**20 + room),
        cost_estimate=pl.CostEstimate(
            flops=int(MEASURED_US.get(name, 0.5) * COST_SCALE * 1.1535e9),
            bytes_accessed=1,
            transcendentals=0,
        ),
        name=name,
    )(*ins, *after)


def out(shape, dtype=f32):
    return jax.ShapeDtypeStruct(shape, dtype)


def above(ids, n_height=0):
    return jnp.where(ids[1] > 0, 1.0, 0.0)


def below(ids, n_height):
    return jnp.where(ids[1] < n_height - 1, 1.0, 0.0)


def first_of_height(ids):
    return jnp.where(ids[1] == 0, 1.0, 0.0)


def y_of(ids):
    return ids[0] // 4


def x_of(ids):
    return lax.rem(ids[0] // 2, 2)


def core_of(ids):
    return lax.rem(ids[0], 2)


def fold(x):
    return jnp.sum(x.reshape(x.shape[0] // 8, 8, x.shape[1]), axis=0)


def rows_at(start, size, unit=16):
    return pl.ds(pl.multiple_of(start, unit), size)


def put_rows(ref, parts):
    ref[...] = jnp.zeros_like(ref)
    for k, part in enumerate(parts):
        ref[k : k + 1, :] = jnp.sum(part, axis=0, keepdims=True)


def put_back_sums(ref, one, two, mean, inverse):
    one = jnp.sum(one, axis=0, keepdims=True)
    two = jnp.sum(two, axis=0, keepdims=True)
    put_rows(ref, [one, (two - mean * one) * inverse])


def gather_sum(refs):
    total = refs[0][...]
    for ref in refs[1:]:
        total = total + ref[...]
    return total


def norm_terms(total, row, amount, gain, shift):
    mean = total[row : row + 1] / amount
    inverse = lax.rsqrt(total[row + 1 : row + 2] / amount - mean * mean + norm_eps)
    scale = gain * inverse
    return mean, inverse, scale, shift - mean * scale


def put_norm(ref, row, terms):
    for k, term in enumerate(terms):
        ref[row + k : row + k + 1, :] = term


def dot(a, b):
    return jnp.dot(a, b, preferred_element_type=f32)


def dot_t(a, b):
    return lax.dot_general(a, b, (((1,), (1,)), ((), ())), preferred_element_type=f32)


def t_dot(a, b):
    return lax.dot_general(a, b, (((0,), (0,)), ((), ())), preferred_element_type=f32)


def prepare_kernel(sz, ig_ref, il_ref, x_ref, halo_ref, s_ref, t_ref):
    m = sz.m

    def split(x, n_rows):
        s_ref[0:n_rows, :] = x[:, :128]
        t_ref[0:n_rows, 0:64] = x[:, 128:]
        parts = []
        for pc in range(2):
            v = s_ref[pl.ds(pc, n_rows // 2, stride=2), :]
            w = t_ref[pl.ds(pc, n_rows // 2, stride=2), :]
            parts.append(jnp.concatenate([v, w[:, :64]], axis=1))
        return parts

    @pl.loop(0, sz.ng)
    def _(n):
        n_rows = sz.hg * sz.wg
        parts = split(ig_ref[n].astype(f32).reshape(n_rows, CIN), n_rows)
        for pc in range(2):
            v = parts[pc].reshape(sz.hg, sz.cg, CIN).astype(bf16)
            for r in range(sz.hg):
                phase = 2 * (r % 2) + pc
                x_ref[rows_at(phase * m + (r // 2) * sz.bg + n * sz.cg, sz.cg), :] = v[r]

    @pl.loop(0, sz.nl // 2)
    def _(pair):
        n_rows = 2 * sz.hl * sz.wl
        both = jnp.concatenate(
            [
                il_ref[2 * pair + k].astype(f32).reshape(sz.hl * sz.wl, CIN)
                for k in range(2)
            ],
            axis=0,
        )
        parts = split(both, n_rows)
        for pc in range(2):
            v = parts[pc].reshape(2 * sz.hl, sz.cl, CIN)
            for r in range(sz.hl):
                phase = 2 * (r % 2) + pc
                joined = jnp.concatenate([v[r], v[sz.hl + r]], axis=0).astype(bf16)
                x_ref[
                    rows_at(phase * m + sz.mg + (r // 2) * sz.bl + pair * 2 * sz.cl, 2 * sz.cl), :
                ] = joined

    for pc in range(2):
        base = (2 + pc) * m
        halo_ref[pc * sz.edge : pc * sz.edge + sz.bg, :] = x_ref[
            base + sz.mg - sz.bg : base + sz.mg, :
        ]
        halo_ref[pc * sz.edge + sz.bg : (pc + 1) * sz.edge, :] = x_ref[
            base + m - sz.bl : base + m, :
        ]


LOW = 128
PACKED = (LOW + 8, 2 * LOW)


def gram_kernel(sz, x_ref, g_ref, full):
    n_rows = sz.m // PARTS
    ones = jnp.ones((8, n_rows), bf16)
    full[...] = jnp.zeros_like(full)

    @pl.loop(0, 4 * PARTS)
    def _(i):
        x = x_ref[rows_at(i * n_rows, n_rows), :]
        full[0:CIN, :] += t_dot(x, x)
        full[CIN : CIN + 8, :] += dot(ones, x)

    g_ref[...] = jnp.zeros_like(g_ref)
    g_ref[0:LOW, 0:CIN] = full[0:LOW, :]
    g_ref[0 : CIN - LOW, CIN:] = full[LOW:CIN, LOW:CIN]
    g_ref[LOW : LOW + 8, 0:CIN] = full[CIN : CIN + 8, :]


def unpack_gram(packed, full):
    full[0:LOW, :] = packed[0:LOW, 0:CIN]
    full[LOW:CIN, 0:LOW] = jnp.transpose(packed[0:LOW, LOW : 2 * LOW])[0 : CIN - LOW]
    full[LOW:CIN, LOW:CIN] = packed[0 : CIN - LOW, CIN:]
    full[CIN : CIN + 8, :] = packed[LOW : LOW + 8, 0:CIN]


def product_norm_terms(total, w_ref, amount, gain, shift):
    w = w_ref[...].astype(f32)
    mean = dot_high(total[CIN : CIN + 8], w)[0:1] / amount
    square = jnp.sum(w * dot_high(total[0:CIN], w), axis=0, keepdims=True) / amount
    inverse = lax.rsqrt(square - mean * mean + norm_eps)
    scale = gain * inverse
    return mean, inverse, scale, shift - mean * scale


def block_diagonal(k_ref, bd_ref):
    rows = lax.broadcasted_iota(jnp.int32, (HALF, HALF), 0) // GW
    cols = lax.broadcasted_iota(jnp.int32, (HALF, HALF), 1) // GW
    same = rows == cols
    for tap in range(9):
        for half in range(2):
            k = k_ref[tap * GW : (tap + 1) * GW, half * HALF : (half + 1) * HALF].astype(f32)
            bd_ref[2 * tap + half] = jnp.where(same, jnp.concatenate([k] * 4, axis=0), 0.0).astype(
                bf16
            )


def strided_product(sz, x_ref, s_ref, zs):
    n_rows = sz.m // PARTS

    @pl.loop(0, PARTS)
    def _(i):
        zs[rows_at(i * n_rows, n_rows), :] = dot(x_ref[rows_at(i * n_rows, n_rows), :], s_ref[...])


def block_dense(acc):
    rows = lax.broadcasted_iota(jnp.int32, (HALF, HALF), 0) // GW
    cols = lax.broadcasted_iota(jnp.int32, (HALF, HALF), 1) // GW
    kept = jnp.where(rows == cols, acc, 0.0)
    return jnp.sum(kept.reshape(4, GW, HALF), axis=0)


def shifted(v, by, width):
    n_rows = v.shape[0]
    col = lax.broadcasted_iota(jnp.int32, v.shape, 0) % width
    if by < 0:
        return jnp.where(col == 0, 0.0, pltpu.roll(v, 1, 0))
    return jnp.where(col == width - 1, 0.0, pltpu.roll(v, n_rows - 1, 0))


def segments(sz):
    g_rows = sz.bg
    l_rows = sz.bl
    return g_rows, l_rows


def conv_product(windows, bd_ref, half, n_rows, transposed):
    acc = None
    cols = pl.ds(pl.multiple_of(half * HALF, HALF), HALF)
    for tap, ref, start in windows:
        x = ref[start : start + n_rows, cols]
        w = bd_ref[2 * tap + half]
        term = dot_t(x, w) if transposed else dot(x, w)
        acc = term if acc is None else acc + term
    return acc


def windows_one(sz, refs, part):
    a00, a01, a01s, a10, a11, a11s = refs
    plain = 0 if part == "g" else sz.mg
    above = 0 if part == "g" else sz.one_l
    here = above + (sz.bg if part == "g" else sz.bl)
    result = []
    for tap in range(9):
        a, b = tap // 3, tap % 3
        if a == 1:
            result.append((tap, (a01s, a00, a01)[b], plain))
        else:
            result.append((tap, (a11s, a10, a11)[b], above if a == 0 else here))
    return result


def windows_two(sz, refs, part, flipped=False):
    base = 0 if part == "g" else sz.two_l
    block = sz.bg if part == "g" else sz.bl
    result = []
    for tap in range(9):
        a, b = tap // 3, tap % 3
        if flipped:
            a, b = 2 - a, 2 - b
        result.append((tap, refs[b], base + a * block))
    return result


def shift_windows(windows, by):
    return [(tap, ref, start + by) for tap, ref, start in windows]


def conv_forward(sz, windows_of, bd_ref, z_ref, st_ref, sums, more=()):
    sums[0:16, :] = jnp.zeros((16, C), f32)

    @pl.loop(0, 2)
    def _(half):
        cols = pl.ds(pl.multiple_of(half * HALF, HALF), HALF)
        for part, first, n_all, n_rows in (
            ("g", 0, sz.mg, sz.mg // 2),
            ("l", sz.mg, sz.ml, sz.ml),
        ):
            for k in range(n_all // n_rows):
                z = conv_product(
                    shift_windows(windows_of(part), k * n_rows), bd_ref, half, n_rows, False
                )
                z_ref[first + k * n_rows : first + (k + 1) * n_rows, cols] = z
                sums[0:8, cols] += fold(z)
                sums[8:16, cols] += fold(z * z)

    put_rows(st_ref, [sums[0:8, :], sums[8:16, :]] + list(more))


def first_act_kernel(
    sz,
    flag_ref,
    x_ref,
    halo_ref,
    w_ref,
    t0,
    t1,
    t2,
    t3,
    vt_ref,
    nrm_ref,
    a00,
    a01,
    a10,
    a11,
    a01s,
    a11s,
    zs,
    gram_scr,
):
    unpack_gram(gather_sum((t0, t1, t2, t3)), gram_scr)
    terms = product_norm_terms(
        gram_scr, w_ref, 4 * sz.amount, vt_ref[G1A : G1A + 1, :], vt_ref[B1A : B1A + 1, :]
    )
    nrm_ref[...] = jnp.zeros_like(nrm_ref)
    put_norm(nrm_ref, 0, terms)
    scale, shift = terms[2], terms[3]
    g_rows, l_rows = segments(sz)
    third = sz.m // PARTS

    def activate(src, dst, dst_s, n_rows, width, factor=None):
        v = zs[src, :] * scale + shift
        a = silu(v)
        if factor is not None:
            a = a * factor
        dst[0][dst[1], :] = a.astype(bf16)
        if dst_s is not None:
            dst_s[dst[1], :] = shifted(a, -1, width).astype(bf16)

    plan = [(a00, None, False), (a01, a01s, False), (a10, None, True), (a11, a11s, True)]
    for phase, (dst, dst_s, bordered) in enumerate(plan):

        @pl.loop(0, PARTS)
        def _(i):
            zs[rows_at(i * third, third), :] = dot(
                x_ref[rows_at(phase * sz.m + i * third, third), :], w_ref[...]
            )

        g_first = sz.bg if bordered else 0
        l_first = sz.one_l + sz.bl if bordered else sz.mg

        @pl.loop(0, sz.mg // g_rows)
        def _(i):
            activate(
                rows_at(i * g_rows, g_rows),
                (dst, rows_at(g_first + i * g_rows, g_rows)),
                dst_s,
                g_rows,
                sz.cg,
            )

        @pl.loop(0, sz.ml // l_rows)
        def _(i):
            activate(
                rows_at(sz.mg + i * l_rows, l_rows),
                (dst, rows_at(l_first + i * l_rows, l_rows)),
                dst_s,
                l_rows,
                sz.cl,
            )

    flag = above(flag_ref)
    for pc, (dst, dst_s) in enumerate(((a10, None), (a11, a11s))):
        zs[0 : sz.edge, :] = dot(halo_ref[pc * sz.edge : (pc + 1) * sz.edge, :], w_ref[...])

        @pl.loop(0, sz.bg // g_rows)
        def _(i):
            rows = rows_at(i * g_rows, g_rows)
            activate(rows, (dst, rows), dst_s, g_rows, sz.cg, flag)

        @pl.loop(0, sz.bl // l_rows)
        def _(i):
            activate(
                rows_at(sz.bg + i * l_rows, l_rows),
                (dst, rows_at(sz.one_l + i * l_rows, l_rows)),
                dst_s,
                l_rows,
                sz.cl,
                flag,
            )


def first_conv_kernel(
    sz, x_ref, s_ref, k_ref, a00, a01, a10, a11, a01s, a11s, z_ref, st_ref, bd_ref, sums
):
    block_diagonal(k_ref, bd_ref)
    third = sz.m // PARTS
    refs = (a00, a01, a01s, a10, a11, a11s)
    zero = jnp.zeros((8, C), f32)

    def step(i, carry):
        total, square = carry
        z = dot(x_ref[rows_at(i * third, third), :], s_ref[...])
        return total + fold(z), square + fold(z * z)

    more = lax.fori_loop(0, PARTS, step, (zero, zero))
    conv_forward(
        sz, lambda part: windows_one(sz, refs, part), bd_ref, z_ref, st_ref, sums, more
    )


def each_crop(sz, one):
    @pl.loop(0, sz.ng, unroll=2)
    def _(n):
        one([rows_at(i * sz.bg + n * sz.cg, sz.cg) for i in range(sz.rg)], (n,))

    @pl.loop(0, sz.nl // 2, unroll=3)
    def _(pair):
        first = sz.ng + 2 * pair
        one(
            [rows_at(sz.mg + i * sz.bl + pair * 2 * sz.cl, 2 * sz.cl) for i in range(sz.rl)],
            (first, first + 1),
        )


def add_pool(ref, crops, value):
    if len(crops) == 1:
        ref[pl.ds(crops[0], 1), :] = jnp.sum(value, axis=0, keepdims=True)
    else:
        n = value.shape[0] // 2
        ref[pl.ds(crops[0], 1), :] = jnp.sum(value[:n], axis=0, keepdims=True)
        ref[pl.ds(crops[1], 1), :] = jnp.sum(value[n:], axis=0, keepdims=True)


def crop_rows(ref, crops, n_rows):
    if len(crops) == 1:
        return ref[pl.ds(crops[0], 1), :]
    n = n_rows // 2
    return jnp.concatenate(
        [jnp.broadcast_to(ref[pl.ds(crop, 1), :], (n, ref.shape[1])) for crop in crops], axis=0
    )


def pool_kernel(sz, gain_row, shift_row, strided, z_ref, t0, t1, t2, t3, vt_ref, pool_ref, nrm_ref, ps):
    terms = norm_terms(
        gather_sum((t0, t1, t2, t3)),
        0,
        sz.amount,
        vt_ref[gain_row : gain_row + 1, :],
        vt_ref[shift_row : shift_row + 1, :],
    )
    nrm_ref[...] = jnp.zeros_like(nrm_ref)
    put_norm(nrm_ref, 0, terms)
    if strided:
        put_norm(
            nrm_ref,
            4,
            norm_terms(
                gather_sum((t0, t1, t2, t3)),
                2,
                sz.amount,
                vt_ref[G1S : G1S + 1, :],
                vt_ref[B1S : B1S + 1, :],
            ),
        )
    scale, shift = terms[2], terms[3]
    ps[...] = jnp.zeros_like(ps)

    def one(pieces, crops):
        acc = None
        for rows in pieces:
            c = silu(z_ref[rows, :] * scale + shift)
            acc = c if acc is None else acc + c
        add_pool(ps, crops, acc)

    each_crop(sz, one)
    pool_ref[...] = ps[...].astype(bf16)


def inverse_area(sz):
    crop = lax.broadcasted_iota(jnp.int32, (sz.crops, 1), 0)
    return jnp.where(crop < sz.ng, 1.0 / sz.area_g, 1.0 / sz.area_l).astype(f32)


def dot_high(a, b):
    return jnp.dot(a, b, precision=highest, preferred_element_type=f32)


def gather_short(refs):
    total = refs[0][...].astype(f32)
    for ref in refs[1:]:
        total = total + ref[...].astype(f32)
    return total


def gated_product_kernel(
    sz,
    bias_row,
    shift_row,
    z_in_ref,
    nrm_ref,
    p0,
    p1,
    p2,
    p3,
    d_ref,
    u_ref,
    w_ref,
    vt_ref,
    q_ref,
    z_ref,
    st_ref,
    gate_ref,
    pooled_ref,
    pre_ref,
):
    pooled = gather_short((p0, p1, p2, p3)) * inverse_area(sz)
    pooled_ref[...] = pooled
    pre = dot_high(pooled, d_ref[...].astype(f32)) + vt_ref[bias_row : bias_row + 1, 0:HID]
    pre_ref[...] = pre
    gate = dot_high(silu(pre), u_ref[...].astype(f32)) + vt_ref[shift_row : shift_row + 1, :]
    gate_ref[...] = sigmoid(gate)
    scale = nrm_ref[2:3, :]
    shift = nrm_ref[3:4, :]

    def one(pieces, crops):
        g = crop_rows(gate_ref, crops, 2 * sz.cl)
        for rows in pieces:
            c = silu(z_in_ref[rows, :] * scale + shift)
            q_ref[rows, :] = (c * g).astype(bf16)

    each_crop(sz, one)
    n_rows = sz.m // PARTS
    zero = jnp.zeros((8, C), f32)

    def step(i, carry):
        total, square = carry
        rows = rows_at(i * n_rows, n_rows)
        z = dot(q_ref[rows, :], w_ref[...])
        z_ref[rows, :] = z
        return total + fold(z), square + fold(z * z)

    put_rows(st_ref, lax.fori_loop(0, PARTS, step, (zero, zero)))


ROWS = 352
PARTS = 1


def put_edges(sz, src, top_ref, bottom_ref):
    for ref, g, l in (
        (top_ref, 0, sz.mg),
        (bottom_ref, sz.mg - sz.bg, sz.m - sz.bl),
    ):
        if ref is not None:
            ref[0 : sz.bg, :] = src[g : g + sz.bg, :]
            ref[sz.bg : sz.edge, :] = src[l : l + sz.bl, :]


def middle_kernel(
    sz,
    zc_ref,
    x_ref,
    s_ref,
    t0,
    t1,
    t2,
    t3,
    nrm_a_ref,
    vt_ref,
    pre_ref,
    mb_ref,
    nrm_ref,
    top_ref,
    bottom_ref,
    zs,
):
    strided_product(sz, x_ref, s_ref, zs)
    terms = norm_terms(
        gather_sum((t0, t1, t2, t3)),
        0,
        sz.amount,
        vt_ref[G1C : G1C + 1, :],
        vt_ref[B1C : B1C + 1, :],
    )
    nrm_ref[...] = jnp.zeros_like(nrm_ref)
    put_norm(nrm_ref, 0, terms)
    scale = terms[2]
    scale_s = nrm_a_ref[6:7, :]
    shift = terms[3] + nrm_a_ref[7:8, :]

    @pl.loop(0, sz.m // ROWS)
    def _(i):
        rows = rows_at(i * ROWS, ROWS)
        pre = zc_ref[rows, :] * scale + zs[rows, :] * scale_s + shift
        pre_ref[rows, :] = pre
        mb_ref[rows, :] = silu(pre).astype(bf16)

    put_edges(sz, mb_ref, top_ref, bottom_ref)


def product_kernel(sz, x_ref, w_ref, z_ref, st_ref):
    n_rows = sz.m // PARTS
    zero = jnp.zeros((8, C), f32)

    def step(i, carry):
        total, square = carry
        rows = rows_at(i * n_rows, n_rows)
        z = dot(x_ref[rows, :], w_ref[...])
        z_ref[rows, :] = z
        return total + fold(z), square + fold(z * z)

    put_rows(st_ref, lax.fori_loop(0, PARTS, step, (zero, zero)))


def put_variants(refs, rows, value, width):
    refs[0][rows, :] = shifted(value, -1, width).astype(bf16)
    refs[1][rows, :] = value.astype(bf16)
    refs[2][rows, :] = shifted(value, 1, width).astype(bf16)


def second_conv_kernel(
    sz,
    flag_ref,
    z_in_ref,
    top_ref,
    bottom_ref,
    w_ref,
    k_ref,
    t0,
    t1,
    t2,
    t3,
    vt_ref,
    z_ref,
    st_ref,
    nrm_ref,
    a1,
    a0,
    a2,
    bd_ref,
    zs,
    sums,
):
    block_diagonal(k_ref, bd_ref)
    terms = norm_terms(
        gather_sum((t0, t1, t2, t3)),
        0,
        sz.amount,
        vt_ref[G2A : G2A + 1, :],
        vt_ref[B2A : B2A + 1, :],
    )
    nrm_ref[...] = jnp.zeros_like(nrm_ref)
    put_norm(nrm_ref, 0, terms)
    scale, shift = terms[2], terms[3]
    g_rows, l_rows = segments(sz)
    refs = (a0, a1, a2)

    @pl.loop(0, sz.mg // g_rows)
    def _(i):
        a = silu(z_in_ref[rows_at(i * g_rows, g_rows), :] * scale + shift)
        put_variants(refs, rows_at(sz.bg + i * g_rows, g_rows), a, sz.cg)

    @pl.loop(0, sz.ml // l_rows)
    def _(i):
        a = silu(z_in_ref[rows_at(sz.mg + i * l_rows, l_rows), :] * scale + shift)
        put_variants(refs, rows_at(sz.two_l + sz.bl + i * l_rows, l_rows), a, sz.cl)

    for k, src in enumerate((top_ref, bottom_ref)):
        flag = (above, below)[k](flag_ref, sz.n_height)
        zs[...] = dot(src[...], w_ref[...])
        g_first = 0 if k == 0 else (sz.rg + 1) * sz.bg
        l_first = sz.two_l + (0 if k == 0 else (sz.rl + 1) * sz.bl)

        @pl.loop(0, sz.bg // g_rows)
        def _(i):
            a = silu(zs[rows_at(i * g_rows, g_rows), :] * scale + shift) * flag
            put_variants(refs, rows_at(g_first + i * g_rows, g_rows), a, sz.cg)

        @pl.loop(0, sz.bl // l_rows)
        def _(i):
            a = silu(zs[rows_at(sz.bg + i * l_rows, l_rows), :] * scale + shift) * flag
            put_variants(refs, rows_at(l_first + i * l_rows, l_rows), a, sz.cl)

    conv_forward(sz, lambda part: windows_two(sz, refs, part), bd_ref, z_ref, st_ref, sums)


def output_kernel(
    sz, pre_ref, z_ref, t0, t1, t2, t3, vt_ref, cg_ref, cl_ref, og_ref, ol_ref, dn_ref, st_ref, nrm_ref, sums
):
    terms = norm_terms(
        gather_sum((t0, t1, t2, t3)),
        0,
        sz.amount,
        vt_ref[G2C : G2C + 1, :],
        vt_ref[B2C : B2C + 1, :],
    )
    nrm_ref[...] = jnp.zeros_like(nrm_ref)
    put_norm(nrm_ref, 0, terms)
    mean, inverse, scale, shift = terms
    sums[...] = jnp.zeros_like(sums)

    def piece(rows, cot):
        z = z_ref[rows, :]
        pre = silu(pre_ref[rows, :]) + z * scale + shift
        s = sigmoid(pre)
        dn = cot * (s * (1.0 + pre * (1.0 - s)))
        dn_ref[rows, :] = dn
        return pre * s, fold(dn), fold(dn * z)

    @pl.loop(0, sz.ng, unroll=2)
    def _(n):
        one, two = 0.0, 0.0
        for i in range(sz.rg):
            rows = rows_at(i * sz.bg + n * sz.cg, sz.cg)
            value, add_one, add_two = piece(rows, cg_ref[n, i].astype(f32))
            og_ref[n, i] = value.astype(bf16)
            one, two = one + add_one, two + add_two
        sums[0:8, :] += one
        sums[8:16, :] += two

    @pl.loop(0, sz.nl // 2, unroll=3)
    def _(pair):
        one, two = 0.0, 0.0
        for i in range(sz.rl):
            rows = rows_at(sz.mg + i * sz.bl + pair * 2 * sz.cl, 2 * sz.cl)
            cot = jnp.concatenate(
                [cl_ref[2 * pair + k, i].astype(f32) for k in range(2)], axis=0
            )
            value, add_one, add_two = piece(rows, cot)
            for k in range(2):
                ol_ref[2 * pair + k, i] = value[k * sz.cl : (k + 1) * sz.cl].astype(bf16)
            one, two = one + add_one, two + add_two
        sums[0:8, :] += one
        sums[8:16, :] += two

    put_back_sums(st_ref, sums[0:8, :], sums[8:16, :], mean, inverse)


def back_terms(total, row_one, row_two, amount, nrm_ref, nrm_row):
    mean = nrm_ref[nrm_row : nrm_row + 1, :]
    inverse = nrm_ref[nrm_row + 1 : nrm_row + 2, :]
    scale = nrm_ref[nrm_row + 2 : nrm_row + 3, :]
    one = total[row_one : row_one + 1] / amount
    two = total[row_two : row_two + 1] / amount
    return scale, one, mean, inverse * two


def norm_back(dn, z, terms):
    scale, one, mean, slope = terms
    return scale * (dn - one - (z - mean) * slope)


def gate_grad_kernel(
    sz,
    strided,
    dn_ref,
    z_ref,
    t0,
    t1,
    t2,
    t3,
    nrm_ref,
    w_ref,
    z_in_ref,
    nrm_in_ref,
    *refs,
):
    if strided:
        x_ref, s_ref, nrm_a_ref, dz_ref, dzs_ref, dq_ref, dg_ref, ps, zs = refs
        strided_product(sz, x_ref, s_ref, zs)
    else:
        dz_ref, dq_ref, dg_ref, ps = refs
    total = gather_sum((t0, t1, t2, t3))
    terms = back_terms(total, 0, 1, sz.amount, nrm_ref, 0)

    @pl.loop(0, sz.m // ROWS)
    def _(i):
        rows = rows_at(i * ROWS, ROWS)
        dz_ref[rows, :] = norm_back(dn_ref[rows, :], z_ref[rows, :], terms).astype(bf16)

    if strided:
        terms_s = back_terms(total, 0, 2, sz.amount, nrm_a_ref, 4)

        @pl.loop(0, sz.m // ROWS)
        def _(i):
            rows = rows_at(i * ROWS, ROWS)
            dzs_ref[rows, :] = norm_back(dn_ref[rows, :], zs[rows, :], terms_s).astype(bf16)

    n_rows = sz.m // PARTS

    @pl.loop(0, PARTS)
    def _(i):
        rows = rows_at(i * n_rows, n_rows)
        dq_ref[rows, :] = dot_t(dz_ref[rows, :], w_ref[...])

    ps[...] = jnp.zeros_like(ps)
    scale = nrm_in_ref[2:3, :]
    shift = nrm_in_ref[3:4, :]

    def one(pieces, crops):
        acc = None
        for rows in pieces:
            term = dq_ref[rows, :] * silu(z_in_ref[rows, :] * scale + shift)
            acc = term if acc is None else acc + term
        add_pool(ps, crops, acc)

    each_crop(sz, one)
    dg_ref[...] = ps[...].astype(bf16)


def excite_back_kernel(
    sz,
    dq_ref,
    z_ref,
    nrm_ref,
    g0,
    g1,
    g2,
    g3,
    gate_ref,
    pre_ref,
    d_ref,
    u_ref,
    dn_ref,
    st_ref,
    dv_ref,
    du_ref,
    pool,
    sums,
):
    gate = gate_ref[...]
    dv = gather_short((g0, g1, g2, g3)) * gate * (1.0 - gate)
    dv_ref[...] = dv
    du = lax.dot_general(
        dv,
        u_ref[...].astype(f32),
        (((1,), (1,)), ((), ())),
        precision=highest,
        preferred_element_type=f32,
    ) * silu_slope(pre_ref[...])
    du_ref[...] = du
    pool[...] = (
        lax.dot_general(
            du,
            d_ref[...].astype(f32),
            (((1,), (1,)), ((), ())),
            precision=highest,
            preferred_element_type=f32,
        )
        * inverse_area(sz)
    )
    mean = nrm_ref[0:1, :]
    inverse = nrm_ref[1:2, :]
    scale = nrm_ref[2:3, :]
    shift = nrm_ref[3:4, :]
    sums[...] = jnp.zeros_like(sums)

    def one(pieces, crops):
        g = crop_rows(gate_ref, crops, 2 * sz.cl)
        p = crop_rows(pool, crops, 2 * sz.cl)
        total, with_z = 0.0, 0.0
        for rows in pieces:
            z = z_ref[rows, :]
            dn = (dq_ref[rows, :] * g + p) * silu_slope(z * scale + shift)
            dn_ref[rows, :] = dn
            total, with_z = total + fold(dn), with_z + fold(dn * z)
        sums[0:8, :] += total
        sums[8:16, :] += with_z

    each_crop(sz, one)
    put_back_sums(st_ref, sums[0:8, :], sums[8:16, :], mean, inverse)


def put_flat(value_ref, width, flat_ref, slots):
    if width == 128:
        for j in range(C // 128):
            flat_ref[:, j * 128 : (j + 1) * 128] = value_ref[pl.ds(j, width, stride=C // 128), :]
        return
    n_lines = width // int(np.gcd(C, width))
    n_groups = width // n_lines
    per = C // n_groups
    lane = lax.broadcasted_iota(jnp.int32, (n_groups, C), 1)
    lines = [jnp.zeros((n_groups, C), f32) for _ in range(n_lines)]
    for u in range(per):
        row = value_ref[pl.ds(u, n_groups, stride=per), :]
        row = jnp.concatenate([row] + [jnp.zeros_like(row)] * (C // 128 - 1), axis=1)
        line, at = divmod(u * width, C)
        moved = pltpu.roll(row, at, 1) if at else row
        lines[line] = jnp.where(lane >= at, lines[line] + moved, lines[line])
        if at + width > C:
            lines[line + 1] = jnp.where(
                lane < at + width - C, lines[line + 1] + moved, lines[line + 1]
            )
    for j in range(C // 128):
        for k, line in enumerate(lines):
            slots[pl.ds(k, n_groups, stride=n_lines), :] = line[:, j * 128 : (j + 1) * 128]
        flat_ref[:, j * 128 : (j + 1) * 128] = slots[0:width, :]


def excite_weights_kernel(
    width, flag_ref, dv_ref, du_ref, pooled_ref, pre_ref, dd_ref, de_ref, du_out, df_ref, wide, slots
):
    flag = first_of_height(flag_ref)
    dv = dv_ref[...] * flag
    du = du_ref[...] * flag

    def cross(a, b):
        return lax.dot_general(
            a, b, (((0,), (0,)), ((), ())), precision=highest, preferred_element_type=f32
        )

    wide[...] = cross(pooled_ref[...], du)
    put_flat(wide, width, dd_ref, slots)
    du_out[...] = cross(silu(pre_ref[...]), dv)
    de_ref[...] = jnp.broadcast_to(jnp.sum(du, axis=0, keepdims=True), de_ref.shape)
    df_ref[...] = jnp.broadcast_to(jnp.sum(dv, axis=0, keepdims=True), df_ref.shape)


def weight_kernel(x_ref, dz_ref, w_ref):
    n_rows = dz_ref.shape[0]
    n = 128 if x_ref.shape[1] % 128 == 0 else x_ref.shape[1]
    for k in range(x_ref.shape[1] // n):
        w_ref[k * n : (k + 1) * n, :] = t_dot(x_ref[0:n_rows, k * n : (k + 1) * n], dz_ref[...])


def norm_back_kernel(sz, dn_ref, z_ref, t0, t1, t2, t3, nrm_ref, dz_ref, top_ref, bottom_ref=None):
    terms = back_terms(gather_sum((t0, t1, t2, t3)), 0, 1, sz.amount, nrm_ref, 0)

    @pl.loop(0, sz.m // ROWS)
    def _(i):
        rows = rows_at(i * ROWS, ROWS)
        dz_ref[rows, :] = norm_back(dn_ref[rows, :], z_ref[rows, :], terms).astype(bf16)

    put_edges(sz, dz_ref, top_ref, bottom_ref)


def conv_weights(sz, windows_of, dz_ref, dk_ref):
    @pl.loop(0, 2)
    def _(half):
        cols = pl.ds(pl.multiple_of(half * HALF, HALF), HALF)
        win_g = windows_of("g")
        win_l = windows_of("l")
        for tap in range(9):
            _, ref_g, start_g = win_g[tap]
            _, ref_l, start_l = win_l[tap]
            acc = t_dot(ref_g[start_g : start_g + sz.mg, cols], dz_ref[0 : sz.mg, cols])
            acc = acc + t_dot(ref_l[start_l : start_l + sz.ml, cols], dz_ref[sz.mg : sz.m, cols])
            dk_ref[tap * GW : (tap + 1) * GW, cols] = block_dense(acc)


def shift_all(src, dst, by, spans):
    for first, n_all, n_rows, width in spans:

        @pl.loop(0, n_all // n_rows)
        def _(i):
            rows = rows_at(first + i * n_rows, n_rows)
            dst[rows, :] = shifted(src[rows, :].astype(f32), by, width).astype(bf16)


def second_conv_weights_kernel(sz, a1, dz_ref, dk_ref, a0, a2):
    g_rows, l_rows = segments(sz)
    spans = ((0, sz.two_l, g_rows, sz.cg), (sz.two_l, sz.two - sz.two_l, l_rows, sz.cl))
    shift_all(a1, a0, -1, spans)
    shift_all(a1, a2, 1, spans)
    conv_weights(sz, lambda part: windows_two(sz, (a0, a1, a2), part), dz_ref, dk_ref)


def first_conv_weights_kernel(sz, a00, a01, a10, a11, dz_ref, dk_ref, a01s, a11s):
    g_rows, l_rows = segments(sz)
    shift_all(a01, a01s, -1, ((0, sz.mg, g_rows, sz.cg), (sz.mg, sz.ml, l_rows, sz.cl)))
    shift_all(
        a11,
        a11s,
        -1,
        ((0, sz.one_l, g_rows, sz.cg), (sz.one_l, sz.one - sz.one_l, l_rows, sz.cl)),
    )
    refs = (a00, a01, a01s, a10, a11, a11s)
    conv_weights(sz, lambda part: windows_one(sz, refs, part), dz_ref, dk_ref)


def second_conv_back_kernel(
    sz, dz_ref, top_ref, bottom_ref, k_ref, z_ref, nrm_ref, dn_ref, st_ref, v0, v1, v2, bd_ref, sums
):
    block_diagonal(k_ref, bd_ref)
    refs = (v0, v1, v2)
    g_rows, l_rows = segments(sz)

    @pl.loop(0, sz.mg // g_rows)
    def _(i):
        v = dz_ref[rows_at(i * g_rows, g_rows), :].astype(f32)
        put_variants(refs, rows_at(sz.bg + i * g_rows, g_rows), v, sz.cg)

    @pl.loop(0, sz.ml // l_rows)
    def _(i):
        v = dz_ref[rows_at(sz.mg + i * l_rows, l_rows), :].astype(f32)
        put_variants(refs, rows_at(sz.two_l + sz.bl + i * l_rows, l_rows), v, sz.cl)

    for k, src in enumerate((top_ref, bottom_ref)):
        g_first = 0 if k == 0 else (sz.rg + 1) * sz.bg
        l_first = sz.two_l + (0 if k == 0 else (sz.rl + 1) * sz.bl)

        @pl.loop(0, sz.bg // g_rows)
        def _(i):
            v = src[rows_at(i * g_rows, g_rows), :].astype(f32)
            put_variants(refs, rows_at(g_first + i * g_rows, g_rows), v, sz.cg)

        @pl.loop(0, sz.bl // l_rows)
        def _(i):
            v = src[rows_at(sz.bg + i * l_rows, l_rows), :].astype(f32)
            put_variants(refs, rows_at(l_first + i * l_rows, l_rows), v, sz.cl)

    @pl.loop(0, 2)
    def _(half):
        cols = pl.ds(pl.multiple_of(half * HALF, HALF), HALF)
        for part, first, n_all, n_rows in (
            ("g", 0, sz.mg, sz.mg // 2),
            ("l", sz.mg, sz.ml, sz.ml),
        ):
            for k in range(n_all // n_rows):
                dn_ref[first + k * n_rows : first + (k + 1) * n_rows, cols] = conv_product(
                    shift_windows(windows_two(sz, refs, part, True), k * n_rows),
                    bd_ref,
                    half,
                    n_rows,
                    True,
                )

    slope_pass(sz.m, dn_ref, z_ref, nrm_ref, st_ref, sums)


def slope_pass(n_all, dn_ref, z_ref, nrm_ref, st_ref, sums):
    mean = nrm_ref[0:1, :]
    inverse = nrm_ref[1:2, :]
    scale = nrm_ref[2:3, :]
    shift = nrm_ref[3:4, :]
    sums[...] = jnp.zeros_like(sums)

    @pl.loop(0, n_all // ROWS)
    def _(i):
        rows = rows_at(i * ROWS, ROWS)
        z = z_ref[rows, :]
        dn = dn_ref[rows, :] * silu_slope(z * scale + shift)
        dn_ref[rows, :] = dn
        sums[0:8, :] += fold(dn)
        sums[8:16, :] += fold(dn * ((z - mean) * inverse))

    put_rows(st_ref, [sums[0:8, :], sums[8:16, :]])


def middle_back_kernel(
    sz,
    dn_d_ref,
    zd_ref,
    t0,
    t1,
    t2,
    t3,
    nrm_d_ref,
    w_ref,
    dpre_ref,
    pre_ref,
    zc_ref,
    x_ref,
    s_ref,
    nrm_c_ref,
    nrm_a_ref,
    dz_ref,
    dn_ref,
    st_ref,
    zs,
    sums,
):
    strided_product(sz, x_ref, s_ref, zs)
    terms = back_terms(gather_sum((t0, t1, t2, t3)), 0, 1, sz.amount, nrm_d_ref, 0)

    @pl.loop(0, sz.m // ROWS)
    def _(i):
        rows = rows_at(i * ROWS, ROWS)
        dz_ref[rows, :] = norm_back(dn_d_ref[rows, :], zd_ref[rows, :], terms).astype(bf16)

    n_rows = sz.m // PARTS

    @pl.loop(0, PARTS)
    def _(i):
        rows = rows_at(i * n_rows, n_rows)
        dn_ref[rows, :] = dot_t(dz_ref[rows, :], w_ref[...])

    mean_c = nrm_c_ref[0:1, :]
    inverse_c = nrm_c_ref[1:2, :]
    mean_s = nrm_a_ref[4:5, :]
    inverse_s = nrm_a_ref[5:6, :]
    sums[...] = jnp.zeros_like(sums)

    @pl.loop(0, sz.m // ROWS)
    def _(i):
        rows = rows_at(i * ROWS, ROWS)
        dn = (dn_ref[rows, :] + dpre_ref[rows, :]) * silu_slope(pre_ref[rows, :])
        dn_ref[rows, :] = dn
        sums[0:8, :] += fold(dn)
        sums[8:16, :] += fold(dn * ((zc_ref[rows, :] - mean_c) * inverse_c))
        sums[16:24, :] += fold(dn * ((zs[rows, :] - mean_s) * inverse_s))

    put_rows(st_ref, [sums[0:8, :], sums[8:16, :], sums[16:24, :]])


def first_conv_back_kernel(sz, dz_ref, below_ref, k_ref, v0, v1, bd_ref):
    block_diagonal(k_ref, bd_ref)
    g_rows, l_rows = segments(sz)

    def put(rows, v, width):
        v0[rows, :] = v.astype(bf16)
        v1[rows, :] = shifted(v, 1, width).astype(bf16)

    for src, g_src, l_src, g_dst, l_dst, g_all, l_all in (
        (dz_ref, 0, sz.mg, 0, sz.one_l, sz.mg, sz.ml),
        (below_ref, 0, sz.bg, sz.mg, sz.one_l + sz.ml, sz.bg, sz.bl),
    ):

        @pl.loop(0, g_all // g_rows)
        def _(i):
            v = src[rows_at(g_src + i * g_rows, g_rows), :].astype(f32)
            put(rows_at(g_dst + i * g_rows, g_rows), v, sz.cg)

        @pl.loop(0, l_all // l_rows)
        def _(i):
            v = src[rows_at(l_src + i * l_rows, l_rows), :].astype(f32)
            put(rows_at(l_dst + i * l_rows, l_rows), v, sz.cl)


def parity_back_kernel(sz, phase, v0, v1, bd_ref, x_ref, w_ref, nrm_ref, *refs):
    if phase:
        st_in, dn_ref, st_ref, zs, da, sums = refs
    else:
        dn_ref, st_ref, zs, da, sums = refs
    mean = nrm_ref[0:1, :]
    inverse = nrm_ref[1:2, :]
    scale = nrm_ref[2:3, :]
    shift = nrm_ref[3:4, :]
    sums[...] = jnp.zeros_like(sums)
    third = sz.m // PARTS
    pr, pc = phase // 2, phase % 2
    taps = []
    for a, down in (((1, 0),), ((2, 0), (0, 1)))[pr]:
        for b, right in (((1, 0),), ((2, 0), (0, 1)))[pc]:
            taps.append((3 * a + b, down, right))

    @pl.loop(0, 2)
    def _(half):
        cols = pl.ds(pl.multiple_of(half * HALF, HALF), HALF)
        for first, base, block, n_all, n_rows in (
            (0, 0, sz.bg, sz.mg, sz.mg // 2),
            (sz.mg, sz.one_l, sz.bl, sz.ml, sz.ml),
        ):
            for k in range(n_all // n_rows):
                windows = [
                    (tap, (v0, v1)[right], base + down * block + k * n_rows)
                    for tap, down, right in taps
                ]
                da[first + k * n_rows : first + (k + 1) * n_rows, cols] = conv_product(
                    windows, bd_ref, half, n_rows, True
                )

    @pl.loop(0, PARTS)
    def _(i):
        zs[rows_at(i * third, third), :] = dot(
            x_ref[rows_at(phase * sz.m + i * third, third), :], w_ref[...]
        )

    @pl.loop(0, sz.m // ROWS)
    def _(i):
        rows = rows_at(i * ROWS, ROWS)
        z = zs[rows, :]
        dn = da[rows, :] * silu_slope(z * scale + shift)
        dn_ref[rows, :] = dn.astype(bf16)
        sums[0:8, :] += fold(dn)
        sums[8:16, :] += fold(dn * ((z - mean) * inverse))

    put_rows(st_ref, [sums[0:8, :], sums[8:16, :]])
    if phase:
        st_ref[...] += st_in[...]


def image_norm_back_kernel(sz, dn0, dn1, dn2, dn3, x_ref, w_ref, t0, t1, t2, t3, nrm_ref, dz_ref, zs):
    terms = back_terms(gather_sum((t0, t1, t2, t3)), 0, 1, 4 * sz.amount, nrm_ref, 0)
    zs[...] = dot(x_ref[...], w_ref[...])
    for phase in range(4):

        @pl.loop(0, sz.m // ROWS)
        def _(i):
            rows = rows_at(i * ROWS, ROWS)
            rows_all = rows_at(phase * sz.m + i * ROWS, ROWS)
            dz_ref[rows_all, :] = norm_back(
                (dn0, dn1, dn2, dn3)[phase][rows, :].astype(f32), zs[rows_all, :], terms
            ).astype(bf16)


def image_product_kernel(sz, dz_ref, w_ref, dzs_ref, ws_ref, dx_ref):
    dx_ref[...] = dot_t(dz_ref[...], w_ref[...])
    dx_ref[0 : sz.m, :] += dot_t(dzs_ref[...], ws_ref[...])


def place_kernel(n_crops, height, width, first_row, block, m, dx_ref, o_ref, mark_ref, s_ref, t_ref):
    half = width // 2
    mark_ref[...] = jnp.zeros_like(mark_ref)
    count = s_ref.shape[0]

    @pl.loop(0, n_crops // count)
    def _(step):
        for c in range(count):
            n = step * count + c
            for r in range(height):
                for pc in range(2):
                    at = (2 * (r % 2) + pc) * m + first_row + (r // 2) * block + n * half
                    v = dx_ref[rows_at(at, half, 8), :]
                    rows = pl.ds(r * width + pc, half, stride=2)
                    s_ref[c, rows, :] = v[:, :128]
                    t_ref[c, rows, :] = jnp.concatenate([v[:, 128:], v[:, 128:]], axis=1)
        for c in range(count):
            n = step * count + c
            o_ref[n, :, :, 0:128] = s_ref[c].reshape(height, width, 128)
            o_ref[n, :, :, 128:CIN] = t_ref[c][:, :64].reshape(height, width, 64)


def over_height(x):
    n = lax.axis_size("height")
    return [x] + [lax.ppermute(x, "height", [(i, i ^ k) for i in range(n)]) for k in range(1, n)]


def step_down(x):
    n = lax.axis_size("height")
    return lax.ppermute(x, "height", [(i, i + 1) for i in range(n - 1)])


def step_up(x):
    n = lax.axis_size("height")
    return lax.ppermute(x, "height", [(i + 1, i) for i in range(n - 1)])


MATRIX_ROWS = [a * b // C for a, b in matrix_shapes()]
ROW_BOUNDS = [int(v) for v in np.cumsum([0] + MATRIX_ROWS)]
UNIT = 112


def across(x, mask, senders=None):
    n = lax.axis_size("batch")
    return lax.ppermute(
        x, "batch", [(i, i ^ mask) for i in range(n) if senders is None or i in senders]
    )


def take_flat(whole, start, width, low_ref, value, slots):
    if width == 128:
        for j in range(C // 128):
            value[pl.ds(j, width, stride=C // 128), :] = whole[
                start : start + width, j * 128 : (j + 1) * 128
            ]
    else:
        n_lines = width // int(np.gcd(C, width))
        n_groups = width // n_lines
        per = C // n_groups
        lane = lax.broadcasted_iota(jnp.int32, (n_groups, C), 1)
        blocks = [[] for _ in range(n_lines)]
        for j in range(C // 128):
            slots[0:width, :] = whole[start : start + width, j * 128 : (j + 1) * 128]
            for k in range(n_lines):
                blocks[k].append(slots[pl.ds(k, n_groups, stride=n_lines), :])
        lines = [jnp.concatenate(block, axis=1) for block in blocks]
        for u in range(per):
            line, at = divmod(u * width, C)
            row = pltpu.roll(lines[line], C - at, 1) if at else lines[line]
            if at + width > C:
                row = jnp.where(lane < C - at, row, pltpu.roll(lines[line + 1], C - at, 1))
            value[pl.ds(u, n_groups, stride=per), :] = jnp.where(lane < width, row, 0.0)[:, 0:128]
    low_ref[...] = value[...].astype(bf16)


def assemble_kernel(n_rows, idx_ref, *refs):
    ins, outs = refs[:2], refs[2:-4]
    shards, whole, value, slots = refs[-4:]
    for core, ref in enumerate(ins):
        for q in range(4):
            for k in range(4):
                at = (idx_ref[0] ^ (2 * q + core)) * 4 + (idx_ref[1] ^ k)
                shards[at] = ref[4 * q + k].astype(f32)
    for s in range(32):
        whole[s * n_rows : (s + 1) * n_rows, :] = shards[s, 0:n_rows, :]
    for k, (ref, start) in enumerate(zip(outs, ROW_BOUNDS)):
        if k in (2, 8):
            take_flat(whole, start, MATRIX_ROWS[k], ref, value, slots)
        elif k in (3, 9):
            n = MATRIX_ROWS[k]
            value[0:HID, :] = jnp.zeros((HID, 128), f32)
            for j in range(C // 128):
                value[0:n, :] = whole[start : start + n, j * 128 : (j + 1) * 128]
                ref[:, j * 128 : (j + 1) * 128] = value[0:HID, :].astype(bf16)
        else:
            ref[...] = whole[start : start + ref.shape[0], :].astype(bf16)


def merge_kernel(*refs):
    *ins, merged = refs
    n = ins[0].shape[0]
    for q, ref in enumerate(ins):
        merged[q * n : (q + 1) * n] = ref[...]


def gather_weights(lines, n_rows, place_ids, beside):
    (mine,) = call(
        functools.partial(round_rows_kernel, n_rows),
        [out((UNIT, C), bf16)],
        [],
        lines,
        name="round_weights",
        after=[place_ids],
    )
    quarter = jnp.stack(over_height(mine))
    after, extra = beside(quarter)
    planes = [quarter] + [across(quarter, mask) for mask in (2, 4, 6)]
    (merged,) = call(
        merge_kernel, [out((16, UNIT, C), bf16)], [], *planes, name="merge_planes", after=after
    )
    planes = [merged, across(merged, 1)]
    matrices = call(
        functools.partial(assemble_kernel, n_rows),
        [
            out((C, HID) if k in (2, 8) else (HID if k in (3, 9) else rows, C), bf16)
            for k, rows in enumerate(MATRIX_ROWS)
        ],
        [
            pltpu.VMEM((32, UNIT, C), f32),
            pltpu.VMEM((32 * n_rows, C), f32),
            pltpu.VMEM((C, 128), f32),
            pltpu.VMEM((HID, 128), f32),
        ],
        place_ids,
        *planes,
        smem=1,
        name="assemble",
        room=6 * 2**20,
    )
    return matrices, extra


def pack_kernel(n_rows, first_shard, sources, core_ref, *refs):
    n_src = len(sources)
    ins, (mine_ref, other_ref, buf) = refs[:n_src], refs[n_src:]
    for shard in range(buf.shape[0]):
        low = (first_shard + shard) * n_rows
        for (start, stop), ref in zip(sources, ins):
            a, b = max(low, start), min(low + n_rows, stop)
            if a < b:
                buf[shard, a - low : b - low, :] = ref[a - start : b - start, :]
        buf[shard, n_rows:, :] = jnp.zeros((UNIT - n_rows, C), f32)
    core = core_of(core_ref)
    for unit in range(buf.shape[0] // 8):
        for h in range(4):
            mine_ref[unit * 4 + h] = buf[(unit * 2 + core) * 4 + h]
            other_ref[unit * 4 + h] = buf[(unit * 2 + 1 - core) * 4 + h].astype(bf16)


def pack(n_rows, first_unit, n_units, sources, arrays, place_ids, name, after=()):
    shape = (4 * n_units, UNIT, C)
    mine, other = call(
        functools.partial(pack_kernel, n_rows, 8 * first_unit, sources),
        [out(shape), out(shape, bf16)],
        [pltpu.VMEM((8 * n_units, UNIT, C), f32)],
        place_ids,
        *arrays,
        smem=1,
        name=name,
        after=after,
    )
    return mine, across(other, 1)


def sum_core_kernel(place_ref, a0_ref, b0_ref, a_ref, b_ref, sum_ref, y_ref, x_ref):
    n = a0_ref.shape[0]
    sum_ref[0:n] = a0_ref[...] + b0_ref[...].astype(f32)
    sum_ref[n:] = a_ref[...] + b_ref[...].astype(f32)
    y, x = y_of(place_ref), x_of(place_ref)
    for h in range(4):
        y_ref[h] = sum_ref[8 - 4 * y + h].astype(bf16)
        x_ref[h] = sum_ref[12 - 12 * x + h].astype(bf16)


def second_parts_kernel(place_ref, sum_ref, gy_ref, gx_ref, keep_ref, y_ref, x_ref):
    y, x = y_of(place_ref), x_of(place_ref)
    for h in range(4):
        by_y = sum_ref[4 + 4 * y + h] + gy_ref[h].astype(f32)
        by_x = sum_ref[12 * x + h] + gx_ref[h].astype(f32)
        keep_ref[h] = jnp.where(x == y, by_x, by_y)
        y_ref[h] = by_x.astype(bf16)
        x_ref[h] = by_y.astype(bf16)


def early_parts_kernel(place_ref, sum_ref, gy_ref, gx_ref, keep_ref, s1, s2, s3):
    same = y_of(place_ref) == x_of(place_ref)
    for k, ref in enumerate((keep_ref, s1, s2, s3)):
        at = place_ref[1] ^ k
        got = jnp.where(same, gy_ref[at].astype(f32), gx_ref[at].astype(f32))
        ref[...] = (sum_ref[at] + got).astype(ref.dtype)


class EarlySum:
    def __init__(self, n_rows, place_ids):
        self.n_rows, self.ids = n_rows, place_ids

    def pack(self, sources, arrays):
        self.mine, self.got = pack(
            self.n_rows, 1, 3, sources, arrays, self.ids, "pack_early"
        )
        return [self.mine]

    def pack_first_unit(self, sources, arrays, after):
        self.mine_first, self.got_first = pack(
            self.n_rows, 0, 1, sources, arrays, self.ids, "pack_unit_0", after
        )
        return [self.mine_first]

    def first(self, after):
        four = out((4, UNIT, C), bf16)
        self.total, y_low, x_low = call(
            sum_core_kernel,
            [out((16, UNIT, C)), four, four],
            [],
            self.ids,
            self.mine_first,
            self.got_first,
            self.mine,
            self.got,
            smem=1,
            name="sum_core",
            after=after,
        )
        self.got = [across(y_low, 4), across(x_low, 2)]
        return [self.total]

    def second(self, after):
        four = out((4, UNIT, C), bf16)
        self.keep, y_low, x_low = call(
            second_parts_kernel,
            [out((4, UNIT, C)), four, four],
            [],
            self.ids,
            self.total,
            *self.got,
            smem=1,
            name="second_parts",
            after=after,
        )
        self.got = [across(y_low, 4, [2, 3, 4, 5]), across(x_low, 2, [0, 1, 6, 7])]
        return [self.keep]

    def height(self, after):
        low = out((UNIT, C), bf16)
        mine, *sends = call(
            early_parts_kernel,
            [out((UNIT, C)), low, low, low],
            [],
            self.ids,
            self.keep,
            *self.got,
            smem=1,
            name="early_parts",
            after=after,
        )
        self.result = [mine] + [
            lax.ppermute(send, "height", [(i, i ^ k) for i in range(4)])
            for k, send in zip((1, 2, 3), sends)
        ]
        return [self.result[0]]


HALF_UNIT = 64


def first_halves_kernel(n_rows, place_ref, g_ref, mine_ref, other_ref, buf):
    n_first = g_ref.shape[0]
    buf[...] = jnp.zeros_like(buf)
    buf[0, 0:n_rows, :] = g_ref[0:n_rows, :]
    buf[1, 0 : n_first - n_rows, :] = g_ref[n_rows:n_first, :]
    core = core_of(place_ref)
    for shard in range(2):
        mine_ref[shard] = buf[shard, rows_at(core * HALF_UNIT, HALF_UNIT), :]
        other_ref[shard] = buf[shard, rows_at((1 - core) * HALF_UNIT, HALF_UNIT), :].astype(bf16)


def first_parts_kernel(place_ref, mine_ref, got_ref, keep_ref, s1, s2, s3):
    for k, ref in enumerate((keep_ref, s1, s2, s3)):
        at = lax.rem(place_ref[1] ^ k, 2)
        ref[...] = (mine_ref[at] + got_ref[at].astype(f32)).astype(ref.dtype)


def sum_low_kernel(*refs):
    *ins, sum_ref, low_ref = refs
    total = ins[0][...]
    for ref in ins[1:]:
        total = total + ref[...].astype(f32)
    sum_ref[...] = total
    low_ref[...] = total.astype(bf16)


def sum_first_matrix(n_rows, grad, place_ids, work):
    pair = (2, HALF_UNIT, C)
    mine, other = call(
        functools.partial(first_halves_kernel, n_rows),
        [out(pair), out(pair, bf16)],
        [pltpu.VMEM((2, 2 * HALF_UNIT, C), f32)],
        place_ids,
        grad,
        smem=1,
        name="first_halves",
    )
    got = across(other, 1)
    beside = work.pop(0)([mine])
    one, low = out((HALF_UNIT, C)), out((HALF_UNIT, C), bf16)
    mine, *sends = call(
        first_parts_kernel,
        [one, low, low, low],
        [],
        place_ids,
        mine,
        got,
        smem=1,
        name="first_parts",
        after=beside,
    )
    got = [
        lax.ppermute(send, "height", [(h, h ^ k) for h in range(4)])
        for k, send in zip((1, 2, 3), sends)
    ]
    beside = []
    while work:
        beside = beside + work.pop(0)([mine])
    total, low_total = call(
        sum_low_kernel, [one, low], [], mine, *got, name="first_height", after=beside
    )
    got = [across(low_total, mask, [mask, mask + 1]) for mask in (2, 4, 6)]
    total, low_total = call(sum_low_kernel, [one, low], [], total, *got, name="first_plane")
    return [total, across(low_total, 1, [1])]


def lamb_kernel(
    n_rows,
    place_ref,
    a0,
    a1,
    a2,
    a3,
    first_half_ref,
    second_half_ref,
    w_ref,
    m_ref,
    v_ref,
    first_ref,
    second_ref,
    update_ref,
    sums_ref,
    g_ref,
):
    shard = place_ref[0] * 4 + place_ref[1]
    early = a0[...] + a1[...].astype(f32) + a2[...].astype(f32) + a3[...].astype(f32)
    g_ref[...] = early
    n_first = MATRIX_ROWS[0]

    @pl.when(shard == 0)
    def _():
        g_ref[0:HALF_UNIT, :] = first_half_ref[...]
        g_ref[HALF_UNIT:n_rows, :] = second_half_ref[0 : n_rows - HALF_UNIT, :].astype(f32)

    @pl.when(shard == 1)
    def _():
        rest = n_first - n_rows
        g_ref[0:HALF_UNIT, :] = first_half_ref[...]
        g_ref[HALF_UNIT:rest, :] = second_half_ref[0 : rest - HALF_UNIT, :].astype(f32)

    w, m, v = (as_rows(ref, n_rows) for ref in (w_ref, m_ref, v_ref))
    first, second, update = lamb_terms(w, g_ref[0:n_rows, :], m, v, weight_decay)
    put_as_lines(first_ref, first)
    put_as_lines(second_ref, second)
    update_ref[...] = update
    member = membership(n_rows, shard)
    sums_ref[...] = jnp.zeros_like(sums_ref)
    for k, value in enumerate((w, update)):
        by_row = jnp.sum(value * value, axis=1, keepdims=True)
        sums_ref[k : k + 1, 0:128] = jnp.sum(member * by_row, axis=0, keepdims=True)


def membership(n_rows, shard):
    row = lax.broadcasted_iota(jnp.int32, (n_rows, 128), 0) + shard * n_rows
    lane = lax.broadcasted_iota(jnp.int32, (n_rows, 128), 1)
    result = jnp.zeros((n_rows, 128), f32)
    for k in range(len(MATRIX_ROWS)):
        inside = (row >= ROW_BOUNDS[k]) & (row < ROW_BOUNDS[k + 1]) & (lane == k)
        result = jnp.where(inside, 1.0, result)
    return result


VEC_ROWS = 24


LINES = 72
LINE_F1 = 4 * C // 128
LINE_E2 = LINE_F1 + (E2 - F1) * C // 128
LINE_F2 = LINE_E2 + SE_B // 128


def as_lines(flat):
    return jnp.pad(flat, (0, LINES * 128 - flat.shape[0])).reshape(LINES, 128)


def from_lines(lines):
    return lines.reshape(-1)[: sum(vector_sizes())]


def line_pieces():
    return ((LINE_F1, F1, E2 - F1), (LINE_F2, F2, 18 - F2))


def tables_kernel(*refs):
    lines = refs[-1]
    n = len(refs) // 2
    lane = lax.broadcasted_iota(jnp.int32, (LINES, 128), 1)
    for src, dst in zip(refs[:n], refs[n : 2 * n]):
        dst[...] = jnp.zeros_like(dst)
        for j in range(C // 128):
            dst[0:4, j * 128 : (j + 1) * 128] = src[pl.ds(j, 4, stride=C // 128), :]
        head = src[LINE_F1 : LINE_F1 + 1, :]
        dst[E1 : E1 + 1, 0:128] = jnp.where(lane[0:1] < SE_A, head, 0.0)
        here = pltpu.roll(src[...], 128 - SE_A, 1)
        below = pltpu.roll(here, LINES - 1, 0)
        lines[...] = jnp.where(lane < 128 - SE_A, here, below)
        dst[E2 : E2 + 1, 0:128] = lines[LINE_E2 : LINE_E2 + 1, :]
        for line, row, count in line_pieces():
            for j in range(C // 128):
                dst[row : row + count, j * 128 : (j + 1) * 128] = lines[
                    pl.ds(line + j, count, stride=C // 128), :
                ]


def put_lines(table, dst, lines):
    lane = lax.broadcasted_iota(jnp.int32, (LINES, 128), 1)
    line_at = lax.broadcasted_iota(jnp.int32, (LINES, 128), 0)
    lines[...] = jnp.zeros_like(lines)
    lines[LINE_F1 : LINE_F1 + 1, :] = pltpu.roll(table[E1 : E1 + 1, 0:128], 128 - SE_A, 1)
    lines[LINE_E2 + 1 : LINE_E2 + 2, :] = table[E2 : E2 + 1, 0:128]
    for line, row, count in line_pieces():
        for j in range(C // 128):
            lines[pl.ds(line + 1 + j, count, stride=C // 128), :] = table[
                row : row + count, j * 128 : (j + 1) * 128
            ]
    before = pltpu.roll(lines[...], SE_A, 1)
    here = pltpu.roll(before, LINES - 1, 0)
    dst[...] = jnp.where(lane < SE_A, before, here)
    for j in range(C // 128):
        dst[pl.ds(j, 4, stride=C // 128), :] = table[0:4, j * 128 : (j + 1) * 128]


def as_rows(ref, n_rows):
    return jnp.concatenate(
        [ref[pl.ds(j, n_rows, stride=C // 128), :] for j in range(C // 128)], axis=1
    )


def put_as_lines(ref, value):
    for j in range(C // 128):
        ref[pl.ds(j, value.shape[0], stride=C // 128), :] = value[:, j * 128 : (j + 1) * 128]


def round_rows_kernel(n_rows, *refs):
    n = len(refs) // 2
    for src, dst in zip(refs[:n], refs[n:]):
        rows = as_rows(src, n_rows)
        fill = jnp.zeros((dst.shape[0] - n_rows, C), f32)
        dst[...] = jnp.concatenate([rows, fill], axis=0).astype(bf16)


def vector_grads_kernel(a, b, cs, d, e, f, de1, df1, de2, df2, sums_ref, o_ref):
    o_ref[...] = jnp.zeros_like(o_ref)
    plan = [
        (G1A, a, 1),
        (B1A, a, 0),
        (G1B, b, 1),
        (B1B, b, 0),
        (F1, df1, 0),
        (G1C, cs, 1),
        (B1C, cs, 0),
        (G1S, cs, 2),
        (B1S, cs, 0),
        (G2A, d, 1),
        (B2A, d, 0),
        (G2B, e, 1),
        (B2B, e, 0),
        (F2, df2, 0),
        (G2C, f, 1),
        (B2C, f, 0),
    ]
    for row, ref, k in plan:
        o_ref[row : row + 1, :] = ref[k : k + 1, :]
    o_ref[E1 : E1 + 1, 0:HID] = de1[0:1, :]
    o_ref[E2 : E2 + 1, 0:HID] = de2[0:1, :]
    o_ref[VEC_ROWS : VEC_ROWS + 8, :] = sums_ref[...]


def finish_kernel(
    n_rows,
    place_ref,
    r0,
    r1,
    r2,
    r3,
    w_ref,
    update_ref,
    vec_ref,
    vf_ref,
    vs_ref,
    new_w_ref,
    new_v_ref,
    new_vf_ref,
    new_vs_ref,
    norm_ref,
    slots,
    lines,
):
    place = place_ref[1]
    shard = place_ref[0] * 4 + place
    for k, ref in enumerate((r0, r1, r2, r3)):
        slots[place ^ k] = ref[...]
    total = slots[0] + slots[1] + slots[2] + slots[3]
    norms = jnp.sqrt(total[VEC_ROWS : VEC_ROWS + 8, 0:128])
    norm_ref[...] = norms
    lane = lax.broadcasted_iota(jnp.int32, (1, 128), 1)
    ratio = jnp.where(
        lane < len(MATRIX_ROWS), learn_rate * (norms[0:1] / norms[1:2]), 0.0
    )
    by_row = jnp.sum(membership(n_rows, shard) * ratio, axis=1, keepdims=True)
    put_as_lines(new_w_ref, as_rows(w_ref, n_rows) - by_row * update_ref[...])
    vec = vec_ref[...]
    first, second, update = lamb_terms(vec, total[0:VEC_ROWS], vf_ref[...], vs_ref[...], 0.0)
    put_lines(first, new_vf_ref, lines)
    put_lines(second, new_vs_ref, lines)
    size = jnp.sqrt(jnp.sum(vec * vec, axis=1, keepdims=True))
    change = jnp.sqrt(jnp.sum(update * update, axis=1, keepdims=True))
    put_lines(vec - learn_rate * (size / change) * update, new_v_ref, lines)


def lamb_terms(param, grad_val, first_old, second_old, decay):
    first_new = beta_one * first_old + (1.0 - beta_one) * grad_val
    second_new = beta_two * second_old + (1.0 - beta_two) * grad_val * grad_val
    update = (
        first_new
        / (1.0 - beta_one**STEP)
        / (jnp.sqrt(second_new / (1.0 - beta_two**STEP)) + adam_eps)
        + decay * param
    )
    return (first_new, second_new, update)


def body(
    image_glob,
    image_loc,
    cot_glob,
    cot_loc,
    weights,
    first_moment,
    second_moment,
    vectors,
    vec_first,
    vec_second,
):
    n_height = lax.axis_size("height")
    place = lax.axis_index("height")
    sz = Sizes(image_glob, image_loc, n_height)
    m = sz.m
    part = functools.partial
    place_ids = jnp.stack([lax.axis_index("batch"), place]).astype(jnp.int32)
    shapes = matrix_shapes()
    mat_lengths = [dims_pair[0] * dims_pair[1] for dims_pair in shapes]
    def prepare(before):
        x, x_edge = call(
            part(prepare_kernel, sz),
            [out((4 * m, CIN), bf16), out((2 * sz.edge, CIN), bf16)],
            [pltpu.VMEM((sz.hg * sz.wg, 128), f32)] * 2,
            image_glob,
            image_loc,
            name="prepare",
            after=before,
            room=6 * 2**20,
        )
        x_above = step_down(x_edge)
        gram_scr = pltpu.VMEM((CIN + 8, CIN), f32)
        (gram,) = call(part(gram_kernel, sz), [out(PACKED)], [gram_scr], x, name="gram", after=[x_above])
        gram = over_height(gram)
        return x, x_above, gram, gram_scr

    by_rows = (
        weights.shape[0] % C == 0
        and weights.shape[0] // C <= UNIT
        and lax.axis_size("batch") == 8
        and n_height == 4
    )
    shard_rows = weights.shape[0] // C
    table = out((VEC_ROWS, C))
    tables = call(
        tables_kernel,
        [table] * 3,
        [pltpu.VMEM((LINES, 128), f32)],
        *(as_lines(v) for v in (vectors, vec_first, vec_second)),
        name="tables",
    )
    vt = tables[0]
    early = list(tables)
    if by_rows:
        w_lines, m_lines, v_lines = (
            v.reshape(-1, 128) for v in (weights, first_moment, second_moment)
        )

    if by_rows:

        def beside(quarter):
            prepared = prepare([quarter])
            return early + [prepared[1]] + prepared[2][1:], prepared

        matrices, prepared = gather_weights(w_lines, shard_rows, place_ids, beside)
    else:
        prepared = prepare([])
        gathered = lax.all_gather(weights.astype(bf16), both_axes, axis=0, tiled=True)
        matrices = [
            flat_piece.reshape(dims_pair)
            for flat_piece, dims_pair in zip(cut_pieces(gathered, mat_lengths), shapes)
        ]
    w1, k1, d1, u1, p1, s1, w2, k2, d2, u2, p2 = matrices
    x, x_above, gram, gram_scr = prepared
    if not by_rows:
        d1 = jnp.pad(d1, ((0, 0), (0, HID - SE_A)))
        u1 = jnp.pad(u1, ((0, HID - SE_A), (0, 0)))
    st8 = out((8, C))
    mat = out((m, C))
    mat_low = out((m, C), bf16)
    pool_low = out((sz.crops, C), bf16)
    pool_scr = pltpu.VMEM((sz.crops, C), f32)
    sum_scr = pltpu.VMEM((24, C), f32)

    bd_scr = pltpu.VMEM((18, HALF, HALF), bf16)
    low_scr = pltpu.VMEM((m, C), bf16)
    mat_scr = pltpu.VMEM((m, C), f32)
    one_scr = pltpu.VMEM((sz.one, C), bf16)
    two_scr = pltpu.VMEM((sz.two, C), bf16)
    edge_scr = pltpu.VMEM((sz.edge, C), f32)
    edge = out((sz.edge, C), bf16)
    one_shape = out((sz.one, C), bf16)
    nrm_a, *act_a = call(
        part(first_act_kernel, sz),
        [st8, mat_low, mat_low, one_shape, one_shape, mat_low, one_shape],
        [mat_scr, gram_scr],
        place_ids,
        x,
        x_above,
        w1,
        *gram,
        vt,
        smem=1,
        name="first_act",
    )
    zb, st_b = call(
        part(first_conv_kernel, sz),
        [mat, st8],
        [bd_scr, sum_scr],
        x,
        s1,
        k1,
        *act_a,
        name="first_conv",
    )
    act_a = act_a[:4]
    st_b = over_height(st_b)
    pool_b, nrm_b = call(
        part(pool_kernel, sz, G1B, B1B, True), [pool_low, st8], [pool_scr], zb, *st_b, vt, name="pool_b",
    )
    pool_b = over_height(pool_b)
    hid = out((sz.crops, HID))
    crop_mat = out((sz.crops, C))
    qb, zc, st_c, gate_b, pooled_b, hidden_b = call(
        part(gated_product_kernel, sz, E1, F1),
        [mat_low, mat, st8, crop_mat, crop_mat, hid],
        [],
        zb,
        nrm_b,
        *pool_b,
        d1,
        u1,
        p1,
        vt,
        name="gated_b",
    )
    st_c = over_height(st_c)
    pre_mid, mid_low, nrm_c, mid_top, mid_bottom = call(
        part(middle_kernel, sz),
        [mat, mat_low, st8, edge, edge],
        [mat_scr],
        zc,
        x,
        s1,
        *st_c,
        nrm_b,
        vt,
        name="middle",
    )
    mid_above = step_down(mid_bottom)
    mid_below = step_up(mid_top)
    zd, st_d = call(
        part(product_kernel, sz), [mat, st8], [], mid_low, w2, name="product_d"
    )
    st_d = over_height(st_d)
    two_shape = out((sz.two, C), bf16)
    ze, st_e, nrm_d, act_d = call(
        part(second_conv_kernel, sz),
        [mat, st8, st8, two_shape],
        [two_scr, two_scr, bd_scr, edge_scr, sum_scr],
        place_ids,
        zd,
        mid_above,
        mid_below,
        w2,
        k2,
        *st_d,
        vt,
        smem=1,
        name="second_conv",
    )
    st_e = over_height(st_e)
    pool_e, nrm_e = call(
        part(pool_kernel, sz, G2B, B2B, False), [pool_low, st8], [pool_scr], ze, *st_e, vt, name="pool_e",
    )
    pool_e = over_height(pool_e)
    qe, zf, st_f, gate_e, pooled_e, hidden_e = call(
        part(gated_product_kernel, sz, E2, F2),
        [mat_low, mat, st8, crop_mat, crop_mat, hid],
        [],
        ze,
        nrm_e,
        *pool_e,
        d2,
        u2,
        p2,
        vt,
        name="gated_e",
    )
    st_f = over_height(st_f)
    out_glob, out_loc, dpre, bst_f, nrm_f = call(
        part(output_kernel, sz),
        [out(cot_glob.shape, bf16), out(cot_loc.shape, bf16), mat, st8, st8],
        [sum_scr],
        pre_mid,
        zf,
        *st_f,
        vt,
        cot_glob,
        cot_loc,
        name="output",
        room=6 * 2**20,
    )
    bst_f_all = over_height(bst_f)

    dzf, dqe, dg_e = call(
        part(gate_grad_kernel, sz, False),
        [mat_low, mat, pool_low],
        [pool_scr],
        dpre,
        zf,
        *bst_f_all,
        nrm_f,
        p2,
        ze,
        nrm_e,
        name="gate_grad_e",
    )
    dg_e = over_height(dg_e)
    (mat_f,) = call(
        weight_kernel, [out((C, C))], [], qe, dzf, name="weight_f"
    )
    dn_e, bst_e, dv_e, du_e = call(
        part(excite_back_kernel, sz),
        [mat, st8, crop_mat, hid],
        [pool_scr, sum_scr],
        dqe,
        ze,
        nrm_e,
        *dg_e,
        gate_e,
        hidden_e,
        d2,
        u2,
        name="excite_back_e",
        after=[mat_f],
    )
    bst_e_all = over_height(bst_e)
    se_outs = lambda width: [out((width, C)), out((8, HID)), out((HID, C)), st8]
    se_scr = [pltpu.VMEM((C, HID), f32), pltpu.VMEM((HID, 128), f32)]
    dd2, de2, du2, df2 = call(
        part(excite_weights_kernel, SE_B),
        se_outs(SE_B),
        se_scr,
        place_ids,
        dv_e,
        du_e,
        pooled_e,
        hidden_e,
        smem=1,
        name="excite_weights_e",
    )
    dze, dze_top, dze_bottom = call(
        part(norm_back_kernel, sz),
        [mat_low, edge, edge],
        [],
        dn_e,
        ze,
        *bst_e_all,
        nrm_e,
        name="norm_back_e",
        after=[dd2],
    )
    dze_above = step_down(dze_bottom)
    dze_below = step_up(dze_top)
    (mat_e,) = call(
        part(second_conv_weights_kernel, sz),
        [out((9 * GW, C))],
        [two_scr, two_scr],
        act_d,
        dze,
        name="second_conv_weights",
    )
    dn_d, bst_d = call(
        part(second_conv_back_kernel, sz),
        [mat, st8],
        [two_scr, two_scr, two_scr, bd_scr, sum_scr],
        dze,
        dze_above,
        dze_below,
        k2,
        zd,
        nrm_d,
        name="second_conv_back",
        after=[mat_e],
    )
    bst_d_all = over_height(bst_d)
    dzd, dn_mid, bst_cs = call(
        part(middle_back_kernel, sz),
        [mat_low, mat, st8],
        [mat_scr, sum_scr],
        dn_d,
        zd,
        *bst_d_all,
        nrm_d,
        w2,
        dpre,
        pre_mid,
        zc,
        x,
        s1,
        nrm_c,
        nrm_b,
        name="middle_back",
    )
    bst_cs_all = over_height(bst_cs)
    spans = list(zip(ROW_BOUNDS[:-1], ROW_BOUNDS[1:]))
    early = EarlySum(shard_rows, place_ids)
    dzc, dzs, dqb, dg_b = call(
        part(gate_grad_kernel, sz, True),
        [mat_low, mat_low, mat, pool_low],
        [pool_scr, mat_scr],
        dn_mid,
        zc,
        *bst_cs_all,
        nrm_c,
        p1,
        zb,
        nrm_b,
        x,
        s1,
        nrm_b,
        name="gate_grad_b",
    )
    dg_b = over_height(dg_b)
    (mat_d,) = call(
        weight_kernel,
        [out((C, C))],
        [],
        mid_low,
        dzd,
        name="weight_d",
        after=[dzc],
    )
    (mat_c,) = call(
        weight_kernel, [out((C, C))], [], qb, dzc, name="weight_c"
    )
    (mat_s,) = call(
        weight_kernel, [out((CIN, C))], [], x, dzs, name="weight_s"
    )
    dn_b, bst_b, dv_b, du_b = call(
        part(excite_back_kernel, sz),
        [mat, st8, crop_mat, hid],
        [pool_scr, sum_scr],
        dqb,
        zb,
        nrm_b,
        *dg_b,
        gate_b,
        hidden_b,
        d1,
        u1,
        name="excite_back_b",
        after=[mat_d, mat_c, mat_s],
    )
    bst_b_all = over_height(bst_b)
    dd1, de1, du1, df1 = call(
        part(excite_weights_kernel, SE_A),
        se_outs(SE_A),
        se_scr,
        place_ids,
        dv_b,
        du_b,
        pooled_b,
        hidden_b,
        smem=1,
        name="excite_weights_b",
    )
    dzb, dzb_top = call(
        part(norm_back_kernel, sz),
        [mat_low, edge],
        [],
        dn_b,
        zb,
        *bst_b_all,
        nrm_b,
        name="norm_back_b",
        after=early.pack(spans[3:], [du1, mat_c, mat_s, mat_d, mat_e, dd2, du2, mat_f])
        if by_rows
        else [dd1],
    )
    dzb_below = step_up(dzb_top)
    (mat_b,) = call(
        part(first_conv_weights_kernel, sz),
        [out((9 * GW, C))],
        [low_scr, one_scr],
        *act_a,
        dzb,
        name="first_conv_weights",
    )
    hold = [mat_b]
    if by_rows:
        hold = hold + early.pack_first_unit(spans[1:4], [mat_b, dd1, du1], [dzb_below])
    v0, v1, bd1 = call(
        part(first_conv_back_kernel, sz),
        [one_shape, one_shape, out((18, HALF, HALF), bf16)],
        [],
        dzb,
        dzb_below,
        k1,
        name="first_conv_back",
        after=hold,
    )
    dn_a, bst_a = [], []
    hold = [[], [], [], []]
    if by_rows:
        hold[1] = early.first([v0])
    for phase in range(4):
        dn_phase, *bst_a = call(
            part(parity_back_kernel, sz, phase),
            [mat_low, st8],
            [mat_scr, mat_scr, sum_scr],
            v0,
            v1,
            bd1,
            x,
            w1,
            nrm_a,
            *bst_a,
            name="parity_back_%d" % phase,
            after=hold[phase],
        )
        dn_a.append(dn_phase)
    (bst_a,) = bst_a
    bst_a_all = over_height(bst_a)
    hold = []
    if by_rows:
        hold = early.second([bst_a])
    (dza,) = call(
        part(image_norm_back_kernel, sz),
        [out((4 * m, C), bf16)],
        [pltpu.VMEM((4 * m, C), f32)],
        *dn_a,
        x,
        w1,
        *bst_a_all,
        nrm_a,
        name="image_norm_back",
        after=hold,
    )
    (mat_a,) = call(
        weight_kernel,
        [out((CIN, C))],
        [],
        x,
        dza,
        name="weight_a",

    )
    made = {}

    def image_product(beside):
        (made["dx"],) = call(
            part(image_product_kernel, sz),
            [out((4 * m, CIN))],
            [],
            dza,
            w1,
            dzs,
            s1,
            name="image_product",
            after=beside,
        )
        return [made["dx"]]

    def place_maps(key, shape, first_row, block, beside):
        n_crops, height, width = shape[:3]
        made[key], mark = call(
            part(place_kernel, n_crops, height, width, first_row, block, m),
            [out(shape), out((8, 128))],
            [pltpu.VMEM((6, height * width, 128), f32)] * 2,
            made["dx"],
            name="place_" + key,
            room=8 * 2**20,
            after=beside,
        )
        return [mark]

    work = [
        image_product,
        lambda beside: place_maps("glob", image_glob.shape, 0, sz.bg, beside),
        lambda beside: place_maps("loc", image_loc.shape, sz.mg, sz.bl, beside),
    ]
    if not by_rows:
        for one_work in work:
            one_work([])
    if by_rows:
        work[0] = lambda beside: early.height(image_product(beside))
        last = sum_first_matrix(shard_rows, mat_a, place_ids, work)
        shard_out = out((shard_rows, C))
        lines_out = out(w_lines.shape)
        new_first, new_second, update, sums = call(
            part(lamb_kernel, shard_rows),
            [lines_out, lines_out, shard_out, st8],
            [pltpu.VMEM((UNIT, C), f32)],
            place_ids,
            *early.result,
            *last,
            w_lines,
            m_lines,
            v_lines,
            smem=1,
            name="lamb",
        )
        (small,) = call(
            vector_grads_kernel,
            [out((VEC_ROWS + 8, C))],
            [],
            bst_a,
            bst_b,
            bst_cs,
            bst_d,
            bst_e,
            bst_f,
            de1,
            df1,
            de2,
            df2,
            sums,
            name="vector_grads",
        )
        small = small + across(small, 1)
        other_x, other_y, other_both = (across(small, mask) for mask in (2, 4, 6))
        small = (small + other_x) + (other_y + other_both)
        new_weights, new_v, new_vf, new_vs, norms = call(
            part(finish_kernel, shard_rows),
            [lines_out] + [out((LINES, 128))] * 3 + [out((8, 128))],
            [pltpu.VMEM((4, VEC_ROWS + 8, C), f32), pltpu.VMEM((LINES, 128), f32)],
            place_ids,
            *over_height(small),
            w_lines,
            update,
            *tables,
            smem=1,
            name="finish",
            room=2 * 2**20,
        )
        maps_out = (out_glob, out_loc, made["glob"], made["loc"])
        return maps_out + (
            new_weights.reshape(-1),
            new_first.reshape(-1),
            new_second.reshape(-1),
            from_lines(new_v),
            from_lines(new_vf),
            from_lines(new_vs),
            norms[:2, : len(MATRIX_ROWS)],
        )

    maps_out = (out_glob, out_loc, made["glob"], made["loc"])
    flat_grad = jnp.concatenate(
        [
            piece.reshape(-1)
            for piece in (
                mat_a,
                mat_b,
                dd1,
                du1[:SE_A],
                mat_c,
                mat_s,
                mat_d,
                mat_e,
                dd2,
                du2,
                mat_f,
            )
        ]
    )
    vec_grad = jnp.concatenate(
        [
            bst_a[1],
            bst_a[0],
            bst_b[1],
            bst_b[0],
            de1[0, :SE_A],
            df1[0],
            bst_cs[1],
            bst_cs[0],
            bst_cs[2],
            bst_cs[0],
            bst_d[1],
            bst_d[0],
            bst_e[1],
            bst_e[0],
            de2[0],
            df2[0],
            bst_f[1],
            bst_f[0],
        ]
    )
    grad_shard = lax.psum_scatter(flat_grad, both_axes, scatter_dimension=0, tiled=True)
    shard_len = weights.shape[0]
    device_index = lax.axis_index("batch") * n_height + lax.axis_index("height")
    position = device_index * shard_len + lax.iota(jnp.int32, shard_len)
    bounds = np.cumsum([0] + mat_lengths)
    lower_edge = jnp.asarray(bounds[:-1], jnp.int32)
    upper_edge = jnp.asarray(bounds[1:], jnp.int32)
    member = (
        (position[:, None] >= lower_edge[None, :]) & (position[:, None] < upper_edge[None, :])
    ).astype(f32)
    new_first, new_second, update = lamb_terms(
        weights, grad_shard, first_moment, second_moment, weight_decay
    )
    part_sums = jnp.dot(jnp.stack([weights * weights, update * update]), member, precision=highest)
    vec_total, totals = lax.psum((vec_grad, part_sums), both_axes)
    norm_pair = jnp.sqrt(totals)
    trust_ratio = learn_rate * (norm_pair[0] / norm_pair[1])
    new_weights = weights - jnp.dot(member, trust_ratio, precision=highest) * update
    vec_one_new, vec_two_new, vec_update = lamb_terms(vectors, vec_total, vec_first, vec_second, 0.0)
    vec_pieces = []
    for param_piece, update_piece in zip(
        cut_pieces(vectors, vector_sizes()), cut_pieces(vec_update, vector_sizes())
    ):
        ratio_val = jnp.sqrt(jnp.sum(param_piece * param_piece)) / jnp.sqrt(
            jnp.sum(update_piece * update_piece)
        )
        vec_pieces.append(param_piece - learn_rate * ratio_val * update_piece)
    new_vectors = jnp.concatenate(vec_pieces)
    return maps_out + (
        new_weights,
        new_first,
        new_second,
        new_vectors,
        vec_one_new,
        vec_two_new,
        norm_pair,
    )


def solution(mesh):
    maps = P("batch", "height", None, None)
    entries = P(("batch", "height"))
    return jax.shard_map(
        body,
        mesh=mesh,
        in_specs=(maps, maps, maps, maps, entries, entries, entries, P(), P(), P()),
        out_specs=(maps, maps, maps, maps, entries, entries, entries, P(), P(), P(), P()),
        check_vma=False,
    )
```

```python
import functools

import jax
import jax.numpy as jnp
import numpy as np
from jax import lax
from jax.experimental import pallas as pl
from jax.experimental.pallas import tpu as pltpu
from jax.sharding import PartitionSpec as P

CIN = 192
C = 512
GW = 64
GROUPS = 8
SE_A = 48
SE_B = 128
STEP = 10
HID = 128
HALF = 256

norm_eps = 1e-05
beta_one = 0.9
beta_two = 0.999
adam_eps = 1e-06
weight_decay = 0.01
learn_rate = 0.4
highest = lax.Precision.HIGHEST
bf16 = jnp.bfloat16
f32 = jnp.float32
both_axes = ("batch", "height")

G1A, B1A, G1B, B1B, E1, F1, G1C, B1C, G1S, B1S, G2A, B2A, G2B, B2B, E2, F2, G2C, B2C = range(18)


def matrix_shapes():
    return [
        (CIN, C),
        (9 * GW, C),
        (C, SE_A),
        (SE_A, C),
        (C, C),
        (CIN, C),
        (C, C),
        (9 * GW, C),
        (C, SE_B),
        (SE_B, C),
        (C, C),
    ]


def vector_sizes():
    return [C, C, C, C, SE_A, C, C, C, C, C, C, C, C, C, SE_B, C, C, C]


def cut_pieces(flat_vec, lengths):
    pieces = []
    offset = 0
    for length in lengths:
        pieces.append(flat_vec[offset : offset + length])
        offset += length
    return pieces


class Sizes:
    def __init__(self, image_glob, image_loc, n_height):
        self.ng, self.hg, self.wg = image_glob.shape[:3]
        self.nl, self.hl, self.wl = image_loc.shape[:3]
        self.rg, self.cg = self.hg // 2, self.wg // 2
        self.rl, self.cl = self.hl // 2, self.wl // 2
        self.bg, self.bl = self.ng * self.cg, self.nl * self.cl
        self.mg, self.ml = self.rg * self.bg, self.rl * self.bl
        self.m = self.mg + self.ml
        self.edge = self.bg + self.bl
        self.n_height = n_height
        self.crops = -(-(self.ng + self.nl) // 16) * 16
        self.area_g = self.rg * self.cg * n_height
        self.area_l = self.rl * self.cl * n_height
        self.amount = n_height * self.m
        self.one_l = (self.rg + 1) * self.bg
        self.one = self.one_l + (self.rl + 1) * self.bl
        self.two_l = (self.rg + 2) * self.bg
        self.two = self.two_l + (self.rl + 2) * self.bl


def sigmoid(v):
    return 0.5 * jnp.tanh(0.5 * v) + 0.5


def silu(v):
    return v * sigmoid(v)


def silu_slope(v):
    s = sigmoid(v)
    return s * (1.0 + v * (1.0 - s))


def padded_bytes(shape, dtype):
    size = np.dtype(dtype).itemsize
    dims = list(shape)
    dims[-1] = -(-dims[-1] // 128) * 128
    if len(dims) > 1:
        rows = 32 // size
        dims[-2] = -(-dims[-2] // rows) * rows
    return int(np.prod(dims)) * size


COST_SCALE = 1.0
MEASURED_US = {
    "first_conv_back": 1.5,
    "parity_back_0": 2.6,
    "parity_back_1": 3.0,
    "parity_back_2": 3.0,
    "parity_back_3": 3.7,
    "first_conv": 5.0,
    "first_act": 7.5,
    "second_conv": 6.3,
    "second_conv_back": 5.9,
    "image_norm_back": 5.8,
    "second_conv_weights": 4.9,
    "first_conv_weights": 4.5,
    "middle_back": 4.4,
    "gate_grad_b": 4.2,
    "gram": 3.6,
    "image_product": 3.6,
    "place_glob": 3.1,
    "output": 2.9,
    "assemble": 2.9,
    "gate_grad_e": 2.7,
    "excite_back_b": 2.6,
    "excite_back_e": 2.6,
    "place_loc": 2.5,
    "gated_b": 2.4,
    "gated_e": 2.4,
    "finish": 1.9,
    "middle": 1.8,
    "prepare": 1.4,
    "excite_weights_b": 1.3,
    "excite_weights_e": 1.2,
    "product_d": 1.1,
    "weight_a": 1.1,
    "pack_0": 1.0,
    "pack_1": 1.0,
    "pool_b": 1.0,
    "pool_e": 1.0,
    "lamb": 1.0,
    "weight_f": 0.9,
    "weight_d": 0.9,
    "weight_c": 0.9,
}


def call(kernel, outs, scratch, *ins, smem=0, name=None, after=(), room=0):
    held = sum(padded_bytes(s.shape, s.dtype) for s in scratch)
    n_in, n_after = len(ins), len(after)

    def run(*refs):
        kernel(*refs[:n_in], *refs[n_in + n_after :])

    return pl.pallas_call(
        run,
        out_shape=tuple(outs),
        in_specs=[pl.BlockSpec(memory_space=pltpu.SMEM)] * smem
        + [pl.BlockSpec(memory_space=pltpu.VMEM)] * (n_in - smem)
        + [pl.BlockSpec(memory_space=pl.ANY)] * n_after,
        out_specs=tuple(pl.BlockSpec(memory_space=pltpu.VMEM) for _ in outs),
        scratch_shapes=list(scratch),
        compiler_params=pltpu.CompilerParams(vmem_limit_bytes=held + 4 * 2**20 + room),
        cost_estimate=pl.CostEstimate(
            flops=int(MEASURED_US.get(name, 0.5) * COST_SCALE * 1.1535e9),
            bytes_accessed=1,
            transcendentals=0,
        ),
        name=name,
    )(*ins, *after)


def out(shape, dtype=f32):
    return jax.ShapeDtypeStruct(shape, dtype)


def above(ids, n_height=0):
    return jnp.where(ids[1] > 0, 1.0, 0.0)


def below(ids, n_height):
    return jnp.where(ids[1] < n_height - 1, 1.0, 0.0)


def first_of_height(ids):
    return jnp.where(ids[1] == 0, 1.0, 0.0)


def y_of(ids):
    return ids[0] // 4


def x_of(ids):
    return lax.rem(ids[0] // 2, 2)


def core_of(ids):
    return lax.rem(ids[0], 2)


def fold(x):
    return jnp.sum(x.reshape(x.shape[0] // 8, 8, x.shape[1]), axis=0)


def rows_at(start, size, unit=16):
    return pl.ds(pl.multiple_of(start, unit), size)


def put_rows(ref, parts):
    ref[...] = jnp.zeros_like(ref)
    for k, part in enumerate(parts):
        ref[k : k + 1, :] = jnp.sum(part, axis=0, keepdims=True)


def put_back_sums(ref, one, two, mean, inverse):
    one = jnp.sum(one, axis=0, keepdims=True)
    two = jnp.sum(two, axis=0, keepdims=True)
    put_rows(ref, [one, (two - mean * one) * inverse])


def gather_sum(refs):
    total = refs[0][...]
    for ref in refs[1:]:
        total = total + ref[...]
    return total


def norm_terms(total, row, amount, gain, shift):
    mean = total[row : row + 1] / amount
    inverse = lax.rsqrt(total[row + 1 : row + 2] / amount - mean * mean + norm_eps)
    scale = gain * inverse
    return mean, inverse, scale, shift - mean * scale


def put_norm(ref, row, terms):
    for k, term in enumerate(terms):
        ref[row + k : row + k + 1, :] = term


def dot(a, b):
    return jnp.dot(a, b, preferred_element_type=f32)


def dot_t(a, b):
    return lax.dot_general(a, b, (((1,), (1,)), ((), ())), preferred_element_type=f32)


def t_dot(a, b):
    return lax.dot_general(a, b, (((0,), (0,)), ((), ())), preferred_element_type=f32)


def prepare_kernel(sz, ig_ref, il_ref, x_ref, halo_ref, s_ref, t_ref):
    m = sz.m

    def split(x, n_rows):
        s_ref[0:n_rows, :] = x[:, :128]
        t_ref[0:n_rows, 0:64] = x[:, 128:]
        parts = []
        for pc in range(2):
            v = s_ref[pl.ds(pc, n_rows // 2, stride=2), :]
            w = t_ref[pl.ds(pc, n_rows // 2, stride=2), :]
            parts.append(jnp.concatenate([v, w[:, :64]], axis=1))
        return parts

    @pl.loop(0, sz.ng)
    def _(n):
        n_rows = sz.hg * sz.wg
        parts = split(ig_ref[n].astype(f32).reshape(n_rows, CIN), n_rows)
        for pc in range(2):
            v = parts[pc].reshape(sz.hg, sz.cg, CIN).astype(bf16)
            for r in range(sz.hg):
                phase = 2 * (r % 2) + pc
                x_ref[rows_at(phase * m + (r // 2) * sz.bg + n * sz.cg, sz.cg), :] = v[r]

    @pl.loop(0, sz.nl // 2)
    def _(pair):
        n_rows = 2 * sz.hl * sz.wl
        both = jnp.concatenate(
            [
                il_ref[2 * pair + k].astype(f32).reshape(sz.hl * sz.wl, CIN)
                for k in range(2)
            ],
            axis=0,
        )
        parts = split(both, n_rows)
        for pc in range(2):
            v = parts[pc].reshape(2 * sz.hl, sz.cl, CIN)
            for r in range(sz.hl):
                phase = 2 * (r % 2) + pc
                joined = jnp.concatenate([v[r], v[sz.hl + r]], axis=0).astype(bf16)
                x_ref[
                    rows_at(phase * m + sz.mg + (r // 2) * sz.bl + pair * 2 * sz.cl, 2 * sz.cl), :
                ] = joined

    for pc in range(2):
        base = (2 + pc) * m
        halo_ref[pc * sz.edge : pc * sz.edge + sz.bg, :] = x_ref[
            base + sz.mg - sz.bg : base + sz.mg, :
        ]
        halo_ref[pc * sz.edge + sz.bg : (pc + 1) * sz.edge, :] = x_ref[
            base + m - sz.bl : base + m, :
        ]


LOW = 128
PACKED = (LOW + 8, 2 * LOW)


def gram_kernel(sz, x_ref, g_ref, full):
    n_rows = sz.m // PARTS
    ones = jnp.ones((8, n_rows), bf16)
    full[...] = jnp.zeros_like(full)

    @pl.loop(0, 4 * PARTS)
    def _(i):
        x = x_ref[rows_at(i * n_rows, n_rows), :]
        full[0:CIN, :] += t_dot(x, x)
        full[CIN : CIN + 8, :] += dot(ones, x)

    g_ref[...] = jnp.zeros_like(g_ref)
    g_ref[0:LOW, 0:CIN] = full[0:LOW, :]
    g_ref[0 : CIN - LOW, CIN:] = full[LOW:CIN, LOW:CIN]
    g_ref[LOW : LOW + 8, 0:CIN] = full[CIN : CIN + 8, :]


def unpack_gram(packed, full):
    full[0:LOW, :] = packed[0:LOW, 0:CIN]
    full[LOW:CIN, 0:LOW] = jnp.transpose(packed[0:LOW, LOW : 2 * LOW])[0 : CIN - LOW]
    full[LOW:CIN, LOW:CIN] = packed[0 : CIN - LOW, CIN:]
    full[CIN : CIN + 8, :] = packed[LOW : LOW + 8, 0:CIN]


def product_norm_terms(total, w_ref, amount, gain, shift):
    w = w_ref[...].astype(f32)
    mean = dot_high(total[CIN : CIN + 8], w)[0:1] / amount
    square = jnp.sum(w * dot_high(total[0:CIN], w), axis=0, keepdims=True) / amount
    inverse = lax.rsqrt(square - mean * mean + norm_eps)
    scale = gain * inverse
    return mean, inverse, scale, shift - mean * scale


def block_diagonal(k_ref, bd_ref):
    rows = lax.broadcasted_iota(jnp.int32, (HALF, HALF), 0) // GW
    cols = lax.broadcasted_iota(jnp.int32, (HALF, HALF), 1) // GW
    same = rows == cols
    for tap in range(9):
        for half in range(2):
            k = k_ref[tap * GW : (tap + 1) * GW, half * HALF : (half + 1) * HALF].astype(f32)
            bd_ref[2 * tap + half] = jnp.where(same, jnp.concatenate([k] * 4, axis=0), 0.0).astype(
                bf16
            )


def strided_product(sz, x_ref, s_ref, zs):
    n_rows = sz.m // PARTS

    @pl.loop(0, PARTS)
    def _(i):
        zs[rows_at(i * n_rows, n_rows), :] = dot(x_ref[rows_at(i * n_rows, n_rows), :], s_ref[...])


def block_dense(acc):
    rows = lax.broadcasted_iota(jnp.int32, (HALF, HALF), 0) // GW
    cols = lax.broadcasted_iota(jnp.int32, (HALF, HALF), 1) // GW
    kept = jnp.where(rows == cols, acc, 0.0)
    return jnp.sum(kept.reshape(4, GW, HALF), axis=0)


def shifted(v, by, width):
    n_rows = v.shape[0]
    col = lax.broadcasted_iota(jnp.int32, v.shape, 0) % width
    if by < 0:
        return jnp.where(col == 0, 0.0, pltpu.roll(v, 1, 0))
    return jnp.where(col == width - 1, 0.0, pltpu.roll(v, n_rows - 1, 0))


def segments(sz):
    g_rows = sz.bg
    l_rows = sz.bl
    return g_rows, l_rows


def conv_product(windows, bd_ref, half, n_rows, transposed):
    acc = None
    cols = pl.ds(pl.multiple_of(half * HALF, HALF), HALF)
    for tap, ref, start in windows:
        x = ref[start : start + n_rows, cols]
        w = bd_ref[2 * tap + half]
        term = dot_t(x, w) if transposed else dot(x, w)
        acc = term if acc is None else acc + term
    return acc


def windows_one(sz, refs, part):
    a00, a01, a01s, a10, a11, a11s = refs
    plain = 0 if part == "g" else sz.mg
    above = 0 if part == "g" else sz.one_l
    here = above + (sz.bg if part == "g" else sz.bl)
    result = []
    for tap in range(9):
        a, b = tap // 3, tap % 3
        if a == 1:
            result.append((tap, (a01s, a00, a01)[b], plain))
        else:
            result.append((tap, (a11s, a10, a11)[b], above if a == 0 else here))
    return result


def windows_two(sz, refs, part, flipped=False):
    base = 0 if part == "g" else sz.two_l
    block = sz.bg if part == "g" else sz.bl
    result = []
    for tap in range(9):
        a, b = tap // 3, tap % 3
        if flipped:
            a, b = 2 - a, 2 - b
        result.append((tap, refs[b], base + a * block))
    return result


def shift_windows(windows, by):
    return [(tap, ref, start + by) for tap, ref, start in windows]


def conv_forward(sz, windows_of, bd_ref, z_ref, st_ref, sums, more=()):
    sums[0:16, :] = jnp.zeros((16, C), f32)

    @pl.loop(0, 2)
    def _(half):
        cols = pl.ds(pl.multiple_of(half * HALF, HALF), HALF)
        for part, first, n_all, n_rows in (
            ("g", 0, sz.mg, sz.mg // 2),
            ("l", sz.mg, sz.ml, sz.ml),
        ):
            for k in range(n_all // n_rows):
                z = conv_product(
                    shift_windows(windows_of(part), k * n_rows), bd_ref, half, n_rows, False
                )
                z_ref[first + k * n_rows : first + (k + 1) * n_rows, cols] = z
                sums[0:8, cols] += fold(z)
                sums[8:16, cols] += fold(z * z)

    put_rows(st_ref, [sums[0:8, :], sums[8:16, :]] + list(more))


def first_act_kernel(
    sz,
    flag_ref,
    x_ref,
    halo_ref,
    w_ref,
    t0,
    t1,
    t2,
    t3,
    vt_ref,
    nrm_ref,
    a00,
    a01,
    a10,
    a11,
    a01s,
    a11s,
    zs,
    gram_scr,
):
    unpack_gram(gather_sum((t0, t1, t2, t3)), gram_scr)
    terms = product_norm_terms(
        gram_scr, w_ref, 4 * sz.amount, vt_ref[G1A : G1A + 1, :], vt_ref[B1A : B1A + 1, :]
    )
    nrm_ref[...] = jnp.zeros_like(nrm_ref)
    put_norm(nrm_ref, 0, terms)
    scale, shift = terms[2], terms[3]
    g_rows, l_rows = segments(sz)
    third = sz.m // PARTS

    def activate(src, dst, dst_s, n_rows, width, factor=None):
        v = zs[src, :] * scale + shift
        a = silu(v)
        if factor is not None:
            a = a * factor
        dst[0][dst[1], :] = a.astype(bf16)
        if dst_s is not None:
            dst_s[dst[1], :] = shifted(a, -1, width).astype(bf16)

    plan = [(a00, None, False), (a01, a01s, False), (a10, None, True), (a11, a11s, True)]
    for phase, (dst, dst_s, bordered) in enumerate(plan):

        @pl.loop(0, PARTS)
        def _(i):
            zs[rows_at(i * third, third), :] = dot(
                x_ref[rows_at(phase * sz.m + i * third, third), :], w_ref[...]
            )

        g_first = sz.bg if bordered else 0
        l_first = sz.one_l + sz.bl if bordered else sz.mg

        @pl.loop(0, sz.mg // g_rows)
        def _(i):
            activate(
                rows_at(i * g_rows, g_rows),
                (dst, rows_at(g_first + i * g_rows, g_rows)),
                dst_s,
                g_rows,
                sz.cg,
            )

        @pl.loop(0, sz.ml // l_rows)
        def _(i):
            activate(
                rows_at(sz.mg + i * l_rows, l_rows),
                (dst, rows_at(l_first + i * l_rows, l_rows)),
                dst_s,
                l_rows,
                sz.cl,
            )

    flag = above(flag_ref)
    for pc, (dst, dst_s) in enumerate(((a10, None), (a11, a11s))):
        zs[0 : sz.edge, :] = dot(halo_ref[pc * sz.edge : (pc + 1) * sz.edge, :], w_ref[...])

        @pl.loop(0, sz.bg // g_rows)
        def _(i):
            rows = rows_at(i * g_rows, g_rows)
            activate(rows, (dst, rows), dst_s, g_rows, sz.cg, flag)

        @pl.loop(0, sz.bl // l_rows)
        def _(i):
            activate(
                rows_at(sz.bg + i * l_rows, l_rows),
                (dst, rows_at(sz.one_l + i * l_rows, l_rows)),
                dst_s,
                l_rows,
                sz.cl,
                flag,
            )


def first_conv_kernel(
    sz, x_ref, s_ref, k_ref, a00, a01, a10, a11, a01s, a11s, z_ref, st_ref, bd_ref, sums
):
    block_diagonal(k_ref, bd_ref)
    third = sz.m // PARTS
    refs = (a00, a01, a01s, a10, a11, a11s)
    zero = jnp.zeros((8, C), f32)

    def step(i, carry):
        total, square = carry
        z = dot(x_ref[rows_at(i * third, third), :], s_ref[...])
        return total + fold(z), square + fold(z * z)

    more = lax.fori_loop(0, PARTS, step, (zero, zero))
    conv_forward(
        sz, lambda part: windows_one(sz, refs, part), bd_ref, z_ref, st_ref, sums, more
    )


def each_crop(sz, one):
    @pl.loop(0, sz.ng, unroll=2)
    def _(n):
        one([rows_at(i * sz.bg + n * sz.cg, sz.cg) for i in range(sz.rg)], (n,))

    @pl.loop(0, sz.nl // 2, unroll=3)
    def _(pair):
        first = sz.ng + 2 * pair
        one(
            [rows_at(sz.mg + i * sz.bl + pair * 2 * sz.cl, 2 * sz.cl) for i in range(sz.rl)],
            (first, first + 1),
        )


def add_pool(ref, crops, value):
    if len(crops) == 1:
        ref[pl.ds(crops[0], 1), :] = jnp.sum(value, axis=0, keepdims=True)
    else:
        n = value.shape[0] // 2
        ref[pl.ds(crops[0], 1), :] = jnp.sum(value[:n], axis=0, keepdims=True)
        ref[pl.ds(crops[1], 1), :] = jnp.sum(value[n:], axis=0, keepdims=True)


def crop_rows(ref, crops, n_rows):
    if len(crops) == 1:
        return ref[pl.ds(crops[0], 1), :]
    n = n_rows // 2
    return jnp.concatenate(
        [jnp.broadcast_to(ref[pl.ds(crop, 1), :], (n, ref.shape[1])) for crop in crops], axis=0
    )


def pool_kernel(sz, gain_row, shift_row, strided, z_ref, t0, t1, t2, t3, vt_ref, pool_ref, nrm_ref, ps):
    terms = norm_terms(
        gather_sum((t0, t1, t2, t3)),
        0,
        sz.amount,
        vt_ref[gain_row : gain_row + 1, :],
        vt_ref[shift_row : shift_row + 1, :],
    )
    nrm_ref[...] = jnp.zeros_like(nrm_ref)
    put_norm(nrm_ref, 0, terms)
    if strided:
        put_norm(
            nrm_ref,
            4,
            norm_terms(
                gather_sum((t0, t1, t2, t3)),
                2,
                sz.amount,
                vt_ref[G1S : G1S + 1, :],
                vt_ref[B1S : B1S + 1, :],
            ),
        )
    scale, shift = terms[2], terms[3]
    ps[...] = jnp.zeros_like(ps)

    def one(pieces, crops):
        acc = None
        for rows in pieces:
            c = silu(z_ref[rows, :] * scale + shift)
            acc = c if acc is None else acc + c
        add_pool(ps, crops, acc)

    each_crop(sz, one)
    pool_ref[...] = ps[...].astype(bf16)


def inverse_area(sz):
    crop = lax.broadcasted_iota(jnp.int32, (sz.crops, 1), 0)
    return jnp.where(crop < sz.ng, 1.0 / sz.area_g, 1.0 / sz.area_l).astype(f32)


def dot_high(a, b):
    return jnp.dot(a, b, precision=highest, preferred_element_type=f32)


def gather_short(refs):
    total = refs[0][...].astype(f32)
    for ref in refs[1:]:
        total = total + ref[...].astype(f32)
    return total


def gated_product_kernel(
    sz,
    bias_row,
    shift_row,
    z_in_ref,
    nrm_ref,
    p0,
    p1,
    p2,
    p3,
    d_ref,
    u_ref,
    w_ref,
    vt_ref,
    q_ref,
    z_ref,
    st_ref,
    gate_ref,
    pooled_ref,
    pre_ref,
):
    pooled = gather_short((p0, p1, p2, p3)) * inverse_area(sz)
    pooled_ref[...] = pooled
    pre = dot_high(pooled, d_ref[...].astype(f32)) + vt_ref[bias_row : bias_row + 1, 0:HID]
    pre_ref[...] = pre
    gate = dot_high(silu(pre), u_ref[...].astype(f32)) + vt_ref[shift_row : shift_row + 1, :]
    gate_ref[...] = sigmoid(gate)
    scale = nrm_ref[2:3, :]
    shift = nrm_ref[3:4, :]

    def one(pieces, crops):
        g = crop_rows(gate_ref, crops, 2 * sz.cl)
        for rows in pieces:
            c = silu(z_in_ref[rows, :] * scale + shift)
            q_ref[rows, :] = (c * g).astype(bf16)

    each_crop(sz, one)
    n_rows = sz.m // PARTS
    zero = jnp.zeros((8, C), f32)

    def step(i, carry):
        total, square = carry
        rows = rows_at(i * n_rows, n_rows)
        z = dot(q_ref[rows, :], w_ref[...])
        z_ref[rows, :] = z
        return total + fold(z), square + fold(z * z)

    put_rows(st_ref, lax.fori_loop(0, PARTS, step, (zero, zero)))


ROWS = 352
PARTS = 1


def put_edges(sz, src, top_ref, bottom_ref):
    for ref, g, l in (
        (top_ref, 0, sz.mg),
        (bottom_ref, sz.mg - sz.bg, sz.m - sz.bl),
    ):
        if ref is not None:
            ref[0 : sz.bg, :] = src[g : g + sz.bg, :]
            ref[sz.bg : sz.edge, :] = src[l : l + sz.bl, :]


def middle_kernel(
    sz,
    zc_ref,
    x_ref,
    s_ref,
    t0,
    t1,
    t2,
    t3,
    nrm_a_ref,
    vt_ref,
    pre_ref,
    mb_ref,
    nrm_ref,
    top_ref,
    bottom_ref,
    zs,
):
    strided_product(sz, x_ref, s_ref, zs)
    terms = norm_terms(
        gather_sum((t0, t1, t2, t3)),
        0,
        sz.amount,
        vt_ref[G1C : G1C + 1, :],
        vt_ref[B1C : B1C + 1, :],
    )
    nrm_ref[...] = jnp.zeros_like(nrm_ref)
    put_norm(nrm_ref, 0, terms)
    scale = terms[2]
    scale_s = nrm_a_ref[6:7, :]
    shift = terms[3] + nrm_a_ref[7:8, :]

    @pl.loop(0, sz.m // ROWS)
    def _(i):
        rows = rows_at(i * ROWS, ROWS)
        pre = zc_ref[rows, :] * scale + zs[rows, :] * scale_s + shift
        pre_ref[rows, :] = pre
        mb_ref[rows, :] = silu(pre).astype(bf16)

    put_edges(sz, mb_ref, top_ref, bottom_ref)


def product_kernel(sz, x_ref, w_ref, z_ref, st_ref):
    n_rows = sz.m // PARTS
    zero = jnp.zeros((8, C), f32)

    def step(i, carry):
        total, square = carry
        rows = rows_at(i * n_rows, n_rows)
        z = dot(x_ref[rows, :], w_ref[...])
        z_ref[rows, :] = z
        return total + fold(z), square + fold(z * z)

    put_rows(st_ref, lax.fori_loop(0, PARTS, step, (zero, zero)))


def put_variants(refs, rows, value, width):
    refs[0][rows, :] = shifted(value, -1, width).astype(bf16)
    refs[1][rows, :] = value.astype(bf16)
    refs[2][rows, :] = shifted(value, 1, width).astype(bf16)


def second_conv_kernel(
    sz,
    flag_ref,
    z_in_ref,
    top_ref,
    bottom_ref,
    w_ref,
    k_ref,
    t0,
    t1,
    t2,
    t3,
    vt_ref,
    z_ref,
    st_ref,
    nrm_ref,
    a1,
    a0,
    a2,
    bd_ref,
    zs,
    sums,
):
    block_diagonal(k_ref, bd_ref)
    terms = norm_terms(
        gather_sum((t0, t1, t2, t3)),
        0,
        sz.amount,
        vt_ref[G2A : G2A + 1, :],
        vt_ref[B2A : B2A + 1, :],
    )
    nrm_ref[...] = jnp.zeros_like(nrm_ref)
    put_norm(nrm_ref, 0, terms)
    scale, shift = terms[2], terms[3]
    g_rows, l_rows = segments(sz)
    refs = (a0, a1, a2)

    @pl.loop(0, sz.mg // g_rows)
    def _(i):
        a = silu(z_in_ref[rows_at(i * g_rows, g_rows), :] * scale + shift)
        put_variants(refs, rows_at(sz.bg + i * g_rows, g_rows), a, sz.cg)

    @pl.loop(0, sz.ml // l_rows)
    def _(i):
        a = silu(z_in_ref[rows_at(sz.mg + i * l_rows, l_rows), :] * scale + shift)
        put_variants(refs, rows_at(sz.two_l + sz.bl + i * l_rows, l_rows), a, sz.cl)

    for k, src in enumerate((top_ref, bottom_ref)):
        flag = (above, below)[k](flag_ref, sz.n_height)
        zs[...] = dot(src[...], w_ref[...])
        g_first = 0 if k == 0 else (sz.rg + 1) * sz.bg
        l_first = sz.two_l + (0 if k == 0 else (sz.rl + 1) * sz.bl)

        @pl.loop(0, sz.bg // g_rows)
        def _(i):
            a = silu(zs[rows_at(i * g_rows, g_rows), :] * scale + shift) * flag
            put_variants(refs, rows_at(g_first + i * g_rows, g_rows), a, sz.cg)

        @pl.loop(0, sz.bl // l_rows)
        def _(i):
            a = silu(zs[rows_at(sz.bg + i * l_rows, l_rows), :] * scale + shift) * flag
            put_variants(refs, rows_at(l_first + i * l_rows, l_rows), a, sz.cl)

    conv_forward(sz, lambda part: windows_two(sz, refs, part), bd_ref, z_ref, st_ref, sums)


def output_kernel(
    sz, pre_ref, z_ref, t0, t1, t2, t3, vt_ref, cg_ref, cl_ref, og_ref, ol_ref, dn_ref, st_ref, nrm_ref, sums
):
    terms = norm_terms(
        gather_sum((t0, t1, t2, t3)),
        0,
        sz.amount,
        vt_ref[G2C : G2C + 1, :],
        vt_ref[B2C : B2C + 1, :],
    )
    nrm_ref[...] = jnp.zeros_like(nrm_ref)
    put_norm(nrm_ref, 0, terms)
    mean, inverse, scale, shift = terms
    sums[...] = jnp.zeros_like(sums)

    def piece(rows, cot):
        z = z_ref[rows, :]
        pre = silu(pre_ref[rows, :]) + z * scale + shift
        s = sigmoid(pre)
        dn = cot * (s * (1.0 + pre * (1.0 - s)))
        dn_ref[rows, :] = dn
        return pre * s, fold(dn), fold(dn * z)

    @pl.loop(0, sz.ng, unroll=2)
    def _(n):
        one, two = 0.0, 0.0
        for i in range(sz.rg):
            rows = rows_at(i * sz.bg + n * sz.cg, sz.cg)
            value, add_one, add_two = piece(rows, cg_ref[n, i].astype(f32))
            og_ref[n, i] = value.astype(bf16)
            one, two = one + add_one, two + add_two
        sums[0:8, :] += one
        sums[8:16, :] += two

    @pl.loop(0, sz.nl // 2, unroll=3)
    def _(pair):
        one, two = 0.0, 0.0
        for i in range(sz.rl):
            rows = rows_at(sz.mg + i * sz.bl + pair * 2 * sz.cl, 2 * sz.cl)
            cot = jnp.concatenate(
                [cl_ref[2 * pair + k, i].astype(f32) for k in range(2)], axis=0
            )
            value, add_one, add_two = piece(rows, cot)
            for k in range(2):
                ol_ref[2 * pair + k, i] = value[k * sz.cl : (k + 1) * sz.cl].astype(bf16)
            one, two = one + add_one, two + add_two
        sums[0:8, :] += one
        sums[8:16, :] += two

    put_back_sums(st_ref, sums[0:8, :], sums[8:16, :], mean, inverse)


def back_terms(total, row_one, row_two, amount, nrm_ref, nrm_row):
    mean = nrm_ref[nrm_row : nrm_row + 1, :]
    inverse = nrm_ref[nrm_row + 1 : nrm_row + 2, :]
    scale = nrm_ref[nrm_row + 2 : nrm_row + 3, :]
    one = total[row_one : row_one + 1] / amount
    two = total[row_two : row_two + 1] / amount
    return scale, one, mean, inverse * two


def norm_back(dn, z, terms):
    scale, one, mean, slope = terms
    return scale * (dn - one - (z - mean) * slope)


def gate_grad_kernel(
    sz,
    strided,
    dn_ref,
    z_ref,
    t0,
    t1,
    t2,
    t3,
    nrm_ref,
    w_ref,
    z_in_ref,
    nrm_in_ref,
    *refs,
):
    if strided:
        x_ref, s_ref, nrm_a_ref, dz_ref, dzs_ref, dq_ref, dg_ref, ps, zs = refs
        strided_product(sz, x_ref, s_ref, zs)
    else:
        dz_ref, dq_ref, dg_ref, ps = refs
    total = gather_sum((t0, t1, t2, t3))
    terms = back_terms(total, 0, 1, sz.amount, nrm_ref, 0)

    @pl.loop(0, sz.m // ROWS)
    def _(i):
        rows = rows_at(i * ROWS, ROWS)
        dz_ref[rows, :] = norm_back(dn_ref[rows, :], z_ref[rows, :], terms).astype(bf16)

    if strided:
        terms_s = back_terms(total, 0, 2, sz.amount, nrm_a_ref, 4)

        @pl.loop(0, sz.m // ROWS)
        def _(i):
            rows = rows_at(i * ROWS, ROWS)
            dzs_ref[rows, :] = norm_back(dn_ref[rows, :], zs[rows, :], terms_s).astype(bf16)

    n_rows = sz.m // PARTS

    @pl.loop(0, PARTS)
    def _(i):
        rows = rows_at(i * n_rows, n_rows)
        dq_ref[rows, :] = dot_t(dz_ref[rows, :], w_ref[...])

    ps[...] = jnp.zeros_like(ps)
    scale = nrm_in_ref[2:3, :]
    shift = nrm_in_ref[3:4, :]

    def one(pieces, crops):
        acc = None
        for rows in pieces:
            term = dq_ref[rows, :] * silu(z_in_ref[rows, :] * scale + shift)
            acc = term if acc is None else acc + term
        add_pool(ps, crops, acc)

    each_crop(sz, one)
    dg_ref[...] = ps[...].astype(bf16)


def excite_back_kernel(
    sz,
    dq_ref,
    z_ref,
    nrm_ref,
    g0,
    g1,
    g2,
    g3,
    gate_ref,
    pre_ref,
    d_ref,
    u_ref,
    dn_ref,
    st_ref,
    dv_ref,
    du_ref,
    pool,
    sums,
):
    gate = gate_ref[...]
    dv = gather_short((g0, g1, g2, g3)) * gate * (1.0 - gate)
    dv_ref[...] = dv
    du = lax.dot_general(
        dv,
        u_ref[...].astype(f32),
        (((1,), (1,)), ((), ())),
        precision=highest,
        preferred_element_type=f32,
    ) * silu_slope(pre_ref[...])
    du_ref[...] = du
    pool[...] = (
        lax.dot_general(
            du,
            d_ref[...].astype(f32),
            (((1,), (1,)), ((), ())),
            precision=highest,
            preferred_element_type=f32,
        )
        * inverse_area(sz)
    )
    mean = nrm_ref[0:1, :]
    inverse = nrm_ref[1:2, :]
    scale = nrm_ref[2:3, :]
    shift = nrm_ref[3:4, :]
    sums[...] = jnp.zeros_like(sums)

    def one(pieces, crops):
        g = crop_rows(gate_ref, crops, 2 * sz.cl)
        p = crop_rows(pool, crops, 2 * sz.cl)
        total, with_z = 0.0, 0.0
        for rows in pieces:
            z = z_ref[rows, :]
            dn = (dq_ref[rows, :] * g + p) * silu_slope(z * scale + shift)
            dn_ref[rows, :] = dn
            total, with_z = total + fold(dn), with_z + fold(dn * z)
        sums[0:8, :] += total
        sums[8:16, :] += with_z

    each_crop(sz, one)
    put_back_sums(st_ref, sums[0:8, :], sums[8:16, :], mean, inverse)


def put_flat(value_ref, width, flat_ref, slots):
    if width == 128:
        for j in range(C // 128):
            flat_ref[:, j * 128 : (j + 1) * 128] = value_ref[pl.ds(j, width, stride=C // 128), :]
        return
    n_lines = width // int(np.gcd(C, width))
    n_groups = width // n_lines
    per = C // n_groups
    lane = lax.broadcasted_iota(jnp.int32, (n_groups, C), 1)
    lines = [jnp.zeros((n_groups, C), f32) for _ in range(n_lines)]
    for u in range(per):
        row = value_ref[pl.ds(u, n_groups, stride=per), :]
        row = jnp.concatenate([row] + [jnp.zeros_like(row)] * (C // 128 - 1), axis=1)
        line, at = divmod(u * width, C)
        moved = pltpu.roll(row, at, 1) if at else row
        lines[line] = jnp.where(lane >= at, lines[line] + moved, lines[line])
        if at + width > C:
            lines[line + 1] = jnp.where(
                lane < at + width - C, lines[line + 1] + moved, lines[line + 1]
            )
    for j in range(C // 128):
        for k, line in enumerate(lines):
            slots[pl.ds(k, n_groups, stride=n_lines), :] = line[:, j * 128 : (j + 1) * 128]
        flat_ref[:, j * 128 : (j + 1) * 128] = slots[0:width, :]


def excite_weights_kernel(
    width, flag_ref, dv_ref, du_ref, pooled_ref, pre_ref, dd_ref, de_ref, du_out, df_ref, wide, slots
):
    flag = first_of_height(flag_ref)
    dv = dv_ref[...] * flag
    du = du_ref[...] * flag

    def cross(a, b):
        return lax.dot_general(
            a, b, (((0,), (0,)), ((), ())), precision=highest, preferred_element_type=f32
        )

    wide[...] = cross(pooled_ref[...], du)
    put_flat(wide, width, dd_ref, slots)
    du_out[...] = cross(silu(pre_ref[...]), dv)
    de_ref[...] = jnp.broadcast_to(jnp.sum(du, axis=0, keepdims=True), de_ref.shape)
    df_ref[...] = jnp.broadcast_to(jnp.sum(dv, axis=0, keepdims=True), df_ref.shape)


def weight_kernel(x_ref, dz_ref, w_ref):
    n_rows = dz_ref.shape[0]
    n = 128 if x_ref.shape[1] % 128 == 0 else x_ref.shape[1]
    for k in range(x_ref.shape[1] // n):
        w_ref[k * n : (k + 1) * n, :] = t_dot(x_ref[0:n_rows, k * n : (k + 1) * n], dz_ref[...])


def norm_back_kernel(sz, dn_ref, z_ref, t0, t1, t2, t3, nrm_ref, dz_ref, top_ref, bottom_ref=None):
    terms = back_terms(gather_sum((t0, t1, t2, t3)), 0, 1, sz.amount, nrm_ref, 0)

    @pl.loop(0, sz.m // ROWS)
    def _(i):
        rows = rows_at(i * ROWS, ROWS)
        dz_ref[rows, :] = norm_back(dn_ref[rows, :], z_ref[rows, :], terms).astype(bf16)

    put_edges(sz, dz_ref, top_ref, bottom_ref)


def conv_weights(sz, windows_of, dz_ref, dk_ref):
    @pl.loop(0, 2)
    def _(half):
        cols = pl.ds(pl.multiple_of(half * HALF, HALF), HALF)
        win_g = windows_of("g")
        win_l = windows_of("l")
        for tap in range(9):
            _, ref_g, start_g = win_g[tap]
            _, ref_l, start_l = win_l[tap]
            acc = t_dot(ref_g[start_g : start_g + sz.mg, cols], dz_ref[0 : sz.mg, cols])
            acc = acc + t_dot(ref_l[start_l : start_l + sz.ml, cols], dz_ref[sz.mg : sz.m, cols])
            dk_ref[tap * GW : (tap + 1) * GW, cols] = block_dense(acc)


def shift_all(src, dst, by, spans):
    for first, n_all, n_rows, width in spans:

        @pl.loop(0, n_all // n_rows)
        def _(i):
            rows = rows_at(first + i * n_rows, n_rows)
            dst[rows, :] = shifted(src[rows, :].astype(f32), by, width).astype(bf16)


def second_conv_weights_kernel(sz, a1, dz_ref, dk_ref, a0, a2):
    g_rows, l_rows = segments(sz)
    spans = ((0, sz.two_l, g_rows, sz.cg), (sz.two_l, sz.two - sz.two_l, l_rows, sz.cl))
    shift_all(a1, a0, -1, spans)
    shift_all(a1, a2, 1, spans)
    conv_weights(sz, lambda part: windows_two(sz, (a0, a1, a2), part), dz_ref, dk_ref)


def first_conv_weights_kernel(sz, a00, a01, a10, a11, dz_ref, dk_ref, a01s, a11s):
    g_rows, l_rows = segments(sz)
    shift_all(a01, a01s, -1, ((0, sz.mg, g_rows, sz.cg), (sz.mg, sz.ml, l_rows, sz.cl)))
    shift_all(
        a11,
        a11s,
        -1,
        ((0, sz.one_l, g_rows, sz.cg), (sz.one_l, sz.one - sz.one_l, l_rows, sz.cl)),
    )
    refs = (a00, a01, a01s, a10, a11, a11s)
    conv_weights(sz, lambda part: windows_one(sz, refs, part), dz_ref, dk_ref)


def second_conv_back_kernel(
    sz, dz_ref, top_ref, bottom_ref, k_ref, z_ref, nrm_ref, dn_ref, st_ref, v0, v1, v2, bd_ref, sums
):
    block_diagonal(k_ref, bd_ref)
    refs = (v0, v1, v2)
    g_rows, l_rows = segments(sz)

    @pl.loop(0, sz.mg // g_rows)
    def _(i):
        v = dz_ref[rows_at(i * g_rows, g_rows), :].astype(f32)
        put_variants(refs, rows_at(sz.bg + i * g_rows, g_rows), v, sz.cg)

    @pl.loop(0, sz.ml // l_rows)
    def _(i):
        v = dz_ref[rows_at(sz.mg + i * l_rows, l_rows), :].astype(f32)
        put_variants(refs, rows_at(sz.two_l + sz.bl + i * l_rows, l_rows), v, sz.cl)

    for k, src in enumerate((top_ref, bottom_ref)):
        g_first = 0 if k == 0 else (sz.rg + 1) * sz.bg
        l_first = sz.two_l + (0 if k == 0 else (sz.rl + 1) * sz.bl)

        @pl.loop(0, sz.bg // g_rows)
        def _(i):
            v = src[rows_at(i * g_rows, g_rows), :].astype(f32)
            put_variants(refs, rows_at(g_first + i * g_rows, g_rows), v, sz.cg)

        @pl.loop(0, sz.bl // l_rows)
        def _(i):
            v = src[rows_at(sz.bg + i * l_rows, l_rows), :].astype(f32)
            put_variants(refs, rows_at(l_first + i * l_rows, l_rows), v, sz.cl)

    @pl.loop(0, 2)
    def _(half):
        cols = pl.ds(pl.multiple_of(half * HALF, HALF), HALF)
        for part, first, n_all, n_rows in (
            ("g", 0, sz.mg, sz.mg // 2),
            ("l", sz.mg, sz.ml, sz.ml),
        ):
            for k in range(n_all // n_rows):
                dn_ref[first + k * n_rows : first + (k + 1) * n_rows, cols] = conv_product(
                    shift_windows(windows_two(sz, refs, part, True), k * n_rows),
                    bd_ref,
                    half,
                    n_rows,
                    True,
                )

    slope_pass(sz.m, dn_ref, z_ref, nrm_ref, st_ref, sums)


def slope_pass(n_all, dn_ref, z_ref, nrm_ref, st_ref, sums):
    mean = nrm_ref[0:1, :]
    inverse = nrm_ref[1:2, :]
    scale = nrm_ref[2:3, :]
    shift = nrm_ref[3:4, :]
    sums[...] = jnp.zeros_like(sums)

    @pl.loop(0, n_all // ROWS)
    def _(i):
        rows = rows_at(i * ROWS, ROWS)
        z = z_ref[rows, :]
        dn = dn_ref[rows, :] * silu_slope(z * scale + shift)
        dn_ref[rows, :] = dn
        sums[0:8, :] += fold(dn)
        sums[8:16, :] += fold(dn * ((z - mean) * inverse))

    put_rows(st_ref, [sums[0:8, :], sums[8:16, :]])


def middle_back_kernel(
    sz,
    dn_d_ref,
    zd_ref,
    t0,
    t1,
    t2,
    t3,
    nrm_d_ref,
    w_ref,
    dpre_ref,
    pre_ref,
    zc_ref,
    x_ref,
    s_ref,
    nrm_c_ref,
    nrm_a_ref,
    dz_ref,
    dn_ref,
    st_ref,
    zs,
    sums,
):
    strided_product(sz, x_ref, s_ref, zs)
    terms = back_terms(gather_sum((t0, t1, t2, t3)), 0, 1, sz.amount, nrm_d_ref, 0)

    @pl.loop(0, sz.m // ROWS)
    def _(i):
        rows = rows_at(i * ROWS, ROWS)
        dz_ref[rows, :] = norm_back(dn_d_ref[rows, :], zd_ref[rows, :], terms).astype(bf16)

    n_rows = sz.m // PARTS

    @pl.loop(0, PARTS)
    def _(i):
        rows = rows_at(i * n_rows, n_rows)
        dn_ref[rows, :] = dot_t(dz_ref[rows, :], w_ref[...])

    mean_c = nrm_c_ref[0:1, :]
    inverse_c = nrm_c_ref[1:2, :]
    mean_s = nrm_a_ref[4:5, :]
    inverse_s = nrm_a_ref[5:6, :]
    sums[...] = jnp.zeros_like(sums)

    @pl.loop(0, sz.m // ROWS)
    def _(i):
        rows = rows_at(i * ROWS, ROWS)
        dn = (dn_ref[rows, :] + dpre_ref[rows, :]) * silu_slope(pre_ref[rows, :])
        dn_ref[rows, :] = dn
        sums[0:8, :] += fold(dn)
        sums[8:16, :] += fold(dn * ((zc_ref[rows, :] - mean_c) * inverse_c))
        sums[16:24, :] += fold(dn * ((zs[rows, :] - mean_s) * inverse_s))

    put_rows(st_ref, [sums[0:8, :], sums[8:16, :], sums[16:24, :]])


def first_conv_back_kernel(sz, dz_ref, below_ref, k_ref, v0, v1, bd_ref):
    block_diagonal(k_ref, bd_ref)
    g_rows, l_rows = segments(sz)

    def put(rows, v, width):
        v0[rows, :] = v.astype(bf16)
        v1[rows, :] = shifted(v, 1, width).astype(bf16)

    for src, g_src, l_src, g_dst, l_dst, g_all, l_all in (
        (dz_ref, 0, sz.mg, 0, sz.one_l, sz.mg, sz.ml),
        (below_ref, 0, sz.bg, sz.mg, sz.one_l + sz.ml, sz.bg, sz.bl),
    ):

        @pl.loop(0, g_all // g_rows)
        def _(i):
            v = src[rows_at(g_src + i * g_rows, g_rows), :].astype(f32)
            put(rows_at(g_dst + i * g_rows, g_rows), v, sz.cg)

        @pl.loop(0, l_all // l_rows)
        def _(i):
            v = src[rows_at(l_src + i * l_rows, l_rows), :].astype(f32)
            put(rows_at(l_dst + i * l_rows, l_rows), v, sz.cl)


def parity_back_kernel(sz, phase, v0, v1, bd_ref, x_ref, w_ref, nrm_ref, *refs):
    if phase:
        st_in, dn_ref, st_ref, zs, da, sums = refs
    else:
        dn_ref, st_ref, zs, da, sums = refs
    mean = nrm_ref[0:1, :]
    inverse = nrm_ref[1:2, :]
    scale = nrm_ref[2:3, :]
    shift = nrm_ref[3:4, :]
    sums[...] = jnp.zeros_like(sums)
    third = sz.m // PARTS
    pr, pc = phase // 2, phase % 2
    taps = []
    for a, down in (((1, 0),), ((2, 0), (0, 1)))[pr]:
        for b, right in (((1, 0),), ((2, 0), (0, 1)))[pc]:
            taps.append((3 * a + b, down, right))

    @pl.loop(0, 2)
    def _(half):
        cols = pl.ds(pl.multiple_of(half * HALF, HALF), HALF)
        for first, base, block, n_all, n_rows in (
            (0, 0, sz.bg, sz.mg, sz.mg // 2),
            (sz.mg, sz.one_l, sz.bl, sz.ml, sz.ml),
        ):
            for k in range(n_all // n_rows):
                windows = [
                    (tap, (v0, v1)[right], base + down * block + k * n_rows)
                    for tap, down, right in taps
                ]
                da[first + k * n_rows : first + (k + 1) * n_rows, cols] = conv_product(
                    windows, bd_ref, half, n_rows, True
                )

    @pl.loop(0, PARTS)
    def _(i):
        zs[rows_at(i * third, third), :] = dot(
            x_ref[rows_at(phase * sz.m + i * third, third), :], w_ref[...]
        )

    @pl.loop(0, sz.m // ROWS)
    def _(i):
        rows = rows_at(i * ROWS, ROWS)
        z = zs[rows, :]
        dn = da[rows, :] * silu_slope(z * scale + shift)
        dn_ref[rows, :] = dn.astype(bf16)
        sums[0:8, :] += fold(dn)
        sums[8:16, :] += fold(dn * ((z - mean) * inverse))

    put_rows(st_ref, [sums[0:8, :], sums[8:16, :]])
    if phase:
        st_ref[...] += st_in[...]


def image_norm_back_kernel(sz, dn0, dn1, dn2, dn3, x_ref, w_ref, t0, t1, t2, t3, nrm_ref, dz_ref, zs):
    terms = back_terms(gather_sum((t0, t1, t2, t3)), 0, 1, 4 * sz.amount, nrm_ref, 0)
    zs[...] = dot(x_ref[...], w_ref[...])
    for phase in range(4):

        @pl.loop(0, sz.m // ROWS)
        def _(i):
            rows = rows_at(i * ROWS, ROWS)
            rows_all = rows_at(phase * sz.m + i * ROWS, ROWS)
            dz_ref[rows_all, :] = norm_back(
                (dn0, dn1, dn2, dn3)[phase][rows, :].astype(f32), zs[rows_all, :], terms
            ).astype(bf16)


def image_product_kernel(sz, dz_ref, w_ref, dzs_ref, ws_ref, dx_ref):
    dx_ref[...] = dot_t(dz_ref[...], w_ref[...])
    dx_ref[0 : sz.m, :] += dot_t(dzs_ref[...], ws_ref[...])


def place_kernel(n_crops, height, width, first_row, block, m, dx_ref, o_ref, mark_ref, s_ref, t_ref):
    half = width // 2
    mark_ref[...] = jnp.zeros_like(mark_ref)
    count = s_ref.shape[0]

    @pl.loop(0, n_crops // count)
    def _(step):
        for c in range(count):
            n = step * count + c
            for r in range(height):
                for pc in range(2):
                    at = (2 * (r % 2) + pc) * m + first_row + (r // 2) * block + n * half
                    v = dx_ref[rows_at(at, half, 8), :]
                    rows = pl.ds(r * width + pc, half, stride=2)
                    s_ref[c, rows, :] = v[:, :128]
                    t_ref[c, rows, :] = jnp.concatenate([v[:, 128:], v[:, 128:]], axis=1)
        for c in range(count):
            n = step * count + c
            o_ref[n, :, :, 0:128] = s_ref[c].reshape(height, width, 128)
            o_ref[n, :, :, 128:CIN] = t_ref[c][:, :64].reshape(height, width, 64)


def over_height(x):
    n = lax.axis_size("height")
    return [x] + [lax.ppermute(x, "height", [(i, i ^ k) for i in range(n)]) for k in range(1, n)]


def step_down(x):
    n = lax.axis_size("height")
    return lax.ppermute(x, "height", [(i, i + 1) for i in range(n - 1)])


def step_up(x):
    n = lax.axis_size("height")
    return lax.ppermute(x, "height", [(i + 1, i) for i in range(n - 1)])


MATRIX_ROWS = [a * b // C for a, b in matrix_shapes()]
ROW_BOUNDS = [int(v) for v in np.cumsum([0] + MATRIX_ROWS)]
UNIT = 112


def across(x, mask, senders=None):
    n = lax.axis_size("batch")
    return lax.ppermute(
        x, "batch", [(i, i ^ mask) for i in range(n) if senders is None or i in senders]
    )


def take_flat(whole, start, width, low_ref, value, slots):
    if width == 128:
        for j in range(C // 128):
            value[pl.ds(j, width, stride=C // 128), :] = whole[
                start : start + width, j * 128 : (j + 1) * 128
            ]
    else:
        n_lines = width // int(np.gcd(C, width))
        n_groups = width // n_lines
        per = C // n_groups
        lane = lax.broadcasted_iota(jnp.int32, (n_groups, C), 1)
        blocks = [[] for _ in range(n_lines)]
        for j in range(C // 128):
            slots[0:width, :] = whole[start : start + width, j * 128 : (j + 1) * 128]
            for k in range(n_lines):
                blocks[k].append(slots[pl.ds(k, n_groups, stride=n_lines), :])
        lines = [jnp.concatenate(block, axis=1) for block in blocks]
        for u in range(per):
            line, at = divmod(u * width, C)
            row = pltpu.roll(lines[line], C - at, 1) if at else lines[line]
            if at + width > C:
                row = jnp.where(lane < C - at, row, pltpu.roll(lines[line + 1], C - at, 1))
            value[pl.ds(u, n_groups, stride=per), :] = jnp.where(lane < width, row, 0.0)[:, 0:128]
    low_ref[...] = value[...].astype(bf16)


def assemble_kernel(n_rows, idx_ref, *refs):
    ins, outs = refs[:2], refs[2:-4]
    shards, whole, value, slots = refs[-4:]
    for core, ref in enumerate(ins):
        for q in range(4):
            for k in range(4):
                at = (idx_ref[0] ^ (2 * q + core)) * 4 + (idx_ref[1] ^ k)
                shards[at] = ref[4 * q + k].astype(f32)
    for s in range(32):
        whole[s * n_rows : (s + 1) * n_rows, :] = shards[s, 0:n_rows, :]
    for k, (ref, start) in enumerate(zip(outs, ROW_BOUNDS)):
        if k in (2, 8):
            take_flat(whole, start, MATRIX_ROWS[k], ref, value, slots)
        elif k in (3, 9):
            n = MATRIX_ROWS[k]
            value[0:HID, :] = jnp.zeros((HID, 128), f32)
            for j in range(C // 128):
                value[0:n, :] = whole[start : start + n, j * 128 : (j + 1) * 128]
                ref[:, j * 128 : (j + 1) * 128] = value[0:HID, :].astype(bf16)
        else:
            ref[...] = whole[start : start + ref.shape[0], :].astype(bf16)


def merge_kernel(*refs):
    *ins, merged = refs
    n = ins[0].shape[0]
    for q, ref in enumerate(ins):
        merged[q * n : (q + 1) * n] = ref[...]


def gather_weights(lines, n_rows, place_ids, beside):
    (mine,) = call(
        functools.partial(round_rows_kernel, n_rows),
        [out((UNIT, C), bf16)],
        [],
        lines,
        name="round_weights",
        after=[place_ids],
    )
    quarter = jnp.stack(over_height(mine))
    after, extra = beside(quarter)
    planes = [quarter] + [across(quarter, mask) for mask in (2, 4, 6)]
    (merged,) = call(
        merge_kernel, [out((16, UNIT, C), bf16)], [], *planes, name="merge_planes", after=after
    )
    planes = [merged, across(merged, 1)]
    matrices = call(
        functools.partial(assemble_kernel, n_rows),
        [
            out((C, HID) if k in (2, 8) else (HID if k in (3, 9) else rows, C), bf16)
            for k, rows in enumerate(MATRIX_ROWS)
        ],
        [
            pltpu.VMEM((32, UNIT, C), f32),
            pltpu.VMEM((32 * n_rows, C), f32),
            pltpu.VMEM((C, 128), f32),
            pltpu.VMEM((HID, 128), f32),
        ],
        place_ids,
        *planes,
        smem=1,
        name="assemble",
        room=6 * 2**20,
    )
    return matrices, extra


def pack_kernel(n_rows, first_shard, sources, core_ref, *refs):
    n_src = len(sources)
    ins, (mine_ref, other_ref, buf) = refs[:n_src], refs[n_src:]
    for shard in range(buf.shape[0]):
        low = (first_shard + shard) * n_rows
        for (start, stop), ref in zip(sources, ins):
            a, b = max(low, start), min(low + n_rows, stop)
            if a < b:
                buf[shard, a - low : b - low, :] = ref[a - start : b - start, :]
        buf[shard, n_rows:, :] = jnp.zeros((UNIT - n_rows, C), f32)
    core = core_of(core_ref)
    for unit in range(buf.shape[0] // 8):
        for h in range(4):
            mine_ref[unit * 4 + h] = buf[(unit * 2 + core) * 4 + h]
            other_ref[unit * 4 + h] = buf[(unit * 2 + 1 - core) * 4 + h].astype(bf16)


def pack(n_rows, first_unit, n_units, sources, arrays, place_ids, name, after=()):
    shape = (4 * n_units, UNIT, C)
    mine, other = call(
        functools.partial(pack_kernel, n_rows, 8 * first_unit, sources),
        [out(shape), out(shape, bf16)],
        [pltpu.VMEM((8 * n_units, UNIT, C), f32)],
        place_ids,
        *arrays,
        smem=1,
        name=name,
        after=after,
    )
    return mine, across(other, 1)


def sum_core_kernel(place_ref, a0_ref, b0_ref, a_ref, b_ref, sum_ref, y_ref, x_ref):
    n = a0_ref.shape[0]
    sum_ref[0:n] = a0_ref[...] + b0_ref[...].astype(f32)
    sum_ref[n:] = a_ref[...] + b_ref[...].astype(f32)
    y, x = y_of(place_ref), x_of(place_ref)
    for h in range(4):
        y_ref[h] = sum_ref[8 - 4 * y + h].astype(bf16)
        x_ref[h] = sum_ref[12 - 12 * x + h].astype(bf16)


def second_parts_kernel(place_ref, sum_ref, gy_ref, gx_ref, keep_ref, y_ref, x_ref):
    y, x = y_of(place_ref), x_of(place_ref)
    for h in range(4):
        by_y = sum_ref[4 + 4 * y + h] + gy_ref[h].astype(f32)
        by_x = sum_ref[12 * x + h] + gx_ref[h].astype(f32)
        keep_ref[h] = jnp.where(x == y, by_x, by_y)
        y_ref[h] = by_x.astype(bf16)
        x_ref[h] = by_y.astype(bf16)


def early_parts_kernel(place_ref, sum_ref, gy_ref, gx_ref, keep_ref, s1, s2, s3):
    same = y_of(place_ref) == x_of(place_ref)
    for k, ref in enumerate((keep_ref, s1, s2, s3)):
        at = place_ref[1] ^ k
        got = jnp.where(same, gy_ref[at].astype(f32), gx_ref[at].astype(f32))
        ref[...] = (sum_ref[at] + got).astype(ref.dtype)


class EarlySum:
    def __init__(self, n_rows, place_ids):
        self.n_rows, self.ids = n_rows, place_ids

    def pack(self, sources, arrays):
        self.mine, self.got = pack(
            self.n_rows, 1, 3, sources, arrays, self.ids, "pack_early"
        )
        return [self.mine]

    def pack_first_unit(self, sources, arrays, after):
        self.mine_first, self.got_first = pack(
            self.n_rows, 0, 1, sources, arrays, self.ids, "pack_unit_0", after
        )
        return [self.mine_first]

    def first(self, after):
        four = out((4, UNIT, C), bf16)
        self.total, y_low, x_low = call(
            sum_core_kernel,
            [out((16, UNIT, C)), four, four],
            [],
            self.ids,
            self.mine_first,
            self.got_first,
            self.mine,
            self.got,
            smem=1,
            name="sum_core",
            after=after,
        )
        self.got = [across(y_low, 4), across(x_low, 2)]
        return [self.total]

    def second(self, after):
        four = out((4, UNIT, C), bf16)
        self.keep, y_low, x_low = call(
            second_parts_kernel,
            [out((4, UNIT, C)), four, four],
            [],
            self.ids,
            self.total,
            *self.got,
            smem=1,
            name="second_parts",
            after=after,
        )
        self.got = [across(y_low, 4, [2, 3, 4, 5]), across(x_low, 2, [0, 1, 6, 7])]
        return [self.keep]

    def height(self, after):
        low = out((UNIT, C), bf16)
        mine, *sends = call(
            early_parts_kernel,
            [out((UNIT, C)), low, low, low],
            [],
            self.ids,
            self.keep,
            *self.got,
            smem=1,
            name="early_parts",
            after=after,
        )
        self.result = [mine] + [
            lax.ppermute(send, "height", [(i, i ^ k) for i in range(4)])
            for k, send in zip((1, 2, 3), sends)
        ]
        return [self.result[0]]


HALF_UNIT = 64


def first_halves_kernel(n_rows, place_ref, g_ref, mine_ref, other_ref, buf):
    n_first = g_ref.shape[0]
    buf[...] = jnp.zeros_like(buf)
    buf[0, 0:n_rows, :] = g_ref[0:n_rows, :]
    buf[1, 0 : n_first - n_rows, :] = g_ref[n_rows:n_first, :]
    core = core_of(place_ref)
    for shard in range(2):
        mine_ref[shard] = buf[shard, rows_at(core * HALF_UNIT, HALF_UNIT), :]
        other_ref[shard] = buf[shard, rows_at((1 - core) * HALF_UNIT, HALF_UNIT), :].astype(bf16)


def first_parts_kernel(place_ref, mine_ref, got_ref, keep_ref, s1, s2, s3):
    for k, ref in enumerate((keep_ref, s1, s2, s3)):
        at = lax.rem(place_ref[1] ^ k, 2)
        ref[...] = (mine_ref[at] + got_ref[at].astype(f32)).astype(ref.dtype)


def sum_low_kernel(*refs):
    *ins, sum_ref, low_ref = refs
    total = ins[0][...]
    for ref in ins[1:]:
        total = total + ref[...].astype(f32)
    sum_ref[...] = total
    low_ref[...] = total.astype(bf16)


def sum_first_matrix(n_rows, grad, place_ids, work):
    pair = (2, HALF_UNIT, C)
    mine, other = call(
        functools.partial(first_halves_kernel, n_rows),
        [out(pair), out(pair, bf16)],
        [pltpu.VMEM((2, 2 * HALF_UNIT, C), f32)],
        place_ids,
        grad,
        smem=1,
        name="first_halves",
    )
    got = across(other, 1)
    beside = work.pop(0)([mine])
    one, low = out((HALF_UNIT, C)), out((HALF_UNIT, C), bf16)
    mine, *sends = call(
        first_parts_kernel,
        [one, low, low, low],
        [],
        place_ids,
        mine,
        got,
        smem=1,
        name="first_parts",
        after=beside,
    )
    got = [
        lax.ppermute(send, "height", [(h, h ^ k) for h in range(4)])
        for k, send in zip((1, 2, 3), sends)
    ]
    beside = []
    while work:
        beside = beside + work.pop(0)([mine])
    total, low_total = call(
        sum_low_kernel, [one, low], [], mine, *got, name="first_height", after=beside
    )
    got = [across(low_total, mask, [mask, mask + 1]) for mask in (2, 4, 6)]
    total, low_total = call(sum_low_kernel, [one, low], [], total, *got, name="first_plane")
    return [total, across(low_total, 1, [1])]


def lamb_kernel(
    n_rows,
    place_ref,
    a0,
    a1,
    a2,
    a3,
    first_half_ref,
    second_half_ref,
    w_ref,
    m_ref,
    v_ref,
    first_ref,
    second_ref,
    update_ref,
    sums_ref,
    g_ref,
):
    shard = place_ref[0] * 4 + place_ref[1]
    early = a0[...] + a1[...].astype(f32) + a2[...].astype(f32) + a3[...].astype(f32)
    g_ref[...] = early
    n_first = MATRIX_ROWS[0]

    @pl.when(shard == 0)
    def _():
        g_ref[0:HALF_UNIT, :] = first_half_ref[...]
        g_ref[HALF_UNIT:n_rows, :] = second_half_ref[0 : n_rows - HALF_UNIT, :].astype(f32)

    @pl.when(shard == 1)
    def _():
        rest = n_first - n_rows
        g_ref[0:HALF_UNIT, :] = first_half_ref[...]
        g_ref[HALF_UNIT:rest, :] = second_half_ref[0 : rest - HALF_UNIT, :].astype(f32)

    w, m, v = (as_rows(ref, n_rows) for ref in (w_ref, m_ref, v_ref))
    first, second, update = lamb_terms(w, g_ref[0:n_rows, :], m, v, weight_decay)
    put_as_lines(first_ref, first)
    put_as_lines(second_ref, second)
    update_ref[...] = update
    member = membership(n_rows, shard)
    sums_ref[...] = jnp.zeros_like(sums_ref)
    for k, value in enumerate((w, update)):
        by_row = jnp.sum(value * value, axis=1, keepdims=True)
        sums_ref[k : k + 1, 0:128] = jnp.sum(member * by_row, axis=0, keepdims=True)


def membership(n_rows, shard):
    row = lax.broadcasted_iota(jnp.int32, (n_rows, 128), 0) + shard * n_rows
    lane = lax.broadcasted_iota(jnp.int32, (n_rows, 128), 1)
    result = jnp.zeros((n_rows, 128), f32)
    for k in range(len(MATRIX_ROWS)):
        inside = (row >= ROW_BOUNDS[k]) & (row < ROW_BOUNDS[k + 1]) & (lane == k)
        result = jnp.where(inside, 1.0, result)
    return result


VEC_ROWS = 24


LINES = 72
LINE_F1 = 4 * C // 128
LINE_E2 = LINE_F1 + (E2 - F1) * C // 128
LINE_F2 = LINE_E2 + SE_B // 128


def as_lines(flat):
    return jnp.pad(flat, (0, LINES * 128 - flat.shape[0])).reshape(LINES, 128)


def from_lines(lines):
    return lines.reshape(-1)[: sum(vector_sizes())]


def line_pieces():
    return ((LINE_F1, F1, E2 - F1), (LINE_F2, F2, 18 - F2))


def tables_kernel(*refs):
    lines = refs[-1]
    n = len(refs) // 2
    lane = lax.broadcasted_iota(jnp.int32, (LINES, 128), 1)
    for src, dst in zip(refs[:n], refs[n : 2 * n]):
        dst[...] = jnp.zeros_like(dst)
        for j in range(C // 128):
            dst[0:4, j * 128 : (j + 1) * 128] = src[pl.ds(j, 4, stride=C // 128), :]
        head = src[LINE_F1 : LINE_F1 + 1, :]
        dst[E1 : E1 + 1, 0:128] = jnp.where(lane[0:1] < SE_A, head, 0.0)
        here = pltpu.roll(src[...], 128 - SE_A, 1)
        below = pltpu.roll(here, LINES - 1, 0)
        lines[...] = jnp.where(lane < 128 - SE_A, here, below)
        dst[E2 : E2 + 1, 0:128] = lines[LINE_E2 : LINE_E2 + 1, :]
        for line, row, count in line_pieces():
            for j in range(C // 128):
                dst[row : row + count, j * 128 : (j + 1) * 128] = lines[
                    pl.ds(line + j, count, stride=C // 128), :
                ]


def put_lines(table, dst, lines):
    lane = lax.broadcasted_iota(jnp.int32, (LINES, 128), 1)
    line_at = lax.broadcasted_iota(jnp.int32, (LINES, 128), 0)
    lines[...] = jnp.zeros_like(lines)
    lines[LINE_F1 : LINE_F1 + 1, :] = pltpu.roll(table[E1 : E1 + 1, 0:128], 128 - SE_A, 1)
    lines[LINE_E2 + 1 : LINE_E2 + 2, :] = table[E2 : E2 + 1, 0:128]
    for line, row, count in line_pieces():
        for j in range(C // 128):
            lines[pl.ds(line + 1 + j, count, stride=C // 128), :] = table[
                row : row + count, j * 128 : (j + 1) * 128
            ]
    before = pltpu.roll(lines[...], SE_A, 1)
    here = pltpu.roll(before, LINES - 1, 0)
    dst[...] = jnp.where(lane < SE_A, before, here)
    for j in range(C // 128):
        dst[pl.ds(j, 4, stride=C // 128), :] = table[0:4, j * 128 : (j + 1) * 128]


def as_rows(ref, n_rows):
    return jnp.concatenate(
        [ref[pl.ds(j, n_rows, stride=C // 128), :] for j in range(C // 128)], axis=1
    )


def put_as_lines(ref, value):
    for j in range(C // 128):
        ref[pl.ds(j, value.shape[0], stride=C // 128), :] = value[:, j * 128 : (j + 1) * 128]


def round_rows_kernel(n_rows, *refs):
    n = len(refs) // 2
    for src, dst in zip(refs[:n], refs[n:]):
        rows = as_rows(src, n_rows)
        fill = jnp.zeros((dst.shape[0] - n_rows, C), f32)
        dst[...] = jnp.concatenate([rows, fill], axis=0).astype(bf16)


def vector_grads_kernel(a, b, cs, d, e, f, de1, df1, de2, df2, sums_ref, o_ref):
    o_ref[...] = jnp.zeros_like(o_ref)
    plan = [
        (G1A, a, 1),
        (B1A, a, 0),
        (G1B, b, 1),
        (B1B, b, 0),
        (F1, df1, 0),
        (G1C, cs, 1),
        (B1C, cs, 0),
        (G1S, cs, 2),
        (B1S, cs, 0),
        (G2A, d, 1),
        (B2A, d, 0),
        (G2B, e, 1),
        (B2B, e, 0),
        (F2, df2, 0),
        (G2C, f, 1),
        (B2C, f, 0),
    ]
    for row, ref, k in plan:
        o_ref[row : row + 1, :] = ref[k : k + 1, :]
    o_ref[E1 : E1 + 1, 0:HID] = de1[0:1, :]
    o_ref[E2 : E2 + 1, 0:HID] = de2[0:1, :]
    o_ref[VEC_ROWS : VEC_ROWS + 8, :] = sums_ref[...]


def finish_kernel(
    n_rows,
    place_ref,
    r0,
    r1,
    r2,
    r3,
    w_ref,
    update_ref,
    vec_ref,
    vf_ref,
    vs_ref,
    new_w_ref,
    new_v_ref,
    new_vf_ref,
    new_vs_ref,
    norm_ref,
    slots,
    lines,
):
    place = place_ref[1]
    shard = place_ref[0] * 4 + place
    for k, ref in enumerate((r0, r1, r2, r3)):
        slots[place ^ k] = ref[...]
    total = slots[0] + slots[1] + slots[2] + slots[3]
    norms = jnp.sqrt(total[VEC_ROWS : VEC_ROWS + 8, 0:128])
    norm_ref[...] = norms
    lane = lax.broadcasted_iota(jnp.int32, (1, 128), 1)
    ratio = jnp.where(
        lane < len(MATRIX_ROWS), learn_rate * (norms[0:1] / norms[1:2]), 0.0
    )
    by_row = jnp.sum(membership(n_rows, shard) * ratio, axis=1, keepdims=True)
    put_as_lines(new_w_ref, as_rows(w_ref, n_rows) - by_row * update_ref[...])
    vec = vec_ref[...]
    first, second, update = lamb_terms(vec, total[0:VEC_ROWS], vf_ref[...], vs_ref[...], 0.0)
    put_lines(first, new_vf_ref, lines)
    put_lines(second, new_vs_ref, lines)
    size = jnp.sqrt(jnp.sum(vec * vec, axis=1, keepdims=True))
    change = jnp.sqrt(jnp.sum(update * update, axis=1, keepdims=True))
    put_lines(vec - learn_rate * (size / change) * update, new_v_ref, lines)


def lamb_terms(param, grad_val, first_old, second_old, decay):
    first_new = beta_one * first_old + (1.0 - beta_one) * grad_val
    second_new = beta_two * second_old + (1.0 - beta_two) * grad_val * grad_val
    update = (
        first_new
        / (1.0 - beta_one**STEP)
        / (jnp.sqrt(second_new / (1.0 - beta_two**STEP)) + adam_eps)
        + decay * param
    )
    return (first_new, second_new, update)


def body(
    image_glob,
    image_loc,
    cot_glob,
    cot_loc,
    weights,
    first_moment,
    second_moment,
    vectors,
    vec_first,
    vec_second,
):
    n_height = lax.axis_size("height")
    place = lax.axis_index("height")
    sz = Sizes(image_glob, image_loc, n_height)
    m = sz.m
    part = functools.partial
    place_ids = jnp.stack([lax.axis_index("batch"), place]).astype(jnp.int32)
    shapes = matrix_shapes()
    mat_lengths = [dims_pair[0] * dims_pair[1] for dims_pair in shapes]
    def prepare(before):
        x, x_edge = call(
            part(prepare_kernel, sz),
            [out((4 * m, CIN), bf16), out((2 * sz.edge, CIN), bf16)],
            [pltpu.VMEM((sz.hg * sz.wg, 128), f32)] * 2,
            image_glob,
            image_loc,
            name="prepare",
            after=before,
            room=6 * 2**20,
        )
        x_above = step_down(x_edge)
        gram_scr = pltpu.VMEM((CIN + 8, CIN), f32)
        (gram,) = call(part(gram_kernel, sz), [out(PACKED)], [gram_scr], x, name="gram")
        gram = over_height(gram)
        return x, x_above, gram, gram_scr

    by_rows = (
        weights.shape[0] % C == 0
        and weights.shape[0] // C <= UNIT
        and lax.axis_size("batch") == 8
        and n_height == 4
    )
    shard_rows = weights.shape[0] // C
    table = out((VEC_ROWS, C))
    tables = call(
        tables_kernel,
        [table] * 3,
        [pltpu.VMEM((LINES, 128), f32)],
        *(as_lines(v) for v in (vectors, vec_first, vec_second)),
        name="tables",
    )
    vt = tables[0]
    early = list(tables)
    if by_rows:
        w_lines, m_lines, v_lines = (
            v.reshape(-1, 128) for v in (weights, first_moment, second_moment)
        )

    if by_rows:

        def beside(quarter):
            prepared = prepare([quarter])
            return early + [prepared[1]] + prepared[2][1:], prepared

        matrices, prepared = gather_weights(w_lines, shard_rows, place_ids, beside)
    else:
        prepared = prepare([])
        gathered = lax.all_gather(weights.astype(bf16), both_axes, axis=0, tiled=True)
        matrices = [
            flat_piece.reshape(dims_pair)
            for flat_piece, dims_pair in zip(cut_pieces(gathered, mat_lengths), shapes)
        ]
    w1, k1, d1, u1, p1, s1, w2, k2, d2, u2, p2 = matrices
    x, x_above, gram, gram_scr = prepared
    if not by_rows:
        d1 = jnp.pad(d1, ((0, 0), (0, HID - SE_A)))
        u1 = jnp.pad(u1, ((0, HID - SE_A), (0, 0)))
    st8 = out((8, C))
    mat = out((m, C))
    mat_low = out((m, C), bf16)
    pool_low = out((sz.crops, C), bf16)
    pool_scr = pltpu.VMEM((sz.crops, C), f32)
    sum_scr = pltpu.VMEM((24, C), f32)

    bd_scr = pltpu.VMEM((18, HALF, HALF), bf16)
    low_scr = pltpu.VMEM((m, C), bf16)
    mat_scr = pltpu.VMEM((m, C), f32)
    one_scr = pltpu.VMEM((sz.one, C), bf16)
    two_scr = pltpu.VMEM((sz.two, C), bf16)
    edge_scr = pltpu.VMEM((sz.edge, C), f32)
    edge = out((sz.edge, C), bf16)
    one_shape = out((sz.one, C), bf16)
    nrm_a, *act_a = call(
        part(first_act_kernel, sz),
        [st8, mat_low, mat_low, one_shape, one_shape, mat_low, one_shape],
        [mat_scr, gram_scr],
        place_ids,
        x,
        x_above,
        w1,
        *gram,
        vt,
        smem=1,
        name="first_act",
    )
    zb, st_b = call(
        part(first_conv_kernel, sz),
        [mat, st8],
        [bd_scr, sum_scr],
        x,
        s1,
        k1,
        *act_a,
        name="first_conv",
    )
    act_a = act_a[:4]
    st_b = over_height(st_b)
    pool_b, nrm_b = call(
        part(pool_kernel, sz, G1B, B1B, True), [pool_low, st8], [pool_scr], zb, *st_b, vt, name="pool_b",
    )
    pool_b = over_height(pool_b)
    hid = out((sz.crops, HID))
    crop_mat = out((sz.crops, C))
    qb, zc, st_c, gate_b, pooled_b, hidden_b = call(
        part(gated_product_kernel, sz, E1, F1),
        [mat_low, mat, st8, crop_mat, crop_mat, hid],
        [],
        zb,
        nrm_b,
        *pool_b,
        d1,
        u1,
        p1,
        vt,
        name="gated_b",
    )
    st_c = over_height(st_c)
    pre_mid, mid_low, nrm_c, mid_top, mid_bottom = call(
        part(middle_kernel, sz),
        [mat, mat_low, st8, edge, edge],
        [mat_scr],
        zc,
        x,
        s1,
        *st_c,
        nrm_b,
        vt,
        name="middle",
    )
    mid_above = step_down(mid_bottom)
    mid_below = step_up(mid_top)
    zd, st_d = call(
        part(product_kernel, sz), [mat, st8], [], mid_low, w2, name="product_d"
    )
    st_d = over_height(st_d)
    two_shape = out((sz.two, C), bf16)
    ze, st_e, nrm_d, act_d = call(
        part(second_conv_kernel, sz),
        [mat, st8, st8, two_shape],
        [two_scr, two_scr, bd_scr, edge_scr, sum_scr],
        place_ids,
        zd,
        mid_above,
        mid_below,
        w2,
        k2,
        *st_d,
        vt,
        smem=1,
        name="second_conv",
    )
    st_e = over_height(st_e)
    pool_e, nrm_e = call(
        part(pool_kernel, sz, G2B, B2B, False), [pool_low, st8], [pool_scr], ze, *st_e, vt, name="pool_e",
    )
    pool_e = over_height(pool_e)
    qe, zf, st_f, gate_e, pooled_e, hidden_e = call(
        part(gated_product_kernel, sz, E2, F2),
        [mat_low, mat, st8, crop_mat, crop_mat, hid],
        [],
        ze,
        nrm_e,
        *pool_e,
        d2,
        u2,
        p2,
        vt,
        name="gated_e",
    )
    st_f = over_height(st_f)
    out_glob, out_loc, dpre, bst_f, nrm_f = call(
        part(output_kernel, sz),
        [out(cot_glob.shape, bf16), out(cot_loc.shape, bf16), mat, st8, st8],
        [sum_scr],
        pre_mid,
        zf,
        *st_f,
        vt,
        cot_glob,
        cot_loc,
        name="output",
        room=6 * 2**20,
    )
    bst_f_all = over_height(bst_f)

    dzf, dqe, dg_e = call(
        part(gate_grad_kernel, sz, False),
        [mat_low, mat, pool_low],
        [pool_scr],
        dpre,
        zf,
        *bst_f_all,
        nrm_f,
        p2,
        ze,
        nrm_e,
        name="gate_grad_e",
    )
    dg_e = over_height(dg_e)
    (mat_f,) = call(
        weight_kernel, [out((C, C))], [], qe, dzf, name="weight_f"
    )
    dn_e, bst_e, dv_e, du_e = call(
        part(excite_back_kernel, sz),
        [mat, st8, crop_mat, hid],
        [pool_scr, sum_scr],
        dqe,
        ze,
        nrm_e,
        *dg_e,
        gate_e,
        hidden_e,
        d2,
        u2,
        name="excite_back_e",
        after=[mat_f],
    )
    bst_e_all = over_height(bst_e)
    se_outs = lambda width: [out((width, C)), out((8, HID)), out((HID, C)), st8]
    se_scr = [pltpu.VMEM((C, HID), f32), pltpu.VMEM((HID, 128), f32)]
    dd2, de2, du2, df2 = call(
        part(excite_weights_kernel, SE_B),
        se_outs(SE_B),
        se_scr,
        place_ids,
        dv_e,
        du_e,
        pooled_e,
        hidden_e,
        smem=1,
        name="excite_weights_e",
    )
    dze, dze_top, dze_bottom = call(
        part(norm_back_kernel, sz),
        [mat_low, edge, edge],
        [],
        dn_e,
        ze,
        *bst_e_all,
        nrm_e,
        name="norm_back_e",
        after=[dd2],
    )
    dze_above = step_down(dze_bottom)
    dze_below = step_up(dze_top)
    (mat_e,) = call(
        part(second_conv_weights_kernel, sz),
        [out((9 * GW, C))],
        [two_scr, two_scr],
        act_d,
        dze,
        name="second_conv_weights",
    )
    dn_d, bst_d = call(
        part(second_conv_back_kernel, sz),
        [mat, st8],
        [two_scr, two_scr, two_scr, bd_scr, sum_scr],
        dze,
        dze_above,
        dze_below,
        k2,
        zd,
        nrm_d,
        name="second_conv_back",
        after=[mat_e],
    )
    bst_d_all = over_height(bst_d)
    dzd, dn_mid, bst_cs = call(
        part(middle_back_kernel, sz),
        [mat_low, mat, st8],
        [mat_scr, sum_scr],
        dn_d,
        zd,
        *bst_d_all,
        nrm_d,
        w2,
        dpre,
        pre_mid,
        zc,
        x,
        s1,
        nrm_c,
        nrm_b,
        name="middle_back",
    )
    bst_cs_all = over_height(bst_cs)
    spans = list(zip(ROW_BOUNDS[:-1], ROW_BOUNDS[1:]))
    early = EarlySum(shard_rows, place_ids)
    dzc, dzs, dqb, dg_b = call(
        part(gate_grad_kernel, sz, True),
        [mat_low, mat_low, mat, pool_low],
        [pool_scr, mat_scr],
        dn_mid,
        zc,
        *bst_cs_all,
        nrm_c,
        p1,
        zb,
        nrm_b,
        x,
        s1,
        nrm_b,
        name="gate_grad_b",
    )
    dg_b = over_height(dg_b)
    (mat_d,) = call(
        weight_kernel,
        [out((C, C))],
        [],
        mid_low,
        dzd,
        name="weight_d",
        after=[dzc],
    )
    (mat_c,) = call(
        weight_kernel, [out((C, C))], [], qb, dzc, name="weight_c"
    )
    (mat_s,) = call(
        weight_kernel, [out((CIN, C))], [], x, dzs, name="weight_s"
    )
    dn_b, bst_b, dv_b, du_b = call(
        part(excite_back_kernel, sz),
        [mat, st8, crop_mat, hid],
        [pool_scr, sum_scr],
        dqb,
        zb,
        nrm_b,
        *dg_b,
        gate_b,
        hidden_b,
        d1,
        u1,
        name="excite_back_b",
        after=[mat_d, mat_c, mat_s],
    )
    bst_b_all = over_height(bst_b)
    dd1, de1, du1, df1 = call(
        part(excite_weights_kernel, SE_A),
        se_outs(SE_A),
        se_scr,
        place_ids,
        dv_b,
        du_b,
        pooled_b,
        hidden_b,
        smem=1,
        name="excite_weights_b",
    )
    dzb, dzb_top = call(
        part(norm_back_kernel, sz),
        [mat_low, edge],
        [],
        dn_b,
        zb,
        *bst_b_all,
        nrm_b,
        name="norm_back_b",
        after=early.pack(spans[3:], [du1, mat_c, mat_s, mat_d, mat_e, dd2, du2, mat_f])
        if by_rows
        else [dd1],
    )
    dzb_below = step_up(dzb_top)
    (mat_b,) = call(
        part(first_conv_weights_kernel, sz),
        [out((9 * GW, C))],
        [low_scr, one_scr],
        *act_a,
        dzb,
        name="first_conv_weights",
    )
    hold = [mat_b]
    if by_rows:
        hold = hold + early.pack_first_unit(spans[1:4], [mat_b, dd1, du1], [])
    v0, v1, bd1 = call(
        part(first_conv_back_kernel, sz),
        [one_shape, one_shape, out((18, HALF, HALF), bf16)],
        [],
        dzb,
        dzb_below,
        k1,
        name="first_conv_back",
        after=hold,
    )
    dn_a, bst_a = [], []
    hold = [[], [], [], []]
    if by_rows:
        hold[0] = early.first([])
    for phase in range(4):
        dn_phase, *bst_a = call(
            part(parity_back_kernel, sz, phase),
            [mat_low, st8],
            [mat_scr, mat_scr, sum_scr],
            v0,
            v1,
            bd1,
            x,
            w1,
            nrm_a,
            *bst_a,
            name="parity_back_%d" % phase,
            after=hold[phase],
        )
        dn_a.append(dn_phase)
    (bst_a,) = bst_a
    bst_a_all = over_height(bst_a)
    hold = []
    if by_rows:
        hold = early.second([bst_a])
    (dza,) = call(
        part(image_norm_back_kernel, sz),
        [out((4 * m, C), bf16)],
        [pltpu.VMEM((4 * m, C), f32)],
        *dn_a,
        x,
        w1,
        *bst_a_all,
        nrm_a,
        name="image_norm_back",
        after=hold,
    )
    (mat_a,) = call(
        weight_kernel,
        [out((CIN, C))],
        [],
        x,
        dza,
        name="weight_a",

    )
    made = {}

    def image_product(beside):
        (made["dx"],) = call(
            part(image_product_kernel, sz),
            [out((4 * m, CIN))],
            [],
            dza,
            w1,
            dzs,
            s1,
            name="image_product",
            after=beside,
        )
        return [made["dx"]]

    def place_maps(key, shape, first_row, block, beside):
        n_crops, height, width = shape[:3]
        made[key], mark = call(
            part(place_kernel, n_crops, height, width, first_row, block, m),
            [out(shape), out((8, 128))],
            [pltpu.VMEM((6, height * width, 128), f32)] * 2,
            made["dx"],
            name="place_" + key,
            room=8 * 2**20,
            after=beside,
        )
        return [mark]

    work = [
        image_product,
        lambda beside: place_maps("glob", image_glob.shape, 0, sz.bg, beside),
        lambda beside: place_maps("loc", image_loc.shape, sz.mg, sz.bl, beside),
    ]
    if not by_rows:
        for one_work in work:
            one_work([])
    if by_rows:
        work[0] = lambda beside: early.height(image_product(beside))
        last = sum_first_matrix(shard_rows, mat_a, place_ids, work)
        shard_out = out((shard_rows, C))
        lines_out = out(w_lines.shape)
        new_first, new_second, update, sums = call(
            part(lamb_kernel, shard_rows),
            [lines_out, lines_out, shard_out, st8],
            [pltpu.VMEM((UNIT, C), f32)],
            place_ids,
            *early.result,
            *last,
            w_lines,
            m_lines,
            v_lines,
            smem=1,
            name="lamb",
        )
        (small,) = call(
            vector_grads_kernel,
            [out((VEC_ROWS + 8, C))],
            [],
            bst_a,
            bst_b,
            bst_cs,
            bst_d,
            bst_e,
            bst_f,
            de1,
            df1,
            de2,
            df2,
            sums,
            name="vector_grads",
        )
        small = small + across(small, 1)
        other_x, other_y, other_both = (across(small, mask) for mask in (2, 4, 6))
        small = (small + other_x) + (other_y + other_both)
        new_weights, new_v, new_vf, new_vs, norms = call(
            part(finish_kernel, shard_rows),
            [lines_out] + [out((LINES, 128))] * 3 + [out((8, 128))],
            [pltpu.VMEM((4, VEC_ROWS + 8, C), f32), pltpu.VMEM((LINES, 128), f32)],
            place_ids,
            *over_height(small),
            w_lines,
            update,
            *tables,
            smem=1,
            name="finish",
            room=2 * 2**20,
        )
        maps_out = (out_glob, out_loc, made["glob"], made["loc"])
        return maps_out + (
            new_weights.reshape(-1),
            new_first.reshape(-1),
            new_second.reshape(-1),
            from_lines(new_v),
            from_lines(new_vf),
            from_lines(new_vs),
            norms[:2, : len(MATRIX_ROWS)],
        )

    maps_out = (out_glob, out_loc, made["glob"], made["loc"])
    flat_grad = jnp.concatenate(
        [
            piece.reshape(-1)
            for piece in (
                mat_a,
                mat_b,
                dd1,
                du1[:SE_A],
                mat_c,
                mat_s,
                mat_d,
                mat_e,
                dd2,
                du2,
                mat_f,
            )
        ]
    )
    vec_grad = jnp.concatenate(
        [
            bst_a[1],
            bst_a[0],
            bst_b[1],
            bst_b[0],
            de1[0, :SE_A],
            df1[0],
            bst_cs[1],
            bst_cs[0],
            bst_cs[2],
            bst_cs[0],
            bst_d[1],
            bst_d[0],
            bst_e[1],
            bst_e[0],
            de2[0],
            df2[0],
            bst_f[1],
            bst_f[0],
        ]
    )
    grad_shard = lax.psum_scatter(flat_grad, both_axes, scatter_dimension=0, tiled=True)
    shard_len = weights.shape[0]
    device_index = lax.axis_index("batch") * n_height + lax.axis_index("height")
    position = device_index * shard_len + lax.iota(jnp.int32, shard_len)
    bounds = np.cumsum([0] + mat_lengths)
    lower_edge = jnp.asarray(bounds[:-1], jnp.int32)
    upper_edge = jnp.asarray(bounds[1:], jnp.int32)
    member = (
        (position[:, None] >= lower_edge[None, :]) & (position[:, None] < upper_edge[None, :])
    ).astype(f32)
    new_first, new_second, update = lamb_terms(
        weights, grad_shard, first_moment, second_moment, weight_decay
    )
    part_sums = jnp.dot(jnp.stack([weights * weights, update * update]), member, precision=highest)
    vec_total, totals = lax.psum((vec_grad, part_sums), both_axes)
    norm_pair = jnp.sqrt(totals)
    trust_ratio = learn_rate * (norm_pair[0] / norm_pair[1])
    new_weights = weights - jnp.dot(member, trust_ratio, precision=highest) * update
    vec_one_new, vec_two_new, vec_update = lamb_terms(vectors, vec_total, vec_first, vec_second, 0.0)
    vec_pieces = []
    for param_piece, update_piece in zip(
        cut_pieces(vectors, vector_sizes()), cut_pieces(vec_update, vector_sizes())
    ):
        ratio_val = jnp.sqrt(jnp.sum(param_piece * param_piece)) / jnp.sqrt(
            jnp.sum(update_piece * update_piece)
        )
        vec_pieces.append(param_piece - learn_rate * ratio_val * update_piece)
    new_vectors = jnp.concatenate(vec_pieces)
    return maps_out + (
        new_weights,
        new_first,
        new_second,
        new_vectors,
        vec_one_new,
        vec_two_new,
        norm_pair,
    )


def solution(mesh):
    maps = P("batch", "height", None, None)
    entries = P(("batch", "height"))
    return jax.shard_map(
        body,
        mesh=mesh,
        in_specs=(maps, maps, maps, maps, entries, entries, entries, P(), P(), P()),
        out_specs=(maps, maps, maps, maps, entries, entries, entries, P(), P(), P(), P()),
        check_vma=False,
    )
```
